32 devices in a mesh: docs: 2 (over y), ctx: 8 (over z, x), heads: 2 (over core).
Axes of the slice: x: 2, y: 2, z: 4, core: 2. Of those that a mesh axis runs over, the one named last changes fastest.
Arguments:
- queries_nope: bfloat16 [1536, 512], P(('docs', 'ctx'), 'heads'), parts along dimension 0, may hold values from -6 to 6
- queries_rope: bfloat16 [1536, 256], P(('docs', 'ctx'), 'heads'), parts along dimension 0, may hold values from -13 to 13
- latent: bfloat16 [1536, 512], P(('docs', 'ctx')), parts along dimension 0, may hold values from -6 to 6
- key_rope: bfloat16 [1536, 64], P(('docs', 'ctx')), parts along dimension 0, may hold values from -6 to 6
- key_up: bfloat16 [512, 512], P(None, 'heads'), may hold values from -0.25 to 0.25
- value_up: bfloat16 [512, 512], P(None, 'heads'), may hold values from -0.25 to 0.25
- out_proj: bfloat16 [512, 7168], P('heads'), may hold values from -0.25 to 0.25
- span_order: int32 [32], P('docs'), parts along dimension 0, may hold values from 0 to 15, as said below
Outputs:
- attn_out: bfloat16 [1536, 7168], P(('docs', 'ctx'), 'heads'), parts along dimension 0
The draws below stay inside these ranges and needn't reach their ends.
There are 2 independent parts, one for each index of `docs`. The reference program is written for one: setup_inputs(seed, part) draws one part's arguments, and reference() takes and returns one part's arrays. A program takes and returns all parts, laid end to end along the dimension named above; an argument that names none is the same for every part. Nothing has to cross between parts.
Inputs may be any that keep to these rules, and one draw needn't show every extreme that they name: `span_order`: a permutation of the spans in which entries 2 d and 2 d + 1 sum to 15.
All inputs are finite; a program needn't handle non-finite values.
Results may differ from the reference program's by a relative error of at most 0.01.
Values may be sent and summed in bfloat16 or wider, within the bound.
No kernel may reach another device: no remote copies, remote signals or barrier semaphores. Data moves between devices by JAX's collectives and lax.ppermute only.
A program may use at most 64 MiB of HBM per device.

```python
import math
import jax
import jax.numpy as jnp
from jax import lax

D = 7168
DC = 512
DH = 128
DR = 64
TOK_DEV = 96
SLOTS = 16
TOKENS = 768
HEADS = 4


def draw_key_rope(key, part):
    key = jax.random.fold_in(key, 11)
    drawn_draw = jnp.clip(jax.random.normal(key, (TOKENS, DR), jnp.float32), -6.0, 6.0)
    return drawn_draw.astype(jnp.bfloat16)


def draw_queries_rope(key, part):
    key = jax.random.fold_in(key, 12)
    drawn_draw = jnp.clip(jax.random.normal(key, (TOKENS, HEADS * DR), jnp.float32), -6.0, 6.0)
    return drawn_draw.astype(jnp.bfloat16)


def draw_span_order(key, part):
    key = jax.random.fold_in(key, 13)
    lower = jax.random.permutation(key, SLOTS // 2).astype(jnp.int32)
    paired = jnp.stack([lower, SLOTS - 1 - lower], axis=1)
    return paired.reshape(SLOTS).astype(jnp.int32)


def shard_levels(stream_key, dims, pieces, smallest, top_value):
    level, own = 1.0, jax.random.fold_in(stream_key, 6)
    for position, blocks in pieces:
        draws = jnp.exp(jax.random.uniform(jax.random.fold_in(own, position), (blocks,), jnp.float32, smallest / len(pieces), top_value / len(pieces)))
        level = level * jnp.repeat(draws, dims[position] // blocks).reshape([-1 if axis == position else 1 for axis in range(len(dims))])
    return level


def gaussian(own_key, extent, deviation, limit, split=(), kind=jnp.bfloat16):
    drawn = jax.random.normal(own_key, extent, jnp.float32) * deviation
    if len(split) > 0:
        drawn = shard_levels(own_key, extent, split, -0.22, 0.18) * drawn
    return jnp.clip(drawn, min=-limit, max=limit).astype(kind)


def setup_inputs(seed: int = 0, part: int = 0) -> dict:
    seeds = jax.random.split(jax.random.key(seed), 9)
    part_splits = jax.random.split(jax.random.fold_in(seeds[8], part), 9)
    queries_nope = gaussian(part_splits[0], (TOKENS, HEADS * DH), 1.0, 6.0, ((0, 8), (1, 2)))
    queries_rope = draw_queries_rope(jax.random.fold_in(jax.random.fold_in(seeds[8], part), 71), part)
    latent = gaussian(part_splits[2], (TOKENS, DC), 1.0, 6.0, ((0, 8),))
    key_rope = draw_key_rope(jax.random.fold_in(jax.random.fold_in(seeds[8], part), 71), part)
    key_up = gaussian(seeds[4], (DC, HEADS * DH), DC ** -0.5, 0.25, ((1, 2),))
    value_up = gaussian(seeds[5], (DC, HEADS * DH), DC ** -0.5, 0.25, ((1, 2),))
    out_proj = gaussian(seeds[6], (HEADS * DH, D), (HEADS * DH) ** -0.5, 0.25, ((0, 2),))
    span_order = draw_span_order(jax.random.fold_in(jax.random.fold_in(seeds[8], part), 71), part)
    return {"queries_nope": queries_nope, "queries_rope": queries_rope, "latent": latent, "key_rope": key_rope, "key_up": key_up, "value_up": value_up, "out_proj": out_proj, "span_order": span_order}


def reference(queries_nope, queries_rope, latent, key_rope, key_up, value_up, out_proj, span_order):
    precise = lax.Precision.HIGHEST
    span_rows = TOK_DEV // 2
    row_ids = jnp.arange(TOKENS, dtype=jnp.int32)
    positions = jnp.take(span_order, row_ids // span_rows) * span_rows + row_ids % span_rows
    key_up_heads = key_up.astype(jnp.float32).reshape(DC, HEADS, DH)
    value_heads = value_up.astype(jnp.float32).reshape(DC, HEADS, DH)
    nope_all = queries_nope.astype(jnp.float32).reshape(TOKENS, HEADS, DH)
    query_latent = jnp.einsum('qhd,chd->qhc', nope_all, key_up_heads, precision=precise).astype(jnp.bfloat16)
    query_latent = query_latent.astype(jnp.float32)
    rope_all = queries_rope.astype(jnp.float32).reshape(TOKENS, HEADS, DR)
    latent_all = latent.astype(jnp.float32)
    key_rope_all = key_rope.astype(jnp.float32)
    score_scale = 1.0 / math.sqrt(DH + DR)
    block_rows = math.gcd(TOKENS, 512)

    def attend(block_index):
        first_row = (block_index * block_rows).astype(jnp.int32)
        latent_block = lax.dynamic_slice_in_dim(query_latent, first_row, block_rows, 0)
        rope_block = lax.dynamic_slice_in_dim(rope_all, first_row, block_rows, 0)
        query_pos = lax.dynamic_slice_in_dim(positions, first_row, block_rows, 0)
        scores = jnp.einsum('qhc,kc->hqk', latent_block, latent_all, precision=precise)
        scores = scores + jnp.einsum('qhr,kr->hqk', rope_block, key_rope_all, precision=precise)
        scores = scores * score_scale
        allowed = positions[None, None, :] <= query_pos[None, :, None]
        top_score = lax.optimization_barrier(jnp.max(jnp.where(allowed, scores, jnp.float32(-1e+30)), axis=-1))
        exponent = jnp.where(allowed, jnp.exp(scores - top_score[:, :, None]), jnp.float32(0.0))
        row_total = lax.optimization_barrier(jnp.sum(exponent, axis=-1))
        rounded = lax.optimization_barrier(exponent.astype(jnp.bfloat16))
        summed = jnp.einsum('hqk,kc->qhc', rounded.astype(jnp.float32), latent_all, precision=precise)
        return (summed / row_total.T[:, :, None]).astype(jnp.bfloat16)
    blocks = lax.map(attend, jnp.arange(TOKENS // block_rows, dtype=jnp.int32))
    context = blocks.reshape(TOKENS, HEADS, DC).astype(jnp.float32)
    per_head = jnp.einsum('qhc,chd->qhd', context, value_heads, precision=precise)
    heads_out = per_head.reshape(TOKENS, HEADS * DH).astype(jnp.bfloat16)
    return jnp.dot(heads_out, out_proj, preferred_element_type=jnp.float32).astype(jnp.bfloat16)
```

```python
import functools
import math

import jax
import jax.numpy as jnp
from jax import lax
from jax.experimental import pallas as pl
from jax.experimental.pallas import tpu as pltpu
from jax.sharding import PartitionSpec as P

DC = 512
DH = 128
DR = 64
BF16 = jnp.bfloat16
F32 = jnp.float32
SMALL_VMEM = 20 * 1024 * 1024
LARGE_VMEM = 56 * 1024 * 1024
DIRECT_LIMIT = 8
BLOCK_CHUNKS = 8


def vmem():
    return pl.BlockSpec(memory_space=pltpu.VMEM)


def smem():
    return pl.BlockSpec(memory_space=pltpu.SMEM)


def query_kernel(nope_own, nope_other, rope_own, rope_other, up_own, up_other, out_ref):
    rows = nope_own.shape[0]
    heads = nope_own.shape[1] // DH
    for group, (nope, rope, up) in enumerate(
        ((nope_own, rope_own, up_own), (nope_other, rope_other, up_other))
    ):
        for head in range(heads):
            part = pl.ds((group * heads + head) * rows, rows)
            latent = lax.dot_general(
                nope[:, head * DH : (head + 1) * DH],
                up[:, head * DH : (head + 1) * DH],
                (((1,), (1,)), ((), ())),
                preferred_element_type=F32,
            )
            out_ref[part, :DC] = latent.astype(BF16)
            out_ref[part, DC:] = rope[:, head * DR : (head + 1) * DR]


def attend_kernel(
    chunks, blocks, direct, place, span_order, queries, latent, key_rope, *rest
):
    if direct:
        near = rest[: chunks - 1]
        far = rest[chunks - 1 : 2 * chunks - 2]
        rest = rest[2 * chunks - 2 :]
    else:
        near, far = rest[:2]
        rest = rest[2:]
    (value_own, value_other, proj_own, proj_other, out_ref) = rest[:5]
    keys, running_max, running_sum, context, heads_out = rest[5:]
    rows = latent.shape[0]
    span_rows = rows // 2
    query_rows = queries.shape[0]
    copies = query_rows // rows
    block_rows = keys.shape[0]
    own_index = place[0]
    core = place[1]
    scale = math.log2(math.e) / math.sqrt(DH + DR)

    @pl.when(pl.program_id(0) == 0)
    def attention():
        row = lax.broadcasted_iota(jnp.int32, (rows, 1), 0)
        query_pos = jnp.where(
            row < span_rows,
            span_order[2 * own_index] * span_rows + row,
            span_order[2 * own_index + 1] * span_rows + row - span_rows,
        )
        query_pos = jnp.concatenate([query_pos] * copies, axis=0)
        column = lax.broadcasted_iota(jnp.int32, (1, block_rows), 1)

        def one_block(block, first):
            key_pos = jnp.zeros((1, block_rows), jnp.int32)
            for index in range(block_rows // rows):
                base = index * rows
                if direct:
                    owner = own_index ^ index
                else:
                    owner = block * (block_rows // rows) + index
                for side in range(2):
                    start = base + side * span_rows
                    if direct and index == 0:
                        span = 2 * owner + side
                        keys[pl.ds(start, span_rows), :DC] = latent[pl.ds(side * span_rows, span_rows), :]
                        keys[pl.ds(start, span_rows), DC:] = key_rope[pl.ds(side * span_rows, span_rows), :]
                    else:
                        span = 2 * owner + (core if side == 0 else 1 - core)
                        source = (near, far)[side]
                        if direct:
                            keys[pl.ds(start, span_rows), :] = source[index - 1][...]
                        else:
                            keys[pl.ds(start, span_rows), :] = source[owner]
                    key_pos = jnp.where(
                        column >= start, span_order[span] * span_rows + column - start, key_pos
                    )
            scores = lax.dot_general(
                queries[...], keys[...], (((1,), (1,)), ((), ())), preferred_element_type=F32
            )
            allowed = key_pos <= query_pos
            scores = jnp.where(allowed, scores, F32(-1e30))
            top = jnp.max(scores, axis=-1, keepdims=True)
            if not first:
                old = running_max[...]
                top = jnp.maximum(old, top)
                rescale = jnp.exp2((old - top) * scale)
            expo = jnp.where(allowed, jnp.exp2((scores - top) * scale), F32(0.0))
            total = jnp.sum(expo, axis=-1, keepdims=True)
            added = jnp.dot(expo.astype(BF16), keys[:, :DC], preferred_element_type=F32)
            if not first:
                total = running_sum[...] * rescale + total
                added = context[...] * rescale + added
            return top, total, added

        if blocks == 1:
            top, total, added = one_block(0, True)
        else:
            running_max[...] = jnp.full(running_max.shape, -1e30, F32)
            running_sum[...] = jnp.zeros(running_sum.shape, F32)
            context[...] = jnp.zeros(context.shape, F32)

            def step(block, carry):
                top, total, added = one_block(block, False)
                running_max[...] = top
                running_sum[...] = total
                context[...] = added
                return carry

            lax.fori_loop(0, blocks, step, 0)
            total, added = running_sum[...], context[...]
        mixed = (added / total).astype(BF16)
        heads = value_own.shape[1] // DH
        for group, value in enumerate((value_own, value_other)):
            for head in range(heads):
                place_of = group * heads + head
                per_head = jnp.dot(
                    mixed[place_of * rows : (place_of + 1) * rows],
                    value[:, head * DH : (head + 1) * DH],
                    preferred_element_type=F32,
                )
                heads_out[:, place_of * DH : (place_of + 1) * DH] = per_head.astype(BF16)

    width = heads_out.shape[1] // 2
    out = jnp.dot(heads_out[:, :width], proj_own[...], preferred_element_type=F32)
    out = out + jnp.dot(heads_out[:, width:], proj_other[...], preferred_element_type=F32)
    out_ref[...] = out.astype(BF16)


def per_device(
    chunks, queries_nope, queries_rope, latent, key_rope, key_up, value_up, out_proj, span_order
):
    rows = latent.shape[0]
    span_rows = rows // 2
    width = out_proj.shape[1] // 2
    own_index = lax.axis_index("ctx")
    core = lax.axis_index("heads")
    place = jnp.stack([own_index, core]).astype(jnp.int32)
    direct = chunks <= DIRECT_LIMIT and chunks & (chunks - 1) == 0

    def other_core(array):
        return lax.ppermute(array, "heads", [(0, 1), (1, 0)])

    packed = jnp.concatenate([latent, key_rope], axis=1)
    packed = lax.dynamic_slice_in_dim(packed, core * span_rows, span_rows, 0)
    if direct:
        near = [
            lax.ppermute(packed, "ctx", [(index, index ^ step) for index in range(chunks)])
            for step in range(1, chunks)
        ]
        far = [other_core(chunk) for chunk in near]
        blocks, block_chunks = 1, chunks
    else:
        near = [lax.all_gather(packed, "ctx", axis=0)]
        far = [other_core(near[0])]
        block_chunks = math.gcd(chunks, BLOCK_CHUNKS)
        blocks = chunks // block_chunks
    nope_other = other_core(queries_nope)
    rope_other = other_core(queries_rope)
    up_other = other_core(key_up)
    value_other = other_core(value_up)
    proj_other = other_core(lax.dynamic_slice_in_dim(out_proj, (1 - core) * width, width, 1))

    heads = 2 * (key_up.shape[1] // DH)
    query_rows = heads * rows
    queries = pl.pallas_call(
        query_kernel,
        out_shape=jax.ShapeDtypeStruct((query_rows, DC + DR), BF16),
        in_specs=[vmem()] * 6,
        out_specs=vmem(),
        compiler_params=pltpu.CompilerParams(vmem_limit_bytes=SMALL_VMEM),
        name="queries",
    )(queries_nope, nope_other, queries_rope, rope_other, key_up, up_other)

    tile = width // 4 if width % 512 == 0 else width
    tiles = width // tile
    block_rows = block_chunks * rows
    several = blocks > 1
    grid_spec = pltpu.PrefetchScalarGridSpec(
        num_scalar_prefetch=2,
        grid=(tiles,),
        in_specs=[vmem()] * (3 + len(near) + len(far) + 2)
        + [
            pl.BlockSpec((out_proj.shape[0], tile), lambda t, place, order: (0, place[1] * tiles + t)),
            pl.BlockSpec((out_proj.shape[0], tile), lambda t, place, order: (0, t)),
        ],
        out_specs=pl.BlockSpec((rows, tile), lambda t, place, order: (0, t)),
        scratch_shapes=[
            pltpu.VMEM((block_rows, DC + DR), BF16),
            pltpu.VMEM((query_rows, 1) if several else (8, 128), F32),
            pltpu.VMEM((query_rows, 1) if several else (8, 128), F32),
            pltpu.VMEM((query_rows, DC) if several else (8, 128), F32),
            pltpu.VMEM((rows, heads * DH), BF16),
        ],
    )
    return pl.pallas_call(
        functools.partial(attend_kernel, chunks, blocks, direct),
        out_shape=jax.ShapeDtypeStruct((rows, width), BF16),
        grid_spec=grid_spec,
        compiler_params=pltpu.CompilerParams(vmem_limit_bytes=SMALL_VMEM if direct else LARGE_VMEM),
        name="attend",
    )(
        place,
        span_order,
        queries,
        latent,
        key_rope,
        *near,
        *far,
        value_up,
        value_other,
        out_proj,
        proj_other,
    )


def solution(mesh):
    in_specs = (
        P(("docs", "ctx"), "heads"),
        P(("docs", "ctx"), "heads"),
        P(("docs", "ctx"), None),
        P(("docs", "ctx"), None),
        P(None, "heads"),
        P(None, "heads"),
        P("heads", None),
        P("docs"),
    )
    out_specs = P(("docs", "ctx"), "heads")
    return jax.shard_map(
        functools.partial(per_device, mesh.shape["ctx"]),
        mesh=mesh,
        in_specs=in_specs,
        out_specs=out_specs,
        check_vma=False,
    )
```

```python
import functools
import math

import jax
import jax.numpy as jnp
from jax import lax
from jax.experimental import pallas as pl
from jax.experimental.pallas import tpu as pltpu
from jax.sharding import PartitionSpec as P

DC = 512
DH = 128
DR = 64
BF16 = jnp.bfloat16
F32 = jnp.float32
SMALL_VMEM = 20 * 1024 * 1024
LARGE_VMEM = 56 * 1024 * 1024
DIRECT_LIMIT = 8
BLOCK_CHUNKS = 8


def vmem():
    return pl.BlockSpec(memory_space=pltpu.VMEM)


def smem():
    return pl.BlockSpec(memory_space=pltpu.SMEM)


def query_kernel(nope_own, nope_other, rope_own, rope_other, up_own, up_other, out_ref):
    rows = nope_own.shape[0]
    heads = nope_own.shape[1] // DH
    for group, (nope, rope, up) in enumerate(
        ((nope_own, rope_own, up_own), (nope_other, rope_other, up_other))
    ):
        for head in range(heads):
            part = pl.ds((group * heads + head) * rows, rows)
            latent = lax.dot_general(
                nope[:, head * DH : (head + 1) * DH],
                up[:, head * DH : (head + 1) * DH],
                (((1,), (1,)), ((), ())),
                preferred_element_type=F32,
            )
            out_ref[part, :DC] = latent.astype(BF16)
            out_ref[part, DC:] = rope[:, head * DR : (head + 1) * DR]


def attend_kernel(
    blocks, place, span_order, queries, *rest
):
    near, far, value_own, value_other, proj, out_ref = rest[:6]
    keys, running_max, running_sum, context, heads_out = rest[6:]
    rows = out_ref.shape[0]
    span_rows = near.shape[1]
    query_rows = queries.shape[0]
    copies = query_rows // rows
    block_rows = keys.shape[0]
    own_index = place[0]
    core = place[1]
    scale = math.log2(math.e) / math.sqrt(DH + DR)

    @pl.when(pl.program_id(0) == 0)
    def attention():
        row = lax.broadcasted_iota(jnp.int32, (rows, 1), 0)
        query_pos = jnp.where(
            row < span_rows,
            span_order[2 * own_index] * span_rows + row,
            span_order[2 * own_index + 1] * span_rows + row - span_rows,
        )
        query_pos = jnp.concatenate([query_pos] * copies, axis=0)
        column = lax.broadcasted_iota(jnp.int32, (1, block_rows), 1)

        def one_block(block, first):
            key_pos = jnp.zeros((1, block_rows), jnp.int32)
            for index in range(block_rows // rows):
                base = index * rows
                owner = block * (block_rows // rows) + index
                for side in range(2):
                    start = base + side * span_rows
                    span = 2 * owner + (core if side == 0 else 1 - core)
                    keys[pl.ds(start, span_rows), :] = (near, far)[side][owner]
                    key_pos = jnp.where(
                        column >= start, span_order[span] * span_rows + column - start, key_pos
                    )
            scores = lax.dot_general(
                queries[...], keys[...], (((1,), (1,)), ((), ())), preferred_element_type=F32
            )
            allowed = key_pos <= query_pos
            scores = jnp.where(allowed, scores, F32(-1e30))
            top = jnp.max(scores, axis=-1, keepdims=True)
            if not first:
                old = running_max[...]
                top = jnp.maximum(old, top)
                rescale = jnp.exp2((old - top) * scale)
            expo = jnp.where(allowed, jnp.exp2((scores - top) * scale), F32(0.0))
            total = jnp.sum(expo, axis=-1, keepdims=True)
            added = jnp.dot(expo.astype(BF16), keys[:, :DC], preferred_element_type=F32)
            if not first:
                total = running_sum[...] * rescale + total
                added = context[...] * rescale + added
            return top, total, added

        if blocks == 1:
            top, total, added = one_block(0, True)
        else:
            running_max[...] = jnp.full(running_max.shape, -1e30, F32)
            running_sum[...] = jnp.zeros(running_sum.shape, F32)
            context[...] = jnp.zeros(context.shape, F32)

            def step(block, carry):
                top, total, added = one_block(block, False)
                running_max[...] = top
                running_sum[...] = total
                context[...] = added
                return carry

            lax.fori_loop(0, blocks, step, 0)
            total, added = running_sum[...], context[...]
        mixed = (added / total).astype(BF16)
        heads = value_own.shape[1] // DH
        for group, value in enumerate((value_own, value_other)):
            for head in range(heads):
                place_of = group * heads + head
                per_head = jnp.dot(
                    mixed[place_of * rows : (place_of + 1) * rows],
                    value[:, head * DH : (head + 1) * DH],
                    preferred_element_type=F32,
                )
                target = (core ^ group) * heads * DH + head * DH
                heads_out[:, pl.ds(pl.multiple_of(target, DH), DH)] = per_head.astype(BF16)

    out = jnp.dot(heads_out[...], proj[...], preferred_element_type=F32)
    out_ref[...] = out.astype(BF16)


def per_device(
    chunks, queries_nope, queries_rope, latent, key_rope, key_up, value_up, out_proj, span_order
):
    rows = latent.shape[0]
    span_rows = rows // 2
    width = out_proj.shape[1] // 2
    own_index = lax.axis_index("ctx")
    core = lax.axis_index("heads")
    place = jnp.stack([own_index, core]).astype(jnp.int32)
    direct = chunks <= DIRECT_LIMIT and chunks & (chunks - 1) == 0

    def other_core(array):
        return lax.ppermute(array, "heads", [(0, 1), (1, 0)])

    packed = jnp.concatenate([latent, key_rope], axis=1)
    packed = lax.dynamic_slice_in_dim(packed, core * span_rows, span_rows, 0)
    if direct:
        copies = jnp.broadcast_to(packed, (chunks, *packed.shape))
        near = lax.all_to_all(copies, "ctx", 0, 0)
        blocks, block_chunks = 1, chunks
    else:
        near = lax.all_gather(packed, "ctx", axis=0)
        block_chunks = math.gcd(chunks, BLOCK_CHUNKS)
        blocks = chunks // block_chunks
    far = other_core(near)
    nope_other = other_core(queries_nope)
    rope_other = other_core(queries_rope)
    up_other = other_core(key_up)
    value_other = other_core(value_up)
    proj = lax.all_to_all(out_proj, "heads", 1, 0, tiled=True)

    heads = 2 * (key_up.shape[1] // DH)
    query_rows = heads * rows
    queries = pl.pallas_call(
        query_kernel,
        out_shape=jax.ShapeDtypeStruct((query_rows, DC + DR), BF16),
        in_specs=[vmem()] * 6,
        out_specs=vmem(),
        compiler_params=pltpu.CompilerParams(vmem_limit_bytes=SMALL_VMEM),
        name="queries",
    )(queries_nope, nope_other, queries_rope, rope_other, key_up, up_other)

    tile = width // 4 if width % 512 == 0 else width
    tiles = width // tile
    block_rows = block_chunks * rows
    several = blocks > 1
    grid_spec = pltpu.PrefetchScalarGridSpec(
        num_scalar_prefetch=2,
        grid=(tiles,),
        in_specs=[vmem()] * 5
        + [pl.BlockSpec((proj.shape[0], tile), lambda t, place, order: (0, t))],
        out_specs=pl.BlockSpec((rows, tile), lambda t, place, order: (0, t)),
        scratch_shapes=[
            pltpu.VMEM((block_rows, DC + DR), BF16),
            pltpu.VMEM((query_rows, 1) if several else (8, 128), F32),
            pltpu.VMEM((query_rows, 1) if several else (8, 128), F32),
            pltpu.VMEM((query_rows, DC) if several else (8, 128), F32),
            pltpu.VMEM((rows, heads * DH), BF16),
        ],
    )
    return pl.pallas_call(
        functools.partial(attend_kernel, blocks),
        out_shape=jax.ShapeDtypeStruct((rows, width), BF16),
        grid_spec=grid_spec,
        compiler_params=pltpu.CompilerParams(vmem_limit_bytes=SMALL_VMEM if direct else LARGE_VMEM),
        name="attend",
    )(
        place,
        span_order,
        queries,
        near,
        far,
        value_up,
        value_other,
        proj,
    )


def solution(mesh):
    in_specs = (
        P(("docs", "ctx"), "heads"),
        P(("docs", "ctx"), "heads"),
        P(("docs", "ctx"), None),
        P(("docs", "ctx"), None),
        P(None, "heads"),
        P(None, "heads"),
        P("heads", None),
        P("docs"),
    )
    out_specs = P(("docs", "ctx"), "heads")
    return jax.shard_map(
        functools.partial(per_device, mesh.shape["ctx"]),
        mesh=mesh,
        in_specs=in_specs,
        out_specs=out_specs,
        check_vma=False,
    )
```

```python
import functools
import math

import jax
import jax.numpy as jnp
from jax import lax
from jax.experimental import pallas as pl
from jax.experimental.pallas import tpu as pltpu
from jax.sharding import PartitionSpec as P

DC = 512
DH = 128
DR = 64
BF16 = jnp.bfloat16
F32 = jnp.float32
MASKED = -1e30
SMALL_VMEM = 20 * 1024 * 1024
LARGE_VMEM = 56 * 1024 * 1024
FAR = (4, 6)
NEAR = (2, 3)
BESIDE = (1, 1)
RELAYED = (5, 7)


def vmem():
    return pl.BlockSpec(memory_space=pltpu.VMEM)


def anywhere():
    return pl.BlockSpec(memory_space=pl.ANY)


def hbm():
    return pl.BlockSpec(memory_space=pltpu.HBM)


def smem():
    return pl.BlockSpec(memory_space=pltpu.SMEM)


def pack_kernel(latent, key_rope, out_ref):
    out_ref[:, :DC] = latent[...]
    out_ref[:, DC:] = key_rope[...].astype(F32).T.astype(BF16)


def bundle_kernel(packed, nope, rope, key_up, value_up, out_proj, small_ref, proj_ref, sems):
    core = lax.axis_index("heads")
    width = proj_ref.shape[1]
    base = pl.multiple_of((1 - core) * width, 128)
    copies = [pltpu.make_async_copy(out_proj.at[:, pl.ds(base, width)], proj_ref, sems.at[0])]
    row = 0
    for index, part in enumerate((key_up, value_up, nope, rope)):
        target = small_ref.at[pl.ds(row, part.shape[0]), pl.ds(0, part.shape[1])]
        copies.append(pltpu.make_async_copy(part, target, sems.at[1 + index]))
        row += part.shape[0]
    for copy in copies:
        copy.start()
    for copy in copies:
        copy.wait()


def query_kernel(order, span_order, nope_own, rope_own, up_own, other, out_ref, bias_ref):
    rows = nope_own.shape[0]
    heads = nope_own.shape[1] // DH
    span_rows = rows // 2
    own_index = lax.axis_index("ctx")
    core = lax.axis_index("heads")
    up_other = other.at[pl.ds(0, DC)]
    nope_other = other.at[pl.ds(2 * DC, rows)]
    rope_other = other.at[pl.ds(2 * DC + rows, rows)]
    for group, (nope, rope, up) in enumerate(
        ((nope_own, rope_own, up_own), (nope_other, rope_other, up_other))
    ):
        for head in range(heads):
            part = pl.ds((group * heads + head) * rows, rows)
            latent = lax.dot_general(
                nope[:, head * DH : (head + 1) * DH],
                up[:, head * DH : (head + 1) * DH],
                (((1,), (1,)), ((), ())),
                preferred_element_type=F32,
            )
            out_ref[part, :DC] = latent.astype(BF16)
            out_ref[part, DC:] = rope[:, head * DR : (head + 1) * DR]
    block_rows = 8 * rows
    row = lax.broadcasted_iota(jnp.int32, (rows, 1), 0)
    query_pos = jnp.where(
        row < span_rows,
        span_order[2 * own_index] * span_rows + row,
        span_order[2 * own_index + 1] * span_rows + row - span_rows,
    )
    column = lax.broadcasted_iota(jnp.int32, (1, block_rows), 1)

    def bias_block(block):
        key_pos = jnp.zeros((1, block_rows), jnp.int32)
        for index in range(8):
            if order is None:
                owner = block * 8 + index
            else:
                owner = own_index ^ jnp.where(core == 0, order[index][0], order[index][1])
            for side in range(2):
                start = index * rows + side * span_rows
                first = span_order[2 * owner + side] * span_rows
                key_pos = jnp.where(column >= start, first + column - start, key_pos)
        return jnp.where(key_pos <= query_pos, F32(0.0), F32(MASKED))

    if order is not None:
        bias_ref[0] = bias_block(0)
    else:

        def step(block, carry):
            bias_ref[block] = bias_block(block)
            return carry

        lax.fori_loop(0, bias_ref.shape[0], step, 0)


def attend_kernel(chunk_count, queries, bias, *rest):
    chunks = rest[:chunk_count]
    value_own, other, proj_own, proj_other, out_ref = rest[chunk_count : chunk_count + 5]
    scratch = rest[chunk_count + 5 :]
    proj, out_tiles, proj_sems, out_sems = scratch[:4]
    blocks, rows, block_rows = bias.shape
    copies = queries.shape[0] // rows
    half = proj_own.shape[0]
    width = out_ref.shape[1]
    core = lax.axis_index("heads")
    scale = math.log2(math.e) / math.sqrt(DH + DR)

    base = pl.multiple_of(core * width, 128)
    fetches = (
        pltpu.make_async_copy(
            proj_own.at[:, pl.ds(base, width)], proj.at[pl.ds(0, half)], proj_sems.at[0]
        ),
        pltpu.make_async_copy(proj_other, proj.at[pl.ds(half, half)], proj_sems.at[1]),
    )
    for fetch in fetches:
        fetch.start()

    def one_block(keys, bias_block, old):
        scores = lax.dot_general(
            queries[...], keys[...], (((1,), (1,)), ((), ())), preferred_element_type=F32
        )
        scores = scores + jnp.concatenate([bias_block] * copies, axis=0)
        top = jnp.max(scores, axis=-1, keepdims=True)
        if old is not None:
            top = jnp.maximum(old[0], top)
            rescale = jnp.exp2((old[0] - top) * scale)
            scores = jnp.where(scores > 0.5 * MASKED, scores, 2.0 * MASKED)
        expo = jnp.exp2((scores - top) * scale)
        total = jnp.sum(expo, axis=-1, keepdims=True)
        added = jnp.dot(expo.astype(BF16), keys[:, :DC], preferred_element_type=F32)
        if old is not None:
            total = old[1] * rescale + total
            added = old[2] * rescale + added
        return top, total, added

    if blocks == 1:
        keys = scratch[4]
        for index, chunk in enumerate(chunks):
            keys[pl.ds(index * rows, rows), :] = chunk[...]
        top, total, added = one_block(keys, bias[0], None)
    else:
        running = scratch[4:7]
        running[0][...] = jnp.full(running[0].shape, MASKED, F32)
        running[1][...] = jnp.zeros(running[1].shape, F32)
        running[2][...] = jnp.zeros(running[2].shape, F32)

        def step(block, carry):
            keys = chunks[0].at[pl.ds(pl.multiple_of(block * block_rows, block_rows), block_rows)]
            new = one_block(keys, bias[block], [state[...] for state in running])
            for state, value in zip(running, new):
                state[...] = value
            return carry

        lax.fori_loop(0, blocks, step, 0)
        total, added = running[1][...], running[2][...]
    mixed = (added / total).astype(BF16)
    heads = value_own.shape[1] // DH
    parts = []
    for group, value in enumerate((value_own, other.at[pl.ds(DC, DC)])):
        for head in range(heads):
            first = (group * heads + head) * rows
            per_head = jnp.dot(
                mixed[first : first + rows],
                value[:, head * DH : (head + 1) * DH],
                preferred_element_type=F32,
            )
            parts.append(per_head.astype(BF16))
    heads_out = jnp.concatenate(parts, axis=1)

    for fetch in fetches:
        fetch.wait()
    tiles = out_sems.shape[0]
    tile = width // tiles
    sends = []
    for index in range(tiles):
        part = pl.ds(index * tile, tile)
        out = jnp.dot(heads_out, proj[:, part], preferred_element_type=F32)
        out_tiles[:, part] = out.astype(BF16)
        sends.append(
            pltpu.make_async_copy(out_tiles.at[:, part], out_ref.at[:, part], out_sems.at[index])
        )
        sends[-1].start()
    for send in sends:
        send.wait()


def per_device(
    count, queries_nope, queries_rope, latent, key_rope, key_up, value_up, out_proj, span_order
):
    rows = latent.shape[0]
    width = out_proj.shape[1] // 2
    heads = 2 * (key_up.shape[1] // DH)
    query_rows = heads * rows
    direct = count == 8
    small = pltpu.CompilerParams(vmem_limit_bytes=SMALL_VMEM)

    def in_hbm(*arrays):
        return [pltpu.with_memory_space_constraint(array, pltpu.HBM) for array in arrays]

    def other_core(array):
        return lax.ppermute(array, "heads", [(0, 1), (1, 0)])

    def partners(array, steps):
        pairs = [
            (2 * index + core, 2 * (index ^ steps[core]) + core)
            for index in range(count)
            for core in range(2)
        ]
        return lax.ppermute(array, ("ctx", "heads"), pairs)

    packed = pl.pallas_call(
        pack_kernel,
        out_shape=jax.ShapeDtypeStruct((rows, DC + DR), BF16),
        in_specs=[vmem()] * 2,
        out_specs=vmem(),
        compiler_params=small,
        name="pack",
    )(*in_hbm(latent, key_rope.T))
    if direct:
        far = partners(packed, FAR)
        near = partners(packed, NEAR)
        beside = partners(packed, BESIDE)
        relayed = partners(far, (1, 1))
        chunks = [packed, beside]
        order = [(0, 0), BESIDE]
        for chunk, steps in ((near, NEAR), (far, FAR), (relayed, RELAYED)):
            chunks += [chunk, other_core(chunk)]
            order += [steps, steps[::-1]]
        blocks = 1
    else:
        chunks = [lax.all_gather(packed, "ctx", axis=0, tiled=True)]
        order = None
        blocks = count // 8

    small_rows = 2 * DC + 2 * rows
    bundle, proj_bundle = pl.pallas_call(
        bundle_kernel,
        out_shape=(
            jax.ShapeDtypeStruct((small_rows, key_up.shape[1]), BF16),
            jax.ShapeDtypeStruct((out_proj.shape[0], width), BF16),
        ),
        in_specs=[anywhere()] + [hbm()] * 5,
        out_specs=(anywhere(), anywhere()),
        scratch_shapes=[pltpu.SemaphoreType.DMA((5,))],
        compiler_params=small,
        name="bundle",
    )(packed, *in_hbm(queries_nope, queries_rope, key_up, value_up, out_proj))
    other = other_core(bundle)
    proj_other = other_core(proj_bundle)

    queries, bias = pl.pallas_call(
        functools.partial(query_kernel, order),
        out_shape=(
            jax.ShapeDtypeStruct((query_rows, DC + DR), BF16),
            jax.ShapeDtypeStruct((blocks, rows, 8 * rows), F32),
        ),
        in_specs=[smem()] + [vmem()] * 4,
        out_specs=(vmem(), vmem()),
        compiler_params=small,
        name="queries",
    )(span_order, queries_nope, queries_rope, key_up, other)

    tiles = 4 if width % 512 == 0 else 1
    scratch = [
        pltpu.VMEM((2 * out_proj.shape[0], width), BF16),
        pltpu.VMEM((rows, width), BF16),
        pltpu.SemaphoreType.DMA((2,)),
        pltpu.SemaphoreType.DMA((tiles,)),
    ]
    if direct:
        scratch.append(pltpu.VMEM((count * rows, DC + DR), BF16))
    else:
        scratch += [pltpu.VMEM((query_rows, size), F32) for size in (1, 1, DC)]
    return pl.pallas_call(
        functools.partial(attend_kernel, len(chunks)),
        out_shape=jax.ShapeDtypeStruct((rows, width), BF16),
        in_specs=[vmem()] * (2 + len(chunks) + 2) + [hbm(), anywhere()],
        out_specs=anywhere(),
        scratch_shapes=scratch,
        compiler_params=pltpu.CompilerParams(
            vmem_limit_bytes=SMALL_VMEM if direct else LARGE_VMEM
        ),
        name="attend",
    )(queries, bias, *chunks, value_up, other, *in_hbm(out_proj), proj_other)


def solution(mesh):
    in_specs = (
        P(("docs", "ctx"), "heads"),
        P(("docs", "ctx"), "heads"),
        P(("docs", "ctx"), None),
        P(("docs", "ctx"), None),
        P(None, "heads"),
        P(None, "heads"),
        P("heads", None),
        P("docs"),
    )
    out_specs = P(("docs", "ctx"), "heads")
    return jax.shard_map(
        functools.partial(per_device, mesh.shape["ctx"]),
        mesh=mesh,
        in_specs=in_specs,
        out_specs=out_specs,
        check_vma=False,
    )
```

```python
import functools
import math

import jax
import jax.numpy as jnp
from jax import lax
from jax.experimental import pallas as pl
from jax.experimental.pallas import tpu as pltpu
from jax.sharding import PartitionSpec as P

DC = 512
DH = 128
DR = 64
BF16 = jnp.bfloat16
F32 = jnp.float32
MASKED = -1e30
BLOCK_CHUNKS = 8
CUT_COST, QUERY_COST, EARLY_COST = 0, 0, 30
SMALL_VMEM = 20 * 1024 * 1024
LARGE_VMEM = 56 * 1024 * 1024
FAR = (4, 6)
NEAR = (2, 3)
BESIDE = (1, 1)
RELAYED = (5, 7)


def vmem():
    return pl.BlockSpec(memory_space=pltpu.VMEM)


def anywhere():
    return pl.BlockSpec(memory_space=pl.ANY)


def hbm():
    return pl.BlockSpec(memory_space=pltpu.HBM)


def cost(microseconds):
    return pl.CostEstimate(flops=int(microseconds * 1.1e9), bytes_accessed=0, transcendentals=0)


def smem():
    return pl.BlockSpec(memory_space=pltpu.SMEM)


def pack_kernel(latent, key_rope_turned, out_ref):
    rows = latent.shape[0]
    group = rows // 6
    out_ref[:rows] = latent[...]
    rope = key_rope_turned[...].astype(F32).T.astype(BF16)
    parts = [rope[index * group : (index + 1) * group] for index in range(6)]
    parts.append(jnp.zeros((group, DC - 6 * DR), BF16))
    out_ref[rows:] = jnp.concatenate(parts, axis=1)


def unpack(chunk, keys, base):
    rows = 6 * chunk.shape[0] // 7
    group = rows // 6
    keys[pl.ds(base, rows), :DC] = chunk[:rows]
    for index in range(6):
        part = chunk[rows:, index * DR : (index + 1) * DR]
        keys[pl.ds(base + index * group, group), DC:] = part


def cut_kernel(_, out_proj, out_ref, sem):
    width = out_ref.shape[1]
    base = pl.multiple_of((1 - lax.axis_index("heads")) * width, 128)
    copy = pltpu.make_async_copy(out_proj.at[:, pl.ds(base, width)], out_ref, sem)
    copy.start()
    copy.wait()


def query_kernel(order, span_order, _, nope, rope, up, out_ref, *biases):
    rows = nope.shape[0]
    heads = nope.shape[1] // DH
    span_rows = rows // 2
    own_index = lax.axis_index("ctx")
    core = lax.axis_index("heads")
    for head in range(heads):
        part = pl.ds(head * rows, rows)
        latent = lax.dot_general(
            nope[:, head * DH : (head + 1) * DH],
            up[:, head * DH : (head + 1) * DH],
            (((1,), (1,)), ((), ())),
            preferred_element_type=F32,
        )
        out_ref[part, :DC] = latent.astype(BF16)
        out_ref[part, DC:] = rope[:, head * DR : (head + 1) * DR]
    row = lax.broadcasted_iota(jnp.int32, (rows, 1), 0)
    query_pos = jnp.where(
        row < span_rows,
        span_order[2 * own_index] * span_rows + row,
        span_order[2 * own_index + 1] * span_rows + row - span_rows,
    )

    def bias_of(owners):
        column = lax.broadcasted_iota(jnp.int32, (1, len(owners) * rows), 1)
        key_pos = jnp.zeros(column.shape, jnp.int32)
        for index, owner in enumerate(owners):
            for side in range(2):
                start = index * rows + side * span_rows
                first = span_order[2 * owner + side] * span_rows
                key_pos = jnp.where(column >= start, first + column - start, key_pos)
        return jnp.where(key_pos <= query_pos, F32(0.0), F32(MASKED))

    if order is not None:
        for steps, bias_ref in zip(order, biases):
            bias_ref[0] = bias_of(
                [own_index ^ jnp.where(core == 0, step[0], step[1]) for step in steps]
            )
    else:
        bias_ref = biases[0]

        def step(block, carry):
            bias_ref[block] = bias_of([block * BLOCK_CHUNKS + index for index in range(BLOCK_CHUNKS)])
            return carry

        lax.fori_loop(0, bias_ref.shape[0], step, 0)


def attend_block(queries, keys, bias, old):
    copies = 2 * queries[0].shape[0] // bias.shape[0]
    scale = math.log2(math.e) / math.sqrt(DH + DR)
    both = jnp.concatenate([part[...] for part in queries], axis=0)
    scores = lax.dot_general(
        both, keys[...], (((1,), (1,)), ((), ())), preferred_element_type=F32
    )
    scores = scores + jnp.concatenate([bias] * copies, axis=0)
    top = jnp.max(scores, axis=-1, keepdims=True)
    if old is not None:
        top = jnp.maximum(old[0], top)
        rescale = jnp.exp2((old[0] - top) * scale)
    expo = jnp.exp2((scores - top) * scale)
    total = jnp.sum(expo, axis=-1, keepdims=True)
    added = jnp.dot(expo.astype(BF16), keys[:, :DC], preferred_element_type=F32)
    if old is not None:
        total = old[1] * rescale + total
        added = old[2] * rescale + added
    return top, total, added


def early_kernel(queries_own, queries_other, bias, *rest):
    queries = (queries_own, queries_other)
    chunks, running, keys = rest[:-4], rest[-4:-1], rest[-1]
    blocks, rows, _ = bias.shape
    if blocks == 1:
        for index, chunk in enumerate(chunks):
            unpack(chunk, keys, index * rows)
        values = attend_block(queries, keys, bias[0], None)
        for state, value in zip(running, values):
            state[...] = value
        return
    gathered = chunks[0]

    def fill(block):
        for index in range(BLOCK_CHUNKS):
            unpack(gathered.at[block * BLOCK_CHUNKS + index], keys, index * rows)

    first = lax.axis_index("ctx") // BLOCK_CHUNKS
    fill(first)
    values = attend_block(queries, keys, bias[first], None)
    for state, value in zip(running, values):
        state[...] = value

    def step(index, carry):
        block = index + jnp.where(index >= first, 1, 0)
        fill(block)
        new = attend_block(queries, keys, bias[block], [state[...] for state in running])
        for state, value in zip(running, new):
            state[...] = value
        return carry

    lax.fori_loop(0, blocks - 1, step, 0)


def finish_kernel(late_count, queries_own, queries_other, top, total, context, *rest):
    bias, chunks = rest[:late_count][:1], rest[1 : 1 + late_count]
    rest = rest[len(bias) + len(chunks) :]
    value_own, value_other, proj_own, proj_other, out_ref, proj, out_tiles, keys, proj_sems, out_sems = rest
    rows, width = out_ref.shape
    half = proj_own.shape[0]
    core = lax.axis_index("heads")

    base = pl.multiple_of(core * width, 128)
    fetches = (
        pltpu.make_async_copy(
            proj_own.at[:, pl.ds(base, width)], proj.at[pl.ds(0, half)], proj_sems.at[0]
        ),
        pltpu.make_async_copy(proj_other, proj.at[pl.ds(half, half)], proj_sems.at[1]),
    )
    for fetch in fetches:
        fetch.start()

    running = (top[...], total[...], context[...])
    if late_count:
        for index, chunk in enumerate(chunks):
            unpack(chunk, keys, index * rows)
        running = attend_block((queries_own, queries_other), keys, bias[0][0], running)
    mixed = (running[2] / running[1]).astype(BF16)
    heads = value_own.shape[1] // DH
    parts = []
    for group, value in enumerate((value_own, value_other)):
        for head in range(heads):
            first = (group * heads + head) * rows
            per_head = jnp.dot(
                mixed[first : first + rows],
                value[:, head * DH : (head + 1) * DH],
                preferred_element_type=F32,
            )
            parts.append(per_head.astype(BF16))
    heads_out = jnp.concatenate(parts, axis=1)

    for fetch in fetches:
        fetch.wait()
    tiles = out_sems.shape[0]
    tile = width // tiles
    sends = []
    for index in range(tiles):
        part = pl.ds(index * tile, tile)
        out = jnp.dot(heads_out, proj[:, part], preferred_element_type=F32)
        out_tiles[:, part] = out.astype(BF16)
        sends.append(
            pltpu.make_async_copy(out_tiles.at[:, part], out_ref.at[:, part], out_sems.at[index])
        )
        sends[-1].start()
    for send in sends:
        send.wait()


def per_device(
    count, queries_nope, queries_rope, latent, key_rope, key_up, value_up, out_proj, span_order
):
    rows = latent.shape[0]
    width = out_proj.shape[1] // 2
    heads = 2 * (key_up.shape[1] // DH)
    query_rows = heads * rows
    direct = count == 8
    small = pltpu.CompilerParams(vmem_limit_bytes=SMALL_VMEM)

    def in_hbm(*arrays):
        return [pltpu.with_memory_space_constraint(array, pltpu.HBM) for array in arrays]

    def other_core(array):
        return lax.ppermute(array, "heads", [(0, 1), (1, 0)])

    def partners(array, steps):
        pairs = [
            (2 * index + core, 2 * (index ^ steps[core]) + core)
            for index in range(count)
            for core in range(2)
        ]
        return lax.ppermute(array, ("ctx", "heads"), pairs)

    def cut(after):
        return pl.pallas_call(
            cut_kernel,
            out_shape=jax.ShapeDtypeStruct((out_proj.shape[0], width), BF16),
            in_specs=[anywhere(), hbm()],
            out_specs=anywhere(),
            scratch_shapes=[pltpu.SemaphoreType.DMA],
            compiler_params=small,
            cost_estimate=cost(CUT_COST),
            name="cut",
        )(after, *in_hbm(out_proj))

    packed = pl.pallas_call(
        pack_kernel,
        out_shape=jax.ShapeDtypeStruct((rows + rows // 6, DC), BF16),
        in_specs=[vmem()] * 2,
        out_specs=vmem(),
        compiler_params=small,
        name="pack",
    )(*in_hbm(latent, key_rope.T))
    if direct:
        far = partners(packed, FAR)
        near = partners(packed, NEAR)
        beside = partners(packed, BESIDE)
        proj_cut = cut(near)
        far, _ = lax.optimization_barrier((far, proj_cut))
        relayed = partners(far, (1, 1))
        early = [packed, beside, near, other_core(near), far, other_core(far)]
        late = [relayed, other_core(relayed)]
        order = [
            [(0, 0), BESIDE, NEAR, NEAR[::-1], FAR, FAR[::-1]],
            [RELAYED, RELAYED[::-1]],
        ]
        bias_shapes = [(1, rows, len(steps) * rows) for steps in order]
    else:
        proj_cut = cut(packed)
        early, late, order = [lax.all_gather(packed, "ctx", axis=0)], [], None
        bias_shapes = [(count // BLOCK_CHUNKS, rows, BLOCK_CHUNKS * rows)]

    queries, *biases = pl.pallas_call(
        functools.partial(query_kernel, order),
        out_shape=[jax.ShapeDtypeStruct((query_rows // 2, DC + DR), BF16)]
        + [jax.ShapeDtypeStruct(shape, F32) for shape in bias_shapes],
        in_specs=[smem(), anywhere()] + [vmem()] * 3,
        out_specs=[vmem()] * (1 + len(bias_shapes)),
        compiler_params=small,
        cost_estimate=cost(QUERY_COST),
        name="queries",
    )(span_order, packed, *in_hbm(queries_nope, queries_rope, key_up))
    queries_other = other_core(queries)
    value_other = other_core(value_up)
    proj_other = other_core(proj_cut)
    running = pl.pallas_call(
        early_kernel,
        out_shape=[jax.ShapeDtypeStruct((query_rows, size), F32) for size in (1, 1, DC)],
        in_specs=[vmem()] * (3 + len(early)),
        out_specs=[vmem()] * 3,
        scratch_shapes=[pltpu.VMEM((bias_shapes[0][2], DC + DR), BF16)],
        compiler_params=pltpu.CompilerParams(
            vmem_limit_bytes=SMALL_VMEM if direct else LARGE_VMEM
        ),
        cost_estimate=cost(EARLY_COST),
        name="early",
    )(queries, queries_other, biases[0], *early)

    tiles = 4 if width % 512 == 0 else 1
    return pl.pallas_call(
        functools.partial(finish_kernel, len(late)),
        out_shape=jax.ShapeDtypeStruct((rows, width), BF16),
        in_specs=[vmem()] * (5 + len(biases[1:]) + len(late) + 2) + [hbm(), anywhere()],
        out_specs=anywhere(),
        scratch_shapes=[
            pltpu.VMEM((2 * out_proj.shape[0], width), BF16),
            pltpu.VMEM((rows, width), BF16),
            pltpu.VMEM((max(1, len(late)) * rows, DC + DR), BF16),
            pltpu.SemaphoreType.DMA((2,)),
            pltpu.SemaphoreType.DMA((tiles,)),
        ],
        compiler_params=small,
        name="finish",
    )(
        queries,
        queries_other,
        *running,
        *biases[1:],
        *late,
        value_up,
        value_other,
        *in_hbm(out_proj),
        proj_other,
    )


def solution(mesh):
    in_specs = (
        P(("docs", "ctx"), "heads"),
        P(("docs", "ctx"), "heads"),
        P(("docs", "ctx"), None),
        P(("docs", "ctx"), None),
        P(None, "heads"),
        P(None, "heads"),
        P("heads", None),
        P("docs"),
    )
    out_specs = P(("docs", "ctx"), "heads")
    return jax.shard_map(
        functools.partial(per_device, mesh.shape["ctx"]),
        mesh=mesh,
        in_specs=in_specs,
        out_specs=out_specs,
        check_vma=False,
    )
```

```python
import functools
import math

import jax
import jax.numpy as jnp
from jax import lax
from jax.experimental import pallas as pl
from jax.experimental.pallas import tpu as pltpu
from jax.sharding import PartitionSpec as P

DC = 512
DH = 128
DR = 64
BF16 = jnp.bfloat16
F32 = jnp.float32
MASKED = -1e30
BLOCK_CHUNKS = 8
CUT_COST, QUERY_COST, FIRST_COST, SECOND_COST = 0, 0, 0, 30
SMALL_VMEM = 20 * 1024 * 1024
LARGE_VMEM = 56 * 1024 * 1024
FAR = (4, 6)
NEAR = (2, 3)
BESIDE = (1, 1)
RELAYED = (5, 7)


def vmem():
    return pl.BlockSpec(memory_space=pltpu.VMEM)


def anywhere():
    return pl.BlockSpec(memory_space=pl.ANY)


def hbm():
    return pl.BlockSpec(memory_space=pltpu.HBM)


def cost(microseconds):
    return pl.CostEstimate(flops=int(microseconds * 1.1e9), bytes_accessed=0, transcendentals=0)


def smem():
    return pl.BlockSpec(memory_space=pltpu.SMEM)


def pack_kernel(latent, key_rope_turned, out_ref):
    rows = latent.shape[0]
    group = rows // 6
    out_ref[:rows] = latent[...]
    rope = key_rope_turned[...].astype(F32).T.astype(BF16)
    parts = [rope[index * group : (index + 1) * group] for index in range(6)]
    parts.append(jnp.zeros((group, DC - 6 * DR), BF16))
    out_ref[rows:] = jnp.concatenate(parts, axis=1)


def unpack(chunk, keys, base):
    rows = 6 * chunk.shape[0] // 7
    group = rows // 6
    keys[pl.ds(base, rows), :DC] = chunk[:rows]
    for index in range(6):
        part = chunk[rows:, index * DR : (index + 1) * DR]
        keys[pl.ds(base + index * group, group), DC:] = part


def cut_kernel(_, out_proj, own_ref, other_ref, sems):
    width = own_ref.shape[1]
    core = lax.axis_index("heads")
    copies = []
    for index, (part, target) in enumerate(((1 - core, other_ref), (core, own_ref))):
        columns = pl.ds(pl.multiple_of(part * width, 128), width)
        copies.append(pltpu.make_async_copy(out_proj.at[:, columns], target, sems.at[index]))
    for copy in copies:
        copy.start()
    for copy in copies:
        copy.wait()


def query_kernel(order, span_order, _, nope, rope, up, *outs):
    rows = nope.shape[0]
    heads = nope.shape[1] // DH
    span_rows = rows // 2
    own_index = lax.axis_index("ctx")
    core = lax.axis_index("heads")
    for head in range(heads):
        latent = lax.dot_general(
            nope[:, head * DH : (head + 1) * DH],
            up[:, head * DH : (head + 1) * DH],
            (((1,), (1,)), ((), ())),
            preferred_element_type=F32,
        )
        outs[head][:, :DC] = latent.astype(BF16)
        outs[head][:, DC:] = rope[:, head * DR : (head + 1) * DR]
    biases = outs[heads:]
    row = lax.broadcasted_iota(jnp.int32, (rows, 1), 0)
    query_pos = jnp.where(
        row < span_rows,
        span_order[2 * own_index] * span_rows + row,
        span_order[2 * own_index + 1] * span_rows + row - span_rows,
    )

    def bias_of(owners):
        column = lax.broadcasted_iota(jnp.int32, (1, len(owners) * rows), 1)
        key_pos = jnp.zeros(column.shape, jnp.int32)
        for index, owner in enumerate(owners):
            for side in range(2):
                start = index * rows + side * span_rows
                first = span_order[2 * owner + side] * span_rows
                key_pos = jnp.where(column >= start, first + column - start, key_pos)
        return jnp.where(key_pos <= query_pos, F32(0.0), F32(MASKED))

    if order is not None:
        for steps, bias_ref in zip(order, biases):
            bias_ref[0] = bias_of(
                [own_index ^ jnp.where(core == 0, step[0], step[1]) for step in steps]
            )
    else:
        bias_ref = biases[0]

        def step(block, carry):
            bias_ref[block] = bias_of([block * BLOCK_CHUNKS + index for index in range(BLOCK_CHUNKS)])
            return carry

        lax.fori_loop(0, bias_ref.shape[0], step, 0)


def attend_block(queries, keys, bias, old):
    copies = len(queries)
    scale = math.log2(math.e) / math.sqrt(DH + DR)
    heads = jnp.concatenate([part[...] for part in queries], axis=0)
    scores = lax.dot_general(
        heads, keys[...], (((1,), (1,)), ((), ())), preferred_element_type=F32
    )
    scores = scores + jnp.concatenate([bias] * copies, axis=0)
    top = jnp.max(scores, axis=-1, keepdims=True)
    if old is not None:
        top = jnp.maximum(old[0], top)
        rescale = jnp.exp2((old[0] - top) * scale)
    expo = jnp.exp2((scores - top) * scale)
    total = jnp.sum(expo, axis=-1, keepdims=True)
    added = jnp.dot(expo.astype(BF16), keys[:, :DC], preferred_element_type=F32)
    if old is not None:
        total = old[1] * rescale + total
        added = old[2] * rescale + added
    return top, total, added


def chunks_kernel(heads, chunk_count, passed, later, *rest):
    queries, bias, rest = rest[:heads], rest[heads], rest[heads + 1 :]
    chunks, rest = rest[:chunk_count], rest[chunk_count + later :]
    if passed:
        rest[-2][...] = rest[0][...]
        rest = rest[1:-2] + rest[-1:]
    old, running, keys = rest[:-4], rest[-4:-1], rest[-1]
    rows = bias.shape[1]
    for index, chunk in enumerate(chunks):
        unpack(chunk, keys, index * rows)
    before = [state[...] for state in old] if old else None
    values = attend_block(queries, keys, bias[0], before)
    for state, value in zip(running, values):
        state[...] = value


def gathered_kernel(heads, *rest):
    queries, (bias, gathered) = rest[:heads], rest[heads : heads + 2]
    running, keys = rest[heads + 2 : heads + 5], rest[heads + 5]
    blocks, rows, _ = bias.shape

    def fill(block):
        for index in range(BLOCK_CHUNKS):
            unpack(gathered.at[block * BLOCK_CHUNKS + index], keys, index * rows)

    first = lax.axis_index("ctx") // BLOCK_CHUNKS
    fill(first)
    values = attend_block(queries, keys, bias[first], None)
    for state, value in zip(running, values):
        state[...] = value

    def step(index, carry):
        block = index + jnp.where(index >= first, 1, 0)
        fill(block)
        new = attend_block(queries, keys, bias[block], [state[...] for state in running])
        for state, value in zip(running, new):
            state[...] = value
        return carry

    lax.fori_loop(0, blocks - 1, step, 0)


def finish_kernel(heads, chunk_count, *rest):
    queries, (top, total, context), rest = rest[:heads], rest[heads : heads + 3], rest[heads + 3 :]
    bias, chunks = rest[:chunk_count][:1], rest[1 : 1 + chunk_count]
    rest = rest[len(bias) + len(chunks) :]
    value_own, value_other, proj_own, proj_other, out_ref, out_tiles, keys, out_sems = rest
    rows, width = out_ref.shape
    running = (top[...], total[...], context[...])
    if chunk_count:
        for index, chunk in enumerate(chunks):
            unpack(chunk, keys, index * rows)
        running = attend_block(queries, keys, bias[0][0], running)
    mixed = (running[2] / running[1]).astype(BF16)
    half = heads // 2
    sides = []
    for group, value in enumerate((value_own, value_other)):
        parts = []
        for head in range(half):
            first = (group * half + head) * rows
            per_head = jnp.dot(
                mixed[first : first + rows],
                value[:, head * DH : (head + 1) * DH],
                preferred_element_type=F32,
            )
            parts.append(per_head.astype(BF16))
        sides.append(jnp.concatenate(parts, axis=1))
    tiles = out_sems.shape[0]
    tile = width // tiles
    sends = []
    for index in range(tiles):
        part = pl.ds(index * tile, tile)
        out = jnp.dot(sides[0], proj_own[:, part], preferred_element_type=F32)
        out = out + jnp.dot(sides[1], proj_other[:, part], preferred_element_type=F32)
        out_tiles[:, part] = out.astype(BF16)
        sends.append(
            pltpu.make_async_copy(out_tiles.at[:, part], out_ref.at[:, part], out_sems.at[index])
        )
        sends[-1].start()
    for send in sends:
        send.wait()


def per_device(
    count, queries_nope, queries_rope, latent, key_rope, key_up, value_up, out_proj, span_order
):
    rows = latent.shape[0]
    width = out_proj.shape[1] // 2
    heads = 2 * (key_up.shape[1] // DH)
    query_rows = heads * rows
    direct = count == 8
    small = pltpu.CompilerParams(vmem_limit_bytes=SMALL_VMEM)

    def in_hbm(*arrays):
        return [pltpu.with_memory_space_constraint(array, pltpu.HBM) for array in arrays]

    def other_core(array):
        return lax.ppermute(array, "heads", [(0, 1), (1, 0)])

    def partners(array, steps):
        pairs = [
            (2 * index + core, 2 * (index ^ steps[core]) + core)
            for index in range(count)
            for core in range(2)
        ]
        return lax.ppermute(array, ("ctx", "heads"), pairs)

    def cut(after):
        return pl.pallas_call(
            cut_kernel,
            out_shape=[jax.ShapeDtypeStruct((out_proj.shape[0], width), BF16)] * 2,
            in_specs=[anywhere(), hbm()],
            out_specs=[anywhere()] * 2,
            scratch_shapes=[pltpu.SemaphoreType.DMA((2,))],
            compiler_params=small,
            cost_estimate=cost(CUT_COST),
            name="cut",
        )(after, *in_hbm(out_proj))

    def attend(name, estimate, queries, bias, chunks, passed, old, *before):
        return pl.pallas_call(
            functools.partial(chunks_kernel, heads, len(chunks), len(passed), len(before)),
            out_shape=[jax.ShapeDtypeStruct((query_rows, size), F32) for size in (1, 1, DC)]
            + [jax.ShapeDtypeStruct(chunk.shape, BF16) for chunk in passed],
            in_specs=[vmem()] * (heads + 1 + len(chunks))
            + [anywhere()] * len(before)
            + [vmem()] * (len(passed) + len(old)),
            out_specs=[vmem()] * (3 + len(passed)),
            scratch_shapes=[pltpu.VMEM((len(chunks) * rows, DC + DR), BF16)],
            compiler_params=small,
            cost_estimate=cost(estimate),
            name=name,
        )(*queries, bias, *chunks, *before, *passed, *old)

    packed = pl.pallas_call(
        pack_kernel,
        out_shape=jax.ShapeDtypeStruct((rows + rows // 6, DC), BF16),
        in_specs=[vmem()] * 2,
        out_specs=vmem(),
        compiler_params=small,
        name="pack",
    )(*in_hbm(latent, key_rope.T))
    if direct:
        order = [
            [(0, 0), BESIDE, NEAR],
            [NEAR[::-1], FAR, FAR[::-1], RELAYED],
            [RELAYED[::-1]],
        ]
        bias_shapes = [(1, rows, len(steps) * rows) for steps in order]
    else:
        order = None
        bias_shapes = [(count // BLOCK_CHUNKS, rows, BLOCK_CHUNKS * rows)]
    outs = pl.pallas_call(
        functools.partial(query_kernel, order),
        out_shape=[jax.ShapeDtypeStruct((rows, DC + DR), BF16)] * (heads // 2)
        + [jax.ShapeDtypeStruct(shape, F32) for shape in bias_shapes],
        in_specs=[smem(), anywhere()] + [vmem()] * 3,
        out_specs=[vmem()] * (heads // 2 + len(bias_shapes)),
        compiler_params=small,
        cost_estimate=cost(QUERY_COST),
        name="queries",
    )(*in_hbm(span_order), packed, *in_hbm(queries_nope, queries_rope, key_up))
    queries, biases = outs[: heads // 2], outs[heads // 2 :]
    both = [*queries, *map(other_core, queries)]
    value_other = other_core(value_up)
    proj_own, proj_cut = cut(queries[0])
    proj_other = other_core(proj_cut)

    if direct:
        far = partners(packed, FAR)
        near = partners(packed, NEAR)
        beside = partners(packed, BESIDE)
        relayed = partners(far, (1, 1))
        *running, far_after = attend(
            "first", FIRST_COST, both, biases[0], [packed, beside, near], [far], [], proj_cut
        )
        last = [other_core(relayed)]
        running = attend(
            "second",
            SECOND_COST,
            both,
            biases[1],
            [other_core(near), far, other_core(far_after), relayed],
            [],
            running,
        )
    else:
        last = []
        running = pl.pallas_call(
            functools.partial(gathered_kernel, heads),
            out_shape=[jax.ShapeDtypeStruct((query_rows, size), F32) for size in (1, 1, DC)],
            in_specs=[vmem()] * (heads + 2),
            out_specs=[vmem()] * 3,
            scratch_shapes=[pltpu.VMEM((BLOCK_CHUNKS * rows, DC + DR), BF16)],
            compiler_params=pltpu.CompilerParams(vmem_limit_bytes=LARGE_VMEM),
            name="gathered",
        )(*both, biases[0], lax.all_gather(packed, "ctx", axis=0))

    tiles = 7 if width % 896 == 0 else 1
    return pl.pallas_call(
        functools.partial(finish_kernel, heads, len(last)),
        out_shape=jax.ShapeDtypeStruct((rows, width), BF16),
        in_specs=[vmem()] * (heads + 3 + len(biases[2:]) + len(last) + 4),
        out_specs=anywhere(),
        scratch_shapes=[
            pltpu.VMEM((rows, width), BF16),
            pltpu.VMEM((rows, DC + DR), BF16),
            pltpu.SemaphoreType.DMA((tiles,)),
        ],
        compiler_params=small,
        name="finish",
    )(*both, *running, *biases[2:], *last, value_up, value_other, proj_own, proj_other)


def solution(mesh):
    in_specs = (
        P(("docs", "ctx"), "heads"),
        P(("docs", "ctx"), "heads"),
        P(("docs", "ctx"), None),
        P(("docs", "ctx"), None),
        P(None, "heads"),
        P(None, "heads"),
        P("heads", None),
        P("docs"),
    )
    out_specs = P(("docs", "ctx"), "heads")
    return jax.shard_map(
        functools.partial(per_device, mesh.shape["ctx"]),
        mesh=mesh,
        in_specs=in_specs,
        out_specs=out_specs,
        check_vma=False,
    )
```

```python
import functools
import math

import jax
import jax.numpy as jnp
from jax import lax
from jax.experimental import pallas as pl
from jax.experimental.pallas import tpu as pltpu
from jax.sharding import PartitionSpec as P

DC = 512
DH = 128
DR = 64
BF16 = jnp.bfloat16
F32 = jnp.float32
MASKED = -1e30
BLOCK_CHUNKS = 8
PREPARE_COST, FIRST_COST, SECOND_COST = 0, 0, 30
SMALL_VMEM = 20 * 1024 * 1024
LARGE_VMEM = 56 * 1024 * 1024
FAR = (4, 6)
NEAR = (2, 3)
BESIDE = (1, 1)
RELAYED = (5, 7)


def vmem():
    return pl.BlockSpec(memory_space=pltpu.VMEM)


def anywhere():
    return pl.BlockSpec(memory_space=pl.ANY)


def hbm():
    return pl.BlockSpec(memory_space=pltpu.HBM)


def cost(microseconds):
    return pl.CostEstimate(flops=int(microseconds * 1.1e9), bytes_accessed=0, transcendentals=0)


def smem():
    return pl.BlockSpec(memory_space=pltpu.SMEM)


def pack_kernel(latent, key_rope_turned, out_ref):
    rows = latent.shape[0]
    group = rows // 6
    out_ref[:rows] = latent[...]
    rope = key_rope_turned[...].astype(F32).T.astype(BF16)
    parts = [rope[index * group : (index + 1) * group] for index in range(6)]
    parts.append(jnp.zeros((group, DC - 6 * DR), BF16))
    out_ref[rows:] = jnp.concatenate(parts, axis=1)


def unpack(chunk, keys, base):
    rows = 6 * chunk.shape[0] // 7
    group = rows // 6
    keys[pl.ds(base, rows), :DC] = chunk[:rows]
    for index in range(6):
        part = chunk[rows:, index * DR : (index + 1) * DR]
        keys[pl.ds(base + index * group, group), DC:] = part


def prepare_kernel(order, span_order, _, nope, rope, up, value_up, out_proj, *outs):
    weights_own, weights_sent, sems = outs[-3:]
    depth, width = out_proj.shape[0], out_proj.shape[1] // 2
    fetches = []
    for index, target in enumerate((weights_sent, weights_own)):
        part = lax.axis_index("heads") ^ (1 - index)
        columns = pl.ds(pl.multiple_of(part * width, 128), width)
        pairs = [(out_proj.at[:, columns], target.at[:, pl.ds(0, width)])]
        for block in range(DC // depth):
            place = pl.ds(width + block * value_up.shape[1], value_up.shape[1])
            pairs.append((value_up.at[pl.ds(block * depth, depth)], target.at[:, place]))
        for place, pair in enumerate(pairs):
            fetches.append(pltpu.make_async_copy(*pair, sems.at[index, place]))
            fetches[-1].start()
    rows = nope.shape[0]
    heads = nope.shape[1] // DH
    span_rows = rows // 2
    own_index = lax.axis_index("ctx")
    core = lax.axis_index("heads")
    for head in range(heads):
        latent = lax.dot_general(
            nope[:, head * DH : (head + 1) * DH],
            up[:, head * DH : (head + 1) * DH],
            (((1,), (1,)), ((), ())),
            preferred_element_type=F32,
        )
        outs[head][:, :DC] = latent.astype(BF16)
        outs[head][:, DC:] = rope[:, head * DR : (head + 1) * DR]
    biases = outs[heads:-3]
    row = lax.broadcasted_iota(jnp.int32, (rows, 1), 0)
    query_pos = jnp.where(
        row < span_rows,
        span_order[2 * own_index] * span_rows + row,
        span_order[2 * own_index + 1] * span_rows + row - span_rows,
    )

    def bias_of(owners):
        column = lax.broadcasted_iota(jnp.int32, (1, len(owners) * rows), 1)
        key_pos = jnp.zeros(column.shape, jnp.int32)
        for index, owner in enumerate(owners):
            for side in range(2):
                start = index * rows + side * span_rows
                first = span_order[2 * owner + side] * span_rows
                key_pos = jnp.where(column >= start, first + column - start, key_pos)
        return jnp.where(key_pos <= query_pos, F32(0.0), F32(MASKED))

    if order is not None:
        for steps, bias_ref in zip(order, biases):
            bias_ref[0] = bias_of(
                [own_index ^ jnp.where(core == 0, step[0], step[1]) for step in steps]
            )
    else:
        bias_ref = biases[0]

        def step(block, carry):
            bias_ref[block] = bias_of([block * BLOCK_CHUNKS + index for index in range(BLOCK_CHUNKS)])
            return carry

        lax.fori_loop(0, bias_ref.shape[0], step, 0)

    for fetch in fetches:
        fetch.wait()


def attend_block(queries, keys, bias, old):
    copies = len(queries)
    scale = math.log2(math.e) / math.sqrt(DH + DR)
    heads = jnp.concatenate([part[...] for part in queries], axis=0)
    scores = lax.dot_general(
        heads, keys[...], (((1,), (1,)), ((), ())), preferred_element_type=F32
    )
    scores = scores + jnp.concatenate([bias] * copies, axis=0)
    top = jnp.max(scores, axis=-1, keepdims=True)
    if old is not None:
        top = jnp.maximum(old[0], top)
        rescale = jnp.exp2((old[0] - top) * scale)
    expo = jnp.exp2((scores - top) * scale)
    total = jnp.sum(expo, axis=-1, keepdims=True)
    added = jnp.dot(expo.astype(BF16), keys[:, :DC], preferred_element_type=F32)
    if old is not None:
        total = old[1] * rescale + total
        added = old[2] * rescale + added
    return top, total, added


def chunks_kernel(heads, chunk_count, passed, later, *rest):
    queries, bias, rest = rest[:heads], rest[heads], rest[heads + 1 :]
    chunks, rest = rest[:chunk_count], rest[chunk_count + later :]
    if passed:
        rest[-2][...] = rest[0][...]
        rest = rest[1:-2] + rest[-1:]
    old, running, keys = rest[:-4], rest[-4:-1], rest[-1]
    rows = bias.shape[1]
    for index, chunk in enumerate(chunks):
        unpack(chunk, keys, index * rows)
    before = [state[...] for state in old] if old else None
    values = attend_block(queries, keys, bias[0], before)
    for state, value in zip(running, values):
        state[...] = value


def gathered_kernel(heads, *rest):
    queries, (bias, gathered) = rest[:heads], rest[heads : heads + 2]
    running, keys = rest[heads + 2 : heads + 5], rest[heads + 5]
    blocks, rows, _ = bias.shape

    def fill(block):
        for index in range(BLOCK_CHUNKS):
            unpack(gathered.at[block * BLOCK_CHUNKS + index], keys, index * rows)

    first = lax.axis_index("ctx") // BLOCK_CHUNKS
    fill(first)
    values = attend_block(queries, keys, bias[first], None)
    for state, value in zip(running, values):
        state[...] = value

    def step(index, carry):
        block = index + jnp.where(index >= first, 1, 0)
        fill(block)
        new = attend_block(queries, keys, bias[block], [state[...] for state in running])
        for state, value in zip(running, new):
            state[...] = value
        return carry

    lax.fori_loop(0, blocks - 1, step, 0)


def finish_kernel(heads, chunk_count, *rest):
    queries, (top, total, context), rest = rest[:heads], rest[heads : heads + 3], rest[heads + 3 :]
    bias, chunks = rest[:chunk_count][:1], rest[1 : 1 + chunk_count]
    rest = rest[len(bias) + len(chunks) :]
    weights, (out_ref, out_tiles, keys, out_sems) = rest[:2], rest[2:]
    rows, width = out_ref.shape
    running = (top[...], total[...], context[...])
    if chunk_count:
        for index, chunk in enumerate(chunks):
            unpack(chunk, keys, index * rows)
        running = attend_block(queries, keys, bias[0][0], running)
    mixed = (running[2] / running[1]).astype(BF16)
    half = heads // 2
    depth = weights[0].shape[0]
    sides = []
    for group, weight in enumerate(weights):
        parts = []
        for head in range(half):
            rows_of = slice((group * half + head) * rows, (group * half + head + 1) * rows)
            per_head = 0.0
            for block in range(DC // depth):
                first = width + block * half * DH + head * DH
                per_head = per_head + jnp.dot(
                    mixed[rows_of, block * depth : (block + 1) * depth],
                    weight[:, first : first + DH],
                    preferred_element_type=F32,
                )
            parts.append(per_head.astype(BF16))
        sides.append(jnp.concatenate(parts, axis=1))
    tiles = out_sems.shape[0]
    tile = width // tiles
    sends = []
    for index in range(tiles):
        part = pl.ds(index * tile, tile)
        out = jnp.dot(sides[0], weights[0][:, part], preferred_element_type=F32)
        out = out + jnp.dot(sides[1], weights[1][:, part], preferred_element_type=F32)
        out_tiles[:, part] = out.astype(BF16)
        sends.append(
            pltpu.make_async_copy(out_tiles.at[:, part], out_ref.at[:, part], out_sems.at[index])
        )
        sends[-1].start()
    for send in sends:
        send.wait()


def per_device(
    count, queries_nope, queries_rope, latent, key_rope, key_up, value_up, out_proj, span_order
):
    rows = latent.shape[0]
    depth, width = out_proj.shape[0], out_proj.shape[1] // 2
    blocks = DC // depth
    heads = 2 * (key_up.shape[1] // DH)
    query_rows = heads * rows
    direct = count == 8
    small = pltpu.CompilerParams(vmem_limit_bytes=SMALL_VMEM)

    def in_hbm(*arrays):
        return [pltpu.with_memory_space_constraint(array, pltpu.HBM) for array in arrays]

    def other_core(array):
        return lax.ppermute(array, "heads", [(0, 1), (1, 0)])

    def partners(array, steps):
        pairs = [
            (2 * index + core, 2 * (index ^ steps[core]) + core)
            for index in range(count)
            for core in range(2)
        ]
        return lax.ppermute(array, ("ctx", "heads"), pairs)

    def attend(name, estimate, queries, bias, chunks, passed, old, *before):
        return pl.pallas_call(
            functools.partial(chunks_kernel, heads, len(chunks), len(passed), len(before)),
            out_shape=[jax.ShapeDtypeStruct((query_rows, size), F32) for size in (1, 1, DC)]
            + [jax.ShapeDtypeStruct(chunk.shape, BF16) for chunk in passed],
            in_specs=[vmem()] * (heads + 1 + len(chunks))
            + [anywhere()] * len(before)
            + [vmem()] * (len(passed) + len(old)),
            out_specs=[vmem()] * (3 + len(passed)),
            scratch_shapes=[pltpu.VMEM((len(chunks) * rows, DC + DR), BF16)],
            compiler_params=small,
            cost_estimate=cost(estimate),
            name=name,
        )(*queries, bias, *chunks, *before, *passed, *old)

    packed = pl.pallas_call(
        pack_kernel,
        out_shape=jax.ShapeDtypeStruct((rows + rows // 6, DC), BF16),
        in_specs=[vmem()] * 2,
        out_specs=vmem(),
        compiler_params=small,
        name="pack",
    )(*in_hbm(latent, key_rope.T))
    if direct:
        order = [
            [(0, 0), BESIDE, NEAR],
            [NEAR[::-1], FAR, FAR[::-1], RELAYED],
            [RELAYED[::-1]],
        ]
        bias_shapes = [(1, rows, len(steps) * rows) for steps in order]
    else:
        order = None
        bias_shapes = [(count // BLOCK_CHUNKS, rows, BLOCK_CHUNKS * rows)]
    outs = pl.pallas_call(
        functools.partial(prepare_kernel, order),
        out_shape=[jax.ShapeDtypeStruct((rows, DC + DR), BF16)] * (heads // 2)
        + [jax.ShapeDtypeStruct(shape, F32) for shape in bias_shapes]
        + [jax.ShapeDtypeStruct((depth, width + blocks * key_up.shape[1]), BF16)] * 2,
        in_specs=[smem(), anywhere()] + [vmem()] * 3 + [hbm()] * 2,
        out_specs=[vmem()] * (heads // 2 + len(bias_shapes)) + [anywhere()] * 2,
        scratch_shapes=[pltpu.SemaphoreType.DMA((2, 1 + blocks))],
        compiler_params=small,
        cost_estimate=cost(PREPARE_COST),
        name="prepare",
    )(*in_hbm(span_order), packed, *in_hbm(queries_nope, queries_rope, key_up, value_up, out_proj))
    queries, biases = outs[: heads // 2], outs[heads // 2 : -2]
    weights = [outs[-2], other_core(outs[-1])]
    both = [*queries, *map(other_core, queries)]

    if direct:
        far = partners(packed, FAR)
        near = partners(packed, NEAR)
        beside = partners(packed, BESIDE)
        relayed = partners(far, (1, 1))
        *running, far_after = attend(
            "first", FIRST_COST, both, biases[0], [packed, beside, near], [far], []
        )
        last = [other_core(relayed)]
        running = attend(
            "second",
            SECOND_COST,
            both,
            biases[1],
            [other_core(near), far, other_core(far_after), relayed],
            [],
            running,
        )
    else:
        last = []
        running = pl.pallas_call(
            functools.partial(gathered_kernel, heads),
            out_shape=[jax.ShapeDtypeStruct((query_rows, size), F32) for size in (1, 1, DC)],
            in_specs=[vmem()] * (heads + 2),
            out_specs=[vmem()] * 3,
            scratch_shapes=[pltpu.VMEM((BLOCK_CHUNKS * rows, DC + DR), BF16)],
            compiler_params=pltpu.CompilerParams(vmem_limit_bytes=LARGE_VMEM),
            name="gathered",
        )(*both, biases[0], lax.all_gather(packed, "ctx", axis=0))

    tiles = 7 if width % 896 == 0 else 1
    return pl.pallas_call(
        functools.partial(finish_kernel, heads, len(last)),
        out_shape=jax.ShapeDtypeStruct((rows, width), BF16),
        in_specs=[vmem()] * (heads + 3 + len(biases[2:]) + len(last) + 2),
        out_specs=anywhere(),
        scratch_shapes=[
            pltpu.VMEM((rows, width), BF16),
            pltpu.VMEM((rows, DC + DR), BF16),
            pltpu.SemaphoreType.DMA((tiles,)),
        ],
        compiler_params=small,
        name="finish",
    )(*both, *running, *biases[2:], *last, *weights)


def solution(mesh):
    in_specs = (
        P(("docs", "ctx"), "heads"),
        P(("docs", "ctx"), "heads"),
        P(("docs", "ctx"), None),
        P(("docs", "ctx"), None),
        P(None, "heads"),
        P(None, "heads"),
        P("heads", None),
        P("docs"),
    )
    out_specs = P(("docs", "ctx"), "heads")
    return jax.shard_map(
        functools.partial(per_device, mesh.shape["ctx"]),
        mesh=mesh,
        in_specs=in_specs,
        out_specs=out_specs,
        check_vma=False,
    )
```

```python
import functools
import math

import jax
import jax.numpy as jnp
from jax import lax
from jax.experimental import pallas as pl
from jax.experimental.pallas import tpu as pltpu
from jax.sharding import PartitionSpec as P

DC = 512
DH = 128
DR = 64
BF16 = jnp.bfloat16
F32 = jnp.float32
MASKED = -1e30
BLOCK_CHUNKS = 8
PREPARE_COST, FIRST_COST, SECOND_COST = 0, 0, 30
SMALL_VMEM = 20 * 1024 * 1024
LARGE_VMEM = 56 * 1024 * 1024
FAR = (4, 6)
NEAR = (2, 3)
BESIDE = (1, 1)
RELAYED = (5, 7)


def vmem():
    return pl.BlockSpec(memory_space=pltpu.VMEM)


def anywhere():
    return pl.BlockSpec(memory_space=pl.ANY)


def hbm():
    return pl.BlockSpec(memory_space=pltpu.HBM)


def cost(microseconds):
    return pl.CostEstimate(flops=int(microseconds * 1.1e9), bytes_accessed=0, transcendentals=0)


def smem():
    return pl.BlockSpec(memory_space=pltpu.SMEM)


def pack_kernel(latent, key_rope_turned, out_ref):
    rows = latent.shape[0]
    group = rows // 6
    out_ref[:rows] = latent[...]
    rope = key_rope_turned[...].astype(F32).T.astype(BF16)
    parts = [rope[index * group : (index + 1) * group] for index in range(6)]
    parts.append(jnp.zeros((group, DC - 6 * DR), BF16))
    out_ref[rows:] = jnp.concatenate(parts, axis=1)


def unpack(chunk, keys, base):
    rows = 6 * chunk.shape[0] // 7
    group = rows // 6
    keys[pl.ds(base, rows), :DC] = chunk[:rows]
    for index in range(6):
        part = chunk[rows:, index * DR : (index + 1) * DR]
        keys[pl.ds(base + index * group, group), DC:] = part


def fetch_weights(value_up, out_proj, target, other, sems):
    depth, width = out_proj.shape[0], out_proj.shape[1] // 2
    part = lax.axis_index("heads") ^ other
    columns = pl.ds(pl.multiple_of(part * width, 128), width)
    pairs = [(out_proj.at[:, columns], target.at[:, pl.ds(0, width)])]
    for block in range(DC // depth):
        place = pl.ds(width + block * value_up.shape[1], value_up.shape[1])
        pairs.append((value_up.at[pl.ds(block * depth, depth)], target.at[:, place]))
    fetches = [pltpu.make_async_copy(*pair, sems.at[i]) for i, pair in enumerate(pairs)]
    for fetch in fetches:
        fetch.start()
    return fetches


def prepare_kernel(order, span_order, _, nope_in, rope_in, up_in, value_up, out_proj, *outs):
    weights_sent, nope, rope, up, input_sems, sems = outs[-6:]
    inputs = [
        pltpu.make_async_copy(source, target, input_sems.at[index])
        for index, (source, target) in enumerate(((nope_in, nope), (rope_in, rope), (up_in, up)))
    ]
    for fetch in inputs:
        fetch.start()
    fetches = fetch_weights(value_up, out_proj, weights_sent, 1, sems)
    for fetch in inputs:
        fetch.wait()
    rows = nope.shape[0]
    heads = nope.shape[1] // DH
    span_rows = rows // 2
    own_index = lax.axis_index("ctx")
    core = lax.axis_index("heads")
    for head in range(heads):
        latent = lax.dot_general(
            nope[:, head * DH : (head + 1) * DH],
            up[:, head * DH : (head + 1) * DH],
            (((1,), (1,)), ((), ())),
            preferred_element_type=F32,
        )
        outs[head][:, :DC] = latent.astype(BF16)
        outs[head][:, DC:] = rope[:, head * DR : (head + 1) * DR]
    biases = outs[heads:-6]
    row = lax.broadcasted_iota(jnp.int32, (rows, 1), 0)
    query_pos = jnp.where(
        row < span_rows,
        span_order[2 * own_index] * span_rows + row,
        span_order[2 * own_index + 1] * span_rows + row - span_rows,
    )

    def bias_of(owners):
        column = lax.broadcasted_iota(jnp.int32, (1, len(owners) * rows), 1)
        key_pos = jnp.zeros(column.shape, jnp.int32)
        for index, owner in enumerate(owners):
            for side in range(2):
                start = index * rows + side * span_rows
                first = span_order[2 * owner + side] * span_rows
                key_pos = jnp.where(column >= start, first + column - start, key_pos)
        return jnp.where(key_pos <= query_pos, F32(0.0), F32(MASKED))

    if order is not None:
        for steps, bias_ref in zip(order, biases):
            bias_ref[0] = bias_of(
                [own_index ^ jnp.where(core == 0, step[0], step[1]) for step in steps]
            )
    else:
        bias_ref = biases[0]

        def step(block, carry):
            bias_ref[block] = bias_of([block * BLOCK_CHUNKS + index for index in range(BLOCK_CHUNKS)])
            return carry

        lax.fori_loop(0, bias_ref.shape[0], step, 0)

    for fetch in fetches:
        fetch.wait()


def attend_block(queries, keys, bias, old):
    copies = len(queries)
    scale = math.log2(math.e) / math.sqrt(DH + DR)
    heads = jnp.concatenate([part[...] for part in queries], axis=0)
    scores = lax.dot_general(
        heads, keys[...], (((1,), (1,)), ((), ())), preferred_element_type=F32
    )
    scores = scores + jnp.concatenate([bias] * copies, axis=0)
    top = jnp.max(scores, axis=-1, keepdims=True)
    if old is not None:
        top = jnp.maximum(old[0], top)
        rescale = jnp.exp2((old[0] - top) * scale)
    expo = jnp.exp2((scores - top) * scale)
    total = jnp.sum(expo, axis=-1, keepdims=True)
    added = jnp.dot(expo.astype(BF16), keys[:, :DC], preferred_element_type=F32)
    if old is not None:
        total = old[1] * rescale + total
        added = old[2] * rescale + added
    return top, total, added


def chunks_kernel(heads, chunk_count, old_count, extras, *rest):
    queries, bias, rest = rest[:heads], rest[heads], rest[heads + 1 :]
    chunks, rest = rest[:chunk_count], rest[chunk_count:]
    old, rest = rest[:old_count], rest[old_count:]
    if extras:
        (value_up, out_proj, passed), rest = rest[:3], rest[3:]
        running, (weights, handed), (keys, sems) = rest[:3], rest[3:5], rest[5:]
        fetches = fetch_weights(value_up, out_proj, weights, 0, sems)
        handed[...] = passed[...]
    else:
        running, (keys,) = rest[:3], rest[3:]
    rows = bias.shape[1]
    for index, chunk in enumerate(chunks):
        unpack(chunk, keys, index * rows)
    before = [state[...] for state in old] if old else None
    values = attend_block(queries, keys, bias[0], before)
    for state, value in zip(running, values):
        state[...] = value
    if extras:
        for fetch in fetches:
            fetch.wait()


def gathered_kernel(heads, *rest):
    queries, (bias, gathered, value_up, out_proj) = rest[:heads], rest[heads : heads + 4]
    running, (weights, keys, sems) = rest[heads + 4 : heads + 7], rest[heads + 7 :]
    fetches = fetch_weights(value_up, out_proj, weights, 0, sems)
    blocks, rows, _ = bias.shape

    def fill(block):
        for index in range(BLOCK_CHUNKS):
            unpack(gathered.at[block * BLOCK_CHUNKS + index], keys, index * rows)

    first = lax.axis_index("ctx") // BLOCK_CHUNKS
    fill(first)
    values = attend_block(queries, keys, bias[first], None)
    for state, value in zip(running, values):
        state[...] = value

    def step(index, carry):
        block = index + jnp.where(index >= first, 1, 0)
        fill(block)
        new = attend_block(queries, keys, bias[block], [state[...] for state in running])
        for state, value in zip(running, new):
            state[...] = value
        return carry

    lax.fori_loop(0, blocks - 1, step, 0)
    for fetch in fetches:
        fetch.wait()


def finish_kernel(heads, chunk_count, *rest):
    queries, (top, total, context), rest = rest[:heads], rest[heads : heads + 3], rest[heads + 3 :]
    bias, chunks = rest[:chunk_count][:1], rest[1 : 1 + chunk_count]
    rest = rest[len(bias) + len(chunks) :]
    weights, (out_ref, out_tiles, keys, out_sems) = rest[:2], rest[2:]
    rows, width = out_ref.shape
    running = (top[...], total[...], context[...])
    if chunk_count:
        for index, chunk in enumerate(chunks):
            unpack(chunk, keys, index * rows)
        running = attend_block(queries, keys, bias[0][0], running)
    mixed = (running[2] / running[1]).astype(BF16)
    half = heads // 2
    depth = weights[0].shape[0]
    sides = []
    for group, weight in enumerate(weights):
        parts = []
        for head in range(half):
            rows_of = slice((group * half + head) * rows, (group * half + head + 1) * rows)
            per_head = 0.0
            for block in range(DC // depth):
                first = width + block * half * DH + head * DH
                per_head = per_head + jnp.dot(
                    mixed[rows_of, block * depth : (block + 1) * depth],
                    weight[:, first : first + DH],
                    preferred_element_type=F32,
                )
            parts.append(per_head.astype(BF16))
        sides.append(jnp.concatenate(parts, axis=1))
    tiles = out_sems.shape[0]
    tile = width // tiles
    sends = []
    for index in range(tiles):
        part = pl.ds(index * tile, tile)
        out = jnp.dot(sides[0], weights[0][:, part], preferred_element_type=F32)
        out = out + jnp.dot(sides[1], weights[1][:, part], preferred_element_type=F32)
        out_tiles[:, part] = out.astype(BF16)
        sends.append(
            pltpu.make_async_copy(out_tiles.at[:, part], out_ref.at[:, part], out_sems.at[index])
        )
        sends[-1].start()
    for send in sends:
        send.wait()


def per_device(
    count, queries_nope, queries_rope, latent, key_rope, key_up, value_up, out_proj, span_order
):
    rows = latent.shape[0]
    depth, width = out_proj.shape[0], out_proj.shape[1] // 2
    blocks = DC // depth
    heads = 2 * (key_up.shape[1] // DH)
    query_rows = heads * rows
    direct = count == 8
    small = pltpu.CompilerParams(vmem_limit_bytes=SMALL_VMEM)

    def in_hbm(*arrays):
        return [pltpu.with_memory_space_constraint(array, pltpu.HBM) for array in arrays]

    def other_core(array):
        return lax.ppermute(array, "heads", [(0, 1), (1, 0)])

    def partners(array, steps):
        pairs = [
            (2 * index + core, 2 * (index ^ steps[core]) + core)
            for index in range(count)
            for core in range(2)
        ]
        return lax.ppermute(array, ("ctx", "heads"), pairs)

    weights_shape = jax.ShapeDtypeStruct((depth, width + blocks * key_up.shape[1]), BF16)

    def attend(name, estimate, queries, bias, chunks, old=(), extras=()):
        more = [weights_shape] + [jax.ShapeDtypeStruct(extras[-1].shape, BF16)] if extras else []
        return pl.pallas_call(
            functools.partial(chunks_kernel, heads, len(chunks), len(old), bool(extras)),
            out_shape=[jax.ShapeDtypeStruct((query_rows, size), F32) for size in (1, 1, DC)] + more,
            in_specs=[vmem()] * (heads + 1 + len(chunks) + len(old))
            + [hbm(), hbm(), vmem()][: len(extras)],
            out_specs=[vmem()] * 3 + [anywhere(), vmem()][: len(more)],
            scratch_shapes=[pltpu.VMEM((len(chunks) * rows, DC + DR), BF16)]
            + [pltpu.SemaphoreType.DMA((1 + blocks,))] * bool(extras),
            compiler_params=small,
            cost_estimate=cost(estimate),
            name=name,
        )(*queries, bias, *chunks, *old, *extras)

    packed = pl.pallas_call(
        pack_kernel,
        out_shape=jax.ShapeDtypeStruct((rows + rows // 6, DC), BF16),
        in_specs=[vmem()] * 2,
        out_specs=vmem(),
        compiler_params=small,
        name="pack",
    )(*in_hbm(latent, key_rope.T))
    if direct:
        order = [
            [(0, 0), BESIDE, NEAR],
            [NEAR[::-1], FAR, FAR[::-1], RELAYED],
            [RELAYED[::-1]],
        ]
        bias_shapes = [(1, rows, len(steps) * rows) for steps in order]
    else:
        order = None
        bias_shapes = [(count // BLOCK_CHUNKS, rows, BLOCK_CHUNKS * rows)]
    outs = pl.pallas_call(
        functools.partial(prepare_kernel, order),
        out_shape=[jax.ShapeDtypeStruct((rows, DC + DR), BF16)] * (heads // 2)
        + [jax.ShapeDtypeStruct(shape, F32) for shape in bias_shapes]
        + [weights_shape],
        in_specs=[smem(), anywhere()] + [hbm()] * 5,
        out_specs=[vmem()] * (heads // 2 + len(bias_shapes)) + [anywhere()],
        scratch_shapes=[
            pltpu.VMEM(queries_nope.shape, BF16),
            pltpu.VMEM(queries_rope.shape, BF16),
            pltpu.VMEM(key_up.shape, BF16),
            pltpu.SemaphoreType.DMA((3,)),
            pltpu.SemaphoreType.DMA((1 + blocks,)),
        ],
        compiler_params=small,
        cost_estimate=cost(PREPARE_COST),
        name="prepare",
    )(*in_hbm(span_order), packed, *in_hbm(queries_nope, queries_rope, key_up, value_up, out_proj))
    queries, biases = outs[: heads // 2], outs[heads // 2 : -1]
    weights_other = other_core(outs[-1])
    both = [*queries, *map(other_core, queries)]

    if direct:
        far = partners(packed, FAR)
        near = partners(packed, NEAR)
        beside = partners(packed, BESIDE)
        relayed = partners(far, (1, 1))
        *running, weights_own, far_after = attend(
            "first",
            FIRST_COST,
            both,
            biases[0],
            [packed, beside, near],
            extras=[*in_hbm(value_up, out_proj), far],
        )
        last = [other_core(relayed)]
        running = attend(
            "second",
            SECOND_COST,
            both,
            biases[1],
            [other_core(near), far, other_core(far_after), relayed],
            running,
        )
    else:
        last = []
        *running, weights_own = pl.pallas_call(
            functools.partial(gathered_kernel, heads),
            out_shape=[jax.ShapeDtypeStruct((query_rows, size), F32) for size in (1, 1, DC)]
            + [weights_shape],
            in_specs=[vmem()] * (heads + 2) + [hbm()] * 2,
            out_specs=[vmem()] * 3 + [anywhere()],
            scratch_shapes=[
                pltpu.VMEM((BLOCK_CHUNKS * rows, DC + DR), BF16),
                pltpu.SemaphoreType.DMA((1 + blocks,)),
            ],
            compiler_params=pltpu.CompilerParams(vmem_limit_bytes=LARGE_VMEM),
            name="gathered",
        )(
            *both,
            biases[0],
            lax.all_gather(packed, "ctx", axis=0),
            *in_hbm(value_up, out_proj),
        )

    tiles = 7 if width % 896 == 0 else 1
    return pl.pallas_call(
        functools.partial(finish_kernel, heads, len(last)),
        out_shape=jax.ShapeDtypeStruct((rows, width), BF16),
        in_specs=[vmem()] * (heads + 3 + len(biases[2:]) + len(last) + 2),
        out_specs=anywhere(),
        scratch_shapes=[
            pltpu.VMEM((rows, width), BF16),
            pltpu.VMEM((rows, DC + DR), BF16),
            pltpu.SemaphoreType.DMA((tiles,)),
        ],
        compiler_params=small,
        name="finish",
    )(*both, *running, *biases[2:], *last, weights_own, weights_other)


def solution(mesh):
    in_specs = (
        P(("docs", "ctx"), "heads"),
        P(("docs", "ctx"), "heads"),
        P(("docs", "ctx"), None),
        P(("docs", "ctx"), None),
        P(None, "heads"),
        P(None, "heads"),
        P("heads", None),
        P("docs"),
    )
    out_specs = P(("docs", "ctx"), "heads")
    return jax.shard_map(
        functools.partial(per_device, mesh.shape["ctx"]),
        mesh=mesh,
        in_specs=in_specs,
        out_specs=out_specs,
        check_vma=False,
    )
```

```python
import functools
import math

import jax
import jax.numpy as jnp
from jax import lax
from jax.experimental import pallas as pl
from jax.experimental.pallas import tpu as pltpu
from jax.sharding import PartitionSpec as P

DC = 512
DH = 128
DR = 64
BF16 = jnp.bfloat16
F32 = jnp.float32
MASKED = -1e30
BLOCK_CHUNKS = 8
PREPARE_COST, FIRST_COST, SECOND_COST = 0, 3, 18
PIECES = 4
SMALL_VMEM = 20 * 1024 * 1024
LARGE_VMEM = 56 * 1024 * 1024
FAR = (4, 6)
NEAR = (2, 3)
BESIDE = (1, 1)
RELAYED = (5, 7)


def vmem():
    return pl.BlockSpec(memory_space=pltpu.VMEM)


def anywhere():
    return pl.BlockSpec(memory_space=pl.ANY)


def hbm():
    return pl.BlockSpec(memory_space=pltpu.HBM)


def cost(microseconds):
    return pl.CostEstimate(flops=int(microseconds * 1.1e9), bytes_accessed=0, transcendentals=0)


def smem():
    return pl.BlockSpec(memory_space=pltpu.SMEM)


def pack_kernel(latent, key_rope_turned, out_ref):
    rows = latent.shape[0]
    group = rows // 6
    out_ref[:rows] = latent[...]
    rope = key_rope_turned[...].astype(F32).T.astype(BF16)
    parts = [rope[index * group : (index + 1) * group] for index in range(6)]
    parts.append(jnp.zeros((group, DC - 6 * DR), BF16))
    out_ref[rows:] = jnp.concatenate(parts, axis=1)


def unpack(chunk, keys, base):
    rows = 6 * chunk.shape[0] // 7
    group = rows // 6
    keys[pl.ds(base, rows), :DC] = chunk[:rows]
    for index in range(6):
        part = chunk[rows:, index * DR : (index + 1) * DR]
        keys[pl.ds(base + index * group, group), DC:] = part


def fetch_weights(value_up, out_proj, target, other, sems):
    depth, width = out_proj.shape[0], out_proj.shape[1] // 2
    part = lax.axis_index("heads") ^ other
    columns = pl.ds(pl.multiple_of(part * width, 128), width)
    pairs = []
    for piece in range(PIECES):
        some = pl.ds(piece * (depth // PIECES), depth // PIECES)
        pairs.append((out_proj.at[some, columns], target.at[some, pl.ds(0, width)]))
    for block in range(DC // depth):
        place = pl.ds(width + block * value_up.shape[1], value_up.shape[1])
        pairs.append((value_up.at[pl.ds(block * depth, depth)], target.at[:, place]))
    fetches = [pltpu.make_async_copy(*pair, sems.at[i]) for i, pair in enumerate(pairs)]
    for fetch in fetches:
        fetch.start()
    return fetches


def prepare_kernel(order, span_order, _, nope_in, rope_in, up_in, value_up, out_proj, *outs):
    weights_sent, nope, rope, up, input_sems, sems = outs[-6:]
    inputs = [
        pltpu.make_async_copy(source, target, input_sems.at[index])
        for index, (source, target) in enumerate(((nope_in, nope), (rope_in, rope), (up_in, up)))
    ]
    for fetch in inputs:
        fetch.start()
    fetches = fetch_weights(value_up, out_proj, weights_sent, 1, sems)
    for fetch in inputs:
        fetch.wait()
    rows = nope.shape[0]
    heads = nope.shape[1] // DH
    span_rows = rows // 2
    own_index = lax.axis_index("ctx")
    core = lax.axis_index("heads")
    for head in range(heads):
        latent = lax.dot_general(
            nope[:, head * DH : (head + 1) * DH],
            up[:, head * DH : (head + 1) * DH],
            (((1,), (1,)), ((), ())),
            preferred_element_type=F32,
        )
        outs[head][:, :DC] = latent.astype(BF16)
        outs[head][:, DC:] = rope[:, head * DR : (head + 1) * DR]
    biases = outs[heads:-6]
    row = lax.broadcasted_iota(jnp.int32, (rows, 1), 0)
    query_pos = jnp.where(
        row < span_rows,
        span_order[2 * own_index] * span_rows + row,
        span_order[2 * own_index + 1] * span_rows + row - span_rows,
    )

    def bias_of(owners):
        column = lax.broadcasted_iota(jnp.int32, (1, len(owners) * rows), 1)
        key_pos = jnp.zeros(column.shape, jnp.int32)
        for index, owner in enumerate(owners):
            for side in range(2):
                start = index * rows + side * span_rows
                first = span_order[2 * owner + side] * span_rows
                key_pos = jnp.where(column >= start, first + column - start, key_pos)
        return jnp.where(key_pos <= query_pos, F32(0.0), F32(MASKED))

    if order is not None:
        for steps, bias_ref in zip(order, biases):
            bias_ref[0] = bias_of(
                [own_index ^ jnp.where(core == 0, step[0], step[1]) for step in steps]
            )
    else:
        bias_ref = biases[0]

        def step(block, carry):
            bias_ref[block] = bias_of([block * BLOCK_CHUNKS + index for index in range(BLOCK_CHUNKS)])
            return carry

        lax.fori_loop(0, bias_ref.shape[0], step, 0)

    for fetch in fetches:
        fetch.wait()


def attend_block(queries, keys, bias, old):
    copies = len(queries)
    scale = math.log2(math.e) / math.sqrt(DH + DR)
    heads = jnp.concatenate([part[...] for part in queries], axis=0)
    scores = lax.dot_general(
        heads, keys[...], (((1,), (1,)), ((), ())), preferred_element_type=F32
    )
    scores = scores + jnp.concatenate([bias] * copies, axis=0)
    top = jnp.max(scores, axis=-1, keepdims=True)
    if old is not None:
        top = jnp.maximum(old[0], top)
        rescale = jnp.exp2((old[0] - top) * scale)
    expo = jnp.exp2((scores - top) * scale)
    total = jnp.sum(expo, axis=-1, keepdims=True)
    added = jnp.dot(expo.astype(BF16), keys[:, :DC], preferred_element_type=F32)
    if old is not None:
        total = old[1] * rescale + total
        added = old[2] * rescale + added
    return top, total, added


def chunks_kernel(heads, chunk_count, old_count, extras, *rest):
    queries, bias, rest = rest[:heads], rest[heads], rest[heads + 1 :]
    chunks, rest = rest[:chunk_count], rest[chunk_count:]
    old, rest = rest[:old_count], rest[old_count:]
    if extras:
        (value_up, out_proj, passed), rest = rest[:3], rest[3:]
        running, (weights, handed), (keys, sems) = rest[:3], rest[3:5], rest[5:]
        fetches = fetch_weights(value_up, out_proj, weights, 0, sems)
        handed[...] = passed[...]
    else:
        running, (keys,) = rest[:3], rest[3:]
    rows = bias.shape[1]
    for index, chunk in enumerate(chunks):
        unpack(chunk, keys, index * rows)
    before = [state[...] for state in old] if old else None
    values = attend_block(queries, keys, bias[0], before)
    for state, value in zip(running, values):
        state[...] = value
    if extras:
        for fetch in fetches:
            fetch.wait()


def gathered_kernel(heads, *rest):
    queries, (bias, gathered, value_up, out_proj) = rest[:heads], rest[heads : heads + 4]
    running, (weights, keys, sems) = rest[heads + 4 : heads + 7], rest[heads + 7 :]
    fetches = fetch_weights(value_up, out_proj, weights, 0, sems)
    blocks, rows, _ = bias.shape

    def fill(block):
        for index in range(BLOCK_CHUNKS):
            unpack(gathered.at[block * BLOCK_CHUNKS + index], keys, index * rows)

    first = lax.axis_index("ctx") // BLOCK_CHUNKS
    fill(first)
    values = attend_block(queries, keys, bias[first], None)
    for state, value in zip(running, values):
        state[...] = value

    def step(index, carry):
        block = index + jnp.where(index >= first, 1, 0)
        fill(block)
        new = attend_block(queries, keys, bias[block], [state[...] for state in running])
        for state, value in zip(running, new):
            state[...] = value
        return carry

    lax.fori_loop(0, blocks - 1, step, 0)
    for fetch in fetches:
        fetch.wait()


def finish_kernel(heads, chunk_count, *rest):
    queries, (top, total, context), rest = rest[:heads], rest[heads : heads + 3], rest[heads + 3 :]
    bias, chunks = rest[:chunk_count][:1], rest[1 : 1 + chunk_count]
    rest = rest[len(bias) + len(chunks) :]
    weights, (out_ref, out_tiles, keys, out_sems) = rest[:2], rest[2:]
    rows, width = out_ref.shape
    running = (top[...], total[...], context[...])
    if chunk_count:
        for index, chunk in enumerate(chunks):
            unpack(chunk, keys, index * rows)
        running = attend_block(queries, keys, bias[0][0], running)
    mixed = (running[2] / running[1]).astype(BF16)
    half = heads // 2
    depth = weights[0].shape[0]
    sides = []
    for group, weight in enumerate(weights):
        parts = []
        for head in range(half):
            rows_of = slice((group * half + head) * rows, (group * half + head + 1) * rows)
            per_head = 0.0
            for block in range(DC // depth):
                first = width + block * half * DH + head * DH
                per_head = per_head + jnp.dot(
                    mixed[rows_of, block * depth : (block + 1) * depth],
                    weight[:, first : first + DH],
                    preferred_element_type=F32,
                )
            parts.append(per_head.astype(BF16))
        sides.append(jnp.concatenate(parts, axis=1))
    tiles = out_sems.shape[0]
    tile = width // tiles
    sends = []
    for index in range(tiles):
        part = pl.ds(index * tile, tile)
        out = jnp.dot(sides[0], weights[0][:, part], preferred_element_type=F32)
        out = out + jnp.dot(sides[1], weights[1][:, part], preferred_element_type=F32)
        out_tiles[:, part] = out.astype(BF16)
        sends.append(
            pltpu.make_async_copy(out_tiles.at[:, part], out_ref.at[:, part], out_sems.at[index])
        )
        sends[-1].start()
    for send in sends:
        send.wait()


def per_device(
    count, queries_nope, queries_rope, latent, key_rope, key_up, value_up, out_proj, span_order
):
    rows = latent.shape[0]
    depth, width = out_proj.shape[0], out_proj.shape[1] // 2
    blocks = DC // depth
    heads = 2 * (key_up.shape[1] // DH)
    query_rows = heads * rows
    direct = count == 8
    small = pltpu.CompilerParams(vmem_limit_bytes=SMALL_VMEM)

    def in_hbm(*arrays):
        return [pltpu.with_memory_space_constraint(array, pltpu.HBM) for array in arrays]

    def other_core(array):
        return lax.ppermute(array, "heads", [(0, 1), (1, 0)])

    def partners(array, steps):
        pairs = [
            (2 * index + core, 2 * (index ^ steps[core]) + core)
            for index in range(count)
            for core in range(2)
        ]
        return lax.ppermute(array, ("ctx", "heads"), pairs)

    weights_shape = jax.ShapeDtypeStruct((depth, width + blocks * key_up.shape[1]), BF16)

    def attend(name, estimate, queries, bias, chunks, old=(), extras=()):
        more = [weights_shape] + [jax.ShapeDtypeStruct(extras[-1].shape, BF16)] if extras else []
        return pl.pallas_call(
            functools.partial(chunks_kernel, heads, len(chunks), len(old), bool(extras)),
            out_shape=[jax.ShapeDtypeStruct((query_rows, size), F32) for size in (1, 1, DC)] + more,
            in_specs=[vmem()] * (heads + 1 + len(chunks) + len(old))
            + [hbm(), hbm(), vmem()][: len(extras)],
            out_specs=[vmem()] * 3 + [anywhere(), vmem()][: len(more)],
            scratch_shapes=[pltpu.VMEM((len(chunks) * rows, DC + DR), BF16)]
            + [pltpu.SemaphoreType.DMA((PIECES + blocks,))] * bool(extras),
            compiler_params=small,
            cost_estimate=cost(estimate),
            name=name,
        )(*queries, bias, *chunks, *old, *extras)

    packed = pl.pallas_call(
        pack_kernel,
        out_shape=jax.ShapeDtypeStruct((rows + rows // 6, DC), BF16),
        in_specs=[vmem()] * 2,
        out_specs=vmem(),
        compiler_params=small,
        name="pack",
    )(*in_hbm(latent, key_rope.T))
    if direct:
        order = [
            [(0, 0), BESIDE, NEAR],
            [NEAR[::-1], FAR, FAR[::-1], RELAYED],
            [RELAYED[::-1]],
        ]
        bias_shapes = [(1, rows, len(steps) * rows) for steps in order]
    else:
        order = None
        bias_shapes = [(count // BLOCK_CHUNKS, rows, BLOCK_CHUNKS * rows)]
    outs = pl.pallas_call(
        functools.partial(prepare_kernel, order),
        out_shape=[jax.ShapeDtypeStruct((rows, DC + DR), BF16)] * (heads // 2)
        + [jax.ShapeDtypeStruct(shape, F32) for shape in bias_shapes]
        + [weights_shape],
        in_specs=[smem(), anywhere()] + [hbm()] * 5,
        out_specs=[vmem()] * (heads // 2 + len(bias_shapes)) + [anywhere()],
        scratch_shapes=[
            pltpu.VMEM(queries_nope.shape, BF16),
            pltpu.VMEM(queries_rope.shape, BF16),
            pltpu.VMEM(key_up.shape, BF16),
            pltpu.SemaphoreType.DMA((3,)),
            pltpu.SemaphoreType.DMA((PIECES + blocks,)),
        ],
        compiler_params=small,
        cost_estimate=cost(PREPARE_COST),
        name="prepare",
    )(*in_hbm(span_order), packed, *in_hbm(queries_nope, queries_rope, key_up, value_up, out_proj))
    queries, biases = outs[: heads // 2], outs[heads // 2 : -1]
    weights_other = other_core(outs[-1])
    both = [*queries, *map(other_core, queries)]

    if direct:
        far = partners(packed, FAR)
        near = partners(packed, NEAR)
        beside = partners(packed, BESIDE)
        relayed = partners(far, (1, 1))
        *running, weights_own, far_after = attend(
            "first",
            FIRST_COST,
            both,
            biases[0],
            [packed, beside, near],
            extras=[*in_hbm(value_up, out_proj), far],
        )
        last = [other_core(relayed)]
        running = attend(
            "second",
            SECOND_COST,
            both,
            biases[1],
            [other_core(near), far, other_core(far_after), relayed],
            running,
        )
    else:
        last = []
        *running, weights_own = pl.pallas_call(
            functools.partial(gathered_kernel, heads),
            out_shape=[jax.ShapeDtypeStruct((query_rows, size), F32) for size in (1, 1, DC)]
            + [weights_shape],
            in_specs=[vmem()] * (heads + 2) + [hbm()] * 2,
            out_specs=[vmem()] * 3 + [anywhere()],
            scratch_shapes=[
                pltpu.VMEM((BLOCK_CHUNKS * rows, DC + DR), BF16),
                pltpu.SemaphoreType.DMA((PIECES + blocks,)),
            ],
            compiler_params=pltpu.CompilerParams(vmem_limit_bytes=LARGE_VMEM),
            name="gathered",
        )(
            *both,
            biases[0],
            lax.all_gather(packed, "ctx", axis=0),
            *in_hbm(value_up, out_proj),
        )

    tiles = 7 if width % 896 == 0 else 1
    return pl.pallas_call(
        functools.partial(finish_kernel, heads, len(last)),
        out_shape=jax.ShapeDtypeStruct((rows, width), BF16),
        in_specs=[vmem()] * (heads + 3 + len(biases[2:]) + len(last) + 2),
        out_specs=anywhere(),
        scratch_shapes=[
            pltpu.VMEM((rows, width), BF16),
            pltpu.VMEM((rows, DC + DR), BF16),
            pltpu.SemaphoreType.DMA((tiles,)),
        ],
        compiler_params=small,
        name="finish",
    )(*both, *running, *biases[2:], *last, weights_own, weights_other)


def solution(mesh):
    in_specs = (
        P(("docs", "ctx"), "heads"),
        P(("docs", "ctx"), "heads"),
        P(("docs", "ctx"), None),
        P(("docs", "ctx"), None),
        P(None, "heads"),
        P(None, "heads"),
        P("heads", None),
        P("docs"),
    )
    out_specs = P(("docs", "ctx"), "heads")
    return jax.shard_map(
        functools.partial(per_device, mesh.shape["ctx"]),
        mesh=mesh,
        in_specs=in_specs,
        out_specs=out_specs,
        check_vma=False,
    )
```

```python
import functools
import math

import jax
import jax.numpy as jnp
from jax import lax
from jax.experimental import pallas as pl
from jax.experimental.pallas import tpu as pltpu
from jax.sharding import PartitionSpec as P

DC = 512
DH = 128
DR = 64
BF16 = jnp.bfloat16
F32 = jnp.float32
MASKED = -1e30
BLOCK_CHUNKS = 8
PREPARE_COST, FIRST_COST, SECOND_COST = 0, 3, 18
PIECES = 4
SMALL_VMEM = 20 * 1024 * 1024
LARGE_VMEM = 56 * 1024 * 1024
FAR = (4, 6)
NEAR = (2, 3)
BESIDE = (1, 1)
RELAYED = (5, 7)


def vmem():
    return pl.BlockSpec(memory_space=pltpu.VMEM)


def anywhere():
    return pl.BlockSpec(memory_space=pl.ANY)


def hbm():
    return pl.BlockSpec(memory_space=pltpu.HBM)


def cost(microseconds):
    return pl.CostEstimate(flops=int(microseconds * 1.1e9), bytes_accessed=0, transcendentals=0)


def smem():
    return pl.BlockSpec(memory_space=pltpu.SMEM)


def pack_kernel(latent, key_rope_turned, out_ref):
    rows = latent.shape[0]
    group = rows // 6
    out_ref[:rows] = latent[...]
    rope = key_rope_turned[...].astype(F32).T.astype(BF16)
    parts = [rope[index * group : (index + 1) * group] for index in range(6)]
    parts.append(jnp.zeros((group, DC - 6 * DR), BF16))
    out_ref[rows:] = jnp.concatenate(parts, axis=1)


def unpack(chunk, keys, base):
    rows = 6 * chunk.shape[0] // 7
    group = rows // 6
    keys[pl.ds(base, rows), :DC] = chunk[:rows]
    for index in range(6):
        part = chunk[rows:, index * DR : (index + 1) * DR]
        keys[pl.ds(base + index * group, group), DC:] = part


def fetch_weights(value_up, out_proj, target, other, value, sems):
    depth, width = out_proj.shape[0], out_proj.shape[1] // 2
    part = lax.axis_index("heads") ^ other
    columns = pl.ds(pl.multiple_of(part * width, 128), width)
    fetches = [pltpu.make_async_copy(value_up, value, sems.at[PIECES])]
    for piece in range(PIECES):
        some = pl.ds(piece * (depth // PIECES), depth // PIECES)
        fetches.append(
            pltpu.make_async_copy(
                out_proj.at[some, columns], target.at[some, pl.ds(0, width)], sems.at[piece]
            )
        )
    for fetch in fetches:
        fetch.start()

    def finish():
        fetches[0].wait()
        columns = value.shape[1]
        for block in range(DC // depth):
            place = pl.ds(width + block * columns, columns)
            target[:, place] = value[pl.ds(block * depth, depth), :]
        for fetch in fetches[1:]:
            fetch.wait()

    return finish


def prepare_kernel(order, span_order, _, nope_in, rope_in, up_in, value_up, out_proj, *outs):
    weights_sent, nope, rope, up, value, input_sems, sems = outs[-7:]
    inputs = [
        pltpu.make_async_copy(source, target, input_sems.at[index])
        for index, (source, target) in enumerate(((nope_in, nope), (rope_in, rope), (up_in, up)))
    ]
    for fetch in inputs:
        fetch.start()
    finish = fetch_weights(value_up, out_proj, weights_sent, 1, value, sems)
    for fetch in inputs:
        fetch.wait()
    rows = nope.shape[0]
    heads = nope.shape[1] // DH
    span_rows = rows // 2
    own_index = lax.axis_index("ctx")
    core = lax.axis_index("heads")
    for head in range(heads):
        latent = lax.dot_general(
            nope[:, head * DH : (head + 1) * DH],
            up[:, head * DH : (head + 1) * DH],
            (((1,), (1,)), ((), ())),
            preferred_element_type=F32,
        )
        outs[head][:, :DC] = latent.astype(BF16)
        outs[head][:, DC:] = rope[:, head * DR : (head + 1) * DR]
    biases = outs[heads:-7]
    row = lax.broadcasted_iota(jnp.int32, (rows, 1), 0)
    query_pos = jnp.where(
        row < span_rows,
        span_order[2 * own_index] * span_rows + row,
        span_order[2 * own_index + 1] * span_rows + row - span_rows,
    )

    def bias_of(owners):
        column = lax.broadcasted_iota(jnp.int32, (1, len(owners) * rows), 1)
        key_pos = jnp.zeros(column.shape, jnp.int32)
        for index, owner in enumerate(owners):
            for side in range(2):
                start = index * rows + side * span_rows
                first = span_order[2 * owner + side] * span_rows
                key_pos = jnp.where(column >= start, first + column - start, key_pos)
        return jnp.where(key_pos <= query_pos, F32(0.0), F32(MASKED))

    if order is not None:
        for steps, bias_ref in zip(order, biases):
            bias_ref[0] = bias_of(
                [own_index ^ jnp.where(core == 0, step[0], step[1]) for step in steps]
            )
    else:
        bias_ref = biases[0]

        def step(block, carry):
            bias_ref[block] = bias_of([block * BLOCK_CHUNKS + index for index in range(BLOCK_CHUNKS)])
            return carry

        lax.fori_loop(0, bias_ref.shape[0], step, 0)

    finish()


def attend_block(queries, keys, bias, old):
    copies = len(queries)
    scale = math.log2(math.e) / math.sqrt(DH + DR)
    heads = jnp.concatenate([part[...] for part in queries], axis=0)
    scores = lax.dot_general(
        heads, keys[...], (((1,), (1,)), ((), ())), preferred_element_type=F32
    )
    scores = scores + jnp.concatenate([bias] * copies, axis=0)
    top = jnp.max(scores, axis=-1, keepdims=True)
    if old is not None:
        top = jnp.maximum(old[0], top)
        rescale = jnp.exp2((old[0] - top) * scale)
    expo = jnp.exp2((scores - top) * scale)
    total = jnp.sum(expo, axis=-1, keepdims=True)
    added = jnp.dot(expo.astype(BF16), keys[:, :DC], preferred_element_type=F32)
    if old is not None:
        total = old[1] * rescale + total
        added = old[2] * rescale + added
    return top, total, added


def chunks_kernel(heads, chunk_count, old_count, extras, *rest):
    queries, bias, rest = rest[:heads], rest[heads], rest[heads + 1 :]
    chunks, rest = rest[:chunk_count], rest[chunk_count:]
    old, rest = rest[:old_count], rest[old_count:]
    if extras:
        (value_up, out_proj, passed), rest = rest[:3], rest[3:]
        running, (weights, handed), (keys, own, sems) = rest[:3], rest[3:5], rest[5:]
        finish = fetch_weights(value_up, out_proj, weights, 0, own, sems)
        handed[...] = passed[...]
    else:
        running, (keys,) = rest[:3], rest[3:]
    rows = bias.shape[1]
    for index, chunk in enumerate(chunks):
        unpack(chunk, keys, index * rows)
    before = [state[...] for state in old] if old else None
    values = attend_block(queries, keys, bias[0], before)
    for state, value in zip(running, values):
        state[...] = value
    if extras:
        finish()


def gathered_kernel(heads, *rest):
    queries, (bias, gathered, value_up, out_proj) = rest[:heads], rest[heads : heads + 4]
    running, (weights, keys, own, sems) = rest[heads + 4 : heads + 7], rest[heads + 7 :]
    finish = fetch_weights(value_up, out_proj, weights, 0, own, sems)
    blocks, rows, _ = bias.shape

    def fill(block):
        for index in range(BLOCK_CHUNKS):
            unpack(gathered.at[block * BLOCK_CHUNKS + index], keys, index * rows)

    first = lax.axis_index("ctx") // BLOCK_CHUNKS
    fill(first)
    values = attend_block(queries, keys, bias[first], None)
    for state, value in zip(running, values):
        state[...] = value

    def step(index, carry):
        block = index + jnp.where(index >= first, 1, 0)
        fill(block)
        new = attend_block(queries, keys, bias[block], [state[...] for state in running])
        for state, value in zip(running, new):
            state[...] = value
        return carry

    lax.fori_loop(0, blocks - 1, step, 0)
    finish()


def finish_kernel(heads, chunk_count, *rest):
    queries, (top, total, context), rest = rest[:heads], rest[heads : heads + 3], rest[heads + 3 :]
    bias, chunks = rest[:chunk_count][:1], rest[1 : 1 + chunk_count]
    rest = rest[len(bias) + len(chunks) :]
    weights, (out_ref, out_tiles, keys, out_sems) = rest[:2], rest[2:]
    rows, width = out_ref.shape
    running = (top[...], total[...], context[...])
    if chunk_count:
        for index, chunk in enumerate(chunks):
            unpack(chunk, keys, index * rows)
        running = attend_block(queries, keys, bias[0][0], running)
    mixed = (running[2] / running[1]).astype(BF16)
    half = heads // 2
    depth = weights[0].shape[0]
    sides = []
    for group, weight in enumerate(weights):
        parts = []
        for head in range(half):
            rows_of = slice((group * half + head) * rows, (group * half + head + 1) * rows)
            per_head = 0.0
            for block in range(DC // depth):
                first = width + block * half * DH + head * DH
                per_head = per_head + jnp.dot(
                    mixed[rows_of, block * depth : (block + 1) * depth],
                    weight[:, first : first + DH],
                    preferred_element_type=F32,
                )
            parts.append(per_head.astype(BF16))
        sides.append(jnp.concatenate(parts, axis=1))
    tiles = out_sems.shape[0]
    tile = width // tiles
    sends = []
    for index in range(tiles):
        part = pl.ds(index * tile, tile)
        out = jnp.dot(sides[0], weights[0][:, part], preferred_element_type=F32)
        out = out + jnp.dot(sides[1], weights[1][:, part], preferred_element_type=F32)
        out_tiles[:, part] = out.astype(BF16)
        sends.append(
            pltpu.make_async_copy(out_tiles.at[:, part], out_ref.at[:, part], out_sems.at[index])
        )
        sends[-1].start()
    for send in sends:
        send.wait()


def per_device(
    count, queries_nope, queries_rope, latent, key_rope, key_up, value_up, out_proj, span_order
):
    rows = latent.shape[0]
    depth, width = out_proj.shape[0], out_proj.shape[1] // 2
    blocks = DC // depth
    heads = 2 * (key_up.shape[1] // DH)
    query_rows = heads * rows
    direct = count == 8
    small = pltpu.CompilerParams(vmem_limit_bytes=SMALL_VMEM)

    def in_hbm(*arrays):
        return [pltpu.with_memory_space_constraint(array, pltpu.HBM) for array in arrays]

    def other_core(array):
        return lax.ppermute(array, "heads", [(0, 1), (1, 0)])

    def partners(array, steps):
        pairs = [
            (2 * index + core, 2 * (index ^ steps[core]) + core)
            for index in range(count)
            for core in range(2)
        ]
        return lax.ppermute(array, ("ctx", "heads"), pairs)

    weights_shape = jax.ShapeDtypeStruct((depth, width + blocks * key_up.shape[1]), BF16)

    def attend(name, estimate, queries, bias, chunks, old=(), extras=()):
        more = [weights_shape] + [jax.ShapeDtypeStruct(extras[-1].shape, BF16)] if extras else []
        return pl.pallas_call(
            functools.partial(chunks_kernel, heads, len(chunks), len(old), bool(extras)),
            out_shape=[jax.ShapeDtypeStruct((query_rows, size), F32) for size in (1, 1, DC)] + more,
            in_specs=[vmem()] * (heads + 1 + len(chunks) + len(old))
            + [hbm(), hbm(), vmem()][: len(extras)],
            out_specs=[vmem()] * (3 + len(more)),
            scratch_shapes=[pltpu.VMEM((len(chunks) * rows, DC + DR), BF16)]
            + [pltpu.VMEM(value_up.shape, BF16), pltpu.SemaphoreType.DMA((PIECES + 1,))][: len(more)],
            compiler_params=small,
            cost_estimate=cost(estimate),
            name=name,
        )(*queries, bias, *chunks, *old, *extras)

    packed = pl.pallas_call(
        pack_kernel,
        out_shape=jax.ShapeDtypeStruct((rows + rows // 6, DC), BF16),
        in_specs=[vmem()] * 2,
        out_specs=vmem(),
        compiler_params=small,
        name="pack",
    )(*in_hbm(latent, key_rope.T))
    if direct:
        order = [
            [(0, 0), BESIDE, NEAR],
            [NEAR[::-1], FAR, FAR[::-1], RELAYED],
            [RELAYED[::-1]],
        ]
        bias_shapes = [(1, rows, len(steps) * rows) for steps in order]
    else:
        order = None
        bias_shapes = [(count // BLOCK_CHUNKS, rows, BLOCK_CHUNKS * rows)]
    outs = pl.pallas_call(
        functools.partial(prepare_kernel, order),
        out_shape=[jax.ShapeDtypeStruct((rows, DC + DR), BF16)] * (heads // 2)
        + [jax.ShapeDtypeStruct(shape, F32) for shape in bias_shapes]
        + [weights_shape],
        in_specs=[smem(), anywhere()] + [hbm()] * 5,
        out_specs=[vmem()] * (heads // 2 + len(bias_shapes) + 1),
        scratch_shapes=[
            pltpu.VMEM(queries_nope.shape, BF16),
            pltpu.VMEM(queries_rope.shape, BF16),
            pltpu.VMEM(key_up.shape, BF16),
            pltpu.VMEM(value_up.shape, BF16),
            pltpu.SemaphoreType.DMA((3,)),
            pltpu.SemaphoreType.DMA((PIECES + 1,)),
        ],
        compiler_params=small,
        cost_estimate=cost(PREPARE_COST),
        name="prepare",
    )(*in_hbm(span_order), packed, *in_hbm(queries_nope, queries_rope, key_up, value_up, out_proj))
    queries, biases = outs[: heads // 2], outs[heads // 2 : -1]
    weights_other = other_core(outs[-1])
    both = [*queries, *map(other_core, queries)]

    if direct:
        far = partners(packed, FAR)
        near = partners(packed, NEAR)
        beside = partners(packed, BESIDE)
        relayed = partners(far, (1, 1))
        *running, weights_own, far_after = attend(
            "first",
            FIRST_COST,
            both,
            biases[0],
            [packed, beside, near],
            extras=[*in_hbm(value_up, out_proj), far],
        )
        last = [other_core(relayed)]
        running = attend(
            "second",
            SECOND_COST,
            both,
            biases[1],
            [other_core(near), far, other_core(far_after), relayed],
            running,
        )
    else:
        last = []
        *running, weights_own = pl.pallas_call(
            functools.partial(gathered_kernel, heads),
            out_shape=[jax.ShapeDtypeStruct((query_rows, size), F32) for size in (1, 1, DC)]
            + [weights_shape],
            in_specs=[vmem()] * (heads + 2) + [hbm()] * 2,
            out_specs=[vmem()] * 4,
            scratch_shapes=[
                pltpu.VMEM((BLOCK_CHUNKS * rows, DC + DR), BF16),
                pltpu.VMEM(value_up.shape, BF16),
                pltpu.SemaphoreType.DMA((PIECES + 1,)),
            ],
            compiler_params=pltpu.CompilerParams(vmem_limit_bytes=LARGE_VMEM),
            name="gathered",
        )(
            *both,
            biases[0],
            lax.all_gather(packed, "ctx", axis=0),
            *in_hbm(value_up, out_proj),
        )

    tiles = 7 if width % 896 == 0 else 1
    return pl.pallas_call(
        functools.partial(finish_kernel, heads, len(last)),
        out_shape=jax.ShapeDtypeStruct((rows, width), BF16),
        in_specs=[vmem()] * (heads + 3 + len(biases[2:]) + len(last) + 2),
        out_specs=anywhere(),
        scratch_shapes=[
            pltpu.VMEM((rows, width), BF16),
            pltpu.VMEM((rows, DC + DR), BF16),
            pltpu.SemaphoreType.DMA((tiles,)),
        ],
        compiler_params=small,
        name="finish",
    )(*both, *running, *biases[2:], *last, weights_own, weights_other)


def solution(mesh):
    in_specs = (
        P(("docs", "ctx"), "heads"),
        P(("docs", "ctx"), "heads"),
        P(("docs", "ctx"), None),
        P(("docs", "ctx"), None),
        P(None, "heads"),
        P(None, "heads"),
        P("heads", None),
        P("docs"),
    )
    out_specs = P(("docs", "ctx"), "heads")
    return jax.shard_map(
        functools.partial(per_device, mesh.shape["ctx"]),
        mesh=mesh,
        in_specs=in_specs,
        out_specs=out_specs,
        check_vma=False,
    )
```

```python
import functools
import math

import jax
import jax.numpy as jnp
from jax import lax
from jax.experimental import pallas as pl
from jax.experimental.pallas import tpu as pltpu
from jax.sharding import PartitionSpec as P

DC = 512
DH = 128
DR = 64
BF16 = jnp.bfloat16
F32 = jnp.float32
MASKED = -1e30
BLOCK_CHUNKS = 8
PREPARE_COST, FIRST_COST, SECOND_COST = 0, 20, 1
SMALL_VMEM = 20 * 1024 * 1024
LARGE_VMEM = 56 * 1024 * 1024
FAR = (4, 6)
NEAR = (2, 1)
CORNER = (3, 3)
RELAYED = (5, 7)


def vmem():
    return pl.BlockSpec(memory_space=pltpu.VMEM)


def anywhere():
    return pl.BlockSpec(memory_space=pl.ANY)


def hbm():
    return pl.BlockSpec(memory_space=pltpu.HBM)


def cost(microseconds):
    return pl.CostEstimate(flops=int(microseconds * 1.1e9), bytes_accessed=0, transcendentals=0)


def pack_kernel(latent, key_rope_turned, out_ref):
    rows = latent.shape[0]
    group = rows // 6
    out_ref[:rows] = latent[...]
    rope = key_rope_turned[...].astype(F32).T.astype(BF16)
    parts = [rope[index * group : (index + 1) * group] for index in range(6)]
    parts.append(jnp.zeros((group, DC - 6 * DR), BF16))
    out_ref[rows:] = jnp.concatenate(parts, axis=1)


def unpack(chunk, keys, base, other=None):
    chunk = chunk[...]
    if other is not None:
        chunk = jnp.where(lax.axis_index("heads") == 0, other[...], chunk)
    rows = 6 * chunk.shape[0] // 7
    group = rows // 6
    keys[pl.ds(base, rows), :DC] = chunk[:rows]
    for index in range(6):
        part = chunk[rows:, index * DR : (index + 1) * DR]
        keys[pl.ds(base + index * group, group), DC:] = part


def prepare_kernel(order, *refs):
    sources, out_proj, rest = refs[:5], refs[5], refs[7:]
    outs, copied, sems = rest[:-6], rest[-6:-1], rest[-1]
    weights = outs[-1]
    depth, width = out_proj.shape[0], out_proj.shape[1] // 2
    fetches = [
        pltpu.make_async_copy(source, target, sems.at[index])
        for index, (source, target) in enumerate(zip(sources, copied))
    ]
    base = pl.multiple_of((1 - lax.axis_index("heads")) * width, 128)
    fetches.append(
        pltpu.make_async_copy(
            out_proj.at[:, pl.ds(base, width)], weights.at[:, pl.ds(0, width)], sems.at[5]
        )
    )
    for fetch in fetches:
        fetch.start()
    nope, rope, up, span_order, value_up = copied
    rows = nope.shape[0]
    heads = nope.shape[1] // DH
    span_rows = rows // 2
    for fetch in fetches[:3]:
        fetch.wait()
    own_index = lax.axis_index("ctx")
    core = lax.axis_index("heads")
    for head in range(heads):
        latent = lax.dot_general(
            nope[:, head * DH : (head + 1) * DH],
            up[:, head * DH : (head + 1) * DH],
            (((1,), (1,)), ((), ())),
            preferred_element_type=F32,
        )
        outs[head][:, :DC] = latent.astype(BF16)
        outs[head][:, DC:] = rope[:, head * DR : (head + 1) * DR]
    biases = outs[heads:-1]
    fetches[3].wait()
    row = lax.broadcasted_iota(jnp.int32, (rows, 1), 0)
    query_pos = jnp.where(
        row < span_rows,
        span_order[2 * own_index] * span_rows + row,
        span_order[2 * own_index + 1] * span_rows + row - span_rows,
    )

    def bias_of(owners):
        column = lax.broadcasted_iota(jnp.int32, (1, len(owners) * rows), 1)
        key_pos = jnp.zeros(column.shape, jnp.int32)
        for index, owner in enumerate(owners):
            for side in range(2):
                start = index * rows + side * span_rows
                first = span_order[2 * owner + side] * span_rows
                key_pos = jnp.where(column >= start, first + column - start, key_pos)
        return jnp.where(key_pos <= query_pos, F32(0.0), F32(MASKED))

    if order is not None:
        for steps, bias_ref in zip(order, biases):
            bias_ref[0] = bias_of(
                [own_index ^ jnp.where(core == 0, step[0], step[1]) for step in steps]
            )
    else:
        bias_ref = biases[0]

        def step(block, carry):
            bias_ref[block] = bias_of([block * BLOCK_CHUNKS + index for index in range(BLOCK_CHUNKS)])
            return carry

        lax.fori_loop(0, bias_ref.shape[0], step, 0)

    fetches[4].wait()
    columns = value_up.shape[1]
    for block in range(DC // depth):
        part = value_up[block * depth : (block + 1) * depth, :]
        weights[:, width + block * columns : width + (block + 1) * columns] = part
    fetches[5].wait()


def attend_block(queries, keys, bias, old):
    copies = len(queries)
    scale = math.log2(math.e) / math.sqrt(DH + DR)
    heads = jnp.concatenate([part[...] for part in queries], axis=0)
    scores = lax.dot_general(
        heads, keys[...], (((1,), (1,)), ((), ())), preferred_element_type=F32
    )
    scores = scores + jnp.concatenate([bias] * copies, axis=0)
    top = jnp.max(scores, axis=-1, keepdims=True)
    if old is not None:
        top = jnp.maximum(old[0], top)
        rescale = jnp.exp2((old[0] - top) * scale)
    expo = jnp.exp2((scores - top) * scale)
    total = jnp.sum(expo, axis=-1, keepdims=True)
    added = jnp.dot(expo.astype(BF16), keys[:, :DC], preferred_element_type=F32)
    if old is not None:
        total = old[1] * rescale + total
        added = old[2] * rescale + added
    return top, total, added


def chunks_kernel(heads, chunk_count, old_count, paired, *rest):
    queries, bias, rest = rest[:heads], rest[heads], rest[heads + 1 :]
    chunks, rest = rest[:chunk_count], rest[chunk_count:]
    old, rest = rest[:old_count], rest[old_count:]
    if len(rest) == 6:
        passed, handed = rest[0], rest[4]
        handed[...] = passed[...]
        rest = rest[1:4] + rest[5:]
    running, keys = rest[:3], rest[3]
    rows = bias.shape[1]
    if paired:
        unpack(chunks[0], keys, 0, chunks[1])
        chunks = chunks[1:]
    for index, chunk in enumerate(chunks):
        if index or not paired:
            unpack(chunk, keys, index * rows)
    before = [state[...] for state in old] if old else None
    values = attend_block(queries, keys, bias[0], before)
    for state, value in zip(running, values):
        state[...] = value


def gathered_kernel(heads, *rest):
    queries, (bias, gathered) = rest[:heads], rest[heads : heads + 2]
    running, keys = rest[heads + 2 : heads + 5], rest[heads + 5]
    blocks, rows, _ = bias.shape

    def fill(block):
        for index in range(BLOCK_CHUNKS):
            unpack(gathered.at[block * BLOCK_CHUNKS + index], keys, index * rows)

    first = lax.axis_index("ctx") // BLOCK_CHUNKS
    fill(first)
    values = attend_block(queries, keys, bias[first], None)
    for state, value in zip(running, values):
        state[...] = value

    def step(index, carry):
        block = index + jnp.where(index >= first, 1, 0)
        fill(block)
        new = attend_block(queries, keys, bias[block], [state[...] for state in running])
        for state, value in zip(running, new):
            state[...] = value
        return carry

    lax.fori_loop(0, blocks - 1, step, 0)


def finish_kernel(heads, chunk_count, *rest):
    queries, (top, total, context), rest = rest[:heads], rest[heads : heads + 3], rest[heads + 3 :]
    bias, chunks = rest[:chunk_count][:1], rest[1 : 1 + chunk_count]
    rest = rest[len(bias) + len(chunks) :]
    value_own, proj_own, weights, out_ref, out_tiles, keys, out_sems = rest
    rows, width = out_ref.shape
    running = (top[...], total[...], context[...])
    if chunk_count:
        for index, chunk in enumerate(chunks):
            unpack(chunk, keys, index * rows)
        running = attend_block(queries, keys, bias[0][0], running)
    mixed = (running[2] / running[1]).astype(BF16)
    half = heads // 2
    depth = weights.shape[0]
    base = lax.axis_index("heads") * width
    sides = []
    for group in range(2):
        parts = []
        for head in range(half):
            first = (group * half + head) * rows
            per_head = 0.0
            for block in range(DC // depth):
                if group == 0:
                    value = value_own[block * depth : (block + 1) * depth, head * DH : (head + 1) * DH]
                else:
                    start = width + (block * half + head) * DH
                    value = weights[:, start : start + DH]
                per_head = per_head + jnp.dot(
                    mixed[first : first + rows, block * depth : (block + 1) * depth],
                    value,
                    preferred_element_type=F32,
                )
            parts.append(per_head.astype(BF16))
        sides.append(jnp.concatenate(parts, axis=1))
    tiles = out_sems.shape[0]
    tile = width // tiles
    sends = []
    for index in range(tiles):
        part = pl.ds(index * tile, tile)
        own = proj_own[:, pl.ds(pl.multiple_of(base + index * tile, 128), tile)]
        out = jnp.dot(sides[0], own, preferred_element_type=F32)
        out = out + jnp.dot(sides[1], weights[:, part], preferred_element_type=F32)
        out_tiles[:, part] = out.astype(BF16)
        sends.append(
            pltpu.make_async_copy(out_tiles.at[:, part], out_ref.at[:, part], out_sems.at[index])
        )
        sends[-1].start()
    for send in sends:
        send.wait()


def per_device(
    count, queries_nope, queries_rope, latent, key_rope, key_up, value_up, out_proj, span_order
):
    rows = latent.shape[0]
    depth, width = out_proj.shape[0], out_proj.shape[1] // 2
    heads = 2 * (key_up.shape[1] // DH)
    query_rows = heads * rows
    direct = count == 8
    small = pltpu.CompilerParams(vmem_limit_bytes=SMALL_VMEM)

    def in_hbm(*arrays):
        return [pltpu.with_memory_space_constraint(array, pltpu.HBM) for array in arrays]

    def other_core(array):
        return lax.ppermute(array, "heads", [(0, 1), (1, 0)])

    def partners(array, steps, cores=(0, 1)):
        pairs = [
            (2 * index + core, 2 * (index ^ steps[core]) + core)
            for index in range(count)
            for core in cores
        ]
        return lax.ppermute(array, ("ctx", "heads"), pairs)

    def attend(name, estimate, queries, bias, chunks, old=(), passed=(), paired=False):
        return pl.pallas_call(
            functools.partial(chunks_kernel, heads, len(chunks), len(old), paired),
            out_shape=[jax.ShapeDtypeStruct((query_rows, size), F32) for size in (1, 1, DC)]
            + [jax.ShapeDtypeStruct(chunk.shape, BF16) for chunk in passed],
            in_specs=[vmem()] * (heads + 1 + len(chunks) + len(old) + len(passed)),
            out_specs=[vmem()] * (3 + len(passed)),
            scratch_shapes=[pltpu.VMEM((bias.shape[2], DC + DR), BF16)],
            compiler_params=small,
            cost_estimate=cost(estimate),
            name=name,
        )(*queries, bias, *chunks, *old, *passed)

    packed = pl.pallas_call(
        pack_kernel,
        out_shape=jax.ShapeDtypeStruct((rows + rows // 6, DC), BF16),
        in_specs=[vmem()] * 2,
        out_specs=vmem(),
        compiler_params=small,
        name="pack",
    )(*in_hbm(latent, key_rope.T))
    if direct:
        order = [
            [(0, 0), NEAR],
            [CORNER, NEAR[::-1], FAR, FAR[::-1], RELAYED],
            [RELAYED[::-1]],
        ]
        bias_shapes = [(1, rows, len(steps) * rows) for steps in order]
    else:
        order = None
        bias_shapes = [(count // BLOCK_CHUNKS, rows, BLOCK_CHUNKS * rows)]
    outs = pl.pallas_call(
        functools.partial(prepare_kernel, order),
        out_shape=[jax.ShapeDtypeStruct((rows, DC + DR), BF16)] * (heads // 2)
        + [jax.ShapeDtypeStruct(shape, F32) for shape in bias_shapes]
        + [jax.ShapeDtypeStruct((depth, width + DC // depth * key_up.shape[1]), BF16)],
        in_specs=[hbm()] * 6 + [anywhere()],
        out_specs=[vmem()] * (heads // 2 + len(bias_shapes) + 1),
        scratch_shapes=[
            pltpu.VMEM(queries_nope.shape, BF16),
            pltpu.VMEM(queries_rope.shape, BF16),
            pltpu.VMEM(key_up.shape, BF16),
            pltpu.SMEM(span_order.shape, jnp.int32),
            pltpu.VMEM(value_up.shape, BF16),
            pltpu.SemaphoreType.DMA((6,)),
        ],
        compiler_params=small,
        cost_estimate=cost(PREPARE_COST),
        name="prepare",
    )(*in_hbm(queries_nope, queries_rope, key_up, span_order, value_up, out_proj), packed)
    queries, biases = outs[: heads // 2], outs[heads // 2 : -1]
    weights_other = other_core(outs[-1])
    both = [*queries, *map(other_core, queries)]

    if direct:
        far = partners(packed, FAR)
        near = partners(packed, NEAR)
        corner = partners(packed, CORNER, cores=(1,))
        relayed = partners(far, (1, 1))
        *running, far_after = attend(
            "first", FIRST_COST, both, biases[0], [packed, near], passed=[far]
        )
        last = [other_core(relayed)]
        running = attend(
            "second",
            SECOND_COST,
            both,
            biases[1],
            [corner, other_core(corner), other_core(near), far, other_core(far_after), relayed],
            running,
            paired=True,
        )
    else:
        last = []
        running = pl.pallas_call(
            functools.partial(gathered_kernel, heads),
            out_shape=[jax.ShapeDtypeStruct((query_rows, size), F32) for size in (1, 1, DC)],
            in_specs=[vmem()] * (heads + 2),
            out_specs=[vmem()] * 3,
            scratch_shapes=[pltpu.VMEM((BLOCK_CHUNKS * rows, DC + DR), BF16)],
            compiler_params=pltpu.CompilerParams(vmem_limit_bytes=LARGE_VMEM),
            name="gathered",
        )(*both, biases[0], lax.all_gather(packed, "ctx", axis=0))

    tiles = 7 if width % 896 == 0 else 1
    return pl.pallas_call(
        functools.partial(finish_kernel, heads, len(last)),
        out_shape=jax.ShapeDtypeStruct((rows, width), BF16),
        in_specs=[vmem()] * (heads + 3 + len(biases[2:]) + len(last) + 3),
        out_specs=anywhere(),
        scratch_shapes=[
            pltpu.VMEM((rows, width), BF16),
            pltpu.VMEM((rows, DC + DR), BF16),
            pltpu.SemaphoreType.DMA((tiles,)),
        ],
        compiler_params=small,
        name="finish",
    )(*both, *running, *biases[2:], *last, value_up, out_proj, weights_other)


def solution(mesh):
    in_specs = (
        P(("docs", "ctx"), "heads"),
        P(("docs", "ctx"), "heads"),
        P(("docs", "ctx"), None),
        P(("docs", "ctx"), None),
        P(None, "heads"),
        P(None, "heads"),
        P("heads", None),
        P("docs"),
    )
    out_specs = P(("docs", "ctx"), "heads")
    return jax.shard_map(
        functools.partial(per_device, mesh.shape["ctx"]),
        mesh=mesh,
        in_specs=in_specs,
        out_specs=out_specs,
        check_vma=False,
    )
```

```python
import functools
import math

import jax
import jax.numpy as jnp
from jax import lax
from jax.experimental import pallas as pl
from jax.experimental.pallas import tpu as pltpu
from jax.sharding import PartitionSpec as P

DC = 512
DH = 128
DR = 64
BF16 = jnp.bfloat16
F32 = jnp.float32
MASKED = -1e30
BLOCK_CHUNKS = 8
PREPARE_COST, FIRST_COST, SECOND_COST = 0, 20, 1
SMALL_VMEM = 20 * 1024 * 1024
LARGE_VMEM = 56 * 1024 * 1024
FAR = (4, 6)
NEAR = (2, 1)
CORNER = (3, 3)
RELAYED = (5, 7)


def vmem():
    return pl.BlockSpec(memory_space=pltpu.VMEM)


def anywhere():
    return pl.BlockSpec(memory_space=pl.ANY)


def hbm():
    return pl.BlockSpec(memory_space=pltpu.HBM)


def cost(microseconds):
    return pl.CostEstimate(flops=int(microseconds * 1.1e9), bytes_accessed=0, transcendentals=0)


def pack_kernel(latent, key_rope_turned, out_ref):
    rows = latent.shape[0]
    group = rows // 6
    out_ref[:rows] = latent[...]
    rope = key_rope_turned[...].astype(F32).T.astype(BF16)
    parts = [rope[index * group : (index + 1) * group] for index in range(6)]
    parts.append(jnp.zeros((group, DC - 6 * DR), BF16))
    out_ref[rows:] = jnp.concatenate(parts, axis=1)


def unpack(chunk, keys, base, other=None):
    chunk = chunk[...]
    if other is not None:
        chunk = jnp.where(lax.axis_index("heads") == 0, other[...], chunk)
    rows = 6 * chunk.shape[0] // 7
    group = rows // 6
    keys[pl.ds(base, rows), :DC] = chunk[:rows]
    for index in range(6):
        part = chunk[rows:, index * DR : (index + 1) * DR]
        keys[pl.ds(base + index * group, group), DC:] = part


def prepare_kernel(order, *refs):
    sources, out_proj, rest = refs[:5], refs[5], refs[7:]
    outs, copied, sems = rest[:-6], rest[-6:-1], rest[-1]
    weights = outs[-1]
    depth, width = out_proj.shape[0], out_proj.shape[1] // 2
    fetches = [
        pltpu.make_async_copy(source, target, sems.at[index])
        for index, (source, target) in enumerate(zip(sources, copied))
    ]
    base = pl.multiple_of((1 - lax.axis_index("heads")) * width, 128)
    fetches.append(
        pltpu.make_async_copy(
            out_proj.at[:, pl.ds(base, width)], weights.at[:, pl.ds(0, width)], sems.at[5]
        )
    )
    for fetch in fetches:
        fetch.start()
    nope, rope, up, span_order, value_up = copied
    rows = nope.shape[0]
    heads = nope.shape[1] // DH
    span_rows = rows // 2
    for fetch in fetches[:3]:
        fetch.wait()
    own_index = lax.axis_index("ctx")
    core = lax.axis_index("heads")
    for head in range(heads):
        latent = lax.dot_general(
            nope[:, head * DH : (head + 1) * DH],
            up[:, head * DH : (head + 1) * DH],
            (((1,), (1,)), ((), ())),
            preferred_element_type=F32,
        )
        outs[head][:, :DC] = latent.astype(BF16)
        outs[head][:, DC:] = rope[:, head * DR : (head + 1) * DR]
    biases = outs[heads:-1]
    fetches[3].wait()
    row = lax.broadcasted_iota(jnp.int32, (rows, 1), 0)
    query_pos = jnp.where(
        row < span_rows,
        span_order[2 * own_index] * span_rows + row,
        span_order[2 * own_index + 1] * span_rows + row - span_rows,
    )

    def bias_of(owners):
        column = lax.broadcasted_iota(jnp.int32, (1, len(owners) * rows), 1)
        key_pos = jnp.zeros(column.shape, jnp.int32)
        for index, owner in enumerate(owners):
            for side in range(2):
                start = index * rows + side * span_rows
                first = span_order[2 * owner + side] * span_rows
                key_pos = jnp.where(column >= start, first + column - start, key_pos)
        return jnp.where(key_pos <= query_pos, F32(0.0), F32(MASKED))

    if order is not None:
        for steps, bias_ref in zip(order, biases):
            bias_ref[0] = bias_of(
                [own_index ^ jnp.where(core == 0, step[0], step[1]) for step in steps]
            )
    else:
        bias_ref = biases[0]

        def step(block, carry):
            bias_ref[block] = bias_of([block * BLOCK_CHUNKS + index for index in range(BLOCK_CHUNKS)])
            return carry

        lax.fori_loop(0, bias_ref.shape[0], step, 0)

    fetches[4].wait()
    columns = value_up.shape[1]
    for block in range(DC // depth):
        part = value_up[block * depth : (block + 1) * depth, :]
        weights[:, width + block * columns : width + (block + 1) * columns] = part
    fetches[5].wait()


def attend_block(queries, keys, bias, old):
    copies = len(queries)
    scale = math.log2(math.e) / math.sqrt(DH + DR)
    heads = jnp.concatenate([part[...] for part in queries], axis=0)
    scores = lax.dot_general(
        heads, keys[...], (((1,), (1,)), ((), ())), preferred_element_type=F32
    )
    scores = scores + jnp.concatenate([bias] * copies, axis=0)
    top = jnp.max(scores, axis=-1, keepdims=True)
    if old is not None:
        top = jnp.maximum(old[0], top)
        rescale = jnp.exp2((old[0] - top) * scale)
    expo = jnp.exp2((scores - top) * scale)
    total = jnp.sum(expo, axis=-1, keepdims=True)
    added = jnp.dot(expo.astype(BF16), keys[:, :DC], preferred_element_type=F32)
    if old is not None:
        total = old[1] * rescale + total
        added = old[2] * rescale + added
    return top, total, added


def chunks_kernel(heads, chunk_count, old_count, paired, *rest):
    queries, bias, rest = rest[:heads], rest[heads], rest[heads + 1 :]
    chunks, rest = rest[:chunk_count], rest[chunk_count:]
    old, rest = rest[:old_count], rest[old_count:]
    if len(rest) == 6:
        passed, handed = rest[0], rest[4]
        handed[...] = passed[...]
        rest = rest[1:4] + rest[5:]
    running, keys = rest[:3], rest[3]
    rows = bias.shape[1]
    if paired:
        unpack(chunks[0], keys, 0, chunks[1])
        chunks = chunks[1:]
    for index, chunk in enumerate(chunks):
        if index or not paired:
            unpack(chunk, keys, index * rows)
    before = [state[...] for state in old] if old else None
    values = attend_block(queries, keys, bias[0], before)
    for state, value in zip(running, values):
        state[...] = value


def gathered_kernel(heads, *rest):
    queries, (bias, gathered) = rest[:heads], rest[heads : heads + 2]
    running, keys = rest[heads + 2 : heads + 5], rest[heads + 5]
    blocks, rows, _ = bias.shape

    def fill(block):
        for index in range(BLOCK_CHUNKS):
            unpack(gathered.at[block * BLOCK_CHUNKS + index], keys, index * rows)

    first = lax.axis_index("ctx") // BLOCK_CHUNKS
    fill(first)
    values = attend_block(queries, keys, bias[first], None)
    for state, value in zip(running, values):
        state[...] = value

    def step(index, carry):
        block = index + jnp.where(index >= first, 1, 0)
        fill(block)
        new = attend_block(queries, keys, bias[block], [state[...] for state in running])
        for state, value in zip(running, new):
            state[...] = value
        return carry

    lax.fori_loop(0, blocks - 1, step, 0)


def finish_kernel(heads, chunk_count, *rest):
    queries, (top, total, context), rest = rest[:heads], rest[heads : heads + 3], rest[heads + 3 :]
    bias, chunks = rest[:chunk_count][:1], rest[1 : 1 + chunk_count]
    rest = rest[len(bias) + len(chunks) :]
    value_own, proj_own, weights, out_ref, out_tiles, keys, out_sems = rest
    rows, width = out_ref.shape
    running = (top[...], total[...], context[...])
    if chunk_count:
        for index, chunk in enumerate(chunks):
            unpack(chunk, keys, index * rows)
        running = attend_block(queries, keys, bias[0][0], running)
    mixed = (running[2] / running[1]).astype(BF16)
    half = heads // 2
    depth = weights.shape[0]
    base = lax.axis_index("heads") * width
    sides = []
    for group in range(2):
        parts = []
        for head in range(half):
            first = (group * half + head) * rows
            per_head = 0.0
            for block in range(DC // depth):
                if group == 0:
                    value = value_own[block * depth : (block + 1) * depth, head * DH : (head + 1) * DH]
                else:
                    start = width + (block * half + head) * DH
                    value = weights[:, start : start + DH]
                per_head = per_head + jnp.dot(
                    mixed[first : first + rows, block * depth : (block + 1) * depth],
                    value,
                    preferred_element_type=F32,
                )
            parts.append(per_head.astype(BF16))
        sides.append(jnp.concatenate(parts, axis=1))
    tiles = out_sems.shape[0]
    tile = width // tiles
    sends = []
    for index in range(tiles):
        part = pl.ds(index * tile, tile)
        own = proj_own[:, pl.ds(pl.multiple_of(base + index * tile, 128), tile)]
        out = jnp.dot(sides[0], own, preferred_element_type=F32)
        out = out + jnp.dot(sides[1], weights[:, part], preferred_element_type=F32)
        out_tiles[:, part] = out.astype(BF16)
        sends.append(
            pltpu.make_async_copy(out_tiles.at[:, part], out_ref.at[:, part], out_sems.at[index])
        )
        sends[-1].start()
    for send in sends:
        send.wait()


def per_device(
    count, queries_nope, queries_rope, latent, key_rope, key_up, value_up, out_proj, span_order
):
    rows = latent.shape[0]
    depth, width = out_proj.shape[0], out_proj.shape[1] // 2
    heads = 2 * (key_up.shape[1] // DH)
    query_rows = heads * rows
    direct = count == 8
    small = pltpu.CompilerParams(vmem_limit_bytes=SMALL_VMEM)

    def in_hbm(*arrays):
        return [pltpu.with_memory_space_constraint(array, pltpu.HBM) for array in arrays]

    def other_core(array):
        return lax.ppermute(array, "heads", [(0, 1), (1, 0)])

    def partners(array, steps, cores=(0, 1)):
        pairs = [
            (2 * index + core, 2 * (index ^ steps[core]) + core)
            for index in range(count)
            for core in cores
        ]
        return lax.ppermute(array, ("ctx", "heads"), pairs)

    def attend(name, estimate, queries, bias, chunks, old=(), passed=(), paired=False):
        return pl.pallas_call(
            functools.partial(chunks_kernel, heads, len(chunks), len(old), paired),
            out_shape=[jax.ShapeDtypeStruct((query_rows, size), F32) for size in (1, 1, DC)]
            + [jax.ShapeDtypeStruct(chunk.shape, BF16) for chunk in passed],
            in_specs=[vmem()] * (heads + 1 + len(chunks) + len(old) + len(passed)),
            out_specs=[vmem()] * (3 + len(passed)),
            scratch_shapes=[pltpu.VMEM((bias.shape[2], DC + DR), BF16)],
            compiler_params=small,
            cost_estimate=cost(estimate),
            name=name,
        )(*queries, bias, *chunks, *old, *passed)

    packed = pl.pallas_call(
        pack_kernel,
        out_shape=jax.ShapeDtypeStruct((rows + rows // 6, DC), BF16),
        in_specs=[vmem()] * 2,
        out_specs=vmem(),
        compiler_params=small,
        name="pack",
    )(*in_hbm(latent, key_rope.T))
    if direct:
        order = [
            [(0, 0), NEAR],
            [CORNER, NEAR[::-1], FAR, FAR[::-1], RELAYED],
            [RELAYED[::-1]],
        ]
        bias_shapes = [(1, rows, len(steps) * rows) for steps in order]
    else:
        order = None
        bias_shapes = [(count // BLOCK_CHUNKS, rows, BLOCK_CHUNKS * rows)]
    outs = pl.pallas_call(
        functools.partial(prepare_kernel, order),
        out_shape=[jax.ShapeDtypeStruct((rows, DC + DR), BF16)] * (heads // 2)
        + [jax.ShapeDtypeStruct(shape, F32) for shape in bias_shapes]
        + [jax.ShapeDtypeStruct((depth, width + DC // depth * key_up.shape[1]), BF16)],
        in_specs=[hbm()] * 6 + [anywhere()],
        out_specs=[vmem()] * (heads // 2 + len(bias_shapes) + 1),
        scratch_shapes=[
            pltpu.VMEM(queries_nope.shape, BF16),
            pltpu.VMEM(queries_rope.shape, BF16),
            pltpu.VMEM(key_up.shape, BF16),
            pltpu.SMEM(span_order.shape, jnp.int32),
            pltpu.VMEM(value_up.shape, BF16),
            pltpu.SemaphoreType.DMA((6,)),
        ],
        compiler_params=small,
        cost_estimate=cost(PREPARE_COST),
        name="prepare",
    )(*in_hbm(queries_nope, queries_rope, key_up, span_order, value_up, out_proj), packed)
    queries, biases = outs[: heads // 2], outs[heads // 2 : -1]
    weights_other = other_core(outs[-1])
    both = [*queries, *map(other_core, queries)]

    if direct:
        far = partners(packed, FAR)
        near = partners(packed, NEAR)
        corner = partners(near, (2, 2), cores=(1,))
        relayed = partners(far, (1, 1))
        *running, far_after = attend(
            "first", FIRST_COST, both, biases[0], [packed, near], passed=[far]
        )
        last = [other_core(relayed)]
        running = attend(
            "second",
            SECOND_COST,
            both,
            biases[1],
            [corner, other_core(corner), other_core(near), far, other_core(far_after), relayed],
            running,
            paired=True,
        )
    else:
        last = []
        running = pl.pallas_call(
            functools.partial(gathered_kernel, heads),
            out_shape=[jax.ShapeDtypeStruct((query_rows, size), F32) for size in (1, 1, DC)],
            in_specs=[vmem()] * (heads + 2),
            out_specs=[vmem()] * 3,
            scratch_shapes=[pltpu.VMEM((BLOCK_CHUNKS * rows, DC + DR), BF16)],
            compiler_params=pltpu.CompilerParams(vmem_limit_bytes=LARGE_VMEM),
            name="gathered",
        )(*both, biases[0], lax.all_gather(packed, "ctx", axis=0))

    tiles = 7 if width % 896 == 0 else 1
    return pl.pallas_call(
        functools.partial(finish_kernel, heads, len(last)),
        out_shape=jax.ShapeDtypeStruct((rows, width), BF16),
        in_specs=[vmem()] * (heads + 3 + len(biases[2:]) + len(last) + 3),
        out_specs=anywhere(),
        scratch_shapes=[
            pltpu.VMEM((rows, width), BF16),
            pltpu.VMEM((rows, DC + DR), BF16),
            pltpu.SemaphoreType.DMA((tiles,)),
        ],
        compiler_params=small,
        name="finish",
    )(*both, *running, *biases[2:], *last, value_up, out_proj, weights_other)


def solution(mesh):
    in_specs = (
        P(("docs", "ctx"), "heads"),
        P(("docs", "ctx"), "heads"),
        P(("docs", "ctx"), None),
        P(("docs", "ctx"), None),
        P(None, "heads"),
        P(None, "heads"),
        P("heads", None),
        P("docs"),
    )
    out_specs = P(("docs", "ctx"), "heads")
    return jax.shard_map(
        functools.partial(per_device, mesh.shape["ctx"]),
        mesh=mesh,
        in_specs=in_specs,
        out_specs=out_specs,
        check_vma=False,
    )
```

```python
import functools
import math

import jax
import jax.numpy as jnp
from jax import lax
from jax.experimental import pallas as pl
from jax.experimental.pallas import tpu as pltpu
from jax.sharding import PartitionSpec as P

DC = 512
DH = 128
DR = 64
BF16 = jnp.bfloat16
F32 = jnp.float32
MASKED = -1e30
BLOCK_CHUNKS = 8
PREPARE_COST, FIRST_COST, SECOND_COST = 0, 20, 1
SMALL_VMEM = 20 * 1024 * 1024
LARGE_VMEM = 56 * 1024 * 1024
FAR = (4, 6)
NEAR = (2, 1)
CORNER = (3, 3)
RELAYED = (5, 7)


def vmem():
    return pl.BlockSpec(memory_space=pltpu.VMEM)


def anywhere():
    return pl.BlockSpec(memory_space=pl.ANY)


def hbm():
    return pl.BlockSpec(memory_space=pltpu.HBM)


def cost(microseconds):
    return pl.CostEstimate(flops=int(microseconds * 1.1e9), bytes_accessed=0, transcendentals=0)


def pack_kernel(latent, key_rope_turned, out_ref):
    rows = latent.shape[0]
    group = rows // 6
    out_ref[:rows] = latent[...]
    rope = key_rope_turned[...].astype(F32).T.astype(BF16)
    parts = [rope[index * group : (index + 1) * group] for index in range(6)]
    parts.append(jnp.zeros((group, DC - 6 * DR), BF16))
    out_ref[rows:] = jnp.concatenate(parts, axis=1)


def unpack(chunk, keys, base, other=None):
    chunk = chunk[...]
    if other is not None:
        chunk = jnp.where(lax.axis_index("heads") == 0, other[...], chunk)
    rows = 6 * chunk.shape[0] // 7
    group = rows // 6
    keys[pl.ds(base, rows), :DC] = chunk[:rows]
    for index in range(6):
        part = chunk[rows:, index * DR : (index + 1) * DR]
        keys[pl.ds(base + index * group, group), DC:] = part


def prepare_kernel(order, *refs):
    sources, (out_proj, packed), rest = refs[:5], refs[5:7], refs[7:]
    outs, copied, sems = rest[:-6], rest[-6:-1], rest[-1]
    weights, packed_after = outs[-2:]
    depth, width = out_proj.shape[0], out_proj.shape[1] // 2
    fetches = [
        pltpu.make_async_copy(source, target, sems.at[index])
        for index, (source, target) in enumerate(zip(sources, copied))
    ]
    base = pl.multiple_of((1 - lax.axis_index("heads")) * width, 128)
    fetches.append(
        pltpu.make_async_copy(
            out_proj.at[:, pl.ds(base, width)], weights.at[:, pl.ds(0, width)], sems.at[5]
        )
    )
    for fetch in fetches:
        fetch.start()
    packed_after[...] = packed[...]
    nope, rope, up, span_order, value_up = copied
    rows = nope.shape[0]
    heads = nope.shape[1] // DH
    span_rows = rows // 2
    for fetch in fetches[:3]:
        fetch.wait()
    own_index = lax.axis_index("ctx")
    core = lax.axis_index("heads")
    for head in range(heads):
        latent = lax.dot_general(
            nope[:, head * DH : (head + 1) * DH],
            up[:, head * DH : (head + 1) * DH],
            (((1,), (1,)), ((), ())),
            preferred_element_type=F32,
        )
        outs[head][:, :DC] = latent.astype(BF16)
        outs[head][:, DC:] = rope[:, head * DR : (head + 1) * DR]
    biases = outs[heads:-2]
    fetches[3].wait()
    row = lax.broadcasted_iota(jnp.int32, (rows, 1), 0)
    query_pos = jnp.where(
        row < span_rows,
        span_order[2 * own_index] * span_rows + row,
        span_order[2 * own_index + 1] * span_rows + row - span_rows,
    )

    def bias_of(owners):
        column = lax.broadcasted_iota(jnp.int32, (1, len(owners) * rows), 1)
        key_pos = jnp.zeros(column.shape, jnp.int32)
        for index, owner in enumerate(owners):
            for side in range(2):
                start = index * rows + side * span_rows
                first = span_order[2 * owner + side] * span_rows
                key_pos = jnp.where(column >= start, first + column - start, key_pos)
        return jnp.where(key_pos <= query_pos, F32(0.0), F32(MASKED))

    if order is not None:
        for steps, bias_ref in zip(order, biases):
            bias_ref[0] = bias_of(
                [own_index ^ jnp.where(core == 0, step[0], step[1]) for step in steps]
            )
    else:
        bias_ref = biases[0]

        def step(block, carry):
            bias_ref[block] = bias_of([block * BLOCK_CHUNKS + index for index in range(BLOCK_CHUNKS)])
            return carry

        lax.fori_loop(0, bias_ref.shape[0], step, 0)

    fetches[4].wait()
    columns = value_up.shape[1]
    for block in range(DC // depth):
        part = value_up[block * depth : (block + 1) * depth, :]
        weights[:, width + block * columns : width + (block + 1) * columns] = part
    fetches[5].wait()


def attend_block(queries, keys, bias, old):
    copies = len(queries)
    scale = math.log2(math.e) / math.sqrt(DH + DR)
    heads = jnp.concatenate([part[...] for part in queries], axis=0)
    scores = lax.dot_general(
        heads, keys[...], (((1,), (1,)), ((), ())), preferred_element_type=F32
    )
    scores = scores + jnp.concatenate([bias] * copies, axis=0)
    top = jnp.max(scores, axis=-1, keepdims=True)
    if old is not None:
        top = jnp.maximum(old[0], top)
        rescale = jnp.exp2((old[0] - top) * scale)
    expo = jnp.exp2((scores - top) * scale)
    total = jnp.sum(expo, axis=-1, keepdims=True)
    added = jnp.dot(expo.astype(BF16), keys[:, :DC], preferred_element_type=F32)
    if old is not None:
        total = old[1] * rescale + total
        added = old[2] * rescale + added
    return top, total, added


def chunks_kernel(heads, chunk_count, old_count, paired, *rest):
    queries, bias, rest = rest[:heads], rest[heads], rest[heads + 1 :]
    chunks, rest = rest[:chunk_count], rest[chunk_count:]
    old, rest = rest[:old_count], rest[old_count:]
    if len(rest) == 6:
        passed, handed = rest[0], rest[4]
        handed[...] = passed[...]
        rest = rest[1:4] + rest[5:]
    running, keys = rest[:3], rest[3]
    rows = bias.shape[1]
    if paired:
        unpack(chunks[0], keys, 0, chunks[1])
        chunks = chunks[1:]
    for index, chunk in enumerate(chunks):
        if index or not paired:
            unpack(chunk, keys, index * rows)
    before = [state[...] for state in old] if old else None
    values = attend_block(queries, keys, bias[0], before)
    for state, value in zip(running, values):
        state[...] = value


def gathered_kernel(heads, *rest):
    queries, (bias, gathered) = rest[:heads], rest[heads : heads + 2]
    running, keys = rest[heads + 2 : heads + 5], rest[heads + 5]
    blocks, rows, _ = bias.shape

    def fill(block):
        for index in range(BLOCK_CHUNKS):
            unpack(gathered.at[block * BLOCK_CHUNKS + index], keys, index * rows)

    first = lax.axis_index("ctx") // BLOCK_CHUNKS
    fill(first)
    values = attend_block(queries, keys, bias[first], None)
    for state, value in zip(running, values):
        state[...] = value

    def step(index, carry):
        block = index + jnp.where(index >= first, 1, 0)
        fill(block)
        new = attend_block(queries, keys, bias[block], [state[...] for state in running])
        for state, value in zip(running, new):
            state[...] = value
        return carry

    lax.fori_loop(0, blocks - 1, step, 0)


def finish_kernel(heads, chunk_count, *rest):
    queries, (top, total, context), rest = rest[:heads], rest[heads : heads + 3], rest[heads + 3 :]
    bias, chunks = rest[:chunk_count][:1], rest[1 : 1 + chunk_count]
    rest = rest[len(bias) + len(chunks) :]
    value_own, proj_own, weights, out_ref, out_tiles, keys, out_sems = rest
    rows, width = out_ref.shape
    running = (top[...], total[...], context[...])
    if chunk_count:
        for index, chunk in enumerate(chunks):
            unpack(chunk, keys, index * rows)
        running = attend_block(queries, keys, bias[0][0], running)
    mixed = (running[2] / running[1]).astype(BF16)
    half = heads // 2
    depth = weights.shape[0]
    base = lax.axis_index("heads") * width
    sides = []
    for group in range(2):
        parts = []
        for head in range(half):
            first = (group * half + head) * rows
            per_head = 0.0
            for block in range(DC // depth):
                if group == 0:
                    value = value_own[block * depth : (block + 1) * depth, head * DH : (head + 1) * DH]
                else:
                    start = width + (block * half + head) * DH
                    value = weights[:, start : start + DH]
                per_head = per_head + jnp.dot(
                    mixed[first : first + rows, block * depth : (block + 1) * depth],
                    value,
                    preferred_element_type=F32,
                )
            parts.append(per_head.astype(BF16))
        sides.append(jnp.concatenate(parts, axis=1))
    tiles = out_sems.shape[0]
    tile = width // tiles
    sends = []
    for index in range(tiles):
        part = pl.ds(index * tile, tile)
        own = proj_own[:, pl.ds(pl.multiple_of(base + index * tile, 128), tile)]
        out = jnp.dot(sides[0], own, preferred_element_type=F32)
        out = out + jnp.dot(sides[1], weights[:, part], preferred_element_type=F32)
        out_tiles[:, part] = out.astype(BF16)
        sends.append(
            pltpu.make_async_copy(out_tiles.at[:, part], out_ref.at[:, part], out_sems.at[index])
        )
        sends[-1].start()
    for send in sends:
        send.wait()


def per_device(
    count, queries_nope, queries_rope, latent, key_rope, key_up, value_up, out_proj, span_order
):
    rows = latent.shape[0]
    depth, width = out_proj.shape[0], out_proj.shape[1] // 2
    heads = 2 * (key_up.shape[1] // DH)
    query_rows = heads * rows
    direct = count == 8
    small = pltpu.CompilerParams(vmem_limit_bytes=SMALL_VMEM)

    def in_hbm(*arrays):
        return [pltpu.with_memory_space_constraint(array, pltpu.HBM) for array in arrays]

    def other_core(array):
        return lax.ppermute(array, "heads", [(0, 1), (1, 0)])

    def partners(array, steps, cores=(0, 1)):
        pairs = [
            (2 * index + core, 2 * (index ^ steps[core]) + core)
            for index in range(count)
            for core in cores
        ]
        return lax.ppermute(array, ("ctx", "heads"), pairs)

    def attend(name, estimate, queries, bias, chunks, old=(), passed=(), paired=False):
        return pl.pallas_call(
            functools.partial(chunks_kernel, heads, len(chunks), len(old), paired),
            out_shape=[jax.ShapeDtypeStruct((query_rows, size), F32) for size in (1, 1, DC)]
            + [jax.ShapeDtypeStruct(chunk.shape, BF16) for chunk in passed],
            in_specs=[vmem()] * (heads + 1 + len(chunks) + len(old) + len(passed)),
            out_specs=[vmem()] * (3 + len(passed)),
            scratch_shapes=[pltpu.VMEM((bias.shape[2], DC + DR), BF16)],
            compiler_params=small,
            cost_estimate=cost(estimate),
            name=name,
        )(*queries, bias, *chunks, *old, *passed)

    packed = pl.pallas_call(
        pack_kernel,
        out_shape=jax.ShapeDtypeStruct((rows + rows // 6, DC), BF16),
        in_specs=[vmem()] * 2,
        out_specs=vmem(),
        compiler_params=small,
        name="pack",
    )(*in_hbm(latent, key_rope.T))
    if direct:
        order = [
            [(0, 0), NEAR],
            [CORNER, NEAR[::-1], FAR, FAR[::-1], RELAYED],
            [RELAYED[::-1]],
        ]
        bias_shapes = [(1, rows, len(steps) * rows) for steps in order]
    else:
        order = None
        bias_shapes = [(count // BLOCK_CHUNKS, rows, BLOCK_CHUNKS * rows)]
    outs = pl.pallas_call(
        functools.partial(prepare_kernel, order),
        out_shape=[jax.ShapeDtypeStruct((rows, DC + DR), BF16)] * (heads // 2)
        + [jax.ShapeDtypeStruct(shape, F32) for shape in bias_shapes]
        + [
            jax.ShapeDtypeStruct((depth, width + DC // depth * key_up.shape[1]), BF16),
            jax.ShapeDtypeStruct(packed.shape, BF16),
        ],
        in_specs=[hbm()] * 6 + [vmem()],
        out_specs=[vmem()] * (heads // 2 + len(bias_shapes) + 2),
        scratch_shapes=[
            pltpu.VMEM(queries_nope.shape, BF16),
            pltpu.VMEM(queries_rope.shape, BF16),
            pltpu.VMEM(key_up.shape, BF16),
            pltpu.SMEM(span_order.shape, jnp.int32),
            pltpu.VMEM(value_up.shape, BF16),
            pltpu.SemaphoreType.DMA((6,)),
        ],
        compiler_params=small,
        cost_estimate=cost(PREPARE_COST),
        name="prepare",
    )(*in_hbm(queries_nope, queries_rope, key_up, span_order, value_up, out_proj), packed)
    queries, biases = outs[: heads // 2], outs[heads // 2 : -2]
    weights, packed_after = outs[-2:]
    weights_other = other_core(weights)
    both = [*queries, *map(other_core, queries)]

    if direct:
        far = partners(packed, FAR)
        near = partners(packed, NEAR)
        corner = partners(packed_after, CORNER, cores=(1,))
        relayed = partners(far, (1, 1))
        *running, far_after = attend(
            "first", FIRST_COST, both, biases[0], [packed, near], passed=[far]
        )
        last = [other_core(relayed)]
        running = attend(
            "second",
            SECOND_COST,
            both,
            biases[1],
            [corner, other_core(corner), other_core(near), far, other_core(far_after), relayed],
            running,
            paired=True,
        )
    else:
        last = []
        running = pl.pallas_call(
            functools.partial(gathered_kernel, heads),
            out_shape=[jax.ShapeDtypeStruct((query_rows, size), F32) for size in (1, 1, DC)],
            in_specs=[vmem()] * (heads + 2),
            out_specs=[vmem()] * 3,
            scratch_shapes=[pltpu.VMEM((BLOCK_CHUNKS * rows, DC + DR), BF16)],
            compiler_params=pltpu.CompilerParams(vmem_limit_bytes=LARGE_VMEM),
            name="gathered",
        )(*both, biases[0], lax.all_gather(packed, "ctx", axis=0))

    tiles = 7 if width % 896 == 0 else 1
    return pl.pallas_call(
        functools.partial(finish_kernel, heads, len(last)),
        out_shape=jax.ShapeDtypeStruct((rows, width), BF16),
        in_specs=[vmem()] * (heads + 3 + len(biases[2:]) + len(last) + 3),
        out_specs=anywhere(),
        scratch_shapes=[
            pltpu.VMEM((rows, width), BF16),
            pltpu.VMEM((rows, DC + DR), BF16),
            pltpu.SemaphoreType.DMA((tiles,)),
        ],
        compiler_params=small,
        name="finish",
    )(*both, *running, *biases[2:], *last, value_up, out_proj, weights_other)


def solution(mesh):
    in_specs = (
        P(("docs", "ctx"), "heads"),
        P(("docs", "ctx"), "heads"),
        P(("docs", "ctx"), None),
        P(("docs", "ctx"), None),
        P(None, "heads"),
        P(None, "heads"),
        P("heads", None),
        P("docs"),
    )
    out_specs = P(("docs", "ctx"), "heads")
    return jax.shard_map(
        functools.partial(per_device, mesh.shape["ctx"]),
        mesh=mesh,
        in_specs=in_specs,
        out_specs=out_specs,
        check_vma=False,
    )
```

```python
import functools
import math

import jax
import jax.numpy as jnp
from jax import lax
from jax.experimental import pallas as pl
from jax.experimental.pallas import tpu as pltpu
from jax.sharding import PartitionSpec as P

DC = 512
DH = 128
DR = 64
BF16 = jnp.bfloat16
F32 = jnp.float32
MASKED = -1e30
BLOCK_CHUNKS = 8
PREPARE_COST, GATE_COST, FIRST_COST, SECOND_COST = 0, 3, 20, 1
SMALL_VMEM = 20 * 1024 * 1024
LARGE_VMEM = 56 * 1024 * 1024
FAR = (4, 6)
NEAR = (2, 1)
CORNER = (3, 3)
RELAYED = (5, 7)


def vmem():
    return pl.BlockSpec(memory_space=pltpu.VMEM)


def anywhere():
    return pl.BlockSpec(memory_space=pl.ANY)


def hbm():
    return pl.BlockSpec(memory_space=pltpu.HBM)


def cost(microseconds):
    return pl.CostEstimate(flops=int(microseconds * 1.1e9), bytes_accessed=0, transcendentals=0)


def pack_kernel(latent, key_rope_turned, out_ref):
    rows = latent.shape[0]
    group = rows // 6
    out_ref[:rows] = latent[...]
    rope = key_rope_turned[...].astype(F32).T.astype(BF16)
    parts = [rope[index * group : (index + 1) * group] for index in range(6)]
    parts.append(jnp.zeros((group, DC - 6 * DR), BF16))
    out_ref[rows:] = jnp.concatenate(parts, axis=1)


def gate_kernel(chunk, out_ref):
    out_ref[...] = chunk[...]


def unpack(chunk, keys, base, other=None):
    chunk = chunk[...]
    if other is not None:
        chunk = jnp.where(lax.axis_index("heads") == 0, other[...], chunk)
    rows = 6 * chunk.shape[0] // 7
    group = rows // 6
    keys[pl.ds(base, rows), :DC] = chunk[:rows]
    for index in range(6):
        part = chunk[rows:, index * DR : (index + 1) * DR]
        keys[pl.ds(base + index * group, group), DC:] = part


def prepare_kernel(order, *refs):
    sources, out_proj, rest = refs[:5], refs[5], refs[7:]
    outs, copied, sems = rest[:-6], rest[-6:-1], rest[-1]
    weights = outs[-1]
    depth, width = out_proj.shape[0], out_proj.shape[1] // 2
    fetches = [
        pltpu.make_async_copy(source, target, sems.at[index])
        for index, (source, target) in enumerate(zip(sources, copied))
    ]
    base = pl.multiple_of((1 - lax.axis_index("heads")) * width, 128)
    fetches.append(
        pltpu.make_async_copy(
            out_proj.at[:, pl.ds(base, width)], weights.at[:, pl.ds(0, width)], sems.at[5]
        )
    )
    for fetch in fetches:
        fetch.start()
    nope, rope, up, span_order, value_up = copied
    rows = nope.shape[0]
    heads = nope.shape[1] // DH
    span_rows = rows // 2
    for fetch in fetches[:3]:
        fetch.wait()
    own_index = lax.axis_index("ctx")
    core = lax.axis_index("heads")
    for head in range(heads):
        latent = lax.dot_general(
            nope[:, head * DH : (head + 1) * DH],
            up[:, head * DH : (head + 1) * DH],
            (((1,), (1,)), ((), ())),
            preferred_element_type=F32,
        )
        part = pl.ds(head * rows, rows)
        outs[0][part, :DC] = latent.astype(BF16)
        outs[0][part, DC:] = rope[:, head * DR : (head + 1) * DR]
    biases = outs[1:-1]
    fetches[3].wait()
    row = lax.broadcasted_iota(jnp.int32, (rows, 1), 0)
    query_pos = jnp.where(
        row < span_rows,
        span_order[2 * own_index] * span_rows + row,
        span_order[2 * own_index + 1] * span_rows + row - span_rows,
    )

    def bias_of(owners):
        column = lax.broadcasted_iota(jnp.int32, (1, len(owners) * rows), 1)
        key_pos = jnp.zeros(column.shape, jnp.int32)
        for index, owner in enumerate(owners):
            for side in range(2):
                start = index * rows + side * span_rows
                first = span_order[2 * owner + side] * span_rows
                key_pos = jnp.where(column >= start, first + column - start, key_pos)
        return jnp.where(key_pos <= query_pos, F32(0.0), F32(MASKED))

    if order is not None:
        for steps, bias_ref in zip(order, biases):
            bias_ref[0] = bias_of(
                [own_index ^ jnp.where(core == 0, step[0], step[1]) for step in steps]
            )
    else:
        bias_ref = biases[0]

        def step(block, carry):
            bias_ref[block] = bias_of([block * BLOCK_CHUNKS + index for index in range(BLOCK_CHUNKS)])
            return carry

        lax.fori_loop(0, bias_ref.shape[0], step, 0)

    fetches[4].wait()
    columns = value_up.shape[1]
    for block in range(DC // depth):
        part = value_up[block * depth : (block + 1) * depth, :]
        weights[:, width + block * columns : width + (block + 1) * columns] = part
    fetches[5].wait()


def attend_block(queries, keys, bias, old):
    copies = len(queries) * queries[0].shape[0] // bias.shape[0]
    scale = math.log2(math.e) / math.sqrt(DH + DR)
    heads = jnp.concatenate([part[...] for part in queries], axis=0)
    scores = lax.dot_general(
        heads, keys[...], (((1,), (1,)), ((), ())), preferred_element_type=F32
    )
    scores = scores + jnp.concatenate([bias] * copies, axis=0)
    top = jnp.max(scores, axis=-1, keepdims=True)
    if old is not None:
        top = jnp.maximum(old[0], top)
        rescale = jnp.exp2((old[0] - top) * scale)
    expo = jnp.exp2((scores - top) * scale)
    total = jnp.sum(expo, axis=-1, keepdims=True)
    added = jnp.dot(expo.astype(BF16), keys[:, :DC], preferred_element_type=F32)
    if old is not None:
        total = old[1] * rescale + total
        added = old[2] * rescale + added
    return top, total, added


def chunks_kernel(chunk_count, old_count, paired, *rest):
    queries, bias, rest = rest[:2], rest[2], rest[3:]
    chunks, rest = rest[:chunk_count], rest[chunk_count:]
    old, rest = rest[:old_count], rest[old_count:]
    if len(rest) == 6:
        passed, handed = rest[0], rest[4]
        handed[...] = passed[...]
        rest = rest[1:4] + rest[5:]
    running, keys = rest[:3], rest[3]
    rows = bias.shape[1]
    if paired:
        unpack(chunks[0], keys, 0, chunks[1])
        chunks = chunks[1:]
    for index, chunk in enumerate(chunks):
        if index or not paired:
            unpack(chunk, keys, index * rows)
    before = [state[...] for state in old] if old else None
    values = attend_block(queries, keys, bias[0], before)
    for state, value in zip(running, values):
        state[...] = value


def gathered_kernel(queries_own, queries_other, bias, gathered, *rest):
    queries = (queries_own, queries_other)
    running, keys = rest[:3], rest[3]
    blocks, rows, _ = bias.shape

    def fill(block):
        for index in range(BLOCK_CHUNKS):
            unpack(gathered.at[block * BLOCK_CHUNKS + index], keys, index * rows)

    first = lax.axis_index("ctx") // BLOCK_CHUNKS
    fill(first)
    values = attend_block(queries, keys, bias[first], None)
    for state, value in zip(running, values):
        state[...] = value

    def step(index, carry):
        block = index + jnp.where(index >= first, 1, 0)
        fill(block)
        new = attend_block(queries, keys, bias[block], [state[...] for state in running])
        for state, value in zip(running, new):
            state[...] = value
        return carry

    lax.fori_loop(0, blocks - 1, step, 0)


def finish_kernel(heads, chunk_count, *rest):
    queries, (top, total, context), rest = rest[:2], rest[2:5], rest[5:]
    bias, chunks = rest[:chunk_count][:1], rest[1 : 1 + chunk_count]
    rest = rest[len(bias) + len(chunks) :]
    value_own, proj_own, weights, out_ref, out_tiles, keys, out_sems = rest
    rows, width = out_ref.shape
    running = (top[...], total[...], context[...])
    if chunk_count:
        for index, chunk in enumerate(chunks):
            unpack(chunk, keys, index * rows)
        running = attend_block(queries, keys, bias[0][0], running)
    mixed = (running[2] / running[1]).astype(BF16)
    half = heads // 2
    depth = weights.shape[0]
    base = lax.axis_index("heads") * width
    sides = []
    for group in range(2):
        parts = []
        for head in range(half):
            first = (group * half + head) * rows
            per_head = 0.0
            for block in range(DC // depth):
                if group == 0:
                    value = value_own[block * depth : (block + 1) * depth, head * DH : (head + 1) * DH]
                else:
                    start = width + (block * half + head) * DH
                    value = weights[:, start : start + DH]
                per_head = per_head + jnp.dot(
                    mixed[first : first + rows, block * depth : (block + 1) * depth],
                    value,
                    preferred_element_type=F32,
                )
            parts.append(per_head.astype(BF16))
        sides.append(jnp.concatenate(parts, axis=1))
    tiles = out_sems.shape[0]
    tile = width // tiles
    sends = []
    for index in range(tiles):
        part = pl.ds(index * tile, tile)
        own = proj_own[:, pl.ds(pl.multiple_of(base + index * tile, 128), tile)]
        out = jnp.dot(sides[0], own, preferred_element_type=F32)
        out = out + jnp.dot(sides[1], weights[:, part], preferred_element_type=F32)
        out_tiles[:, part] = out.astype(BF16)
        sends.append(
            pltpu.make_async_copy(out_tiles.at[:, part], out_ref.at[:, part], out_sems.at[index])
        )
        sends[-1].start()
    for send in sends:
        send.wait()


def per_device(
    count, queries_nope, queries_rope, latent, key_rope, key_up, value_up, out_proj, span_order
):
    rows = latent.shape[0]
    depth, width = out_proj.shape[0], out_proj.shape[1] // 2
    heads = 2 * (key_up.shape[1] // DH)
    query_rows = heads * rows
    direct = count == 8
    small = pltpu.CompilerParams(vmem_limit_bytes=SMALL_VMEM)

    def in_hbm(*arrays):
        return [pltpu.with_memory_space_constraint(array, pltpu.HBM) for array in arrays]

    def other_core(array):
        return lax.ppermute(array, "heads", [(0, 1), (1, 0)])

    def partners(array, steps, cores=(0, 1)):
        pairs = [
            (2 * index + core, 2 * (index ^ steps[core]) + core)
            for index in range(count)
            for core in cores
        ]
        return lax.ppermute(array, ("ctx", "heads"), pairs)

    def attend(name, estimate, queries, bias, chunks, old=(), passed=(), paired=False):
        return pl.pallas_call(
            functools.partial(chunks_kernel, len(chunks), len(old), paired),
            out_shape=[jax.ShapeDtypeStruct((query_rows, size), F32) for size in (1, 1, DC)]
            + [jax.ShapeDtypeStruct(chunk.shape, BF16) for chunk in passed],
            in_specs=[vmem()] * (3 + len(chunks) + len(old) + len(passed)),
            out_specs=[vmem()] * (3 + len(passed)),
            scratch_shapes=[pltpu.VMEM((bias.shape[2], DC + DR), BF16)],
            compiler_params=small,
            cost_estimate=cost(estimate),
            name=name,
        )(*queries, bias, *chunks, *old, *passed)

    packed = pl.pallas_call(
        pack_kernel,
        out_shape=jax.ShapeDtypeStruct((rows + rows // 6, DC), BF16),
        in_specs=[vmem()] * 2,
        out_specs=vmem(),
        compiler_params=small,
        name="pack",
    )(*in_hbm(latent, key_rope.T))
    if direct:
        order = [
            [(0, 0), NEAR],
            [CORNER, NEAR[::-1], FAR, FAR[::-1], RELAYED],
            [RELAYED[::-1]],
        ]
        bias_shapes = [(1, rows, len(steps) * rows) for steps in order]
    else:
        order = None
        bias_shapes = [(count // BLOCK_CHUNKS, rows, BLOCK_CHUNKS * rows)]
    outs = pl.pallas_call(
        functools.partial(prepare_kernel, order),
        out_shape=[jax.ShapeDtypeStruct((query_rows // 2, DC + DR), BF16)]
        + [jax.ShapeDtypeStruct(shape, F32) for shape in bias_shapes]
        + [jax.ShapeDtypeStruct((depth, width + DC // depth * key_up.shape[1]), BF16)],
        in_specs=[hbm()] * 6 + [anywhere()],
        out_specs=[vmem()] * (len(bias_shapes) + 2),
        scratch_shapes=[
            pltpu.VMEM(queries_nope.shape, BF16),
            pltpu.VMEM(queries_rope.shape, BF16),
            pltpu.VMEM(key_up.shape, BF16),
            pltpu.SMEM(span_order.shape, jnp.int32),
            pltpu.VMEM(value_up.shape, BF16),
            pltpu.SemaphoreType.DMA((6,)),
        ],
        compiler_params=small,
        cost_estimate=cost(PREPARE_COST),
        name="prepare",
    )(*in_hbm(queries_nope, queries_rope, key_up, span_order, value_up, out_proj), packed)
    queries, biases = outs[0], outs[1:-1]
    weights_other = other_core(outs[-1])
    both = [queries, other_core(queries)]

    if direct:
        far = partners(packed, FAR)
        near = partners(packed, NEAR)
        corner = partners(packed, CORNER, cores=(1,))
        relayed = partners(far, (1, 1))
        gated = pl.pallas_call(
            gate_kernel,
            out_shape=jax.ShapeDtypeStruct(far.shape, BF16),
            in_specs=[vmem()],
            out_specs=vmem(),
            compiler_params=small,
            cost_estimate=cost(GATE_COST),
            name="gate",
        )(far)
        *running, far_after = attend(
            "first", FIRST_COST, both, biases[0], [packed, near], passed=[gated]
        )
        last = [other_core(relayed)]
        running = attend(
            "second",
            SECOND_COST,
            both,
            biases[1],
            [corner, other_core(corner), other_core(near), far, other_core(far_after), relayed],
            running,
            paired=True,
        )
    else:
        last = []
        running = pl.pallas_call(
            gathered_kernel,
            out_shape=[jax.ShapeDtypeStruct((query_rows, size), F32) for size in (1, 1, DC)],
            in_specs=[vmem()] * 4,
            out_specs=[vmem()] * 3,
            scratch_shapes=[pltpu.VMEM((BLOCK_CHUNKS * rows, DC + DR), BF16)],
            compiler_params=pltpu.CompilerParams(vmem_limit_bytes=LARGE_VMEM),
            name="gathered",
        )(*both, biases[0], lax.all_gather(packed, "ctx", axis=0))

    tiles = 7 if width % 896 == 0 else 1
    return pl.pallas_call(
        functools.partial(finish_kernel, heads, len(last)),
        out_shape=jax.ShapeDtypeStruct((rows, width), BF16),
        in_specs=[vmem()] * (5 + len(biases[2:]) + len(last) + 3),
        out_specs=anywhere(),
        scratch_shapes=[
            pltpu.VMEM((rows, width), BF16),
            pltpu.VMEM((rows, DC + DR), BF16),
            pltpu.SemaphoreType.DMA((tiles,)),
        ],
        compiler_params=small,
        name="finish",
    )(*both, *running, *biases[2:], *last, value_up, out_proj, weights_other)


def solution(mesh):
    in_specs = (
        P(("docs", "ctx"), "heads"),
        P(("docs", "ctx"), "heads"),
        P(("docs", "ctx"), None),
        P(("docs", "ctx"), None),
        P(None, "heads"),
        P(None, "heads"),
        P("heads", None),
        P("docs"),
    )
    out_specs = P(("docs", "ctx"), "heads")
    return jax.shard_map(
        functools.partial(per_device, mesh.shape["ctx"]),
        mesh=mesh,
        in_specs=in_specs,
        out_specs=out_specs,
        check_vma=False,
    )
```

```python
import functools
import math

import jax
import jax.numpy as jnp
from jax import lax
from jax.experimental import pallas as pl
from jax.experimental.pallas import tpu as pltpu
from jax.sharding import PartitionSpec as P

DC = 512
DH = 128
DR = 64
BF16 = jnp.bfloat16
F32 = jnp.float32
MASKED = -1e30
BLOCK_CHUNKS = 8
PREPARE_COST, HAND_COST, PICK_COST, FIRST_COST, SECOND_COST = 0, 3, 3, 20, 1
SMALL_VMEM = 20 * 1024 * 1024
LARGE_VMEM = 56 * 1024 * 1024
FIRST_OUT = (4, 1)
SECOND_OUT = (2, 3)
LAST_OUT = (6, 6)
RELAYED = (5, 7)


def vmem():
    return pl.BlockSpec(memory_space=pltpu.VMEM)


def anywhere():
    return pl.BlockSpec(memory_space=pl.ANY)


def hbm():
    return pl.BlockSpec(memory_space=pltpu.HBM)


def cost(microseconds):
    return pl.CostEstimate(flops=int(microseconds * 1.1e9), bytes_accessed=0, transcendentals=0)


def pack_kernel(latent, key_rope_turned, out_ref):
    rows = latent.shape[0]
    group = rows // 6
    out_ref[:rows] = latent[...]
    rope = key_rope_turned[...].astype(F32).T.astype(BF16)
    parts = [rope[index * group : (index + 1) * group] for index in range(6)]
    parts.append(jnp.zeros((group, DC - 6 * DR), BF16))
    out_ref[rows:] = jnp.concatenate(parts, axis=1)


def hand_kernel(chunk, *refs):
    refs[-1][...] = chunk[...]


def pick_kernel(first, last, out_ref):
    out_ref[...] = jnp.where(lax.axis_index("heads") == 0, first[...], last[...])


def unpack(chunk, keys, base, other=None):
    chunk = chunk[...]
    if other is not None:
        chunk = jnp.where(lax.axis_index("heads") == 0, other[...], chunk)
    rows = 6 * chunk.shape[0] // 7
    group = rows // 6
    keys[pl.ds(base, rows), :DC] = chunk[:rows]
    for index in range(6):
        part = chunk[rows:, index * DR : (index + 1) * DR]
        keys[pl.ds(base + index * group, group), DC:] = part


def prepare_kernel(order, *refs):
    sources, out_proj, rest = refs[:5], refs[5], refs[7:]
    outs, copied, sems = rest[:-6], rest[-6:-1], rest[-1]
    weights = outs[-1]
    depth, width = out_proj.shape[0], out_proj.shape[1] // 2
    fetches = [
        pltpu.make_async_copy(source, target, sems.at[index])
        for index, (source, target) in enumerate(zip(sources, copied))
    ]
    base = pl.multiple_of((1 - lax.axis_index("heads")) * width, 128)
    fetches.append(
        pltpu.make_async_copy(
            out_proj.at[:, pl.ds(base, width)], weights.at[:, pl.ds(0, width)], sems.at[5]
        )
    )
    for fetch in fetches:
        fetch.start()
    nope, rope, up, span_order, value_up = copied
    rows = nope.shape[0]
    heads = nope.shape[1] // DH
    span_rows = rows // 2
    for fetch in fetches[:3]:
        fetch.wait()
    own_index = lax.axis_index("ctx")
    core = lax.axis_index("heads")
    for head in range(heads):
        latent = lax.dot_general(
            nope[:, head * DH : (head + 1) * DH],
            up[:, head * DH : (head + 1) * DH],
            (((1,), (1,)), ((), ())),
            preferred_element_type=F32,
        )
        part = pl.ds(head * rows, rows)
        outs[0][part, :DC] = latent.astype(BF16)
        outs[0][part, DC:] = rope[:, head * DR : (head + 1) * DR]
    biases = outs[1:-1]
    fetches[3].wait()
    row = lax.broadcasted_iota(jnp.int32, (rows, 1), 0)
    query_pos = jnp.where(
        row < span_rows,
        span_order[2 * own_index] * span_rows + row,
        span_order[2 * own_index + 1] * span_rows + row - span_rows,
    )

    def bias_of(owners):
        column = lax.broadcasted_iota(jnp.int32, (1, len(owners) * rows), 1)
        key_pos = jnp.zeros(column.shape, jnp.int32)
        for index, owner in enumerate(owners):
            for side in range(2):
                start = index * rows + side * span_rows
                first = span_order[2 * owner + side] * span_rows
                key_pos = jnp.where(column >= start, first + column - start, key_pos)
        return jnp.where(key_pos <= query_pos, F32(0.0), F32(MASKED))

    if order is not None:
        for steps, bias_ref in zip(order, biases):
            bias_ref[0] = bias_of(
                [own_index ^ jnp.where(core == 0, step[0], step[1]) for step in steps]
            )
    else:
        bias_ref = biases[0]

        def step(block, carry):
            bias_ref[block] = bias_of([block * BLOCK_CHUNKS + index for index in range(BLOCK_CHUNKS)])
            return carry

        lax.fori_loop(0, bias_ref.shape[0], step, 0)

    fetches[4].wait()
    columns = value_up.shape[1]
    for block in range(DC // depth):
        part = value_up[block * depth : (block + 1) * depth, :]
        weights[:, width + block * columns : width + (block + 1) * columns] = part
    fetches[5].wait()


def attend_block(queries, keys, bias, old):
    copies = len(queries) * queries[0].shape[0] // bias.shape[0]
    scale = math.log2(math.e) / math.sqrt(DH + DR)
    heads = jnp.concatenate([part[...] for part in queries], axis=0)
    scores = lax.dot_general(
        heads, keys[...], (((1,), (1,)), ((), ())), preferred_element_type=F32
    )
    scores = scores + jnp.concatenate([bias] * copies, axis=0)
    top = jnp.max(scores, axis=-1, keepdims=True)
    if old is not None:
        top = jnp.maximum(old[0], top)
        rescale = jnp.exp2((old[0] - top) * scale)
    expo = jnp.exp2((scores - top) * scale)
    total = jnp.sum(expo, axis=-1, keepdims=True)
    added = jnp.dot(expo.astype(BF16), keys[:, :DC], preferred_element_type=F32)
    if old is not None:
        total = old[1] * rescale + total
        added = old[2] * rescale + added
    return top, total, added


def chunks_kernel(chunk_count, old_count, paired, *rest):
    queries, bias, rest = rest[:2], rest[2], rest[3:]
    chunks, rest = rest[:chunk_count], rest[chunk_count:]
    old, rest = rest[:old_count], rest[old_count:]
    if len(rest) == 6:
        passed, handed = rest[0], rest[4]
        handed[...] = passed[...]
        rest = rest[1:4] + rest[5:]
    running, keys = rest[:3], rest[3]
    rows = bias.shape[1]
    if paired:
        unpack(chunks[0], keys, 0, chunks[1])
        chunks = chunks[1:]
    for index, chunk in enumerate(chunks):
        if index or not paired:
            unpack(chunk, keys, index * rows)
    before = [state[...] for state in old] if old else None
    values = attend_block(queries, keys, bias[0], before)
    for state, value in zip(running, values):
        state[...] = value


def gathered_kernel(queries_own, queries_other, bias, gathered, *rest):
    queries = (queries_own, queries_other)
    running, keys = rest[:3], rest[3]
    blocks, rows, _ = bias.shape

    def fill(block):
        for index in range(BLOCK_CHUNKS):
            unpack(gathered.at[block * BLOCK_CHUNKS + index], keys, index * rows)

    first = lax.axis_index("ctx") // BLOCK_CHUNKS
    fill(first)
    values = attend_block(queries, keys, bias[first], None)
    for state, value in zip(running, values):
        state[...] = value

    def step(index, carry):
        block = index + jnp.where(index >= first, 1, 0)
        fill(block)
        new = attend_block(queries, keys, bias[block], [state[...] for state in running])
        for state, value in zip(running, new):
            state[...] = value
        return carry

    lax.fori_loop(0, blocks - 1, step, 0)


def finish_kernel(heads, chunk_count, *rest):
    queries, (top, total, context), rest = rest[:2], rest[2:5], rest[5:]
    bias, chunks = rest[:chunk_count][:1], rest[1 : 1 + chunk_count]
    rest = rest[len(bias) + len(chunks) :]
    value_own, proj_own, weights, out_ref, out_tiles, keys, out_sems = rest
    rows, width = out_ref.shape
    running = (top[...], total[...], context[...])
    if chunk_count:
        for index, chunk in enumerate(chunks):
            unpack(chunk, keys, index * rows)
        running = attend_block(queries, keys, bias[0][0], running)
    mixed = (running[2] / running[1]).astype(BF16)
    half = heads // 2
    depth = weights.shape[0]
    base = lax.axis_index("heads") * width
    sides = []
    for group in range(2):
        parts = []
        for head in range(half):
            first = (group * half + head) * rows
            per_head = 0.0
            for block in range(DC // depth):
                if group == 0:
                    value = value_own[block * depth : (block + 1) * depth, head * DH : (head + 1) * DH]
                else:
                    start = width + (block * half + head) * DH
                    value = weights[:, start : start + DH]
                per_head = per_head + jnp.dot(
                    mixed[first : first + rows, block * depth : (block + 1) * depth],
                    value,
                    preferred_element_type=F32,
                )
            parts.append(per_head.astype(BF16))
        sides.append(jnp.concatenate(parts, axis=1))
    tiles = out_sems.shape[0]
    tile = width // tiles
    sends = []
    for index in range(tiles):
        part = pl.ds(index * tile, tile)
        own = proj_own[:, pl.ds(pl.multiple_of(base + index * tile, 128), tile)]
        out = jnp.dot(sides[0], own, preferred_element_type=F32)
        out = out + jnp.dot(sides[1], weights[:, part], preferred_element_type=F32)
        out_tiles[:, part] = out.astype(BF16)
        sends.append(
            pltpu.make_async_copy(out_tiles.at[:, part], out_ref.at[:, part], out_sems.at[index])
        )
        sends[-1].start()
    for send in sends:
        send.wait()


def per_device(
    count, queries_nope, queries_rope, latent, key_rope, key_up, value_up, out_proj, span_order
):
    rows = latent.shape[0]
    depth, width = out_proj.shape[0], out_proj.shape[1] // 2
    heads = 2 * (key_up.shape[1] // DH)
    query_rows = heads * rows
    direct = count == 8
    small = pltpu.CompilerParams(vmem_limit_bytes=SMALL_VMEM)

    def in_hbm(*arrays):
        return [pltpu.with_memory_space_constraint(array, pltpu.HBM) for array in arrays]

    def other_core(array):
        return lax.ppermute(array, "heads", [(0, 1), (1, 0)])

    def partners(array, steps, cores=(0, 1)):
        pairs = [
            (2 * index + core, 2 * (index ^ steps[core]) + core)
            for index in range(count)
            for core in cores
        ]
        return lax.ppermute(array, ("ctx", "heads"), pairs)

    def small_kernel(name, body, estimate, *chunks):
        return pl.pallas_call(
            body,
            out_shape=jax.ShapeDtypeStruct(chunks[0].shape, BF16),
            in_specs=[vmem()] * len(chunks),
            out_specs=vmem(),
            compiler_params=small,
            cost_estimate=cost(estimate),
            name=name,
        )(*chunks)

    def attend(name, estimate, queries, bias, chunks, old=(), passed=(), paired=False):
        return pl.pallas_call(
            functools.partial(chunks_kernel, len(chunks), len(old), paired),
            out_shape=[jax.ShapeDtypeStruct((query_rows, size), F32) for size in (1, 1, DC)]
            + [jax.ShapeDtypeStruct(chunk.shape, BF16) for chunk in passed],
            in_specs=[vmem()] * (3 + len(chunks) + len(old) + len(passed)),
            out_specs=[vmem()] * (3 + len(passed)),
            scratch_shapes=[pltpu.VMEM((bias.shape[2], DC + DR), BF16)],
            compiler_params=small,
            cost_estimate=cost(estimate),
            name=name,
        )(*queries, bias, *chunks, *old, *passed)

    packed = pl.pallas_call(
        pack_kernel,
        out_shape=jax.ShapeDtypeStruct((rows + rows // 6, DC), BF16),
        in_specs=[vmem()] * 2,
        out_specs=vmem(),
        compiler_params=small,
        name="pack",
    )(*in_hbm(latent, key_rope.T))
    if direct:
        order = [
            [(0, 0), FIRST_OUT, FIRST_OUT[::-1], SECOND_OUT, SECOND_OUT[::-1]],
            [LAST_OUT, RELAYED],
            [RELAYED[::-1]],
        ]
        bias_shapes = [(1, rows, len(steps) * rows) for steps in order]
    else:
        order = None
        bias_shapes = [(count // BLOCK_CHUNKS, rows, BLOCK_CHUNKS * rows)]
    outs = pl.pallas_call(
        functools.partial(prepare_kernel, order),
        out_shape=[jax.ShapeDtypeStruct((query_rows // 2, DC + DR), BF16)]
        + [jax.ShapeDtypeStruct(shape, F32) for shape in bias_shapes]
        + [jax.ShapeDtypeStruct((depth, width + DC // depth * key_up.shape[1]), BF16)],
        in_specs=[hbm()] * 6 + [anywhere()],
        out_specs=[vmem()] * (len(bias_shapes) + 2),
        scratch_shapes=[
            pltpu.VMEM(queries_nope.shape, BF16),
            pltpu.VMEM(queries_rope.shape, BF16),
            pltpu.VMEM(key_up.shape, BF16),
            pltpu.SMEM(span_order.shape, jnp.int32),
            pltpu.VMEM(value_up.shape, BF16),
            pltpu.SemaphoreType.DMA((6,)),
        ],
        compiler_params=small,
        cost_estimate=cost(PREPARE_COST),
        name="prepare",
    )(*in_hbm(queries_nope, queries_rope, key_up, span_order, value_up, out_proj), packed)
    queries, biases = outs[0], outs[1:-1]
    weights_other = other_core(outs[-1])
    both = [queries, other_core(queries)]

    if direct:
        out_first = partners(packed, FIRST_OUT)
        out_second = partners(packed, SECOND_OUT)
        out_last = partners(packed, LAST_OUT, cores=(1,))
        picked = small_kernel("pick", pick_kernel, PICK_COST, out_first, out_last)
        out_first = small_kernel("hand_first", hand_kernel, HAND_COST, out_first)
        out_second = small_kernel("hand_second", hand_kernel, HAND_COST, out_second, out_first)
        relayed = partners(picked, (1, 1))
        early = [packed, out_first, other_core(out_first), out_second, other_core(out_second)]
        *running, last_after = attend("first", FIRST_COST, both, biases[0], early, passed=[out_last])
        last = [other_core(relayed)]
        running = attend(
            "second",
            SECOND_COST,
            both,
            biases[1],
            [out_last, lax.ppermute(last_after, "heads", [(1, 0)]), relayed],
            running,
            paired=True,
        )
    else:
        last = []
        running = pl.pallas_call(
            gathered_kernel,
            out_shape=[jax.ShapeDtypeStruct((query_rows, size), F32) for size in (1, 1, DC)],
            in_specs=[vmem()] * 4,
            out_specs=[vmem()] * 3,
            scratch_shapes=[pltpu.VMEM((BLOCK_CHUNKS * rows, DC + DR), BF16)],
            compiler_params=pltpu.CompilerParams(vmem_limit_bytes=LARGE_VMEM),
            name="gathered",
        )(*both, biases[0], lax.all_gather(packed, "ctx", axis=0))

    tiles = 7 if width % 896 == 0 else 1
    return pl.pallas_call(
        functools.partial(finish_kernel, heads, len(last)),
        out_shape=jax.ShapeDtypeStruct((rows, width), BF16),
        in_specs=[vmem()] * (5 + len(biases[2:]) + len(last) + 3),
        out_specs=anywhere(),
        scratch_shapes=[
            pltpu.VMEM((rows, width), BF16),
            pltpu.VMEM((rows, DC + DR), BF16),
            pltpu.SemaphoreType.DMA((tiles,)),
        ],
        compiler_params=small,
        name="finish",
    )(*both, *running, *biases[2:], *last, value_up, out_proj, weights_other)


def solution(mesh):
    in_specs = (
        P(("docs", "ctx"), "heads"),
        P(("docs", "ctx"), "heads"),
        P(("docs", "ctx"), None),
        P(("docs", "ctx"), None),
        P(None, "heads"),
        P(None, "heads"),
        P("heads", None),
        P("docs"),
    )
    out_specs = P(("docs", "ctx"), "heads")
    return jax.shard_map(
        functools.partial(per_device, mesh.shape["ctx"]),
        mesh=mesh,
        in_specs=in_specs,
        out_specs=out_specs,
        check_vma=False,
    )
```

```python
import functools
import math

import jax
import jax.numpy as jnp
from jax import lax
from jax.experimental import pallas as pl
from jax.experimental.pallas import tpu as pltpu
from jax.sharding import PartitionSpec as P

DC = 512
DH = 128
DR = 64
BF16 = jnp.bfloat16
F32 = jnp.float32
MASKED = -1e30
BLOCK_CHUNKS = 8
PREPARE_COST, GATE_COST, FIRST_COST, SECOND_COST = 0, 3, 20, 1
SMALL_VMEM = 20 * 1024 * 1024
LARGE_VMEM = 56 * 1024 * 1024
FAR = (4, 6)
NEAR = (2, 1)
CORNER = (3, 3)
RELAYED = (5, 7)


def vmem():
    return pl.BlockSpec(memory_space=pltpu.VMEM)


def anywhere():
    return pl.BlockSpec(memory_space=pl.ANY)


def hbm():
    return pl.BlockSpec(memory_space=pltpu.HBM)


def cost(microseconds):
    return pl.CostEstimate(flops=int(microseconds * 1.1e9), bytes_accessed=0, transcendentals=0)


def pack_kernel(latent, key_rope_turned, out_ref):
    rows = latent.shape[0]
    group = rows // 6
    out_ref[:rows] = latent[...]
    rope = key_rope_turned[...].astype(F32).T.astype(BF16)
    parts = [rope[index * group : (index + 1) * group] for index in range(6)]
    parts.append(jnp.zeros((group, DC - 6 * DR), BF16))
    out_ref[rows:] = jnp.concatenate(parts, axis=1)


def gate_kernel(chunk, out_ref):
    out_ref[...] = chunk[...]


def unpack(chunk, keys, base, other=None):
    chunk = chunk[...]
    if other is not None:
        chunk = jnp.where(lax.axis_index("heads") == 0, other[...], chunk)
    rows = 6 * chunk.shape[0] // 7
    group = rows // 6
    keys[pl.ds(base, rows), :DC] = chunk[:rows]
    for index in range(6):
        part = chunk[rows:, index * DR : (index + 1) * DR]
        keys[pl.ds(base + index * group, group), DC:] = part


def prepare_kernel(order, *refs):
    sources, out_proj, rest = refs[:5], refs[5], refs[7:]
    outs, copied, sems = rest[:-6], rest[-6:-1], rest[-1]
    weights = outs[-1]
    depth, width = out_proj.shape[0], out_proj.shape[1] // 2
    fetches = [
        pltpu.make_async_copy(source, target, sems.at[index])
        for index, (source, target) in enumerate(zip(sources, copied))
    ]
    base = pl.multiple_of((1 - lax.axis_index("heads")) * width, 128)
    fetches.append(
        pltpu.make_async_copy(
            out_proj.at[:, pl.ds(base, width)], weights.at[:, pl.ds(0, width)], sems.at[5]
        )
    )
    for fetch in fetches:
        fetch.start()
    nope, rope, up, span_order, value_up = copied
    rows = nope.shape[0]
    heads = nope.shape[1] // DH
    span_rows = rows // 2
    for fetch in fetches[:3]:
        fetch.wait()
    own_index = lax.axis_index("ctx")
    core = lax.axis_index("heads")
    for head in range(heads):
        latent = lax.dot_general(
            nope[:, head * DH : (head + 1) * DH],
            up[:, head * DH : (head + 1) * DH],
            (((1,), (1,)), ((), ())),
            preferred_element_type=F32,
        )
        part = pl.ds(head * rows, rows)
        outs[0][part, :DC] = latent.astype(BF16)
        outs[0][part, DC:] = rope[:, head * DR : (head + 1) * DR]
    biases = outs[1:-1]
    fetches[3].wait()
    row = lax.broadcasted_iota(jnp.int32, (rows, 1), 0)
    query_pos = jnp.where(
        row < span_rows,
        span_order[2 * own_index] * span_rows + row,
        span_order[2 * own_index + 1] * span_rows + row - span_rows,
    )

    def bias_of(owners):
        column = lax.broadcasted_iota(jnp.int32, (1, len(owners) * rows), 1)
        key_pos = jnp.zeros(column.shape, jnp.int32)
        for index, owner in enumerate(owners):
            for side in range(2):
                start = index * rows + side * span_rows
                first = span_order[2 * owner + side] * span_rows
                key_pos = jnp.where(column >= start, first + column - start, key_pos)
        return jnp.where(key_pos <= query_pos, F32(0.0), F32(MASKED))

    if order is not None:
        for steps, bias_ref in zip(order, biases):
            bias_ref[0] = bias_of(
                [own_index ^ jnp.where(core == 0, step[0], step[1]) for step in steps]
            )
    else:
        bias_ref = biases[0]

        def step(block, carry):
            bias_ref[block] = bias_of([block * BLOCK_CHUNKS + index for index in range(BLOCK_CHUNKS)])
            return carry

        lax.fori_loop(0, bias_ref.shape[0], step, 0)

    fetches[4].wait()
    columns = value_up.shape[1]
    for block in range(DC // depth):
        part = value_up[block * depth : (block + 1) * depth, :]
        weights[:, width + block * columns : width + (block + 1) * columns] = part
    fetches[5].wait()


def attend_block(queries, keys, bias, old):
    copies = len(queries) * queries[0].shape[0] // bias.shape[0]
    scale = math.log2(math.e) / math.sqrt(DH + DR)
    heads = jnp.concatenate([part[...] for part in queries], axis=0)
    scores = lax.dot_general(
        heads, keys[...], (((1,), (1,)), ((), ())), preferred_element_type=F32
    )
    scores = scores + jnp.concatenate([bias] * copies, axis=0)
    top = jnp.max(scores, axis=-1, keepdims=True)
    if old is not None:
        top = jnp.maximum(old[0], top)
        rescale = jnp.exp2((old[0] - top) * scale)
    expo = jnp.exp2((scores - top) * scale)
    total = jnp.sum(expo, axis=-1, keepdims=True)
    added = jnp.dot(expo.astype(BF16), keys[:, :DC], preferred_element_type=F32)
    if old is not None:
        total = old[1] * rescale + total
        added = old[2] * rescale + added
    return top, total, added


def chunks_kernel(chunk_count, old_count, paired, *rest):
    queries, bias, rest = rest[:2], rest[2], rest[3:]
    chunks, rest = rest[:chunk_count], rest[chunk_count:]
    old, rest = rest[:old_count], rest[old_count:]
    if len(rest) == 6:
        passed, handed = rest[0], rest[4]
        handed[...] = passed[...]
        rest = rest[1:4] + rest[5:]
    running, keys = rest[:3], rest[3]
    rows = bias.shape[1]
    if paired:
        unpack(chunks[0], keys, 0, chunks[1])
        chunks = chunks[1:]
    for index, chunk in enumerate(chunks):
        if index or not paired:
            unpack(chunk, keys, index * rows)
    before = [state[...] for state in old] if old else None
    values = attend_block(queries, keys, bias[0], before)
    for state, value in zip(running, values):
        state[...] = value


def gathered_kernel(queries_own, queries_other, bias, gathered, *rest):
    queries = (queries_own, queries_other)
    running, keys = rest[:3], rest[3]
    blocks, rows, _ = bias.shape

    def fill(block):
        for index in range(BLOCK_CHUNKS):
            unpack(gathered.at[block * BLOCK_CHUNKS + index], keys, index * rows)

    first = lax.axis_index("ctx") // BLOCK_CHUNKS
    fill(first)
    values = attend_block(queries, keys, bias[first], None)
    for state, value in zip(running, values):
        state[...] = value

    def step(index, carry):
        block = index + jnp.where(index >= first, 1, 0)
        fill(block)
        new = attend_block(queries, keys, bias[block], [state[...] for state in running])
        for state, value in zip(running, new):
            state[...] = value
        return carry

    lax.fori_loop(0, blocks - 1, step, 0)


def last_kernel(chunk_count, queries_own, queries_other, top, total, context, *rest):
    bias, chunks = rest[:chunk_count][:1], rest[1 : 1 + chunk_count]
    value_own, weights, out_ref, keys = rest[len(bias) + len(chunks) :]
    rows = out_ref.shape[0]
    running = (top[...], total[...], context[...])
    if chunk_count:
        for index, chunk in enumerate(chunks):
            unpack(chunk, keys, index * rows)
        running = attend_block((queries_own, queries_other), keys, bias[0][0], running)
    mixed = (running[2] * (1.0 / running[1])).astype(BF16)
    columns = value_own.shape[1]
    heads = columns // DH
    depth = weights.shape[0]
    width = weights.shape[1] - DC // depth * columns
    for group in range(2):
        for head in range(heads):
            place = group * heads + head
            per_head = 0.0
            for block in range(DC // depth):
                part = slice(block * depth, (block + 1) * depth)
                if group == 0:
                    value = value_own[part, head * DH : (head + 1) * DH]
                else:
                    start = width + block * columns + head * DH
                    value = weights[:, start : start + DH]
                per_head = per_head + jnp.dot(
                    mixed[place * rows : (place + 1) * rows, part],
                    value,
                    preferred_element_type=F32,
                )
            out_ref[:, place * DH : (place + 1) * DH] = per_head.astype(BF16)


def project_kernel(tiles, heads_out, proj_own, weights, out_ref, out_tiles, sems):
    width = out_ref.shape[1]
    half = heads_out.shape[1] // 2
    base = lax.axis_index("heads") * width
    sends = []
    for index, (start, size) in enumerate(tiles):
        own = proj_own[:, pl.ds(pl.multiple_of(base + start, 128), size)]
        out = jnp.dot(heads_out[:, :half], own, preferred_element_type=F32)
        part = pl.ds(start, size)
        out = out + jnp.dot(heads_out[:, half:], weights[:, part], preferred_element_type=F32)
        out_tiles[:, part] = out.astype(BF16)
        sends.append(
            pltpu.make_async_copy(out_tiles.at[:, part], out_ref.at[:, part], sems.at[index])
        )
        sends[-1].start()
    for send in sends:
        send.wait()


def per_device(
    count, queries_nope, queries_rope, latent, key_rope, key_up, value_up, out_proj, span_order
):
    rows = latent.shape[0]
    depth, width = out_proj.shape[0], out_proj.shape[1] // 2
    heads = 2 * (key_up.shape[1] // DH)
    query_rows = heads * rows
    direct = count == 8
    small = pltpu.CompilerParams(vmem_limit_bytes=SMALL_VMEM)

    def in_hbm(*arrays):
        return [pltpu.with_memory_space_constraint(array, pltpu.HBM) for array in arrays]

    def other_core(array):
        return lax.ppermute(array, "heads", [(0, 1), (1, 0)])

    def partners(array, steps, cores=(0, 1)):
        pairs = [
            (2 * index + core, 2 * (index ^ steps[core]) + core)
            for index in range(count)
            for core in cores
        ]
        return lax.ppermute(array, ("ctx", "heads"), pairs)

    def attend(name, estimate, queries, bias, chunks, old=(), passed=(), paired=False):
        return pl.pallas_call(
            functools.partial(chunks_kernel, len(chunks), len(old), paired),
            out_shape=[jax.ShapeDtypeStruct((query_rows, size), F32) for size in (1, 1, DC)]
            + [jax.ShapeDtypeStruct(chunk.shape, BF16) for chunk in passed],
            in_specs=[vmem()] * (3 + len(chunks) + len(old) + len(passed)),
            out_specs=[vmem()] * (3 + len(passed)),
            scratch_shapes=[pltpu.VMEM((bias.shape[2], DC + DR), BF16)],
            compiler_params=small,
            cost_estimate=cost(estimate),
            name=name,
        )(*queries, bias, *chunks, *old, *passed)

    packed = pl.pallas_call(
        pack_kernel,
        out_shape=jax.ShapeDtypeStruct((rows + rows // 6, DC), BF16),
        in_specs=[vmem()] * 2,
        out_specs=vmem(),
        compiler_params=small,
        name="pack",
    )(*in_hbm(latent, key_rope.T))
    if direct:
        order = [
            [(0, 0), NEAR],
            [CORNER, NEAR[::-1], FAR, FAR[::-1], RELAYED],
            [RELAYED[::-1]],
        ]
        bias_shapes = [(1, rows, len(steps) * rows) for steps in order]
    else:
        order = None
        bias_shapes = [(count // BLOCK_CHUNKS, rows, BLOCK_CHUNKS * rows)]
    outs = pl.pallas_call(
        functools.partial(prepare_kernel, order),
        out_shape=[jax.ShapeDtypeStruct((query_rows // 2, DC + DR), BF16)]
        + [jax.ShapeDtypeStruct(shape, F32) for shape in bias_shapes]
        + [jax.ShapeDtypeStruct((depth, width + DC // depth * key_up.shape[1]), BF16)],
        in_specs=[hbm()] * 6 + [anywhere()],
        out_specs=[vmem()] * (len(bias_shapes) + 2),
        scratch_shapes=[
            pltpu.VMEM(queries_nope.shape, BF16),
            pltpu.VMEM(queries_rope.shape, BF16),
            pltpu.VMEM(key_up.shape, BF16),
            pltpu.SMEM(span_order.shape, jnp.int32),
            pltpu.VMEM(value_up.shape, BF16),
            pltpu.SemaphoreType.DMA((6,)),
        ],
        compiler_params=small,
        cost_estimate=cost(PREPARE_COST),
        name="prepare",
    )(*in_hbm(queries_nope, queries_rope, key_up, span_order, value_up, out_proj), packed)
    queries, biases = outs[0], outs[1:-1]
    weights_other = other_core(outs[-1])
    both = [queries, other_core(queries)]

    if direct:
        far = partners(packed, FAR)
        near = partners(packed, NEAR)
        corner = partners(packed, CORNER, cores=(1,))
        relayed = partners(far, (1, 1))
        gated = pl.pallas_call(
            gate_kernel,
            out_shape=jax.ShapeDtypeStruct(far.shape, BF16),
            in_specs=[vmem()],
            out_specs=vmem(),
            compiler_params=small,
            cost_estimate=cost(GATE_COST),
            name="gate",
        )(far)
        *running, far_after = attend(
            "first", FIRST_COST, both, biases[0], [packed, near], passed=[gated]
        )
        last = [other_core(relayed)]
        running = attend(
            "second",
            SECOND_COST,
            both,
            biases[1],
            [corner, other_core(corner), other_core(near), far, other_core(far_after), relayed],
            running,
            paired=True,
        )
    else:
        last = []
        running = pl.pallas_call(
            gathered_kernel,
            out_shape=[jax.ShapeDtypeStruct((query_rows, size), F32) for size in (1, 1, DC)],
            in_specs=[vmem()] * 4,
            out_specs=[vmem()] * 3,
            scratch_shapes=[pltpu.VMEM((BLOCK_CHUNKS * rows, DC + DR), BF16)],
            compiler_params=pltpu.CompilerParams(vmem_limit_bytes=LARGE_VMEM),
            name="gathered",
        )(*both, biases[0], lax.all_gather(packed, "ctx", axis=0))

    heads_out = pl.pallas_call(
        functools.partial(last_kernel, len(last)),
        out_shape=jax.ShapeDtypeStruct((rows, heads * DH), BF16),
        in_specs=[vmem()] * (5 + len(biases[2:]) + len(last) + 2),
        out_specs=vmem(),
        scratch_shapes=[pltpu.VMEM((rows, DC + DR), BF16)],
        compiler_params=small,
        cost_estimate=cost(0),
        name="last",
    )(*both, *running, *biases[2:], *last, value_up, weights_other)

    tile = 512 if width % 512 == 0 else width
    tiles = [(start, tile) for start in range(0, width, tile)]
    if tile == 512:
        tiles[-1:] = [(width - 512, 256), (width - 256, 256)]
    return pl.pallas_call(
        functools.partial(project_kernel, tiles),
        out_shape=jax.ShapeDtypeStruct((rows, width), BF16),
        in_specs=[vmem()] * 3,
        out_specs=anywhere(),
        scratch_shapes=[
            pltpu.VMEM((rows, width), BF16),
            pltpu.SemaphoreType.DMA((len(tiles),)),
        ],
        compiler_params=small,
        name="project",
    )(heads_out, out_proj, weights_other)


def solution(mesh):
    in_specs = (
        P(("docs", "ctx"), "heads"),
        P(("docs", "ctx"), "heads"),
        P(("docs", "ctx"), None),
        P(("docs", "ctx"), None),
        P(None, "heads"),
        P(None, "heads"),
        P("heads", None),
        P("docs"),
    )
    out_specs = P(("docs", "ctx"), "heads")
    return jax.shard_map(
        functools.partial(per_device, mesh.shape["ctx"]),
        mesh=mesh,
        in_specs=in_specs,
        out_specs=out_specs,
        check_vma=False,
    )
```

```python
import functools
import math

import jax
import jax.numpy as jnp
from jax import lax
from jax.experimental import pallas as pl
from jax.experimental.pallas import tpu as pltpu
from jax.sharding import PartitionSpec as P

DC = 512
DH = 128
DR = 64
BF16 = jnp.bfloat16
F32 = jnp.float32
MASKED = -1e30
BLOCK_CHUNKS = 8
PREPARE_COST, GATE_COST, FIRST_COST, SECOND_COST = 0, 3, 20, 1
SMALL_VMEM = 20 * 1024 * 1024
LARGE_VMEM = 56 * 1024 * 1024
FAR = (4, 6)
NEAR = (2, 1)
CORNER = (3, 3)
RELAYED = (5, 7)


def vmem():
    return pl.BlockSpec(memory_space=pltpu.VMEM)


def anywhere():
    return pl.BlockSpec(memory_space=pl.ANY)


def hbm():
    return pl.BlockSpec(memory_space=pltpu.HBM)


def cost(microseconds):
    return pl.CostEstimate(flops=int(microseconds * 1.1e9), bytes_accessed=0, transcendentals=0)


def pack_kernel(latent, key_rope_turned, out_ref, turned, sems):
    rows = latent.shape[0]
    group = rows // 6
    half = DC // 2
    fetches = [pltpu.make_async_copy(key_rope_turned, turned, sems.at[2])]
    for side in range(2):
        fetches.append(
            pltpu.make_async_copy(
                latent.at[:, pl.ds(side * half, half)],
                out_ref.at[pl.ds(side * rows, rows)],
                sems.at[side],
            )
        )
    for fetch in fetches:
        fetch.start()
    fetches[0].wait()
    rope = turned[...].astype(F32).T.astype(BF16)
    first = 0
    base = 2 * rows
    for size in (group, group // 2):
        parts = [rope[first + index * size : first + (index + 1) * size] for index in range(4)]
        out_ref[pl.ds(base, size), :] = jnp.concatenate(parts, axis=1)
        first += 4 * size
        base += size
    for fetch in fetches[1:]:
        fetch.wait()


def gate_kernel(chunk, out_ref):
    out_ref[...] = chunk[...]


def unpack(chunk, keys, base, other=None):
    chunk = chunk[...]
    if other is not None:
        chunk = jnp.where(lax.axis_index("heads") == 0, other[...], chunk)
    rows = 4 * chunk.shape[0] // 9
    group = rows // 6
    keys[pl.ds(base, rows), : DC // 2] = chunk[:rows]
    keys[pl.ds(base, rows), DC // 2 : DC] = chunk[rows : 2 * rows]
    place = 2 * rows
    for size in (group, group // 2):
        for index in range(4):
            part = chunk[place : place + size, index * DR : (index + 1) * DR]
            keys[pl.ds(base, size), DC:] = part
            base += size
        place += size


def prepare_kernel(order, *refs):
    sources, out_proj, rest = refs[:5], refs[5], refs[7:]
    outs, copied, sems = rest[:-6], rest[-6:-1], rest[-1]
    weights = outs[-1]
    depth, width = out_proj.shape[0], out_proj.shape[1] // 2
    fetches = [
        pltpu.make_async_copy(source, target, sems.at[index])
        for index, (source, target) in enumerate(zip(sources, copied))
    ]
    base = pl.multiple_of((1 - lax.axis_index("heads")) * width, 128)
    fetches.append(
        pltpu.make_async_copy(
            out_proj.at[:, pl.ds(base, width)], weights.at[:, pl.ds(0, width)], sems.at[5]
        )
    )
    for fetch in fetches:
        fetch.start()
    nope, rope, up, span_order, value_up = copied
    rows = nope.shape[0]
    heads = nope.shape[1] // DH
    span_rows = rows // 2
    for fetch in fetches[:3]:
        fetch.wait()
    own_index = lax.axis_index("ctx")
    core = lax.axis_index("heads")
    for head in range(heads):
        latent = lax.dot_general(
            nope[:, head * DH : (head + 1) * DH],
            up[:, head * DH : (head + 1) * DH],
            (((1,), (1,)), ((), ())),
            preferred_element_type=F32,
        )
        part = pl.ds(head * rows, rows)
        outs[0][part, :DC] = latent.astype(BF16)
        outs[0][part, DC:] = rope[:, head * DR : (head + 1) * DR]
    biases = outs[1:-1]
    fetches[3].wait()
    row = lax.broadcasted_iota(jnp.int32, (rows, 1), 0)
    query_pos = jnp.where(
        row < span_rows,
        span_order[2 * own_index] * span_rows + row,
        span_order[2 * own_index + 1] * span_rows + row - span_rows,
    )

    def bias_of(owners):
        column = lax.broadcasted_iota(jnp.int32, (1, len(owners) * rows), 1)
        key_pos = jnp.zeros(column.shape, jnp.int32)
        for index, owner in enumerate(owners):
            for side in range(2):
                start = index * rows + side * span_rows
                first = span_order[2 * owner + side] * span_rows
                key_pos = jnp.where(column >= start, first + column - start, key_pos)
        return jnp.where(key_pos <= query_pos, F32(0.0), F32(MASKED))

    if order is not None:
        for steps, bias_ref in zip(order, biases):
            bias_ref[0] = bias_of(
                [own_index ^ jnp.where(core == 0, step[0], step[1]) for step in steps]
            )
    else:
        bias_ref = biases[0]

        def step(block, carry):
            bias_ref[block] = bias_of([block * BLOCK_CHUNKS + index for index in range(BLOCK_CHUNKS)])
            return carry

        lax.fori_loop(0, bias_ref.shape[0], step, 0)

    fetches[4].wait()
    columns = value_up.shape[1]
    for block in range(DC // depth):
        part = value_up[block * depth : (block + 1) * depth, :]
        weights[:, width + block * columns : width + (block + 1) * columns] = part
    fetches[5].wait()


def attend_block(queries, keys, bias, old):
    copies = len(queries) * queries[0].shape[0] // bias.shape[0]
    scale = math.log2(math.e) / math.sqrt(DH + DR)
    heads = jnp.concatenate([part[...] for part in queries], axis=0)
    scores = lax.dot_general(
        heads, keys[...], (((1,), (1,)), ((), ())), preferred_element_type=F32
    )
    scores = scores + jnp.concatenate([bias] * copies, axis=0)
    top = jnp.max(scores, axis=-1, keepdims=True)
    if old is not None:
        top = jnp.maximum(old[0], top)
        rescale = jnp.exp2((old[0] - top) * scale)
    expo = jnp.exp2((scores - top) * scale)
    total = jnp.sum(expo, axis=-1, keepdims=True)
    added = jnp.dot(expo.astype(BF16), keys[:, :DC], preferred_element_type=F32)
    if old is not None:
        total = old[1] * rescale + total
        added = old[2] * rescale + added
    return top, total, added


def chunks_kernel(chunk_count, old_count, paired, *rest):
    queries, bias, rest = rest[:2], rest[2], rest[3:]
    chunks, rest = rest[:chunk_count], rest[chunk_count:]
    old, rest = rest[:old_count], rest[old_count:]
    if len(rest) == 6:
        passed, handed = rest[0], rest[4]
        handed[...] = passed[...]
        rest = rest[1:4] + rest[5:]
    running, keys = rest[:3], rest[3]
    rows = bias.shape[1]
    if paired:
        unpack(chunks[0], keys, 0, chunks[1])
        chunks = chunks[1:]
    for index, chunk in enumerate(chunks):
        if index or not paired:
            unpack(chunk, keys, index * rows)
    before = [state[...] for state in old] if old else None
    values = attend_block(queries, keys, bias[0], before)
    for state, value in zip(running, values):
        state[...] = value


def gathered_kernel(queries_own, queries_other, bias, gathered, *rest):
    queries = (queries_own, queries_other)
    running, keys = rest[:3], rest[3]
    blocks, rows, _ = bias.shape

    def fill(block):
        for index in range(BLOCK_CHUNKS):
            unpack(gathered.at[block * BLOCK_CHUNKS + index], keys, index * rows)

    first = lax.axis_index("ctx") // BLOCK_CHUNKS
    fill(first)
    values = attend_block(queries, keys, bias[first], None)
    for state, value in zip(running, values):
        state[...] = value

    def step(index, carry):
        block = index + jnp.where(index >= first, 1, 0)
        fill(block)
        new = attend_block(queries, keys, bias[block], [state[...] for state in running])
        for state, value in zip(running, new):
            state[...] = value
        return carry

    lax.fori_loop(0, blocks - 1, step, 0)


def finish_kernel(heads, chunk_count, *rest):
    queries, (top, total, context), rest = rest[:2], rest[2:5], rest[5:]
    bias, chunks = rest[:chunk_count][:1], rest[1 : 1 + chunk_count]
    rest = rest[len(bias) + len(chunks) :]
    value_own, proj_own, weights, out_ref, out_tiles, keys, out_sems = rest
    rows, width = out_ref.shape
    running = (top[...], total[...], context[...])
    if chunk_count:
        for index, chunk in enumerate(chunks):
            unpack(chunk, keys, index * rows)
        running = attend_block(queries, keys, bias[0][0], running)
    mixed = (running[2] / running[1]).astype(BF16)
    half = heads // 2
    depth = weights.shape[0]
    base = lax.axis_index("heads") * width
    sides = []
    for group in range(2):
        parts = []
        for head in range(half):
            first = (group * half + head) * rows
            per_head = 0.0
            for block in range(DC // depth):
                if group == 0:
                    value = value_own[block * depth : (block + 1) * depth, head * DH : (head + 1) * DH]
                else:
                    start = width + (block * half + head) * DH
                    value = weights[:, start : start + DH]
                per_head = per_head + jnp.dot(
                    mixed[first : first + rows, block * depth : (block + 1) * depth],
                    value,
                    preferred_element_type=F32,
                )
            parts.append(per_head.astype(BF16))
        sides.append(jnp.concatenate(parts, axis=1))
    tiles = out_sems.shape[0]
    tile = width // tiles
    sends = []
    for index in range(tiles):
        part = pl.ds(index * tile, tile)
        own = proj_own[:, pl.ds(pl.multiple_of(base + index * tile, 128), tile)]
        out = jnp.dot(sides[0], own, preferred_element_type=F32)
        out = out + jnp.dot(sides[1], weights[:, part], preferred_element_type=F32)
        out_tiles[:, part] = out.astype(BF16)
        sends.append(
            pltpu.make_async_copy(out_tiles.at[:, part], out_ref.at[:, part], out_sems.at[index])
        )
        sends[-1].start()
    for send in sends:
        send.wait()


def per_device(
    count, queries_nope, queries_rope, latent, key_rope, key_up, value_up, out_proj, span_order
):
    rows = latent.shape[0]
    depth, width = out_proj.shape[0], out_proj.shape[1] // 2
    heads = 2 * (key_up.shape[1] // DH)
    query_rows = heads * rows
    direct = count == 8
    small = pltpu.CompilerParams(vmem_limit_bytes=SMALL_VMEM)

    def in_hbm(*arrays):
        return [pltpu.with_memory_space_constraint(array, pltpu.HBM) for array in arrays]

    def other_core(array):
        return lax.ppermute(array, "heads", [(0, 1), (1, 0)])

    def partners(array, steps, cores=(0, 1)):
        pairs = [
            (2 * index + core, 2 * (index ^ steps[core]) + core)
            for index in range(count)
            for core in cores
        ]
        return lax.ppermute(array, ("ctx", "heads"), pairs)

    def attend(name, estimate, queries, bias, chunks, old=(), passed=(), paired=False):
        return pl.pallas_call(
            functools.partial(chunks_kernel, len(chunks), len(old), paired),
            out_shape=[jax.ShapeDtypeStruct((query_rows, size), F32) for size in (1, 1, DC)]
            + [jax.ShapeDtypeStruct(chunk.shape, BF16) for chunk in passed],
            in_specs=[vmem()] * (3 + len(chunks) + len(old) + len(passed)),
            out_specs=[vmem()] * (3 + len(passed)),
            scratch_shapes=[pltpu.VMEM((bias.shape[2], DC + DR), BF16)],
            compiler_params=small,
            cost_estimate=cost(estimate),
            name=name,
        )(*queries, bias, *chunks, *old, *passed)

    packed = pl.pallas_call(
        pack_kernel,
        out_shape=jax.ShapeDtypeStruct((2 * rows + rows // 4, DC // 2), BF16),
        in_specs=[hbm()] * 2,
        out_specs=vmem(),
        scratch_shapes=[
            pltpu.VMEM((DR, rows), BF16),
            pltpu.SemaphoreType.DMA((3,)),
        ],
        compiler_params=small,
        name="pack",
    )(*in_hbm(latent, key_rope.T))
    if direct:
        order = [
            [(0, 0), NEAR],
            [CORNER, NEAR[::-1], FAR, FAR[::-1], RELAYED],
            [RELAYED[::-1]],
        ]
        bias_shapes = [(1, rows, len(steps) * rows) for steps in order]
    else:
        order = None
        bias_shapes = [(count // BLOCK_CHUNKS, rows, BLOCK_CHUNKS * rows)]
    outs = pl.pallas_call(
        functools.partial(prepare_kernel, order),
        out_shape=[jax.ShapeDtypeStruct((query_rows // 2, DC + DR), BF16)]
        + [jax.ShapeDtypeStruct(shape, F32) for shape in bias_shapes]
        + [jax.ShapeDtypeStruct((depth, width + DC // depth * key_up.shape[1]), BF16)],
        in_specs=[hbm()] * 6 + [anywhere()],
        out_specs=[vmem()] * (len(bias_shapes) + 2),
        scratch_shapes=[
            pltpu.VMEM(queries_nope.shape, BF16),
            pltpu.VMEM(queries_rope.shape, BF16),
            pltpu.VMEM(key_up.shape, BF16),
            pltpu.SMEM(span_order.shape, jnp.int32),
            pltpu.VMEM(value_up.shape, BF16),
            pltpu.SemaphoreType.DMA((6,)),
        ],
        compiler_params=small,
        cost_estimate=cost(PREPARE_COST),
        name="prepare",
    )(*in_hbm(queries_nope, queries_rope, key_up, span_order, value_up, out_proj), packed)
    queries, biases = outs[0], outs[1:-1]
    weights_other = other_core(outs[-1])
    both = [queries, other_core(queries)]

    if direct:
        far = partners(packed, FAR)
        near = partners(packed, NEAR)
        corner = partners(packed, CORNER, cores=(1,))
        relayed = partners(far, (1, 1))
        gated = pl.pallas_call(
            gate_kernel,
            out_shape=jax.ShapeDtypeStruct(far.shape, BF16),
            in_specs=[vmem()],
            out_specs=vmem(),
            compiler_params=small,
            cost_estimate=cost(GATE_COST),
            name="gate",
        )(far)
        *running, far_after = attend(
            "first", FIRST_COST, both, biases[0], [packed, near], passed=[gated]
        )
        last = [other_core(relayed)]
        running = attend(
            "second",
            SECOND_COST,
            both,
            biases[1],
            [corner, other_core(corner), other_core(near), far, other_core(far_after), relayed],
            running,
            paired=True,
        )
    else:
        last = []
        running = pl.pallas_call(
            gathered_kernel,
            out_shape=[jax.ShapeDtypeStruct((query_rows, size), F32) for size in (1, 1, DC)],
            in_specs=[vmem()] * 4,
            out_specs=[vmem()] * 3,
            scratch_shapes=[pltpu.VMEM((BLOCK_CHUNKS * rows, DC + DR), BF16)],
            compiler_params=pltpu.CompilerParams(vmem_limit_bytes=LARGE_VMEM),
            name="gathered",
        )(*both, biases[0], lax.all_gather(packed, "ctx", axis=0))

    tiles = 7 if width % 896 == 0 else 1
    return pl.pallas_call(
        functools.partial(finish_kernel, heads, len(last)),
        out_shape=jax.ShapeDtypeStruct((rows, width), BF16),
        in_specs=[vmem()] * (5 + len(biases[2:]) + len(last) + 3),
        out_specs=anywhere(),
        scratch_shapes=[
            pltpu.VMEM((rows, width), BF16),
            pltpu.VMEM((rows, DC + DR), BF16),
            pltpu.SemaphoreType.DMA((tiles,)),
        ],
        compiler_params=small,
        name="finish",
    )(*both, *running, *biases[2:], *last, value_up, out_proj, weights_other)


def solution(mesh):
    in_specs = (
        P(("docs", "ctx"), "heads"),
        P(("docs", "ctx"), "heads"),
        P(("docs", "ctx"), None),
        P(("docs", "ctx"), None),
        P(None, "heads"),
        P(None, "heads"),
        P("heads", None),
        P("docs"),
    )
    out_specs = P(("docs", "ctx"), "heads")
    return jax.shard_map(
        functools.partial(per_device, mesh.shape["ctx"]),
        mesh=mesh,
        in_specs=in_specs,
        out_specs=out_specs,
        check_vma=False,
    )
```

```python
import functools
import math

import jax
import jax.numpy as jnp
from jax import lax
from jax.experimental import pallas as pl
from jax.experimental.pallas import tpu as pltpu
from jax.sharding import PartitionSpec as P

DC = 512
DH = 128
DR = 64
BF16 = jnp.bfloat16
F32 = jnp.float32
MASKED = -1e30
BLOCK_CHUNKS = 8
PREPARE_COST, GATE_COST, FIRST_COST, SECOND_COST = 0, 3, 20, 1
SMALL_VMEM = 20 * 1024 * 1024
LARGE_VMEM = 56 * 1024 * 1024
FAR = (4, 6)
NEAR = (2, 1)
CORNER = (3, 3)
RELAYED = (5, 7)


def vmem():
    return pl.BlockSpec(memory_space=pltpu.VMEM)


def anywhere():
    return pl.BlockSpec(memory_space=pl.ANY)


def hbm():
    return pl.BlockSpec(memory_space=pltpu.HBM)


def cost(microseconds):
    return pl.CostEstimate(flops=int(microseconds * 1.1e9), bytes_accessed=0, transcendentals=0)


def pack_kernel(latent, key_rope_turned, out_ref, turned, sems):
    rows = latent.shape[0]
    group = rows // 6
    half = DC // 2
    fetches = [pltpu.make_async_copy(key_rope_turned, turned, sems.at[2])]
    for side in range(2):
        fetches.append(
            pltpu.make_async_copy(
                latent.at[:, pl.ds(side * half, half)],
                out_ref.at[pl.ds(side * rows, rows)],
                sems.at[side],
            )
        )
    for fetch in fetches:
        fetch.start()
    fetches[0].wait()
    rope = turned[...].astype(F32).T.astype(BF16)
    first = 0
    base = 2 * rows
    for size in (group, group // 2):
        parts = [rope[first + index * size : first + (index + 1) * size] for index in range(4)]
        out_ref[pl.ds(base, size), :] = jnp.concatenate(parts, axis=1)
        first += 4 * size
        base += size
    for fetch in fetches[1:]:
        fetch.wait()


def gate_kernel(chunk, out_ref):
    out_ref[...] = chunk[...]


def unpack(chunk, keys, base, other=None):
    chunk = chunk[...]
    if other is not None:
        chunk = jnp.where(lax.axis_index("heads") == 0, other[...], chunk)
    rows = 4 * chunk.shape[0] // 9
    group = rows // 6
    keys[pl.ds(base, rows), : DC // 2] = chunk[:rows]
    keys[pl.ds(base, rows), DC // 2 : DC] = chunk[rows : 2 * rows]
    place = 2 * rows
    for size in (group, group // 2):
        for index in range(4):
            part = chunk[place : place + size, index * DR : (index + 1) * DR]
            keys[pl.ds(base, size), DC:] = part
            base += size
        place += size


def prepare_kernel(order, *refs):
    sources, (out_proj, packed), rest = refs[:5], refs[5:7], refs[7:]
    outs, copied, sems = rest[:-6], rest[-6:-1], rest[-1]
    weights, packed_after = outs[-2:]
    depth, width = out_proj.shape[0], out_proj.shape[1] // 2
    fetches = [
        pltpu.make_async_copy(source, target, sems.at[index])
        for index, (source, target) in enumerate(zip(sources, copied))
    ]
    base = pl.multiple_of((1 - lax.axis_index("heads")) * width, 128)
    fetches.append(
        pltpu.make_async_copy(
            out_proj.at[:, pl.ds(base, width)], weights.at[:, pl.ds(0, width)], sems.at[5]
        )
    )
    for fetch in fetches:
        fetch.start()
    packed_after[...] = packed[...]
    nope, rope, up, span_order, value_up = copied
    rows = nope.shape[0]
    heads = nope.shape[1] // DH
    span_rows = rows // 2
    for fetch in fetches[:3]:
        fetch.wait()
    own_index = lax.axis_index("ctx")
    core = lax.axis_index("heads")
    for head in range(heads):
        latent = lax.dot_general(
            nope[:, head * DH : (head + 1) * DH],
            up[:, head * DH : (head + 1) * DH],
            (((1,), (1,)), ((), ())),
            preferred_element_type=F32,
        )
        part = pl.ds(head * rows, rows)
        outs[0][part, :DC] = latent.astype(BF16)
        outs[0][part, DC:] = rope[:, head * DR : (head + 1) * DR]
    biases = outs[1:-2]
    fetches[3].wait()
    row = lax.broadcasted_iota(jnp.int32, (rows, 1), 0)
    query_pos = jnp.where(
        row < span_rows,
        span_order[2 * own_index] * span_rows + row,
        span_order[2 * own_index + 1] * span_rows + row - span_rows,
    )

    def bias_of(owners):
        column = lax.broadcasted_iota(jnp.int32, (1, len(owners) * rows), 1)
        key_pos = jnp.zeros(column.shape, jnp.int32)
        for index, owner in enumerate(owners):
            for side in range(2):
                start = index * rows + side * span_rows
                first = span_order[2 * owner + side] * span_rows
                key_pos = jnp.where(column >= start, first + column - start, key_pos)
        return jnp.where(key_pos <= query_pos, F32(0.0), F32(MASKED))

    if order is not None:
        for steps, bias_ref in zip(order, biases):
            bias_ref[0] = bias_of(
                [own_index ^ jnp.where(core == 0, step[0], step[1]) for step in steps]
            )
    else:
        bias_ref = biases[0]

        def step(block, carry):
            bias_ref[block] = bias_of([block * BLOCK_CHUNKS + index for index in range(BLOCK_CHUNKS)])
            return carry

        lax.fori_loop(0, bias_ref.shape[0], step, 0)

    fetches[4].wait()
    columns = value_up.shape[1]
    for block in range(DC // depth):
        part = value_up[block * depth : (block + 1) * depth, :]
        weights[:, width + block * columns : width + (block + 1) * columns] = part
    fetches[5].wait()


def attend_block(queries, keys, bias, old):
    copies = len(queries) * queries[0].shape[0] // bias.shape[0]
    scale = math.log2(math.e) / math.sqrt(DH + DR)
    heads = jnp.concatenate([part[...] for part in queries], axis=0)
    scores = lax.dot_general(
        heads, keys[...], (((1,), (1,)), ((), ())), preferred_element_type=F32
    )
    scores = scores + jnp.concatenate([bias] * copies, axis=0)
    top = jnp.max(scores, axis=-1, keepdims=True)
    if old is not None:
        top = jnp.maximum(old[0], top)
        rescale = jnp.exp2((old[0] - top) * scale)
    expo = jnp.exp2((scores - top) * scale)
    total = jnp.sum(expo, axis=-1, keepdims=True)
    added = jnp.dot(expo.astype(BF16), keys[:, :DC], preferred_element_type=F32)
    if old is not None:
        total = old[1] * rescale + total
        added = old[2] * rescale + added
    return top, total, added


def chunks_kernel(chunk_count, old_count, paired, *rest):
    queries, bias, rest = rest[:2], rest[2], rest[3:]
    chunks, rest = rest[:chunk_count], rest[chunk_count:]
    old, rest = rest[:old_count], rest[old_count:]
    if len(rest) == 6:
        passed, handed = rest[0], rest[4]
        handed[...] = passed[...]
        rest = rest[1:4] + rest[5:]
    running, keys = rest[:3], rest[3]
    rows = bias.shape[1]
    if paired:
        unpack(chunks[0], keys, 0, chunks[1])
        chunks = chunks[1:]
    for index, chunk in enumerate(chunks):
        if index or not paired:
            unpack(chunk, keys, index * rows)
    before = [state[...] for state in old] if old else None
    values = attend_block(queries, keys, bias[0], before)
    for state, value in zip(running, values):
        state[...] = value


def gathered_kernel(queries_own, queries_other, bias, gathered, *rest):
    queries = (queries_own, queries_other)
    running, keys = rest[:3], rest[3]
    blocks, rows, _ = bias.shape

    def fill(block):
        for index in range(BLOCK_CHUNKS):
            unpack(gathered.at[block * BLOCK_CHUNKS + index], keys, index * rows)

    first = lax.axis_index("ctx") // BLOCK_CHUNKS
    fill(first)
    values = attend_block(queries, keys, bias[first], None)
    for state, value in zip(running, values):
        state[...] = value

    def step(index, carry):
        block = index + jnp.where(index >= first, 1, 0)
        fill(block)
        new = attend_block(queries, keys, bias[block], [state[...] for state in running])
        for state, value in zip(running, new):
            state[...] = value
        return carry

    lax.fori_loop(0, blocks - 1, step, 0)


def finish_kernel(heads, chunk_count, *rest):
    queries, (top, total, context), rest = rest[:2], rest[2:5], rest[5:]
    bias, chunks = rest[:chunk_count][:1], rest[1 : 1 + chunk_count]
    rest = rest[len(bias) + len(chunks) :]
    value_own, proj_own, weights, out_ref, out_tiles, keys, out_sems = rest
    rows, width = out_ref.shape
    running = (top[...], total[...], context[...])
    if chunk_count:
        for index, chunk in enumerate(chunks):
            unpack(chunk, keys, index * rows)
        running = attend_block(queries, keys, bias[0][0], running)
    mixed = (running[2] / running[1]).astype(BF16)
    half = heads // 2
    depth = weights.shape[0]
    base = lax.axis_index("heads") * width
    sides = []
    for group in range(2):
        parts = []
        for head in range(half):
            first = (group * half + head) * rows
            per_head = 0.0
            for block in range(DC // depth):
                if group == 0:
                    value = value_own[block * depth : (block + 1) * depth, head * DH : (head + 1) * DH]
                else:
                    start = width + (block * half + head) * DH
                    value = weights[:, start : start + DH]
                per_head = per_head + jnp.dot(
                    mixed[first : first + rows, block * depth : (block + 1) * depth],
                    value,
                    preferred_element_type=F32,
                )
            parts.append(per_head.astype(BF16))
        sides.append(jnp.concatenate(parts, axis=1))
    tiles = out_sems.shape[0]
    tile = width // tiles
    sends = []
    for index in range(tiles):
        part = pl.ds(index * tile, tile)
        own = proj_own[:, pl.ds(pl.multiple_of(base + index * tile, 128), tile)]
        out = jnp.dot(sides[0], own, preferred_element_type=F32)
        out = out + jnp.dot(sides[1], weights[:, part], preferred_element_type=F32)
        out_tiles[:, part] = out.astype(BF16)
        sends.append(
            pltpu.make_async_copy(out_tiles.at[:, part], out_ref.at[:, part], out_sems.at[index])
        )
        sends[-1].start()
    for send in sends:
        send.wait()


def per_device(
    count, queries_nope, queries_rope, latent, key_rope, key_up, value_up, out_proj, span_order
):
    rows = latent.shape[0]
    depth, width = out_proj.shape[0], out_proj.shape[1] // 2
    heads = 2 * (key_up.shape[1] // DH)
    query_rows = heads * rows
    direct = count == 8
    small = pltpu.CompilerParams(vmem_limit_bytes=SMALL_VMEM)

    def in_hbm(*arrays):
        return [pltpu.with_memory_space_constraint(array, pltpu.HBM) for array in arrays]

    def other_core(array):
        return lax.ppermute(array, "heads", [(0, 1), (1, 0)])

    def partners(array, steps, cores=(0, 1)):
        pairs = [
            (2 * index + core, 2 * (index ^ steps[core]) + core)
            for index in range(count)
            for core in cores
        ]
        return lax.ppermute(array, ("ctx", "heads"), pairs)

    def attend(name, estimate, queries, bias, chunks, old=(), passed=(), paired=False):
        return pl.pallas_call(
            functools.partial(chunks_kernel, len(chunks), len(old), paired),
            out_shape=[jax.ShapeDtypeStruct((query_rows, size), F32) for size in (1, 1, DC)]
            + [jax.ShapeDtypeStruct(chunk.shape, BF16) for chunk in passed],
            in_specs=[vmem()] * (3 + len(chunks) + len(old) + len(passed)),
            out_specs=[vmem()] * (3 + len(passed)),
            scratch_shapes=[pltpu.VMEM((bias.shape[2], DC + DR), BF16)],
            compiler_params=small,
            cost_estimate=cost(estimate),
            name=name,
        )(*queries, bias, *chunks, *old, *passed)

    packed = pl.pallas_call(
        pack_kernel,
        out_shape=jax.ShapeDtypeStruct((2 * rows + rows // 4, DC // 2), BF16),
        in_specs=[hbm()] * 2,
        out_specs=vmem(),
        scratch_shapes=[
            pltpu.VMEM((DR, rows), BF16),
            pltpu.SemaphoreType.DMA((3,)),
        ],
        compiler_params=small,
        name="pack",
    )(*in_hbm(latent, key_rope.T))
    if direct:
        order = [
            [(0, 0), NEAR],
            [CORNER, NEAR[::-1], FAR, FAR[::-1], RELAYED],
            [RELAYED[::-1]],
        ]
        bias_shapes = [(1, rows, len(steps) * rows) for steps in order]
    else:
        order = None
        bias_shapes = [(count // BLOCK_CHUNKS, rows, BLOCK_CHUNKS * rows)]
    outs = pl.pallas_call(
        functools.partial(prepare_kernel, order),
        out_shape=[jax.ShapeDtypeStruct((query_rows // 2, DC + DR), BF16)]
        + [jax.ShapeDtypeStruct(shape, F32) for shape in bias_shapes]
        + [
            jax.ShapeDtypeStruct((depth, width + DC // depth * key_up.shape[1]), BF16),
            jax.ShapeDtypeStruct(packed.shape, BF16),
        ],
        in_specs=[hbm()] * 6 + [vmem()],
        out_specs=[vmem()] * (len(bias_shapes) + 3),
        scratch_shapes=[
            pltpu.VMEM(queries_nope.shape, BF16),
            pltpu.VMEM(queries_rope.shape, BF16),
            pltpu.VMEM(key_up.shape, BF16),
            pltpu.SMEM(span_order.shape, jnp.int32),
            pltpu.VMEM(value_up.shape, BF16),
            pltpu.SemaphoreType.DMA((6,)),
        ],
        compiler_params=small,
        cost_estimate=cost(PREPARE_COST),
        name="prepare",
    )(*in_hbm(queries_nope, queries_rope, key_up, span_order, value_up, out_proj), packed)
    queries, biases = outs[0], outs[1:-2]
    weights, packed_after = outs[-2:]
    weights_other = other_core(weights)
    both = [queries, other_core(queries)]

    if direct:
        far = partners(packed, FAR)
        near = partners(packed_after, NEAR)
        corner = partners(packed_after, CORNER, cores=(1,))
        relayed = partners(far, (1, 1))
        gated = pl.pallas_call(
            gate_kernel,
            out_shape=jax.ShapeDtypeStruct(far.shape, BF16),
            in_specs=[vmem()],
            out_specs=vmem(),
            compiler_params=small,
            cost_estimate=cost(GATE_COST),
            name="gate",
        )(far)
        *running, far_after = attend(
            "first", FIRST_COST, both, biases[0], [packed, near], passed=[gated]
        )
        last = [other_core(relayed)]
        running = attend(
            "second",
            SECOND_COST,
            both,
            biases[1],
            [corner, other_core(corner), other_core(near), far, other_core(far_after), relayed],
            running,
            paired=True,
        )
    else:
        last = []
        running = pl.pallas_call(
            gathered_kernel,
            out_shape=[jax.ShapeDtypeStruct((query_rows, size), F32) for size in (1, 1, DC)],
            in_specs=[vmem()] * 4,
            out_specs=[vmem()] * 3,
            scratch_shapes=[pltpu.VMEM((BLOCK_CHUNKS * rows, DC + DR), BF16)],
            compiler_params=pltpu.CompilerParams(vmem_limit_bytes=LARGE_VMEM),
            name="gathered",
        )(*both, biases[0], lax.all_gather(packed, "ctx", axis=0))

    tiles = 7 if width % 896 == 0 else 1
    return pl.pallas_call(
        functools.partial(finish_kernel, heads, len(last)),
        out_shape=jax.ShapeDtypeStruct((rows, width), BF16),
        in_specs=[vmem()] * (5 + len(biases[2:]) + len(last) + 3),
        out_specs=anywhere(),
        scratch_shapes=[
            pltpu.VMEM((rows, width), BF16),
            pltpu.VMEM((rows, DC + DR), BF16),
            pltpu.SemaphoreType.DMA((tiles,)),
        ],
        compiler_params=small,
        name="finish",
    )(*both, *running, *biases[2:], *last, value_up, out_proj, weights_other)


def solution(mesh):
    in_specs = (
        P(("docs", "ctx"), "heads"),
        P(("docs", "ctx"), "heads"),
        P(("docs", "ctx"), None),
        P(("docs", "ctx"), None),
        P(None, "heads"),
        P(None, "heads"),
        P("heads", None),
        P("docs"),
    )
    out_specs = P(("docs", "ctx"), "heads")
    return jax.shard_map(
        functools.partial(per_device, mesh.shape["ctx"]),
        mesh=mesh,
        in_specs=in_specs,
        out_specs=out_specs,
        check_vma=False,
    )
```

```python
import functools
import math

import jax
import jax.numpy as jnp
from jax import lax
from jax.experimental import pallas as pl
from jax.experimental.pallas import tpu as pltpu
from jax.sharding import PartitionSpec as P

DC = 512
DH = 128
DR = 64
BF16 = jnp.bfloat16
F32 = jnp.float32
MASKED = -1e30
BLOCK_CHUNKS = 8
PREPARE_COST, GATE_COST, FIRST_COST, SECOND_COST = 0, 3, 20, 1
SMALL_VMEM = 20 * 1024 * 1024
LARGE_VMEM = 56 * 1024 * 1024
FAR = (4, 6)
NEAR = (2, 1)
CORNER = (3, 3)
RELAYED = (5, 7)


def vmem():
    return pl.BlockSpec(memory_space=pltpu.VMEM)


def anywhere():
    return pl.BlockSpec(memory_space=pl.ANY)


def hbm():
    return pl.BlockSpec(memory_space=pltpu.HBM)


def cost(microseconds):
    return pl.CostEstimate(flops=int(microseconds * 1.1e9), bytes_accessed=0, transcendentals=0)


def pack_kernel(latent, key_rope_turned, out_ref, turned, sems):
    rows = latent.shape[0]
    group = rows // 6
    half = DC // 2
    fetches = [pltpu.make_async_copy(key_rope_turned, turned, sems.at[2])]
    for side in range(2):
        fetches.append(
            pltpu.make_async_copy(
                latent.at[:, pl.ds(side * half, half)],
                out_ref.at[pl.ds(side * rows, rows)],
                sems.at[side],
            )
        )
    for fetch in fetches:
        fetch.start()
    fetches[0].wait()
    rope = turned[...].astype(F32).T.astype(BF16)
    first = 0
    base = 2 * rows
    for size in (group, group // 2):
        parts = [rope[first + index * size : first + (index + 1) * size] for index in range(4)]
        out_ref[pl.ds(base, size), :] = jnp.concatenate(parts, axis=1)
        first += 4 * size
        base += size
    for fetch in fetches[1:]:
        fetch.wait()


def gate_kernel(chunk, out_ref):
    out_ref[...] = chunk[...]


def unpack(chunk, keys, base, other=None):
    chunk = chunk[...]
    if other is not None:
        chunk = jnp.where(lax.axis_index("heads") == 0, other[...], chunk)
    rows = 4 * chunk.shape[0] // 9
    group = rows // 6
    keys[pl.ds(base, rows), : DC // 2] = chunk[:rows]
    keys[pl.ds(base, rows), DC // 2 : DC] = chunk[rows : 2 * rows]
    place = 2 * rows
    for size in (group, group // 2):
        for index in range(4):
            part = chunk[place : place + size, index * DR : (index + 1) * DR]
            keys[pl.ds(base, size), DC:] = part
            base += size
        place += size


def prepare_kernel(order, *refs):
    sources, out_proj, rest = refs[:5], refs[5], refs[7:]
    outs, copied, sems = rest[:-6], rest[-6:-1], rest[-1]
    weights = outs[-1]
    depth, width = out_proj.shape[0], out_proj.shape[1] // 2
    fetches = [
        pltpu.make_async_copy(source, target, sems.at[index])
        for index, (source, target) in enumerate(zip(sources, copied))
    ]
    base = pl.multiple_of((1 - lax.axis_index("heads")) * width, 128)
    fetches.append(
        pltpu.make_async_copy(
            out_proj.at[:, pl.ds(base, width)], weights.at[:, pl.ds(0, width)], sems.at[5]
        )
    )
    for fetch in fetches:
        fetch.start()
    nope, rope, up, span_order, value_up = copied
    rows = nope.shape[0]
    heads = nope.shape[1] // DH
    span_rows = rows // 2
    for fetch in fetches[:3]:
        fetch.wait()
    own_index = lax.axis_index("ctx")
    core = lax.axis_index("heads")
    for head in range(heads):
        latent = lax.dot_general(
            nope[:, head * DH : (head + 1) * DH],
            up[:, head * DH : (head + 1) * DH],
            (((1,), (1,)), ((), ())),
            preferred_element_type=F32,
        )
        part = pl.ds(head * rows, rows)
        outs[0][part, :DC] = latent.astype(BF16)
        outs[0][part, DC:] = rope[:, head * DR : (head + 1) * DR]
    biases = outs[1:-1]
    fetches[3].wait()
    row = lax.broadcasted_iota(jnp.int32, (rows, 1), 0)
    query_pos = jnp.where(
        row < span_rows,
        span_order[2 * own_index] * span_rows + row,
        span_order[2 * own_index + 1] * span_rows + row - span_rows,
    )

    def bias_of(owners):
        column = lax.broadcasted_iota(jnp.int32, (1, len(owners) * rows), 1)
        key_pos = jnp.zeros(column.shape, jnp.int32)
        for index, owner in enumerate(owners):
            for side in range(2):
                start = index * rows + side * span_rows
                first = span_order[2 * owner + side] * span_rows
                key_pos = jnp.where(column >= start, first + column - start, key_pos)
        return jnp.where(key_pos <= query_pos, F32(0.0), F32(MASKED))

    if order is not None:
        for steps, bias_ref in zip(order, biases):
            bias_ref[0] = bias_of(
                [own_index ^ jnp.where(core == 0, step[0], step[1]) for step in steps]
            )
    else:
        bias_ref = biases[0]

        def step(block, carry):
            bias_ref[block] = bias_of([block * BLOCK_CHUNKS + index for index in range(BLOCK_CHUNKS)])
            return carry

        lax.fori_loop(0, bias_ref.shape[0], step, 0)

    fetches[4].wait()
    columns = value_up.shape[1]
    for block in range(DC // depth):
        part = value_up[block * depth : (block + 1) * depth, :]
        weights[:, width + block * columns : width + (block + 1) * columns] = part
    fetches[5].wait()


def attend_block(queries, keys, bias, old):
    copies = len(queries) * queries[0].shape[0] // bias.shape[0]
    scale = math.log2(math.e) / math.sqrt(DH + DR)
    heads = jnp.concatenate([part[...] for part in queries], axis=0)
    scores = lax.dot_general(
        heads, keys[...], (((1,), (1,)), ((), ())), preferred_element_type=F32
    )
    scores = scores + jnp.concatenate([bias] * copies, axis=0)
    top = jnp.max(scores, axis=-1, keepdims=True)
    if old is not None:
        top = jnp.maximum(old[0], top)
        rescale = jnp.exp2((old[0] - top) * scale)
    expo = jnp.exp2((scores - top) * scale)
    total = jnp.sum(expo, axis=-1, keepdims=True)
    added = jnp.dot(expo.astype(BF16), keys[:, :DC], preferred_element_type=F32)
    if old is not None:
        total = old[1] * rescale + total
        added = old[2] * rescale + added
    return top, total, added


def chunks_kernel(chunk_count, old_count, paired, *rest):
    queries, bias, rest = rest[:2], rest[2], rest[3:]
    chunks, rest = rest[:chunk_count], rest[chunk_count:]
    old, rest = rest[:old_count], rest[old_count:]
    if len(rest) == 6:
        passed, handed = rest[0], rest[4]
        handed[...] = passed[...]
        rest = rest[1:4] + rest[5:]
    running, keys = rest[:3], rest[3]
    rows = bias.shape[1]
    if paired:
        unpack(chunks[0], keys, 0, chunks[1])
        chunks = chunks[1:]
    for index, chunk in enumerate(chunks):
        if index or not paired:
            unpack(chunk, keys, index * rows)
    before = [state[...] for state in old] if old else None
    values = attend_block(queries, keys, bias[0], before)
    for state, value in zip(running, values):
        state[...] = value


def gathered_kernel(queries_own, queries_other, bias, gathered, *rest):
    queries = (queries_own, queries_other)
    running, keys = rest[:3], rest[3]
    blocks, rows, _ = bias.shape

    def fill(block):
        for index in range(BLOCK_CHUNKS):
            unpack(gathered.at[block * BLOCK_CHUNKS + index], keys, index * rows)

    first = lax.axis_index("ctx") // BLOCK_CHUNKS
    fill(first)
    values = attend_block(queries, keys, bias[first], None)
    for state, value in zip(running, values):
        state[...] = value

    def step(index, carry):
        block = index + jnp.where(index >= first, 1, 0)
        fill(block)
        new = attend_block(queries, keys, bias[block], [state[...] for state in running])
        for state, value in zip(running, new):
            state[...] = value
        return carry

    lax.fori_loop(0, blocks - 1, step, 0)


def finish_kernel(heads, chunk_count, *rest):
    queries, (top, total, context), rest = rest[:2], rest[2:5], rest[5:]
    bias, chunks = rest[:chunk_count][:1], rest[1 : 1 + chunk_count]
    rest = rest[len(bias) + len(chunks) :]
    value_own, proj_own, weights, out_ref, out_tiles, keys, out_sems = rest
    rows, width = out_ref.shape
    running = (top[...], total[...], context[...])
    if chunk_count:
        for index, chunk in enumerate(chunks):
            unpack(chunk, keys, index * rows)
        running = attend_block(queries, keys, bias[0][0], running)
    mixed = (running[2] * (1.0 / running[1])).astype(BF16)
    half = heads // 2
    depth = weights.shape[0]
    base = lax.axis_index("heads") * width
    parts = []
    for place in range(heads):
        group, head = divmod(place, half)
        if group == 0:
            value = value_own[:, head * DH : (head + 1) * DH]
        else:
            starts = [width + (block * half + head) * DH for block in range(DC // depth)]
            value = jnp.concatenate([weights[:, start : start + DH] for start in starts], axis=0)
        per_head = jnp.dot(
            mixed[place * rows : (place + 1) * rows], value, preferred_element_type=F32
        )
        parts.append(per_head.astype(BF16))
    heads_out = jnp.concatenate(parts, axis=1)
    tiles = out_sems.shape[0]
    tile = width // tiles
    sends = []
    for index in range(tiles):
        part = pl.ds(index * tile, tile)
        own = proj_own[:, pl.ds(pl.multiple_of(base + index * tile, 128), tile)]
        both = jnp.concatenate([own, weights[:, part]], axis=0)
        out = jnp.dot(heads_out, both, preferred_element_type=F32)
        out_tiles[:, part] = out.astype(BF16)
        sends.append(
            pltpu.make_async_copy(out_tiles.at[:, part], out_ref.at[:, part], out_sems.at[index])
        )
        sends[-1].start()
    for send in sends:
        send.wait()


def per_device(
    count, queries_nope, queries_rope, latent, key_rope, key_up, value_up, out_proj, span_order
):
    rows = latent.shape[0]
    depth, width = out_proj.shape[0], out_proj.shape[1] // 2
    heads = 2 * (key_up.shape[1] // DH)
    query_rows = heads * rows
    direct = count == 8
    small = pltpu.CompilerParams(vmem_limit_bytes=SMALL_VMEM)

    def in_hbm(*arrays):
        return [pltpu.with_memory_space_constraint(array, pltpu.HBM) for array in arrays]

    def other_core(array):
        return lax.ppermute(array, "heads", [(0, 1), (1, 0)])

    def partners(array, steps, cores=(0, 1)):
        pairs = [
            (2 * index + core, 2 * (index ^ steps[core]) + core)
            for index in range(count)
            for core in cores
        ]
        return lax.ppermute(array, ("ctx", "heads"), pairs)

    def attend(name, estimate, queries, bias, chunks, old=(), passed=(), paired=False):
        return pl.pallas_call(
            functools.partial(chunks_kernel, len(chunks), len(old), paired),
            out_shape=[jax.ShapeDtypeStruct((query_rows, size), F32) for size in (1, 1, DC)]
            + [jax.ShapeDtypeStruct(chunk.shape, BF16) for chunk in passed],
            in_specs=[vmem()] * (3 + len(chunks) + len(old) + len(passed)),
            out_specs=[vmem()] * (3 + len(passed)),
            scratch_shapes=[pltpu.VMEM((bias.shape[2], DC + DR), BF16)],
            compiler_params=small,
            cost_estimate=cost(estimate),
            name=name,
        )(*queries, bias, *chunks, *old, *passed)

    packed = pl.pallas_call(
        pack_kernel,
        out_shape=jax.ShapeDtypeStruct((2 * rows + rows // 4, DC // 2), BF16),
        in_specs=[hbm()] * 2,
        out_specs=vmem(),
        scratch_shapes=[
            pltpu.VMEM((DR, rows), BF16),
            pltpu.SemaphoreType.DMA((3,)),
        ],
        compiler_params=small,
        name="pack",
    )(*in_hbm(latent, key_rope.T))
    if direct:
        order = [
            [(0, 0), NEAR],
            [CORNER, NEAR[::-1], FAR, FAR[::-1], RELAYED],
            [RELAYED[::-1]],
        ]
        bias_shapes = [(1, rows, len(steps) * rows) for steps in order]
    else:
        order = None
        bias_shapes = [(count // BLOCK_CHUNKS, rows, BLOCK_CHUNKS * rows)]
    outs = pl.pallas_call(
        functools.partial(prepare_kernel, order),
        out_shape=[jax.ShapeDtypeStruct((query_rows // 2, DC + DR), BF16)]
        + [jax.ShapeDtypeStruct(shape, F32) for shape in bias_shapes]
        + [jax.ShapeDtypeStruct((depth, width + DC // depth * key_up.shape[1]), BF16)],
        in_specs=[hbm()] * 6 + [anywhere()],
        out_specs=[vmem()] * (len(bias_shapes) + 2),
        scratch_shapes=[
            pltpu.VMEM(queries_nope.shape, BF16),
            pltpu.VMEM(queries_rope.shape, BF16),
            pltpu.VMEM(key_up.shape, BF16),
            pltpu.SMEM(span_order.shape, jnp.int32),
            pltpu.VMEM(value_up.shape, BF16),
            pltpu.SemaphoreType.DMA((6,)),
        ],
        compiler_params=small,
        cost_estimate=cost(PREPARE_COST),
        name="prepare",
    )(*in_hbm(queries_nope, queries_rope, key_up, span_order, value_up, out_proj), packed)
    queries, biases = outs[0], outs[1:-1]
    weights_other = other_core(outs[-1])
    both = [queries, other_core(queries)]

    if direct:
        far = partners(packed, FAR)
        near = partners(packed, NEAR)
        corner = partners(packed, CORNER, cores=(1,))
        relayed = partners(far, (1, 1))
        gated = pl.pallas_call(
            gate_kernel,
            out_shape=jax.ShapeDtypeStruct(far.shape, BF16),
            in_specs=[vmem()],
            out_specs=vmem(),
            compiler_params=small,
            cost_estimate=cost(GATE_COST),
            name="gate",
        )(far)
        *running, far_after = attend(
            "first", FIRST_COST, both, biases[0], [packed, near], passed=[gated]
        )
        last = [other_core(relayed)]
        running = attend(
            "second",
            SECOND_COST,
            both,
            biases[1],
            [corner, other_core(corner), other_core(near), far, other_core(far_after), relayed],
            running,
            paired=True,
        )
    else:
        last = []
        running = pl.pallas_call(
            gathered_kernel,
            out_shape=[jax.ShapeDtypeStruct((query_rows, size), F32) for size in (1, 1, DC)],
            in_specs=[vmem()] * 4,
            out_specs=[vmem()] * 3,
            scratch_shapes=[pltpu.VMEM((BLOCK_CHUNKS * rows, DC + DR), BF16)],
            compiler_params=pltpu.CompilerParams(vmem_limit_bytes=LARGE_VMEM),
            name="gathered",
        )(*both, biases[0], lax.all_gather(packed, "ctx", axis=0))

    tiles = 7 if width % 896 == 0 else 1
    return pl.pallas_call(
        functools.partial(finish_kernel, heads, len(last)),
        out_shape=jax.ShapeDtypeStruct((rows, width), BF16),
        in_specs=[vmem()] * (5 + len(biases[2:]) + len(last) + 3),
        out_specs=anywhere(),
        scratch_shapes=[
            pltpu.VMEM((rows, width), BF16),
            pltpu.VMEM((rows, DC + DR), BF16),
            pltpu.SemaphoreType.DMA((tiles,)),
        ],
        compiler_params=small,
        name="finish",
    )(*both, *running, *biases[2:], *last, value_up, out_proj, weights_other)


def solution(mesh):
    in_specs = (
        P(("docs", "ctx"), "heads"),
        P(("docs", "ctx"), "heads"),
        P(("docs", "ctx"), None),
        P(("docs", "ctx"), None),
        P(None, "heads"),
        P(None, "heads"),
        P("heads", None),
        P("docs"),
    )
    out_specs = P(("docs", "ctx"), "heads")
    return jax.shard_map(
        functools.partial(per_device, mesh.shape["ctx"]),
        mesh=mesh,
        in_specs=in_specs,
        out_specs=out_specs,
        check_vma=False,
    )
```

```python
import functools
import math

import jax
import jax.numpy as jnp
from jax import lax
from jax.experimental import pallas as pl
from jax.experimental.pallas import tpu as pltpu
from jax.sharding import PartitionSpec as P

DC = 512
DH = 128
DR = 64
BF16 = jnp.bfloat16
F32 = jnp.float32
MASKED = -1e30
BLOCK_CHUNKS = 8
PREPARE_COST, GATE_COST, RELAY_COST, FIRST_COST, SECOND_COST = 0, 6, 0, 20, 1
SMALL_VMEM = 20 * 1024 * 1024
LARGE_VMEM = 56 * 1024 * 1024
FAR = (4, 6)
NEAR = (2, 1)
CORNER = (3, 3)
RELAYED = (5, 7)


def vmem():
    return pl.BlockSpec(memory_space=pltpu.VMEM)


def anywhere():
    return pl.BlockSpec(memory_space=pl.ANY)


def hbm():
    return pl.BlockSpec(memory_space=pltpu.HBM)


def cost(microseconds):
    return pl.CostEstimate(flops=int(microseconds * 1.1e9), bytes_accessed=0, transcendentals=0)


def pack_kernel(latent, key_rope_turned, out_ref, turned, sems):
    rows = latent.shape[0]
    group = rows // 6
    half = DC // 2
    fetches = [pltpu.make_async_copy(key_rope_turned, turned, sems.at[2])]
    for side in range(2):
        fetches.append(
            pltpu.make_async_copy(
                latent.at[:, pl.ds(side * half, half)],
                out_ref.at[pl.ds(side * rows, rows)],
                sems.at[side],
            )
        )
    for fetch in fetches:
        fetch.start()
    fetches[0].wait()
    rope = turned[...].astype(F32).T.astype(BF16)
    first = 0
    base = 2 * rows
    for size in (group, group // 2):
        parts = [rope[first + index * size : first + (index + 1) * size] for index in range(4)]
        out_ref[pl.ds(base, size), :] = jnp.concatenate(parts, axis=1)
        first += 4 * size
        base += size
    for fetch in fetches[1:]:
        fetch.wait()


def gate_kernel(chunk, *refs):
    refs[-1][...] = chunk[...]


def unpack(chunk, keys, base, other=None):
    chunk = chunk[...]
    if other is not None:
        chunk = jnp.where(lax.axis_index("heads") == 0, other[...], chunk)
    rows = 4 * chunk.shape[0] // 9
    group = rows // 6
    keys[pl.ds(base, rows), : DC // 2] = chunk[:rows]
    keys[pl.ds(base, rows), DC // 2 : DC] = chunk[rows : 2 * rows]
    place = 2 * rows
    for size in (group, group // 2):
        for index in range(4):
            part = chunk[place : place + size, index * DR : (index + 1) * DR]
            keys[pl.ds(base, size), DC:] = part
            base += size
        place += size


def prepare_kernel(order, *refs):
    sources, out_proj, rest = refs[:5], refs[5], refs[7:]
    outs, copied, sems = rest[:-6], rest[-6:-1], rest[-1]
    weights = outs[-1]
    depth, width = out_proj.shape[0], out_proj.shape[1] // 2
    fetches = [
        pltpu.make_async_copy(source, target, sems.at[index])
        for index, (source, target) in enumerate(zip(sources, copied))
    ]
    base = pl.multiple_of((1 - lax.axis_index("heads")) * width, 128)
    fetches.append(
        pltpu.make_async_copy(
            out_proj.at[:, pl.ds(base, width)], weights.at[:, pl.ds(0, width)], sems.at[5]
        )
    )
    for fetch in fetches:
        fetch.start()
    nope, rope, up, span_order, value_up = copied
    rows = nope.shape[0]
    heads = nope.shape[1] // DH
    span_rows = rows // 2
    for fetch in fetches[:3]:
        fetch.wait()
    own_index = lax.axis_index("ctx")
    core = lax.axis_index("heads")
    for head in range(heads):
        latent = lax.dot_general(
            nope[:, head * DH : (head + 1) * DH],
            up[:, head * DH : (head + 1) * DH],
            (((1,), (1,)), ((), ())),
            preferred_element_type=F32,
        )
        part = pl.ds(head * rows, rows)
        outs[0][part, :DC] = latent.astype(BF16)
        outs[0][part, DC:] = rope[:, head * DR : (head + 1) * DR]
    biases = outs[1:-1]
    fetches[3].wait()
    row = lax.broadcasted_iota(jnp.int32, (rows, 1), 0)
    query_pos = jnp.where(
        row < span_rows,
        span_order[2 * own_index] * span_rows + row,
        span_order[2 * own_index + 1] * span_rows + row - span_rows,
    )

    def bias_of(owners):
        column = lax.broadcasted_iota(jnp.int32, (1, len(owners) * rows), 1)
        key_pos = jnp.zeros(column.shape, jnp.int32)
        for index, owner in enumerate(owners):
            for side in range(2):
                start = index * rows + side * span_rows
                first = span_order[2 * owner + side] * span_rows
                key_pos = jnp.where(column >= start, first + column - start, key_pos)
        return jnp.where(key_pos <= query_pos, F32(0.0), F32(MASKED))

    if order is not None:
        for steps, bias_ref in zip(order, biases):
            bias_ref[0] = bias_of(
                [own_index ^ jnp.where(core == 0, step[0], step[1]) for step in steps]
            )
    else:
        bias_ref = biases[0]

        def step(block, carry):
            bias_ref[block] = bias_of([block * BLOCK_CHUNKS + index for index in range(BLOCK_CHUNKS)])
            return carry

        lax.fori_loop(0, bias_ref.shape[0], step, 0)

    fetches[4].wait()
    columns = value_up.shape[1]
    for block in range(DC // depth):
        part = value_up[block * depth : (block + 1) * depth, :]
        weights[:, width + block * columns : width + (block + 1) * columns] = part
    fetches[5].wait()


def attend_block(queries, keys, bias, old):
    copies = len(queries) * queries[0].shape[0] // bias.shape[0]
    scale = math.log2(math.e) / math.sqrt(DH + DR)
    heads = jnp.concatenate([part[...] for part in queries], axis=0)
    scores = lax.dot_general(
        heads, keys[...], (((1,), (1,)), ((), ())), preferred_element_type=F32
    )
    scores = scores + jnp.concatenate([bias] * copies, axis=0)
    top = jnp.max(scores, axis=-1, keepdims=True)
    if old is not None:
        top = jnp.maximum(old[0], top)
        rescale = jnp.exp2((old[0] - top) * scale)
    expo = jnp.exp2((scores - top) * scale)
    total = jnp.sum(expo, axis=-1, keepdims=True)
    added = jnp.dot(expo.astype(BF16), keys[:, :DC], preferred_element_type=F32)
    if old is not None:
        total = old[1] * rescale + total
        added = old[2] * rescale + added
    return top, total, added


def chunks_kernel(chunk_count, old_count, *rest):
    queries, bias, rest = rest[:2], rest[2], rest[3:]
    chunks, rest = rest[:chunk_count], rest[chunk_count:]
    old, rest = rest[:old_count], rest[old_count:]
    if len(rest) == 6:
        passed, handed = rest[0], rest[4]
        handed[...] = passed[...]
        rest = rest[1:4] + rest[5:]
    running, keys = rest[:3], rest[3]
    rows = bias.shape[1]
    for index, chunk in enumerate(chunks):
        unpack(chunk, keys, index * rows)
    before = [state[...] for state in old] if old else None
    values = attend_block(queries, keys, bias[0], before)
    for state, value in zip(running, values):
        state[...] = value


def gathered_kernel(queries_own, queries_other, bias, gathered, *rest):
    queries = (queries_own, queries_other)
    running, keys = rest[:3], rest[3]
    blocks, rows, _ = bias.shape

    def fill(block):
        for index in range(BLOCK_CHUNKS):
            unpack(gathered.at[block * BLOCK_CHUNKS + index], keys, index * rows)

    first = lax.axis_index("ctx") // BLOCK_CHUNKS
    fill(first)
    values = attend_block(queries, keys, bias[first], None)
    for state, value in zip(running, values):
        state[...] = value

    def step(index, carry):
        block = index + jnp.where(index >= first, 1, 0)
        fill(block)
        new = attend_block(queries, keys, bias[block], [state[...] for state in running])
        for state, value in zip(running, new):
            state[...] = value
        return carry

    lax.fori_loop(0, blocks - 1, step, 0)


def finish_kernel(heads, chunk_count, *rest):
    queries, (top, total, context), rest = rest[:2], rest[2:5], rest[5:]
    bias, chunks = rest[:chunk_count][:1], rest[1 : 1 + chunk_count]
    rest = rest[len(bias) + len(chunks) :]
    value_own, proj_own, weights, out_ref, out_tiles, keys, out_sems = rest
    rows, width = out_ref.shape
    running = (top[...], total[...], context[...])
    if chunk_count:
        unpack(chunks[0], keys, 0, chunks[1])
        for index, chunk in enumerate(chunks[2:]):
            unpack(chunk, keys, (1 + index) * rows)
        running = attend_block(queries, keys, bias[0][0], running)
    mixed = (running[2] * (1.0 / running[1])).astype(BF16)
    half = heads // 2
    depth = weights.shape[0]
    base = lax.axis_index("heads") * width
    parts = []
    for place in range(heads):
        group, head = divmod(place, half)
        if group == 0:
            value = value_own[:, head * DH : (head + 1) * DH]
        else:
            starts = [width + (block * half + head) * DH for block in range(DC // depth)]
            value = jnp.concatenate([weights[:, start : start + DH] for start in starts], axis=0)
        per_head = jnp.dot(
            mixed[place * rows : (place + 1) * rows], value, preferred_element_type=F32
        )
        parts.append(per_head.astype(BF16))
    heads_out = jnp.concatenate(parts, axis=1)
    tiles = out_sems.shape[0]
    tile = width // tiles
    sends = []
    for index in range(tiles):
        part = pl.ds(index * tile, tile)
        own = proj_own[:, pl.ds(pl.multiple_of(base + index * tile, 128), tile)]
        both = jnp.concatenate([own, weights[:, part]], axis=0)
        out = jnp.dot(heads_out, both, preferred_element_type=F32)
        out_tiles[:, part] = out.astype(BF16)
        sends.append(
            pltpu.make_async_copy(out_tiles.at[:, part], out_ref.at[:, part], out_sems.at[index])
        )
        sends[-1].start()
    for send in sends:
        send.wait()


def per_device(
    count, queries_nope, queries_rope, latent, key_rope, key_up, value_up, out_proj, span_order
):
    rows = latent.shape[0]
    depth, width = out_proj.shape[0], out_proj.shape[1] // 2
    heads = 2 * (key_up.shape[1] // DH)
    query_rows = heads * rows
    direct = count == 8
    small = pltpu.CompilerParams(vmem_limit_bytes=SMALL_VMEM)

    def in_hbm(*arrays):
        return [pltpu.with_memory_space_constraint(array, pltpu.HBM) for array in arrays]

    def other_core(array):
        return lax.ppermute(array, "heads", [(0, 1), (1, 0)])

    def partners(array, steps, cores=(0, 1)):
        pairs = [
            (2 * index + core, 2 * (index ^ steps[core]) + core)
            for index in range(count)
            for core in cores
        ]
        return lax.ppermute(array, ("ctx", "heads"), pairs)

    def gate(name, estimate, *chunks):
        return pl.pallas_call(
            gate_kernel,
            out_shape=jax.ShapeDtypeStruct(chunks[0].shape, BF16),
            in_specs=[vmem()] * len(chunks),
            out_specs=vmem(),
            compiler_params=small,
            cost_estimate=cost(estimate),
            name=name,
        )(*chunks)

    def attend(name, estimate, queries, bias, chunks, old=(), passed=()):
        return pl.pallas_call(
            functools.partial(chunks_kernel, len(chunks), len(old)),
            out_shape=[jax.ShapeDtypeStruct((query_rows, size), F32) for size in (1, 1, DC)]
            + [jax.ShapeDtypeStruct(chunk.shape, BF16) for chunk in passed],
            in_specs=[vmem()] * (3 + len(chunks) + len(old) + len(passed)),
            out_specs=[vmem()] * (3 + len(passed)),
            scratch_shapes=[pltpu.VMEM((bias.shape[2], DC + DR), BF16)],
            compiler_params=small,
            cost_estimate=cost(estimate),
            name=name,
        )(*queries, bias, *chunks, *old, *passed)

    packed = pl.pallas_call(
        pack_kernel,
        out_shape=jax.ShapeDtypeStruct((2 * rows + rows // 4, DC // 2), BF16),
        in_specs=[hbm()] * 2,
        out_specs=vmem(),
        scratch_shapes=[
            pltpu.VMEM((DR, rows), BF16),
            pltpu.SemaphoreType.DMA((3,)),
        ],
        compiler_params=small,
        name="pack",
    )(*in_hbm(latent, key_rope.T))
    if direct:
        order = [
            [(0, 0), NEAR],
            [NEAR[::-1], FAR, FAR[::-1], RELAYED],
            [CORNER, RELAYED[::-1]],
        ]
        bias_shapes = [(1, rows, len(steps) * rows) for steps in order]
    else:
        order = None
        bias_shapes = [(count // BLOCK_CHUNKS, rows, BLOCK_CHUNKS * rows)]
    outs = pl.pallas_call(
        functools.partial(prepare_kernel, order),
        out_shape=[jax.ShapeDtypeStruct((query_rows // 2, DC + DR), BF16)]
        + [jax.ShapeDtypeStruct(shape, F32) for shape in bias_shapes]
        + [jax.ShapeDtypeStruct((depth, width + DC // depth * key_up.shape[1]), BF16)],
        in_specs=[hbm()] * 6 + [anywhere()],
        out_specs=[vmem()] * (len(bias_shapes) + 2),
        scratch_shapes=[
            pltpu.VMEM(queries_nope.shape, BF16),
            pltpu.VMEM(queries_rope.shape, BF16),
            pltpu.VMEM(key_up.shape, BF16),
            pltpu.SMEM(span_order.shape, jnp.int32),
            pltpu.VMEM(value_up.shape, BF16),
            pltpu.SemaphoreType.DMA((6,)),
        ],
        compiler_params=small,
        cost_estimate=cost(PREPARE_COST),
        name="prepare",
    )(*in_hbm(queries_nope, queries_rope, key_up, span_order, value_up, out_proj), packed)
    queries, biases = outs[0], outs[1:-1]
    weights_other = other_core(outs[-1])
    both = [queries, other_core(queries)]

    if direct:
        far = partners(packed, FAR)
        near = partners(packed, NEAR)
        relayed = gate("relay", RELAY_COST, partners(far, (1, 1)))
        corner = partners(near, (2, 2), cores=(1,))
        gated = gate("gate", GATE_COST, far)
        *running, far_after = attend(
            "first", FIRST_COST, both, biases[0], [packed, near], passed=[gated]
        )
        last = [corner, other_core(corner), other_core(relayed)]
        running = attend(
            "second",
            SECOND_COST,
            both,
            biases[1],
            [other_core(near), far, other_core(far_after), relayed],
            running,
        )
    else:
        last = []
        running = pl.pallas_call(
            gathered_kernel,
            out_shape=[jax.ShapeDtypeStruct((query_rows, size), F32) for size in (1, 1, DC)],
            in_specs=[vmem()] * 4,
            out_specs=[vmem()] * 3,
            scratch_shapes=[pltpu.VMEM((BLOCK_CHUNKS * rows, DC + DR), BF16)],
            compiler_params=pltpu.CompilerParams(vmem_limit_bytes=LARGE_VMEM),
            name="gathered",
        )(*both, biases[0], lax.all_gather(packed, "ctx", axis=0))

    tiles = 7 if width % 896 == 0 else 1
    return pl.pallas_call(
        functools.partial(finish_kernel, heads, len(last)),
        out_shape=jax.ShapeDtypeStruct((rows, width), BF16),
        in_specs=[vmem()] * (5 + len(biases[2:]) + len(last) + 3),
        out_specs=anywhere(),
        scratch_shapes=[
            pltpu.VMEM((rows, width), BF16),
            pltpu.VMEM((max(1, len(last) - 1) * rows, DC + DR), BF16),
            pltpu.SemaphoreType.DMA((tiles,)),
        ],
        compiler_params=small,
        name="finish",
    )(*both, *running, *biases[2:], *last, value_up, out_proj, weights_other)


def solution(mesh):
    in_specs = (
        P(("docs", "ctx"), "heads"),
        P(("docs", "ctx"), "heads"),
        P(("docs", "ctx"), None),
        P(("docs", "ctx"), None),
        P(None, "heads"),
        P(None, "heads"),
        P("heads", None),
        P("docs"),
    )
    out_specs = P(("docs", "ctx"), "heads")
    return jax.shard_map(
        functools.partial(per_device, mesh.shape["ctx"]),
        mesh=mesh,
        in_specs=in_specs,
        out_specs=out_specs,
        check_vma=False,
    )
```

```python
import functools
import math

import jax
import jax.numpy as jnp
from jax import lax
from jax.experimental import pallas as pl
from jax.experimental.pallas import tpu as pltpu
from jax.sharding import PartitionSpec as P

DC = 512
DH = 128
DR = 64
BF16 = jnp.bfloat16
F32 = jnp.float32
MASKED = -1e30
BLOCK_CHUNKS = 8
PREPARE_COST, GATE_COST, FIRST_COST, SECOND_COST = 0, 3, 20, 1
SMALL_VMEM = 20 * 1024 * 1024
LARGE_VMEM = 56 * 1024 * 1024
FAR = (4, 6)
NEAR = (1, 2)
CORNER = (3, 3)
RELAYED = (5, 7)


def vmem():
    return pl.BlockSpec(memory_space=pltpu.VMEM)


def anywhere():
    return pl.BlockSpec(memory_space=pl.ANY)


def hbm():
    return pl.BlockSpec(memory_space=pltpu.HBM)


def cost(microseconds):
    return pl.CostEstimate(flops=int(microseconds * 1.1e9), bytes_accessed=0, transcendentals=0)


def pack_kernel(latent, key_rope_turned, out_ref, turned, sems):
    rows = latent.shape[0]
    group = rows // 6
    half = DC // 2
    fetches = [pltpu.make_async_copy(key_rope_turned, turned, sems.at[2])]
    for side in range(2):
        fetches.append(
            pltpu.make_async_copy(
                latent.at[:, pl.ds(side * half, half)],
                out_ref.at[pl.ds(side * rows, rows)],
                sems.at[side],
            )
        )
    for fetch in fetches:
        fetch.start()
    fetches[0].wait()
    rope = turned[...].astype(F32).T.astype(BF16)
    first = 0
    base = 2 * rows
    for size in (group, group // 2):
        parts = [rope[first + index * size : first + (index + 1) * size] for index in range(4)]
        out_ref[pl.ds(base, size), :] = jnp.concatenate(parts, axis=1)
        first += 4 * size
        base += size
    for fetch in fetches[1:]:
        fetch.wait()


def gate_kernel(chunk, out_ref):
    out_ref[...] = chunk[...]


def unpack(chunk, keys, base, other=None):
    chunk = chunk[...]
    if other is not None:
        chunk = jnp.where(lax.axis_index("heads") == 0, other[...], chunk)
    rows = 4 * chunk.shape[0] // 9
    group = rows // 6
    keys[pl.ds(base, rows), : DC // 2] = chunk[:rows]
    keys[pl.ds(base, rows), DC // 2 : DC] = chunk[rows : 2 * rows]
    place = 2 * rows
    for size in (group, group // 2):
        for index in range(4):
            part = chunk[place : place + size, index * DR : (index + 1) * DR]
            keys[pl.ds(base, size), DC:] = part
            base += size
        place += size


def prepare_kernel(order, *refs):
    sources, out_proj, rest = refs[:5], refs[5], refs[7:]
    outs, copied, sems = rest[:-6], rest[-6:-1], rest[-1]
    weights = outs[-1]
    depth, width = out_proj.shape[0], out_proj.shape[1] // 2
    fetches = [
        pltpu.make_async_copy(source, target, sems.at[index])
        for index, (source, target) in enumerate(zip(sources, copied))
    ]
    base = pl.multiple_of((1 - lax.axis_index("heads")) * width, 128)
    fetches.append(
        pltpu.make_async_copy(
            out_proj.at[:, pl.ds(base, width)], weights.at[:, pl.ds(0, width)], sems.at[5]
        )
    )
    for fetch in fetches:
        fetch.start()
    nope, rope, up, span_order, value_up = copied
    rows = nope.shape[0]
    heads = nope.shape[1] // DH
    span_rows = rows // 2
    for fetch in fetches[:3]:
        fetch.wait()
    own_index = lax.axis_index("ctx")
    core = lax.axis_index("heads")
    for head in range(heads):
        latent = lax.dot_general(
            nope[:, head * DH : (head + 1) * DH],
            up[:, head * DH : (head + 1) * DH],
            (((1,), (1,)), ((), ())),
            preferred_element_type=F32,
        )
        part = pl.ds(head * rows, rows)
        outs[0][part, :DC] = latent.astype(BF16)
        outs[0][part, DC:] = rope[:, head * DR : (head + 1) * DR]
    biases = outs[1:-1]
    fetches[3].wait()
    row = lax.broadcasted_iota(jnp.int32, (rows, 1), 0)
    query_pos = jnp.where(
        row < span_rows,
        span_order[2 * own_index] * span_rows + row,
        span_order[2 * own_index + 1] * span_rows + row - span_rows,
    )

    def bias_of(owners):
        column = lax.broadcasted_iota(jnp.int32, (1, len(owners) * rows), 1)
        key_pos = jnp.zeros(column.shape, jnp.int32)
        for index, owner in enumerate(owners):
            for side in range(2):
                start = index * rows + side * span_rows
                first = span_order[2 * owner + side] * span_rows
                key_pos = jnp.where(column >= start, first + column - start, key_pos)
        return jnp.where(key_pos <= query_pos, F32(0.0), F32(MASKED))

    if order is not None:
        for steps, bias_ref in zip(order, biases):
            bias_ref[0] = bias_of(
                [own_index ^ jnp.where(core == 0, step[0], step[1]) for step in steps]
            )
    else:
        bias_ref = biases[0]

        def step(block, carry):
            bias_ref[block] = bias_of([block * BLOCK_CHUNKS + index for index in range(BLOCK_CHUNKS)])
            return carry

        lax.fori_loop(0, bias_ref.shape[0], step, 0)

    fetches[4].wait()
    columns = value_up.shape[1]
    for block in range(DC // depth):
        part = value_up[block * depth : (block + 1) * depth, :]
        weights[:, width + block * columns : width + (block + 1) * columns] = part
    fetches[5].wait()


def attend_block(queries, keys, bias, old):
    copies = len(queries) * queries[0].shape[0] // bias.shape[0]
    scale = math.log2(math.e) / math.sqrt(DH + DR)
    heads = jnp.concatenate([part[...] for part in queries], axis=0)
    scores = lax.dot_general(
        heads, keys[...], (((1,), (1,)), ((), ())), preferred_element_type=F32
    )
    scores = scores + jnp.concatenate([bias] * copies, axis=0)
    top = jnp.max(scores, axis=-1, keepdims=True)
    if old is not None:
        top = jnp.maximum(old[0], top)
        rescale = jnp.exp2((old[0] - top) * scale)
    expo = jnp.exp2((scores - top) * scale)
    total = jnp.sum(expo, axis=-1, keepdims=True)
    added = jnp.dot(expo.astype(BF16), keys[:, :DC], preferred_element_type=F32)
    if old is not None:
        total = old[1] * rescale + total
        added = old[2] * rescale + added
    return top, total, added


def chunks_kernel(chunk_count, old_count, paired, *rest):
    queries, bias, rest = rest[:2], rest[2], rest[3:]
    chunks, rest = rest[:chunk_count], rest[chunk_count:]
    old, rest = rest[:old_count], rest[old_count:]
    if len(rest) == 6:
        passed, handed = rest[0], rest[4]
        handed[...] = passed[...]
        rest = rest[1:4] + rest[5:]
    running, keys = rest[:3], rest[3]
    rows = bias.shape[1]
    if paired:
        unpack(chunks[0], keys, 0, chunks[1])
        chunks = chunks[1:]
    for index, chunk in enumerate(chunks):
        if index or not paired:
            unpack(chunk, keys, index * rows)
    before = [state[...] for state in old] if old else None
    values = attend_block(queries, keys, bias[0], before)
    for state, value in zip(running, values):
        state[...] = value


def gathered_kernel(queries_own, queries_other, bias, gathered, *rest):
    queries = (queries_own, queries_other)
    running, keys = rest[:3], rest[3]
    blocks, rows, _ = bias.shape

    def fill(block):
        for index in range(BLOCK_CHUNKS):
            unpack(gathered.at[block * BLOCK_CHUNKS + index], keys, index * rows)

    first = lax.axis_index("ctx") // BLOCK_CHUNKS
    fill(first)
    values = attend_block(queries, keys, bias[first], None)
    for state, value in zip(running, values):
        state[...] = value

    def step(index, carry):
        block = index + jnp.where(index >= first, 1, 0)
        fill(block)
        new = attend_block(queries, keys, bias[block], [state[...] for state in running])
        for state, value in zip(running, new):
            state[...] = value
        return carry

    lax.fori_loop(0, blocks - 1, step, 0)


def finish_kernel(heads, chunk_count, *rest):
    queries, (top, total, context), rest = rest[:2], rest[2:5], rest[5:]
    bias, chunks = rest[:chunk_count][:1], rest[1 : 1 + chunk_count]
    rest = rest[len(bias) + len(chunks) :]
    value_own, proj_own, weights, out_ref, out_tiles, keys, out_sems = rest
    rows, width = out_ref.shape
    running = (top[...], total[...], context[...])
    if chunk_count:
        for index, chunk in enumerate(chunks):
            unpack(chunk, keys, index * rows)
        running = attend_block(queries, keys, bias[0][0], running)
    mixed = (running[2] * (1.0 / running[1])).astype(BF16)
    half = heads // 2
    depth = weights.shape[0]
    base = lax.axis_index("heads") * width
    parts = []
    for place in range(heads):
        group, head = divmod(place, half)
        if group == 0:
            value = value_own[:, head * DH : (head + 1) * DH]
        else:
            starts = [width + (block * half + head) * DH for block in range(DC // depth)]
            value = jnp.concatenate([weights[:, start : start + DH] for start in starts], axis=0)
        per_head = jnp.dot(
            mixed[place * rows : (place + 1) * rows], value, preferred_element_type=F32
        )
        parts.append(per_head.astype(BF16))
    heads_out = jnp.concatenate(parts, axis=1)
    tiles = out_sems.shape[0]
    tile = width // tiles
    sends = []
    for index in range(tiles):
        part = pl.ds(index * tile, tile)
        own = proj_own[:, pl.ds(pl.multiple_of(base + index * tile, 128), tile)]
        both = jnp.concatenate([own, weights[:, part]], axis=0)
        out = jnp.dot(heads_out, both, preferred_element_type=F32)
        out_tiles[:, part] = out.astype(BF16)
        sends.append(
            pltpu.make_async_copy(out_tiles.at[:, part], out_ref.at[:, part], out_sems.at[index])
        )
        sends[-1].start()
    for send in sends:
        send.wait()


def per_device(
    count, queries_nope, queries_rope, latent, key_rope, key_up, value_up, out_proj, span_order
):
    rows = latent.shape[0]
    depth, width = out_proj.shape[0], out_proj.shape[1] // 2
    heads = 2 * (key_up.shape[1] // DH)
    query_rows = heads * rows
    direct = count == 8
    small = pltpu.CompilerParams(vmem_limit_bytes=SMALL_VMEM)

    def in_hbm(*arrays):
        return [pltpu.with_memory_space_constraint(array, pltpu.HBM) for array in arrays]

    def other_core(array):
        return lax.ppermute(array, "heads", [(0, 1), (1, 0)])

    def partners(array, steps, cores=(0, 1)):
        pairs = [
            (2 * index + core, 2 * (index ^ steps[core]) + core)
            for index in range(count)
            for core in cores
        ]
        return lax.ppermute(array, ("ctx", "heads"), pairs)

    def attend(name, estimate, queries, bias, chunks, old=(), passed=(), paired=False):
        return pl.pallas_call(
            functools.partial(chunks_kernel, len(chunks), len(old), paired),
            out_shape=[jax.ShapeDtypeStruct((query_rows, size), F32) for size in (1, 1, DC)]
            + [jax.ShapeDtypeStruct(chunk.shape, BF16) for chunk in passed],
            in_specs=[vmem()] * (3 + len(chunks) + len(old) + len(passed)),
            out_specs=[vmem()] * (3 + len(passed)),
            scratch_shapes=[pltpu.VMEM((bias.shape[2], DC + DR), BF16)],
            compiler_params=small,
            cost_estimate=cost(estimate),
            name=name,
        )(*queries, bias, *chunks, *old, *passed)

    packed = pl.pallas_call(
        pack_kernel,
        out_shape=jax.ShapeDtypeStruct((2 * rows + rows // 4, DC // 2), BF16),
        in_specs=[hbm()] * 2,
        out_specs=vmem(),
        scratch_shapes=[
            pltpu.VMEM((DR, rows), BF16),
            pltpu.SemaphoreType.DMA((3,)),
        ],
        compiler_params=small,
        name="pack",
    )(*in_hbm(latent, key_rope.T))
    if direct:
        order = [
            [(0, 0), NEAR],
            [CORNER, NEAR[::-1], FAR, FAR[::-1], RELAYED],
            [RELAYED[::-1]],
        ]
        bias_shapes = [(1, rows, len(steps) * rows) for steps in order]
    else:
        order = None
        bias_shapes = [(count // BLOCK_CHUNKS, rows, BLOCK_CHUNKS * rows)]
    outs = pl.pallas_call(
        functools.partial(prepare_kernel, order),
        out_shape=[jax.ShapeDtypeStruct((query_rows // 2, DC + DR), BF16)]
        + [jax.ShapeDtypeStruct(shape, F32) for shape in bias_shapes]
        + [jax.ShapeDtypeStruct((depth, width + DC // depth * key_up.shape[1]), BF16)],
        in_specs=[hbm()] * 6 + [anywhere()],
        out_specs=[vmem()] * (len(bias_shapes) + 2),
        scratch_shapes=[
            pltpu.VMEM(queries_nope.shape, BF16),
            pltpu.VMEM(queries_rope.shape, BF16),
            pltpu.VMEM(key_up.shape, BF16),
            pltpu.SMEM(span_order.shape, jnp.int32),
            pltpu.VMEM(value_up.shape, BF16),
            pltpu.SemaphoreType.DMA((6,)),
        ],
        compiler_params=small,
        cost_estimate=cost(PREPARE_COST),
        name="prepare",
    )(*in_hbm(queries_nope, queries_rope, key_up, span_order, value_up, out_proj), packed)
    queries, biases = outs[0], outs[1:-1]
    weights_other = other_core(outs[-1])
    both = [queries, other_core(queries)]

    if direct:
        far = partners(packed, FAR)
        near = partners(packed, NEAR)
        corner = partners(packed, CORNER, cores=(1,))
        relayed = partners(far, (1, 1))
        gated = pl.pallas_call(
            gate_kernel,
            out_shape=jax.ShapeDtypeStruct(far.shape, BF16),
            in_specs=[vmem()],
            out_specs=vmem(),
            compiler_params=small,
            cost_estimate=cost(GATE_COST),
            name="gate",
        )(far)
        *running, far_after = attend(
            "first", FIRST_COST, both, biases[0], [packed, near], passed=[gated]
        )
        last = [other_core(relayed)]
        running = attend(
            "second",
            SECOND_COST,
            both,
            biases[1],
            [corner, other_core(corner), other_core(near), far, other_core(far_after), relayed],
            running,
            paired=True,
        )
    else:
        last = []
        running = pl.pallas_call(
            gathered_kernel,
            out_shape=[jax.ShapeDtypeStruct((query_rows, size), F32) for size in (1, 1, DC)],
            in_specs=[vmem()] * 4,
            out_specs=[vmem()] * 3,
            scratch_shapes=[pltpu.VMEM((BLOCK_CHUNKS * rows, DC + DR), BF16)],
            compiler_params=pltpu.CompilerParams(vmem_limit_bytes=LARGE_VMEM),
            name="gathered",
        )(*both, biases[0], lax.all_gather(packed, "ctx", axis=0))

    tiles = 7 if width % 896 == 0 else 1
    return pl.pallas_call(
        functools.partial(finish_kernel, heads, len(last)),
        out_shape=jax.ShapeDtypeStruct((rows, width), BF16),
        in_specs=[vmem()] * (5 + len(biases[2:]) + len(last) + 3),
        out_specs=anywhere(),
        scratch_shapes=[
            pltpu.VMEM((rows, width), BF16),
            pltpu.VMEM((rows, DC + DR), BF16),
            pltpu.SemaphoreType.DMA((tiles,)),
        ],
        compiler_params=small,
        name="finish",
    )(*both, *running, *biases[2:], *last, value_up, out_proj, weights_other)


def solution(mesh):
    in_specs = (
        P(("docs", "ctx"), "heads"),
        P(("docs", "ctx"), "heads"),
        P(("docs", "ctx"), None),
        P(("docs", "ctx"), None),
        P(None, "heads"),
        P(None, "heads"),
        P("heads", None),
        P("docs"),
    )
    out_specs = P(("docs", "ctx"), "heads")
    return jax.shard_map(
        functools.partial(per_device, mesh.shape["ctx"]),
        mesh=mesh,
        in_specs=in_specs,
        out_specs=out_specs,
        check_vma=False,
    )
```

```python
import functools
import math

import jax
import jax.numpy as jnp
from jax import lax
from jax.experimental import pallas as pl
from jax.experimental.pallas import tpu as pltpu
from jax.sharding import PartitionSpec as P

DC = 512
DH = 128
DR = 64
BF16 = jnp.bfloat16
F32 = jnp.float32
MASKED = -1e30
BLOCK_CHUNKS = 8
PREPARE_COST, SORT_COST, GATE_COST, FIRST_COST, SECOND_COST = 0, 3, 0, 20, 1
SMALL_VMEM = 20 * 1024 * 1024
LARGE_VMEM = 56 * 1024 * 1024
FAR = (4, 6)
NEAR = (2, 1)
CORNER = (3, 3)
RELAYED = (5, 7)


def vmem():
    return pl.BlockSpec(memory_space=pltpu.VMEM)


def anywhere():
    return pl.BlockSpec(memory_space=pl.ANY)


def hbm():
    return pl.BlockSpec(memory_space=pltpu.HBM)


def cost(microseconds):
    return pl.CostEstimate(flops=int(microseconds * 1.1e9), bytes_accessed=0, transcendentals=0)


def pack_kernel(latent, key_rope_turned, out_ref, turned, sems):
    rows = latent.shape[0]
    group = rows // 6
    half = DC // 2
    fetches = [pltpu.make_async_copy(key_rope_turned, turned, sems.at[2])]
    for side in range(2):
        fetches.append(
            pltpu.make_async_copy(
                latent.at[:, pl.ds(side * half, half)],
                out_ref.at[pl.ds(side * rows, rows)],
                sems.at[side],
            )
        )
    for fetch in fetches:
        fetch.start()
    fetches[0].wait()
    rope = turned[...].astype(F32).T.astype(BF16)
    first = 0
    base = 2 * rows
    for size in (group, group // 2):
        parts = [rope[first + index * size : first + (index + 1) * size] for index in range(4)]
        out_ref[pl.ds(base, size), :] = jnp.concatenate(parts, axis=1)
        first += 4 * size
        base += size
    for fetch in fetches[1:]:
        fetch.wait()


def sort_kernel(second, first, far_ref, near_ref):
    far_first = lax.axis_index("heads") == 0
    far_ref[...] = jnp.where(far_first, first[...], second[...])
    near_ref[...] = jnp.where(far_first, second[...], first[...])


def gate_kernel(chunk, out_ref):
    out_ref[...] = chunk[...]


def unpack(chunk, keys, base, other=None):
    chunk = chunk[...]
    if other is not None:
        chunk = jnp.where(lax.axis_index("heads") == 0, other[...], chunk)
    rows = 4 * chunk.shape[0] // 9
    group = rows // 6
    keys[pl.ds(base, rows), : DC // 2] = chunk[:rows]
    keys[pl.ds(base, rows), DC // 2 : DC] = chunk[rows : 2 * rows]
    place = 2 * rows
    for size in (group, group // 2):
        for index in range(4):
            part = chunk[place : place + size, index * DR : (index + 1) * DR]
            keys[pl.ds(base, size), DC:] = part
            base += size
        place += size


def prepare_kernel(order, *refs):
    sources, out_proj, rest = refs[:5], refs[5], refs[7:]
    outs, copied, sems = rest[:-6], rest[-6:-1], rest[-1]
    weights = outs[-1]
    depth, width = out_proj.shape[0], out_proj.shape[1] // 2
    fetches = [
        pltpu.make_async_copy(source, target, sems.at[index])
        for index, (source, target) in enumerate(zip(sources, copied))
    ]
    base = pl.multiple_of((1 - lax.axis_index("heads")) * width, 128)
    fetches.append(
        pltpu.make_async_copy(
            out_proj.at[:, pl.ds(base, width)], weights.at[:, pl.ds(0, width)], sems.at[5]
        )
    )
    for fetch in fetches:
        fetch.start()
    nope, rope, up, span_order, value_up = copied
    rows = nope.shape[0]
    heads = nope.shape[1] // DH
    span_rows = rows // 2
    for fetch in fetches[:3]:
        fetch.wait()
    own_index = lax.axis_index("ctx")
    core = lax.axis_index("heads")
    for head in range(heads):
        latent = lax.dot_general(
            nope[:, head * DH : (head + 1) * DH],
            up[:, head * DH : (head + 1) * DH],
            (((1,), (1,)), ((), ())),
            preferred_element_type=F32,
        )
        part = pl.ds(head * rows, rows)
        outs[0][part, :DC] = latent.astype(BF16)
        outs[0][part, DC:] = rope[:, head * DR : (head + 1) * DR]
    biases = outs[1:-1]
    fetches[3].wait()
    row = lax.broadcasted_iota(jnp.int32, (rows, 1), 0)
    query_pos = jnp.where(
        row < span_rows,
        span_order[2 * own_index] * span_rows + row,
        span_order[2 * own_index + 1] * span_rows + row - span_rows,
    )

    def bias_of(owners):
        column = lax.broadcasted_iota(jnp.int32, (1, len(owners) * rows), 1)
        key_pos = jnp.zeros(column.shape, jnp.int32)
        for index, owner in enumerate(owners):
            for side in range(2):
                start = index * rows + side * span_rows
                first = span_order[2 * owner + side] * span_rows
                key_pos = jnp.where(column >= start, first + column - start, key_pos)
        return jnp.where(key_pos <= query_pos, F32(0.0), F32(MASKED))

    if order is not None:
        for steps, bias_ref in zip(order, biases):
            bias_ref[0] = bias_of(
                [own_index ^ jnp.where(core == 0, step[0], step[1]) for step in steps]
            )
    else:
        bias_ref = biases[0]

        def step(block, carry):
            bias_ref[block] = bias_of([block * BLOCK_CHUNKS + index for index in range(BLOCK_CHUNKS)])
            return carry

        lax.fori_loop(0, bias_ref.shape[0], step, 0)

    fetches[4].wait()
    columns = value_up.shape[1]
    for block in range(DC // depth):
        part = value_up[block * depth : (block + 1) * depth, :]
        weights[:, width + block * columns : width + (block + 1) * columns] = part
    fetches[5].wait()


def attend_block(queries, keys, bias, old):
    copies = len(queries) * queries[0].shape[0] // bias.shape[0]
    scale = math.log2(math.e) / math.sqrt(DH + DR)
    heads = jnp.concatenate([part[...] for part in queries], axis=0)
    scores = lax.dot_general(
        heads, keys[...], (((1,), (1,)), ((), ())), preferred_element_type=F32
    )
    scores = scores + jnp.concatenate([bias] * copies, axis=0)
    top = jnp.max(scores, axis=-1, keepdims=True)
    if old is not None:
        top = jnp.maximum(old[0], top)
        rescale = jnp.exp2((old[0] - top) * scale)
    expo = jnp.exp2((scores - top) * scale)
    total = jnp.sum(expo, axis=-1, keepdims=True)
    added = jnp.dot(expo.astype(BF16), keys[:, :DC], preferred_element_type=F32)
    if old is not None:
        total = old[1] * rescale + total
        added = old[2] * rescale + added
    return top, total, added


def chunks_kernel(chunk_count, old_count, paired, *rest):
    queries, bias, rest = rest[:2], rest[2], rest[3:]
    chunks, rest = rest[:chunk_count], rest[chunk_count:]
    old, rest = rest[:old_count], rest[old_count:]
    if len(rest) == 6:
        passed, handed = rest[0], rest[4]
        handed[...] = passed[...]
        rest = rest[1:4] + rest[5:]
    running, keys = rest[:3], rest[3]
    rows = bias.shape[1]
    if paired:
        unpack(chunks[0], keys, 0, chunks[1])
        chunks = chunks[1:]
    for index, chunk in enumerate(chunks):
        if index or not paired:
            unpack(chunk, keys, index * rows)
    before = [state[...] for state in old] if old else None
    values = attend_block(queries, keys, bias[0], before)
    for state, value in zip(running, values):
        state[...] = value


def gathered_kernel(queries_own, queries_other, bias, gathered, *rest):
    queries = (queries_own, queries_other)
    running, keys = rest[:3], rest[3]
    blocks, rows, _ = bias.shape

    def fill(block):
        for index in range(BLOCK_CHUNKS):
            unpack(gathered.at[block * BLOCK_CHUNKS + index], keys, index * rows)

    first = lax.axis_index("ctx") // BLOCK_CHUNKS
    fill(first)
    values = attend_block(queries, keys, bias[first], None)
    for state, value in zip(running, values):
        state[...] = value

    def step(index, carry):
        block = index + jnp.where(index >= first, 1, 0)
        fill(block)
        new = attend_block(queries, keys, bias[block], [state[...] for state in running])
        for state, value in zip(running, new):
            state[...] = value
        return carry

    lax.fori_loop(0, blocks - 1, step, 0)


def finish_kernel(heads, chunk_count, *rest):
    queries, (top, total, context), rest = rest[:2], rest[2:5], rest[5:]
    bias, chunks = rest[:chunk_count][:1], rest[1 : 1 + chunk_count]
    rest = rest[len(bias) + len(chunks) :]
    value_own, proj_own, weights, out_ref, out_tiles, keys, out_sems = rest
    rows, width = out_ref.shape
    running = (top[...], total[...], context[...])
    if chunk_count:
        for index, chunk in enumerate(chunks):
            unpack(chunk, keys, index * rows)
        running = attend_block(queries, keys, bias[0][0], running)
    mixed = (running[2] * (1.0 / running[1])).astype(BF16)
    half = heads // 2
    depth = weights.shape[0]
    base = lax.axis_index("heads") * width
    parts = []
    for place in range(heads):
        group, head = divmod(place, half)
        if group == 0:
            value = value_own[:, head * DH : (head + 1) * DH]
        else:
            starts = [width + (block * half + head) * DH for block in range(DC // depth)]
            value = jnp.concatenate([weights[:, start : start + DH] for start in starts], axis=0)
        per_head = jnp.dot(
            mixed[place * rows : (place + 1) * rows], value, preferred_element_type=F32
        )
        parts.append(per_head.astype(BF16))
    heads_out = jnp.concatenate(parts, axis=1)
    tiles = out_sems.shape[0]
    tile = width // tiles
    sends = []
    for index in range(tiles):
        part = pl.ds(index * tile, tile)
        own = proj_own[:, pl.ds(pl.multiple_of(base + index * tile, 128), tile)]
        both = jnp.concatenate([own, weights[:, part]], axis=0)
        out = jnp.dot(heads_out, both, preferred_element_type=F32)
        out_tiles[:, part] = out.astype(BF16)
        sends.append(
            pltpu.make_async_copy(out_tiles.at[:, part], out_ref.at[:, part], out_sems.at[index])
        )
        sends[-1].start()
    for send in sends:
        send.wait()


def per_device(
    count, queries_nope, queries_rope, latent, key_rope, key_up, value_up, out_proj, span_order
):
    rows = latent.shape[0]
    depth, width = out_proj.shape[0], out_proj.shape[1] // 2
    heads = 2 * (key_up.shape[1] // DH)
    query_rows = heads * rows
    direct = count == 8
    small = pltpu.CompilerParams(vmem_limit_bytes=SMALL_VMEM)

    def in_hbm(*arrays):
        return [pltpu.with_memory_space_constraint(array, pltpu.HBM) for array in arrays]

    def other_core(array):
        return lax.ppermute(array, "heads", [(0, 1), (1, 0)])

    def partners(array, steps, cores=(0, 1)):
        pairs = [
            (2 * index + core, 2 * (index ^ steps[core]) + core)
            for index in range(count)
            for core in cores
        ]
        return lax.ppermute(array, ("ctx", "heads"), pairs)

    def attend(name, estimate, queries, bias, chunks, old=(), passed=(), paired=False):
        return pl.pallas_call(
            functools.partial(chunks_kernel, len(chunks), len(old), paired),
            out_shape=[jax.ShapeDtypeStruct((query_rows, size), F32) for size in (1, 1, DC)]
            + [jax.ShapeDtypeStruct(chunk.shape, BF16) for chunk in passed],
            in_specs=[vmem()] * (3 + len(chunks) + len(old) + len(passed)),
            out_specs=[vmem()] * (3 + len(passed)),
            scratch_shapes=[pltpu.VMEM((bias.shape[2], DC + DR), BF16)],
            compiler_params=small,
            cost_estimate=cost(estimate),
            name=name,
        )(*queries, bias, *chunks, *old, *passed)

    packed = pl.pallas_call(
        pack_kernel,
        out_shape=jax.ShapeDtypeStruct((2 * rows + rows // 4, DC // 2), BF16),
        in_specs=[hbm()] * 2,
        out_specs=vmem(),
        scratch_shapes=[
            pltpu.VMEM((DR, rows), BF16),
            pltpu.SemaphoreType.DMA((3,)),
        ],
        compiler_params=small,
        name="pack",
    )(*in_hbm(latent, key_rope.T))
    if direct:
        order = [
            [(0, 0), NEAR],
            [CORNER, NEAR[::-1], FAR, FAR[::-1], RELAYED],
            [RELAYED[::-1]],
        ]
        bias_shapes = [(1, rows, len(steps) * rows) for steps in order]
    else:
        order = None
        bias_shapes = [(count // BLOCK_CHUNKS, rows, BLOCK_CHUNKS * rows)]
    outs = pl.pallas_call(
        functools.partial(prepare_kernel, order),
        out_shape=[jax.ShapeDtypeStruct((query_rows // 2, DC + DR), BF16)]
        + [jax.ShapeDtypeStruct(shape, F32) for shape in bias_shapes]
        + [jax.ShapeDtypeStruct((depth, width + DC // depth * key_up.shape[1]), BF16)],
        in_specs=[hbm()] * 6 + [anywhere()],
        out_specs=[vmem()] * (len(bias_shapes) + 2),
        scratch_shapes=[
            pltpu.VMEM(queries_nope.shape, BF16),
            pltpu.VMEM(queries_rope.shape, BF16),
            pltpu.VMEM(key_up.shape, BF16),
            pltpu.SMEM(span_order.shape, jnp.int32),
            pltpu.VMEM(value_up.shape, BF16),
            pltpu.SemaphoreType.DMA((6,)),
        ],
        compiler_params=small,
        cost_estimate=cost(PREPARE_COST),
        name="prepare",
    )(*in_hbm(queries_nope, queries_rope, key_up, span_order, value_up, out_proj), packed)
    queries, biases = outs[0], outs[1:-1]
    weights_other = other_core(outs[-1])
    both = [queries, other_core(queries)]

    if direct:
        out_second = partners(packed, (NEAR[0], FAR[1]))
        out_first = partners(packed, (FAR[0], NEAR[1]))
        far, near = pl.pallas_call(
            sort_kernel,
            out_shape=[jax.ShapeDtypeStruct(packed.shape, BF16)] * 2,
            in_specs=[vmem()] * 2,
            out_specs=[vmem()] * 2,
            compiler_params=small,
            cost_estimate=cost(SORT_COST),
            name="sort",
        )(out_second, out_first)
        corner = partners(packed, CORNER, cores=(1,))
        relayed = partners(far, (1, 1))
        gated = pl.pallas_call(
            gate_kernel,
            out_shape=jax.ShapeDtypeStruct(far.shape, BF16),
            in_specs=[vmem()],
            out_specs=vmem(),
            compiler_params=small,
            cost_estimate=cost(GATE_COST),
            name="gate",
        )(far)
        *running, far_after = attend(
            "first", FIRST_COST, both, biases[0], [packed, near], passed=[gated]
        )
        last = [other_core(relayed)]
        running = attend(
            "second",
            SECOND_COST,
            both,
            biases[1],
            [corner, other_core(corner), other_core(near), far, other_core(far_after), relayed],
            running,
            paired=True,
        )
    else:
        last = []
        running = pl.pallas_call(
            gathered_kernel,
            out_shape=[jax.ShapeDtypeStruct((query_rows, size), F32) for size in (1, 1, DC)],
            in_specs=[vmem()] * 4,
            out_specs=[vmem()] * 3,
            scratch_shapes=[pltpu.VMEM((BLOCK_CHUNKS * rows, DC + DR), BF16)],
            compiler_params=pltpu.CompilerParams(vmem_limit_bytes=LARGE_VMEM),
            name="gathered",
        )(*both, biases[0], lax.all_gather(packed, "ctx", axis=0))

    tiles = 7 if width % 896 == 0 else 1
    return pl.pallas_call(
        functools.partial(finish_kernel, heads, len(last)),
        out_shape=jax.ShapeDtypeStruct((rows, width), BF16),
        in_specs=[vmem()] * (5 + len(biases[2:]) + len(last) + 3),
        out_specs=anywhere(),
        scratch_shapes=[
            pltpu.VMEM((rows, width), BF16),
            pltpu.VMEM((rows, DC + DR), BF16),
            pltpu.SemaphoreType.DMA((tiles,)),
        ],
        compiler_params=small,
        name="finish",
    )(*both, *running, *biases[2:], *last, value_up, out_proj, weights_other)


def solution(mesh):
    in_specs = (
        P(("docs", "ctx"), "heads"),
        P(("docs", "ctx"), "heads"),
        P(("docs", "ctx"), None),
        P(("docs", "ctx"), None),
        P(None, "heads"),
        P(None, "heads"),
        P("heads", None),
        P("docs"),
    )
    out_specs = P(("docs", "ctx"), "heads")
    return jax.shard_map(
        functools.partial(per_device, mesh.shape["ctx"]),
        mesh=mesh,
        in_specs=in_specs,
        out_specs=out_specs,
        check_vma=False,
    )
```

```python
import functools
import math

import jax
import jax.numpy as jnp
from jax import lax
from jax.experimental import pallas as pl
from jax.experimental.pallas import tpu as pltpu
from jax.sharding import PartitionSpec as P

DC = 512
DH = 128
DR = 64
BF16 = jnp.bfloat16
F32 = jnp.float32
MASKED = -1e30
BLOCK_CHUNKS = 8
PREPARE_COST, GATE_COST, FIRST_COST, SECOND_COST = 0, 3, 20, 1
SMALL_VMEM = 20 * 1024 * 1024
LARGE_VMEM = 56 * 1024 * 1024
FAR = (6, 4)
NEAR = (2, 1)
CORNER = (3, 3)
RELAYED = (7, 5)


def vmem():
    return pl.BlockSpec(memory_space=pltpu.VMEM)


def anywhere():
    return pl.BlockSpec(memory_space=pl.ANY)


def hbm():
    return pl.BlockSpec(memory_space=pltpu.HBM)


def cost(microseconds):
    return pl.CostEstimate(flops=int(microseconds * 1.1e9), bytes_accessed=0, transcendentals=0)


def pack_kernel(latent, key_rope_turned, out_ref, turned, sems):
    rows = latent.shape[0]
    group = rows // 6
    half = DC // 2
    fetches = [pltpu.make_async_copy(key_rope_turned, turned, sems.at[2])]
    for side in range(2):
        fetches.append(
            pltpu.make_async_copy(
                latent.at[:, pl.ds(side * half, half)],
                out_ref.at[pl.ds(side * rows, rows)],
                sems.at[side],
            )
        )
    for fetch in fetches:
        fetch.start()
    fetches[0].wait()
    rope = turned[...].astype(F32).T.astype(BF16)
    first = 0
    base = 2 * rows
    for size in (group, group // 2):
        parts = [rope[first + index * size : first + (index + 1) * size] for index in range(4)]
        out_ref[pl.ds(base, size), :] = jnp.concatenate(parts, axis=1)
        first += 4 * size
        base += size
    for fetch in fetches[1:]:
        fetch.wait()


def gate_kernel(chunk, out_ref):
    out_ref[...] = chunk[...]


def unpack(chunk, keys, base, other=None):
    chunk = chunk[...]
    if other is not None:
        chunk = jnp.where(lax.axis_index("heads") == 0, other[...], chunk)
    rows = 4 * chunk.shape[0] // 9
    group = rows // 6
    keys[pl.ds(base, rows), : DC // 2] = chunk[:rows]
    keys[pl.ds(base, rows), DC // 2 : DC] = chunk[rows : 2 * rows]
    place = 2 * rows
    for size in (group, group // 2):
        for index in range(4):
            part = chunk[place : place + size, index * DR : (index + 1) * DR]
            keys[pl.ds(base, size), DC:] = part
            base += size
        place += size


def prepare_kernel(order, *refs):
    sources, out_proj, rest = refs[:5], refs[5], refs[7:]
    outs, copied, sems = rest[:-6], rest[-6:-1], rest[-1]
    weights = outs[-1]
    depth, width = out_proj.shape[0], out_proj.shape[1] // 2
    fetches = [
        pltpu.make_async_copy(source, target, sems.at[index])
        for index, (source, target) in enumerate(zip(sources, copied))
    ]
    base = pl.multiple_of((1 - lax.axis_index("heads")) * width, 128)
    fetches.append(
        pltpu.make_async_copy(
            out_proj.at[:, pl.ds(base, width)], weights.at[:, pl.ds(0, width)], sems.at[5]
        )
    )
    for fetch in fetches:
        fetch.start()
    nope, rope, up, span_order, value_up = copied
    rows = nope.shape[0]
    heads = nope.shape[1] // DH
    span_rows = rows // 2
    for fetch in fetches[:3]:
        fetch.wait()
    own_index = lax.axis_index("ctx")
    core = lax.axis_index("heads")
    for head in range(heads):
        latent = lax.dot_general(
            nope[:, head * DH : (head + 1) * DH],
            up[:, head * DH : (head + 1) * DH],
            (((1,), (1,)), ((), ())),
            preferred_element_type=F32,
        )
        part = pl.ds(head * rows, rows)
        outs[0][part, :DC] = latent.astype(BF16)
        outs[0][part, DC:] = rope[:, head * DR : (head + 1) * DR]
    biases = outs[1:-1]
    fetches[3].wait()
    row = lax.broadcasted_iota(jnp.int32, (rows, 1), 0)
    query_pos = jnp.where(
        row < span_rows,
        span_order[2 * own_index] * span_rows + row,
        span_order[2 * own_index + 1] * span_rows + row - span_rows,
    )

    def bias_of(owners):
        column = lax.broadcasted_iota(jnp.int32, (1, len(owners) * rows), 1)
        key_pos = jnp.zeros(column.shape, jnp.int32)
        for index, owner in enumerate(owners):
            for side in range(2):
                start = index * rows + side * span_rows
                first = span_order[2 * owner + side] * span_rows
                key_pos = jnp.where(column >= start, first + column - start, key_pos)
        return jnp.where(key_pos <= query_pos, F32(0.0), F32(MASKED))

    if order is not None:
        for steps, bias_ref in zip(order, biases):
            bias_ref[0] = bias_of(
                [own_index ^ jnp.where(core == 0, step[0], step[1]) for step in steps]
            )
    else:
        bias_ref = biases[0]

        def step(block, carry):
            bias_ref[block] = bias_of([block * BLOCK_CHUNKS + index for index in range(BLOCK_CHUNKS)])
            return carry

        lax.fori_loop(0, bias_ref.shape[0], step, 0)

    fetches[4].wait()
    columns = value_up.shape[1]
    for block in range(DC // depth):
        part = value_up[block * depth : (block + 1) * depth, :]
        weights[:, width + block * columns : width + (block + 1) * columns] = part
    fetches[5].wait()


def attend_block(queries, keys, bias, old):
    copies = len(queries) * queries[0].shape[0] // bias.shape[0]
    scale = math.log2(math.e) / math.sqrt(DH + DR)
    heads = jnp.concatenate([part[...] for part in queries], axis=0)
    scores = lax.dot_general(
        heads, keys[...], (((1,), (1,)), ((), ())), preferred_element_type=F32
    )
    scores = scores + jnp.concatenate([bias] * copies, axis=0)
    top = jnp.max(scores, axis=-1, keepdims=True)
    if old is not None:
        top = jnp.maximum(old[0], top)
        rescale = jnp.exp2((old[0] - top) * scale)
    expo = jnp.exp2((scores - top) * scale)
    total = jnp.sum(expo, axis=-1, keepdims=True)
    added = jnp.dot(expo.astype(BF16), keys[:, :DC], preferred_element_type=F32)
    if old is not None:
        total = old[1] * rescale + total
        added = old[2] * rescale + added
    return top, total, added


def chunks_kernel(chunk_count, old_count, paired, *rest):
    queries, bias, rest = rest[:2], rest[2], rest[3:]
    chunks, rest = rest[:chunk_count], rest[chunk_count:]
    old, rest = rest[:old_count], rest[old_count:]
    if len(rest) == 6:
        passed, handed = rest[0], rest[4]
        handed[...] = passed[...]
        rest = rest[1:4] + rest[5:]
    running, keys = rest[:3], rest[3]
    rows = bias.shape[1]
    if paired:
        unpack(chunks[0], keys, 0, chunks[1])
        chunks = chunks[1:]
    for index, chunk in enumerate(chunks):
        if index or not paired:
            unpack(chunk, keys, index * rows)
    before = [state[...] for state in old] if old else None
    values = attend_block(queries, keys, bias[0], before)
    for state, value in zip(running, values):
        state[...] = value


def gathered_kernel(queries_own, queries_other, bias, gathered, *rest):
    queries = (queries_own, queries_other)
    running, keys = rest[:3], rest[3]
    blocks, rows, _ = bias.shape

    def fill(block):
        for index in range(BLOCK_CHUNKS):
            unpack(gathered.at[block * BLOCK_CHUNKS + index], keys, index * rows)

    first = lax.axis_index("ctx") // BLOCK_CHUNKS
    fill(first)
    values = attend_block(queries, keys, bias[first], None)
    for state, value in zip(running, values):
        state[...] = value

    def step(index, carry):
        block = index + jnp.where(index >= first, 1, 0)
        fill(block)
        new = attend_block(queries, keys, bias[block], [state[...] for state in running])
        for state, value in zip(running, new):
            state[...] = value
        return carry

    lax.fori_loop(0, blocks - 1, step, 0)


def finish_kernel(heads, chunk_count, *rest):
    queries, (top, total, context), rest = rest[:2], rest[2:5], rest[5:]
    bias, chunks = rest[:chunk_count][:1], rest[1 : 1 + chunk_count]
    rest = rest[len(bias) + len(chunks) :]
    value_own, proj_own, weights, out_ref, out_tiles, keys, out_sems = rest
    rows, width = out_ref.shape
    running = (top[...], total[...], context[...])
    if chunk_count:
        for index, chunk in enumerate(chunks):
            unpack(chunk, keys, index * rows)
        running = attend_block(queries, keys, bias[0][0], running)
    mixed = (running[2] * (1.0 / running[1])).astype(BF16)
    half = heads // 2
    depth = weights.shape[0]
    base = lax.axis_index("heads") * width
    parts = []
    for place in range(heads):
        group, head = divmod(place, half)
        if group == 0:
            value = value_own[:, head * DH : (head + 1) * DH]
        else:
            starts = [width + (block * half + head) * DH for block in range(DC // depth)]
            value = jnp.concatenate([weights[:, start : start + DH] for start in starts], axis=0)
        per_head = jnp.dot(
            mixed[place * rows : (place + 1) * rows], value, preferred_element_type=F32
        )
        parts.append(per_head.astype(BF16))
    heads_out = jnp.concatenate(parts, axis=1)
    tiles = out_sems.shape[0]
    tile = width // tiles
    sends = []
    for index in range(tiles):
        part = pl.ds(index * tile, tile)
        own = proj_own[:, pl.ds(pl.multiple_of(base + index * tile, 128), tile)]
        both = jnp.concatenate([own, weights[:, part]], axis=0)
        out = jnp.dot(heads_out, both, preferred_element_type=F32)
        out_tiles[:, part] = out.astype(BF16)
        sends.append(
            pltpu.make_async_copy(out_tiles.at[:, part], out_ref.at[:, part], out_sems.at[index])
        )
        sends[-1].start()
    for send in sends:
        send.wait()


def per_device(
    count, queries_nope, queries_rope, latent, key_rope, key_up, value_up, out_proj, span_order
):
    rows = latent.shape[0]
    depth, width = out_proj.shape[0], out_proj.shape[1] // 2
    heads = 2 * (key_up.shape[1] // DH)
    query_rows = heads * rows
    direct = count == 8
    small = pltpu.CompilerParams(vmem_limit_bytes=SMALL_VMEM)

    def in_hbm(*arrays):
        return [pltpu.with_memory_space_constraint(array, pltpu.HBM) for array in arrays]

    def other_core(array):
        return lax.ppermute(array, "heads", [(0, 1), (1, 0)])

    def partners(array, steps, cores=(0, 1)):
        pairs = [
            (2 * index + core, 2 * (index ^ steps[core]) + core)
            for index in range(count)
            for core in cores
        ]
        return lax.ppermute(array, ("ctx", "heads"), pairs)

    def attend(name, estimate, queries, bias, chunks, old=(), passed=(), paired=False):
        return pl.pallas_call(
            functools.partial(chunks_kernel, len(chunks), len(old), paired),
            out_shape=[jax.ShapeDtypeStruct((query_rows, size), F32) for size in (1, 1, DC)]
            + [jax.ShapeDtypeStruct(chunk.shape, BF16) for chunk in passed],
            in_specs=[vmem()] * (3 + len(chunks) + len(old) + len(passed)),
            out_specs=[vmem()] * (3 + len(passed)),
            scratch_shapes=[pltpu.VMEM((bias.shape[2], DC + DR), BF16)],
            compiler_params=small,
            cost_estimate=cost(estimate),
            name=name,
        )(*queries, bias, *chunks, *old, *passed)

    packed = pl.pallas_call(
        pack_kernel,
        out_shape=jax.ShapeDtypeStruct((2 * rows + rows // 4, DC // 2), BF16),
        in_specs=[hbm()] * 2,
        out_specs=vmem(),
        scratch_shapes=[
            pltpu.VMEM((DR, rows), BF16),
            pltpu.SemaphoreType.DMA((3,)),
        ],
        compiler_params=small,
        name="pack",
    )(*in_hbm(latent, key_rope.T))
    if direct:
        order = [
            [(0, 0), NEAR],
            [CORNER, NEAR[::-1], FAR, FAR[::-1], RELAYED],
            [RELAYED[::-1]],
        ]
        bias_shapes = [(1, rows, len(steps) * rows) for steps in order]
    else:
        order = None
        bias_shapes = [(count // BLOCK_CHUNKS, rows, BLOCK_CHUNKS * rows)]
    outs = pl.pallas_call(
        functools.partial(prepare_kernel, order),
        out_shape=[jax.ShapeDtypeStruct((query_rows // 2, DC + DR), BF16)]
        + [jax.ShapeDtypeStruct(shape, F32) for shape in bias_shapes]
        + [jax.ShapeDtypeStruct((depth, width + DC // depth * key_up.shape[1]), BF16)],
        in_specs=[hbm()] * 6 + [anywhere()],
        out_specs=[vmem()] * (len(bias_shapes) + 2),
        scratch_shapes=[
            pltpu.VMEM(queries_nope.shape, BF16),
            pltpu.VMEM(queries_rope.shape, BF16),
            pltpu.VMEM(key_up.shape, BF16),
            pltpu.SMEM(span_order.shape, jnp.int32),
            pltpu.VMEM(value_up.shape, BF16),
            pltpu.SemaphoreType.DMA((6,)),
        ],
        compiler_params=small,
        cost_estimate=cost(PREPARE_COST),
        name="prepare",
    )(*in_hbm(queries_nope, queries_rope, key_up, span_order, value_up, out_proj), packed)
    queries, biases = outs[0], outs[1:-1]
    weights_other = other_core(outs[-1])
    both = [queries, other_core(queries)]

    if direct:
        far = partners(packed, FAR)
        near = partners(packed, NEAR)
        corner = partners(packed, CORNER, cores=(1,))
        relayed = partners(far, (1, 1))
        gated = pl.pallas_call(
            gate_kernel,
            out_shape=jax.ShapeDtypeStruct(far.shape, BF16),
            in_specs=[vmem()],
            out_specs=vmem(),
            compiler_params=small,
            cost_estimate=cost(GATE_COST),
            name="gate",
        )(far)
        *running, far_after = attend(
            "first", FIRST_COST, both, biases[0], [packed, near], passed=[gated]
        )
        last = [other_core(relayed)]
        running = attend(
            "second",
            SECOND_COST,
            both,
            biases[1],
            [corner, other_core(corner), other_core(near), far, other_core(far_after), relayed],
            running,
            paired=True,
        )
    else:
        last = []
        running = pl.pallas_call(
            gathered_kernel,
            out_shape=[jax.ShapeDtypeStruct((query_rows, size), F32) for size in (1, 1, DC)],
            in_specs=[vmem()] * 4,
            out_specs=[vmem()] * 3,
            scratch_shapes=[pltpu.VMEM((BLOCK_CHUNKS * rows, DC + DR), BF16)],
            compiler_params=pltpu.CompilerParams(vmem_limit_bytes=LARGE_VMEM),
            name="gathered",
        )(*both, biases[0], lax.all_gather(packed, "ctx", axis=0))

    tiles = 7 if width % 896 == 0 else 1
    return pl.pallas_call(
        functools.partial(finish_kernel, heads, len(last)),
        out_shape=jax.ShapeDtypeStruct((rows, width), BF16),
        in_specs=[vmem()] * (5 + len(biases[2:]) + len(last) + 3),
        out_specs=anywhere(),
        scratch_shapes=[
            pltpu.VMEM((rows, width), BF16),
            pltpu.VMEM((rows, DC + DR), BF16),
            pltpu.SemaphoreType.DMA((tiles,)),
        ],
        compiler_params=small,
        name="finish",
    )(*both, *running, *biases[2:], *last, value_up, out_proj, weights_other)


def solution(mesh):
    in_specs = (
        P(("docs", "ctx"), "heads"),
        P(("docs", "ctx"), "heads"),
        P(("docs", "ctx"), None),
        P(("docs", "ctx"), None),
        P(None, "heads"),
        P(None, "heads"),
        P("heads", None),
        P("docs"),
    )
    out_specs = P(("docs", "ctx"), "heads")
    return jax.shard_map(
        functools.partial(per_device, mesh.shape["ctx"]),
        mesh=mesh,
        in_specs=in_specs,
        out_specs=out_specs,
        check_vma=False,
    )
```

```python
import functools
import math

import jax
import jax.numpy as jnp
from jax import lax
from jax.experimental import pallas as pl
from jax.experimental.pallas import tpu as pltpu
from jax.sharding import PartitionSpec as P

DC = 512
DH = 128
DR = 64
BF16 = jnp.bfloat16
F32 = jnp.float32
MASKED = -1e30
BLOCK_CHUNKS = 8
PREPARE_COST, GATE_COST, FIRST_COST, SECOND_COST = 0, 3, 20, 1
SMALL_VMEM = 20 * 1024 * 1024
LARGE_VMEM = 56 * 1024 * 1024
FAR = (6, 4)
NEAR = (1, 2)
CORNER = (3, 3)
RELAYED = (7, 5)


def vmem():
    return pl.BlockSpec(memory_space=pltpu.VMEM)


def anywhere():
    return pl.BlockSpec(memory_space=pl.ANY)


def hbm():
    return pl.BlockSpec(memory_space=pltpu.HBM)


def cost(microseconds):
    return pl.CostEstimate(flops=int(microseconds * 1.1e9), bytes_accessed=0, transcendentals=0)


def pack_kernel(latent, key_rope_turned, out_ref, turned, sems):
    rows = latent.shape[0]
    group = rows // 6
    half = DC // 2
    fetches = [pltpu.make_async_copy(key_rope_turned, turned, sems.at[2])]
    for side in range(2):
        fetches.append(
            pltpu.make_async_copy(
                latent.at[:, pl.ds(side * half, half)],
                out_ref.at[pl.ds(side * rows, rows)],
                sems.at[side],
            )
        )
    for fetch in fetches:
        fetch.start()
    fetches[0].wait()
    rope = turned[...].astype(F32).T.astype(BF16)
    first = 0
    base = 2 * rows
    for size in (group, group // 2):
        parts = [rope[first + index * size : first + (index + 1) * size] for index in range(4)]
        out_ref[pl.ds(base, size), :] = jnp.concatenate(parts, axis=1)
        first += 4 * size
        base += size
    for fetch in fetches[1:]:
        fetch.wait()


def gate_kernel(chunk, out_ref):
    out_ref[...] = chunk[...]


def unpack(chunk, keys, base, other=None):
    chunk = chunk[...]
    if other is not None:
        chunk = jnp.where(lax.axis_index("heads") == 0, other[...], chunk)
    rows = 4 * chunk.shape[0] // 9
    group = rows // 6
    keys[pl.ds(base, rows), : DC // 2] = chunk[:rows]
    keys[pl.ds(base, rows), DC // 2 : DC] = chunk[rows : 2 * rows]
    place = 2 * rows
    for size in (group, group // 2):
        for index in range(4):
            part = chunk[place : place + size, index * DR : (index + 1) * DR]
            keys[pl.ds(base, size), DC:] = part
            base += size
        place += size


def prepare_kernel(order, *refs):
    sources, out_proj, rest = refs[:5], refs[5], refs[7:]
    outs, copied, sems = rest[:-6], rest[-6:-1], rest[-1]
    weights = outs[-1]
    depth, width = out_proj.shape[0], out_proj.shape[1] // 2
    fetches = [
        pltpu.make_async_copy(source, target, sems.at[index])
        for index, (source, target) in enumerate(zip(sources, copied))
    ]
    base = pl.multiple_of((1 - lax.axis_index("heads")) * width, 128)
    fetches.append(
        pltpu.make_async_copy(
            out_proj.at[:, pl.ds(base, width)], weights.at[:, pl.ds(0, width)], sems.at[5]
        )
    )
    for fetch in fetches:
        fetch.start()
    nope, rope, up, span_order, value_up = copied
    rows = nope.shape[0]
    heads = nope.shape[1] // DH
    span_rows = rows // 2
    for fetch in fetches[:3]:
        fetch.wait()
    own_index = lax.axis_index("ctx")
    core = lax.axis_index("heads")
    for head in range(heads):
        latent = lax.dot_general(
            nope[:, head * DH : (head + 1) * DH],
            up[:, head * DH : (head + 1) * DH],
            (((1,), (1,)), ((), ())),
            preferred_element_type=F32,
        )
        part = pl.ds(head * rows, rows)
        outs[0][part, :DC] = latent.astype(BF16)
        outs[0][part, DC:] = rope[:, head * DR : (head + 1) * DR]
    biases = outs[1:-1]
    fetches[3].wait()
    row = lax.broadcasted_iota(jnp.int32, (rows, 1), 0)
    query_pos = jnp.where(
        row < span_rows,
        span_order[2 * own_index] * span_rows + row,
        span_order[2 * own_index + 1] * span_rows + row - span_rows,
    )

    def bias_of(owners):
        column = lax.broadcasted_iota(jnp.int32, (1, len(owners) * rows), 1)
        key_pos = jnp.zeros(column.shape, jnp.int32)
        for index, owner in enumerate(owners):
            for side in range(2):
                start = index * rows + side * span_rows
                first = span_order[2 * owner + side] * span_rows
                key_pos = jnp.where(column >= start, first + column - start, key_pos)
        return jnp.where(key_pos <= query_pos, F32(0.0), F32(MASKED))

    if order is not None:
        for steps, bias_ref in zip(order, biases):
            bias_ref[0] = bias_of(
                [own_index ^ jnp.where(core == 0, step[0], step[1]) for step in steps]
            )
    else:
        bias_ref = biases[0]

        def step(block, carry):
            bias_ref[block] = bias_of([block * BLOCK_CHUNKS + index for index in range(BLOCK_CHUNKS)])
            return carry

        lax.fori_loop(0, bias_ref.shape[0], step, 0)

    fetches[4].wait()
    columns = value_up.shape[1]
    for block in range(DC // depth):
        part = value_up[block * depth : (block + 1) * depth, :]
        weights[:, width + block * columns : width + (block + 1) * columns] = part
    fetches[5].wait()


def attend_block(queries, keys, bias, old):
    copies = len(queries) * queries[0].shape[0] // bias.shape[0]
    scale = math.log2(math.e) / math.sqrt(DH + DR)
    heads = jnp.concatenate([part[...] for part in queries], axis=0)
    scores = lax.dot_general(
        heads, keys[...], (((1,), (1,)), ((), ())), preferred_element_type=F32
    )
    scores = scores + jnp.concatenate([bias] * copies, axis=0)
    top = jnp.max(scores, axis=-1, keepdims=True)
    if old is not None:
        top = jnp.maximum(old[0], top)
        rescale = jnp.exp2((old[0] - top) * scale)
    expo = jnp.exp2((scores - top) * scale)
    total = jnp.sum(expo, axis=-1, keepdims=True)
    added = jnp.dot(expo.astype(BF16), keys[:, :DC], preferred_element_type=F32)
    if old is not None:
        total = old[1] * rescale + total
        added = old[2] * rescale + added
    return top, total, added


def chunks_kernel(chunk_count, old_count, paired, *rest):
    queries, bias, rest = rest[:2], rest[2], rest[3:]
    chunks, rest = rest[:chunk_count], rest[chunk_count:]
    old, rest = rest[:old_count], rest[old_count:]
    if len(rest) == 6:
        passed, handed = rest[0], rest[4]
        handed[...] = passed[...]
        rest = rest[1:4] + rest[5:]
    running, keys = rest[:3], rest[3]
    rows = bias.shape[1]
    if paired:
        unpack(chunks[0], keys, 0, chunks[1])
        chunks = chunks[1:]
    for index, chunk in enumerate(chunks):
        if index or not paired:
            unpack(chunk, keys, index * rows)
    before = [state[...] for state in old] if old else None
    values = attend_block(queries, keys, bias[0], before)
    for state, value in zip(running, values):
        state[...] = value


def gathered_kernel(queries_own, queries_other, bias, gathered, *rest):
    queries = (queries_own, queries_other)
    running, keys = rest[:3], rest[3]
    blocks, rows, _ = bias.shape

    def fill(block):
        for index in range(BLOCK_CHUNKS):
            unpack(gathered.at[block * BLOCK_CHUNKS + index], keys, index * rows)

    first = lax.axis_index("ctx") // BLOCK_CHUNKS
    fill(first)
    values = attend_block(queries, keys, bias[first], None)
    for state, value in zip(running, values):
        state[...] = value

    def step(index, carry):
        block = index + jnp.where(index >= first, 1, 0)
        fill(block)
        new = attend_block(queries, keys, bias[block], [state[...] for state in running])
        for state, value in zip(running, new):
            state[...] = value
        return carry

    lax.fori_loop(0, blocks - 1, step, 0)


def finish_kernel(heads, chunk_count, *rest):
    queries, (top, total, context), rest = rest[:2], rest[2:5], rest[5:]
    bias, chunks = rest[:chunk_count][:1], rest[1 : 1 + chunk_count]
    rest = rest[len(bias) + len(chunks) :]
    value_own, proj_own, weights, out_ref, out_tiles, keys, out_sems = rest
    rows, width = out_ref.shape
    running = (top[...], total[...], context[...])
    if chunk_count:
        for index, chunk in enumerate(chunks):
            unpack(chunk, keys, index * rows)
        running = attend_block(queries, keys, bias[0][0], running)
    mixed = (running[2] * (1.0 / running[1])).astype(BF16)
    half = heads // 2
    depth = weights.shape[0]
    base = lax.axis_index("heads") * width
    parts = []
    for place in range(heads):
        group, head = divmod(place, half)
        if group == 0:
            value = value_own[:, head * DH : (head + 1) * DH]
        else:
            starts = [width + (block * half + head) * DH for block in range(DC // depth)]
            value = jnp.concatenate([weights[:, start : start + DH] for start in starts], axis=0)
        per_head = jnp.dot(
            mixed[place * rows : (place + 1) * rows], value, preferred_element_type=F32
        )
        parts.append(per_head.astype(BF16))
    heads_out = jnp.concatenate(parts, axis=1)
    tiles = out_sems.shape[0]
    tile = width // tiles
    sends = []
    for index in range(tiles):
        part = pl.ds(index * tile, tile)
        own = proj_own[:, pl.ds(pl.multiple_of(base + index * tile, 128), tile)]
        both = jnp.concatenate([own, weights[:, part]], axis=0)
        out = jnp.dot(heads_out, both, preferred_element_type=F32)
        out_tiles[:, part] = out.astype(BF16)
        sends.append(
            pltpu.make_async_copy(out_tiles.at[:, part], out_ref.at[:, part], out_sems.at[index])
        )
        sends[-1].start()
    for send in sends:
        send.wait()


def per_device(
    count, queries_nope, queries_rope, latent, key_rope, key_up, value_up, out_proj, span_order
):
    rows = latent.shape[0]
    depth, width = out_proj.shape[0], out_proj.shape[1] // 2
    heads = 2 * (key_up.shape[1] // DH)
    query_rows = heads * rows
    direct = count == 8
    small = pltpu.CompilerParams(vmem_limit_bytes=SMALL_VMEM)

    def in_hbm(*arrays):
        return [pltpu.with_memory_space_constraint(array, pltpu.HBM) for array in arrays]

    def other_core(array):
        return lax.ppermute(array, "heads", [(0, 1), (1, 0)])

    def partners(array, steps, cores=(0, 1)):
        pairs = [
            (2 * index + core, 2 * (index ^ steps[core]) + core)
            for index in range(count)
            for core in cores
        ]
        return lax.ppermute(array, ("ctx", "heads"), pairs)

    def attend(name, estimate, queries, bias, chunks, old=(), passed=(), paired=False):
        return pl.pallas_call(
            functools.partial(chunks_kernel, len(chunks), len(old), paired),
            out_shape=[jax.ShapeDtypeStruct((query_rows, size), F32) for size in (1, 1, DC)]
            + [jax.ShapeDtypeStruct(chunk.shape, BF16) for chunk in passed],
            in_specs=[vmem()] * (3 + len(chunks) + len(old) + len(passed)),
            out_specs=[vmem()] * (3 + len(passed)),
            scratch_shapes=[pltpu.VMEM((bias.shape[2], DC + DR), BF16)],
            compiler_params=small,
            cost_estimate=cost(estimate),
            name=name,
        )(*queries, bias, *chunks, *old, *passed)

    packed = pl.pallas_call(
        pack_kernel,
        out_shape=jax.ShapeDtypeStruct((2 * rows + rows // 4, DC // 2), BF16),
        in_specs=[hbm()] * 2,
        out_specs=vmem(),
        scratch_shapes=[
            pltpu.VMEM((DR, rows), BF16),
            pltpu.SemaphoreType.DMA((3,)),
        ],
        compiler_params=small,
        name="pack",
    )(*in_hbm(latent, key_rope.T))
    if direct:
        order = [
            [(0, 0), NEAR],
            [CORNER, NEAR[::-1], FAR, FAR[::-1], RELAYED],
            [RELAYED[::-1]],
        ]
        bias_shapes = [(1, rows, len(steps) * rows) for steps in order]
    else:
        order = None
        bias_shapes = [(count // BLOCK_CHUNKS, rows, BLOCK_CHUNKS * rows)]
    outs = pl.pallas_call(
        functools.partial(prepare_kernel, order),
        out_shape=[jax.ShapeDtypeStruct((query_rows // 2, DC + DR), BF16)]
        + [jax.ShapeDtypeStruct(shape, F32) for shape in bias_shapes]
        + [jax.ShapeDtypeStruct((depth, width + DC // depth * key_up.shape[1]), BF16)],
        in_specs=[hbm()] * 6 + [anywhere()],
        out_specs=[vmem()] * (len(bias_shapes) + 2),
        scratch_shapes=[
            pltpu.VMEM(queries_nope.shape, BF16),
            pltpu.VMEM(queries_rope.shape, BF16),
            pltpu.VMEM(key_up.shape, BF16),
            pltpu.SMEM(span_order.shape, jnp.int32),
            pltpu.VMEM(value_up.shape, BF16),
            pltpu.SemaphoreType.DMA((6,)),
        ],
        compiler_params=small,
        cost_estimate=cost(PREPARE_COST),
        name="prepare",
    )(*in_hbm(queries_nope, queries_rope, key_up, span_order, value_up, out_proj), packed)
    queries, biases = outs[0], outs[1:-1]
    weights_other = other_core(outs[-1])
    both = [queries, other_core(queries)]

    if direct:
        far = partners(packed, FAR)
        near = partners(packed, NEAR)
        corner = partners(packed, CORNER, cores=(1,))
        relayed = partners(far, (1, 1))
        gated = pl.pallas_call(
            gate_kernel,
            out_shape=jax.ShapeDtypeStruct(far.shape, BF16),
            in_specs=[vmem()],
            out_specs=vmem(),
            compiler_params=small,
            cost_estimate=cost(GATE_COST),
            name="gate",
        )(far)
        *running, far_after = attend(
            "first", FIRST_COST, both, biases[0], [packed, near], passed=[gated]
        )
        last = [other_core(relayed)]
        running = attend(
            "second",
            SECOND_COST,
            both,
            biases[1],
            [corner, other_core(corner), other_core(near), far, other_core(far_after), relayed],
            running,
            paired=True,
        )
    else:
        last = []
        running = pl.pallas_call(
            gathered_kernel,
            out_shape=[jax.ShapeDtypeStruct((query_rows, size), F32) for size in (1, 1, DC)],
            in_specs=[vmem()] * 4,
            out_specs=[vmem()] * 3,
            scratch_shapes=[pltpu.VMEM((BLOCK_CHUNKS * rows, DC + DR), BF16)],
            compiler_params=pltpu.CompilerParams(vmem_limit_bytes=LARGE_VMEM),
            name="gathered",
        )(*both, biases[0], lax.all_gather(packed, "ctx", axis=0))

    tiles = 7 if width % 896 == 0 else 1
    return pl.pallas_call(
        functools.partial(finish_kernel, heads, len(last)),
        out_shape=jax.ShapeDtypeStruct((rows, width), BF16),
        in_specs=[vmem()] * (5 + len(biases[2:]) + len(last) + 3),
        out_specs=anywhere(),
        scratch_shapes=[
            pltpu.VMEM((rows, width), BF16),
            pltpu.VMEM((rows, DC + DR), BF16),
            pltpu.SemaphoreType.DMA((tiles,)),
        ],
        compiler_params=small,
        name="finish",
    )(*both, *running, *biases[2:], *last, value_up, out_proj, weights_other)


def solution(mesh):
    in_specs = (
        P(("docs", "ctx"), "heads"),
        P(("docs", "ctx"), "heads"),
        P(("docs", "ctx"), None),
        P(("docs", "ctx"), None),
        P(None, "heads"),
        P(None, "heads"),
        P("heads", None),
        P("docs"),
    )
    out_specs = P(("docs", "ctx"), "heads")
    return jax.shard_map(
        functools.partial(per_device, mesh.shape["ctx"]),
        mesh=mesh,
        in_specs=in_specs,
        out_specs=out_specs,
        check_vma=False,
    )
```

```python
import functools
import math

import jax
import jax.numpy as jnp
from jax import lax
from jax.experimental import pallas as pl
from jax.experimental.pallas import tpu as pltpu
from jax.sharding import PartitionSpec as P

DC = 512
DH = 128
DR = 64
BF16 = jnp.bfloat16
F32 = jnp.float32
MASKED = -1e30
BLOCK_CHUNKS = 8
PREPARE_COST, GATE_COST, FIRST_COST, SECOND_COST = 0, 3, 20, 1
SMALL_VMEM = 20 * 1024 * 1024
LARGE_VMEM = 56 * 1024 * 1024
FAR = (4, 6)
NEAR = (2, 1)
CORNER = (3, 3)
RELAYED = (5, 7)


def vmem():
    return pl.BlockSpec(memory_space=pltpu.VMEM)


def anywhere():
    return pl.BlockSpec(memory_space=pl.ANY)


def hbm():
    return pl.BlockSpec(memory_space=pltpu.HBM)


def cost(microseconds):
    return pl.CostEstimate(flops=int(microseconds * 1.1e9), bytes_accessed=0, transcendentals=0)


def pack_kernel(latent, key_rope_turned, out_ref, turned, sems):
    rows = latent.shape[0]
    group = rows // 6
    half = DC // 2
    fetches = [pltpu.make_async_copy(key_rope_turned, turned, sems.at[2])]
    for side in range(2):
        fetches.append(
            pltpu.make_async_copy(
                latent.at[:, pl.ds(side * half, half)],
                out_ref.at[pl.ds(side * rows, rows)],
                sems.at[side],
            )
        )
    for fetch in fetches:
        fetch.start()
    fetches[0].wait()
    rope = turned[...].astype(F32).T.astype(BF16)
    first = 0
    base = 2 * rows
    for size in (group, group // 2):
        parts = [rope[first + index * size : first + (index + 1) * size] for index in range(4)]
        out_ref[pl.ds(base, size), :] = jnp.concatenate(parts, axis=1)
        first += 4 * size
        base += size
    for fetch in fetches[1:]:
        fetch.wait()


def gate_kernel(chunk, out_ref):
    out_ref[...] = chunk[...]


def unpack(chunk, keys, base, other=None):
    chunk = chunk[...]
    if other is not None:
        chunk = jnp.where(lax.axis_index("heads") == 0, other[...], chunk)
    rows = 4 * chunk.shape[0] // 9
    group = rows // 6
    keys[pl.ds(base, rows), : DC // 2] = chunk[:rows]
    keys[pl.ds(base, rows), DC // 2 : DC] = chunk[rows : 2 * rows]
    place = 2 * rows
    for size in (group, group // 2):
        for index in range(4):
            part = chunk[place : place + size, index * DR : (index + 1) * DR]
            keys[pl.ds(base, size), DC:] = part
            base += size
        place += size


def prepare_kernel(order, *refs):
    sources, out_proj, rest = refs[:5], refs[5], refs[7:]
    outs, copied, sems = rest[:-6], rest[-6:-1], rest[-1]
    weights = outs[-1]
    depth, width = out_proj.shape[0], out_proj.shape[1] // 2
    fetches = [
        pltpu.make_async_copy(source, target, sems.at[index])
        for index, (source, target) in enumerate(zip(sources, copied))
    ]
    base = pl.multiple_of((1 - lax.axis_index("heads")) * width, 128)
    fetches.append(
        pltpu.make_async_copy(
            out_proj.at[:, pl.ds(base, width)], weights.at[:, pl.ds(0, width)], sems.at[5]
        )
    )
    for fetch in fetches:
        fetch.start()
    nope, rope, up, span_order, value_up = copied
    rows = nope.shape[0]
    heads = nope.shape[1] // DH
    span_rows = rows // 2
    for fetch in fetches[:3]:
        fetch.wait()
    own_index = lax.axis_index("ctx")
    core = lax.axis_index("heads")
    for head in range(heads):
        latent = lax.dot_general(
            nope[:, head * DH : (head + 1) * DH],
            up[:, head * DH : (head + 1) * DH],
            (((1,), (1,)), ((), ())),
            preferred_element_type=F32,
        )
        part = pl.ds(head * rows, rows)
        outs[0][part, :DC] = latent.astype(BF16)
        outs[0][part, DC:] = rope[:, head * DR : (head + 1) * DR]
    biases = outs[1:-1]
    fetches[3].wait()
    row = lax.broadcasted_iota(jnp.int32, (rows, 1), 0)
    query_pos = jnp.where(
        row < span_rows,
        span_order[2 * own_index] * span_rows + row,
        span_order[2 * own_index + 1] * span_rows + row - span_rows,
    )

    def bias_of(owners):
        column = lax.broadcasted_iota(jnp.int32, (1, len(owners) * rows), 1)
        key_pos = jnp.zeros(column.shape, jnp.int32)
        for index, owner in enumerate(owners):
            for side in range(2):
                start = index * rows + side * span_rows
                first = span_order[2 * owner + side] * span_rows
                key_pos = jnp.where(column >= start, first + column - start, key_pos)
        return jnp.where(key_pos <= query_pos, F32(0.0), F32(MASKED))

    if order is not None:
        for steps, bias_ref in zip(order, biases):
            bias_ref[0] = bias_of(
                [own_index ^ jnp.where(core == 0, step[0], step[1]) for step in steps]
            )
    else:
        bias_ref = biases[0]

        def step(block, carry):
            bias_ref[block] = bias_of([block * BLOCK_CHUNKS + index for index in range(BLOCK_CHUNKS)])
            return carry

        lax.fori_loop(0, bias_ref.shape[0], step, 0)

    fetches[4].wait()
    columns = value_up.shape[1]
    for block in range(DC // depth):
        part = value_up[block * depth : (block + 1) * depth, :]
        weights[:, width + block * columns : width + (block + 1) * columns] = part
    fetches[5].wait()


def attend_block(queries, keys, bias, old):
    copies = len(queries) * queries[0].shape[0] // bias.shape[0]
    scale = math.log2(math.e) / math.sqrt(DH + DR)
    heads = jnp.concatenate([part[...] for part in queries], axis=0)
    scores = lax.dot_general(
        heads, keys[...], (((1,), (1,)), ((), ())), preferred_element_type=F32
    )
    scores = scores + jnp.concatenate([bias] * copies, axis=0)
    top = jnp.max(scores, axis=-1, keepdims=True)
    if old is not None:
        top = jnp.maximum(old[0], top)
        rescale = jnp.exp2((old[0] - top) * scale)
    expo = jnp.exp2((scores - top) * scale)
    total = jnp.sum(expo, axis=-1, keepdims=True)
    added = jnp.dot(expo.astype(BF16), keys[:, :DC], preferred_element_type=F32)
    if old is not None:
        total = old[1] * rescale + total
        added = old[2] * rescale + added
    return top, total, added


def chunks_kernel(chunk_count, old_count, paired, *rest):
    queries, bias, rest = rest[:2], rest[2], rest[3:]
    chunks, rest = rest[:chunk_count], rest[chunk_count:]
    old, rest = rest[:old_count], rest[old_count:]
    if len(rest) == 6:
        passed, handed = rest[0], rest[4]
        handed[...] = passed[...]
        rest = rest[1:4] + rest[5:]
    running, keys = rest[:3], rest[3]
    rows = bias.shape[1]
    if paired:
        unpack(chunks[0], keys, 0, chunks[1])
        chunks = chunks[1:]
    for index, chunk in enumerate(chunks):
        if index or not paired:
            unpack(chunk, keys, index * rows)
    before = [state[...] for state in old] if old else None
    values = attend_block(queries, keys, bias[0], before)
    for state, value in zip(running, values):
        state[...] = value


def gathered_kernel(queries_own, queries_other, bias, gathered, *rest):
    queries = (queries_own, queries_other)
    running, keys = rest[:3], rest[3]
    blocks, rows, _ = bias.shape

    def fill(block):
        for index in range(BLOCK_CHUNKS):
            unpack(gathered.at[block * BLOCK_CHUNKS + index], keys, index * rows)

    first = lax.axis_index("ctx") // BLOCK_CHUNKS
    fill(first)
    values = attend_block(queries, keys, bias[first], None)
    for state, value in zip(running, values):
        state[...] = value

    def step(index, carry):
        block = index + jnp.where(index >= first, 1, 0)
        fill(block)
        new = attend_block(queries, keys, bias[block], [state[...] for state in running])
        for state, value in zip(running, new):
            state[...] = value
        return carry

    lax.fori_loop(0, blocks - 1, step, 0)


def finish_kernel(heads, chunk_count, *rest):
    queries, (top, total, context), rest = rest[:2], rest[2:5], rest[5:]
    bias, chunks = rest[:chunk_count][:1], rest[1 : 1 + chunk_count]
    rest = rest[len(bias) + len(chunks) :]
    value_own, proj_own, weights, out_ref, out_tiles, keys, out_sems = rest
    rows, width = out_ref.shape
    running = (top[...], total[...], context[...])
    if chunk_count:
        for index, chunk in enumerate(chunks):
            unpack(chunk, keys, index * rows)
        running = attend_block(queries, keys, bias[0][0], running)
    mixed = (running[2] * (1.0 / running[1])).astype(BF16)
    half = heads // 2
    depth = weights.shape[0]
    base = lax.axis_index("heads") * width
    parts = []
    for place in range(heads):
        group, head = divmod(place, half)
        if group == 0:
            value = value_own[:, head * DH : (head + 1) * DH]
        else:
            starts = [width + (block * half + head) * DH for block in range(DC // depth)]
            value = jnp.concatenate([weights[:, start : start + DH] for start in starts], axis=0)
        per_head = jnp.dot(
            mixed[place * rows : (place + 1) * rows], value, preferred_element_type=F32
        )
        parts.append(per_head.astype(BF16))
    heads_out = jnp.concatenate(parts, axis=1)
    tiles = out_sems.shape[0]
    tile = width // tiles
    sends = []
    for index in range(tiles):
        part = pl.ds(index * tile, tile)
        own = proj_own[:, pl.ds(pl.multiple_of(base + index * tile, 128), tile)]
        both = jnp.concatenate([own, weights[:, part]], axis=0)
        out = jnp.dot(heads_out, both, preferred_element_type=F32)
        out_tiles[:, part] = out.astype(BF16)
        sends.append(
            pltpu.make_async_copy(out_tiles.at[:, part], out_ref.at[:, part], out_sems.at[index])
        )
        sends[-1].start()
    for send in sends:
        send.wait()


def per_device(
    count, queries_nope, queries_rope, latent, key_rope, key_up, value_up, out_proj, span_order
):
    rows = latent.shape[0]
    depth, width = out_proj.shape[0], out_proj.shape[1] // 2
    heads = 2 * (key_up.shape[1] // DH)
    query_rows = heads * rows
    direct = count == 8
    small = pltpu.CompilerParams(vmem_limit_bytes=SMALL_VMEM)

    def in_hbm(*arrays):
        return [pltpu.with_memory_space_constraint(array, pltpu.HBM) for array in arrays]

    def other_core(array):
        return lax.ppermute(array, "heads", [(0, 1), (1, 0)])

    def partners(array, steps, cores=(0, 1)):
        pairs = [
            (2 * index + core, 2 * (index ^ steps[core]) + core)
            for index in range(count)
            for core in cores
        ]
        return lax.ppermute(array, ("ctx", "heads"), pairs)

    def attend(name, estimate, queries, bias, chunks, old=(), passed=(), paired=False):
        return pl.pallas_call(
            functools.partial(chunks_kernel, len(chunks), len(old), paired),
            out_shape=[jax.ShapeDtypeStruct((query_rows, size), F32) for size in (1, 1, DC)]
            + [jax.ShapeDtypeStruct(chunk.shape, BF16) for chunk in passed],
            in_specs=[vmem()] * (3 + len(chunks) + len(old) + len(passed)),
            out_specs=[vmem()] * (3 + len(passed)),
            scratch_shapes=[pltpu.VMEM((bias.shape[2], DC + DR), BF16)],
            compiler_params=small,
            cost_estimate=cost(estimate),
            name=name,
        )(*queries, bias, *chunks, *old, *passed)

    packed = pl.pallas_call(
        pack_kernel,
        out_shape=jax.ShapeDtypeStruct((2 * rows + rows // 4, DC // 2), BF16),
        in_specs=[hbm()] * 2,
        out_specs=vmem(),
        scratch_shapes=[
            pltpu.VMEM((DR, rows), BF16),
            pltpu.SemaphoreType.DMA((3,)),
        ],
        compiler_params=small,
        name="pack",
    )(*in_hbm(latent, key_rope.T))
    if direct:
        order = [
            [(0, 0), NEAR],
            [CORNER, NEAR[::-1], FAR, FAR[::-1], RELAYED],
            [RELAYED[::-1]],
        ]
        bias_shapes = [(1, rows, len(steps) * rows) for steps in order]
    else:
        order = None
        bias_shapes = [(count // BLOCK_CHUNKS, rows, BLOCK_CHUNKS * rows)]
    outs = pl.pallas_call(
        functools.partial(prepare_kernel, order),
        out_shape=[jax.ShapeDtypeStruct((query_rows // 2, DC + DR), BF16)]
        + [jax.ShapeDtypeStruct(shape, F32) for shape in bias_shapes]
        + [jax.ShapeDtypeStruct((depth, width + DC // depth * key_up.shape[1]), BF16)],
        in_specs=[hbm()] * 6 + [anywhere()],
        out_specs=[vmem()] * (len(bias_shapes) + 2),
        scratch_shapes=[
            pltpu.VMEM(queries_nope.shape, BF16),
            pltpu.VMEM(queries_rope.shape, BF16),
            pltpu.VMEM(key_up.shape, BF16),
            pltpu.SMEM(span_order.shape, jnp.int32),
            pltpu.VMEM(value_up.shape, BF16),
            pltpu.SemaphoreType.DMA((6,)),
        ],
        compiler_params=small,
        cost_estimate=cost(PREPARE_COST),
        name="prepare",
    )(*in_hbm(queries_nope, queries_rope, key_up, span_order, value_up, out_proj), packed)
    queries, biases = outs[0], outs[1:-1]
    weights_other = other_core(outs[-1])
    both = [queries, other_core(queries)]

    if direct:
        far = partners(packed, FAR)
        near = partners(packed, NEAR)
        corner = partners(packed, CORNER, cores=(1,))
        relayed = partners(far, (1, 1))
        gated = pl.pallas_call(
            gate_kernel,
            out_shape=jax.ShapeDtypeStruct(far.shape, BF16),
            in_specs=[vmem()],
            out_specs=vmem(),
            compiler_params=small,
            cost_estimate=cost(GATE_COST),
            name="gate",
        )(far)
        *running, far_after = attend(
            "first", FIRST_COST, both, biases[0], [packed, near], passed=[gated]
        )
        last = [other_core(relayed)]
        running = attend(
            "second",
            SECOND_COST,
            both,
            biases[1],
            [corner, other_core(corner), other_core(near), far, other_core(far_after), relayed],
            running,
            paired=True,
        )
    else:
        last = []
        running = pl.pallas_call(
            gathered_kernel,
            out_shape=[jax.ShapeDtypeStruct((query_rows, size), F32) for size in (1, 1, DC)],
            in_specs=[vmem()] * 4,
            out_specs=[vmem()] * 3,
            scratch_shapes=[pltpu.VMEM((BLOCK_CHUNKS * rows, DC + DR), BF16)],
            compiler_params=pltpu.CompilerParams(vmem_limit_bytes=LARGE_VMEM),
            name="gathered",
        )(*both, biases[0], lax.all_gather(packed, "ctx", axis=0))

    tiles = 4 if width % 512 == 0 else 1
    return pl.pallas_call(
        functools.partial(finish_kernel, heads, len(last)),
        out_shape=jax.ShapeDtypeStruct((rows, width), BF16),
        in_specs=[vmem()] * (5 + len(biases[2:]) + len(last) + 3),
        out_specs=anywhere(),
        scratch_shapes=[
            pltpu.VMEM((rows, width), BF16),
            pltpu.VMEM((rows, DC + DR), BF16),
            pltpu.SemaphoreType.DMA((tiles,)),
        ],
        compiler_params=small,
        name="finish",
    )(*both, *running, *biases[2:], *last, value_up, out_proj, weights_other)


def solution(mesh):
    in_specs = (
        P(("docs", "ctx"), "heads"),
        P(("docs", "ctx"), "heads"),
        P(("docs", "ctx"), None),
        P(("docs", "ctx"), None),
        P(None, "heads"),
        P(None, "heads"),
        P("heads", None),
        P("docs"),
    )
    out_specs = P(("docs", "ctx"), "heads")
    return jax.shard_map(
        functools.partial(per_device, mesh.shape["ctx"]),
        mesh=mesh,
        in_specs=in_specs,
        out_specs=out_specs,
        check_vma=False,
    )
```

```python
import functools
import math

import jax
import jax.numpy as jnp
from jax import lax
from jax.experimental import pallas as pl
from jax.experimental.pallas import tpu as pltpu
from jax.sharding import PartitionSpec as P

DC = 512
DH = 128
DR = 64
BF16 = jnp.bfloat16
F32 = jnp.float32
MASKED = -1e30
BLOCK_CHUNKS = 8
PREPARE_COST, ROOM_COST, GATE_COST, FIRST_COST, SECOND_COST = 0, 4, 8, 20, 1
SMALL_VMEM = 20 * 1024 * 1024
LARGE_VMEM = 56 * 1024 * 1024
FAR = (6, 4)
NEAR = (1, 2)
CORNER = (3, 3)
RELAYED = (7, 5)


def vmem():
    return pl.BlockSpec(memory_space=pltpu.VMEM)


def anywhere():
    return pl.BlockSpec(memory_space=pl.ANY)


def hbm():
    return pl.BlockSpec(memory_space=pltpu.HBM)


def cost(microseconds):
    return pl.CostEstimate(flops=int(microseconds * 1.1e9), bytes_accessed=0, transcendentals=0)


def pack_kernel(latent, key_rope_turned, out_ref, turned, sems):
    rows = latent.shape[0]
    group = rows // 6
    half = DC // 2
    fetches = [pltpu.make_async_copy(key_rope_turned, turned, sems.at[2])]
    for side in range(2):
        fetches.append(
            pltpu.make_async_copy(
                latent.at[:, pl.ds(side * half, half)],
                out_ref.at[pl.ds(side * rows, rows)],
                sems.at[side],
            )
        )
    for fetch in fetches:
        fetch.start()
    fetches[0].wait()
    rope = turned[...].astype(F32).T.astype(BF16)
    first = 0
    base = 2 * rows
    for size in (group, group // 2):
        parts = [rope[first + index * size : first + (index + 1) * size] for index in range(4)]
        out_ref[pl.ds(base, size), :] = jnp.concatenate(parts, axis=1)
        first += 4 * size
        base += size
    for fetch in fetches[1:]:
        fetch.wait()


def gate_kernel(chunk, out_ref):
    out_ref[...] = chunk[...]


def unpack(chunk, keys, base, other=None):
    chunk = chunk[...]
    if other is not None:
        chunk = jnp.where(lax.axis_index("heads") == 0, other[...], chunk)
    rows = 4 * chunk.shape[0] // 9
    group = rows // 6
    keys[pl.ds(base, rows), : DC // 2] = chunk[:rows]
    keys[pl.ds(base, rows), DC // 2 : DC] = chunk[rows : 2 * rows]
    place = 2 * rows
    for size in (group, group // 2):
        for index in range(4):
            part = chunk[place : place + size, index * DR : (index + 1) * DR]
            keys[pl.ds(base, size), DC:] = part
            base += size
        place += size


def prepare_kernel(order, *refs):
    sources, out_proj, rest = refs[:5], refs[5], refs[7:]
    outs, copied, sems = rest[:-6], rest[-6:-1], rest[-1]
    weights = outs[-1]
    depth, width = out_proj.shape[0], out_proj.shape[1] // 2
    fetches = [
        pltpu.make_async_copy(source, target, sems.at[index])
        for index, (source, target) in enumerate(zip(sources, copied))
    ]
    base = pl.multiple_of((1 - lax.axis_index("heads")) * width, 128)
    for fetch in fetches:
        fetch.start()
    nope, rope, up, span_order, value_up = copied
    weights[:, :width] = out_proj[:, pl.ds(base, width)]
    rows = nope.shape[0]
    heads = nope.shape[1] // DH
    span_rows = rows // 2
    for fetch in fetches[:3]:
        fetch.wait()
    own_index = lax.axis_index("ctx")
    core = lax.axis_index("heads")
    for head in range(heads):
        latent = lax.dot_general(
            nope[:, head * DH : (head + 1) * DH],
            up[:, head * DH : (head + 1) * DH],
            (((1,), (1,)), ((), ())),
            preferred_element_type=F32,
        )
        part = pl.ds(head * rows, rows)
        outs[0][part, :DC] = latent.astype(BF16)
        outs[0][part, DC:] = rope[:, head * DR : (head + 1) * DR]
    biases = outs[1:-1]
    fetches[3].wait()
    row = lax.broadcasted_iota(jnp.int32, (rows, 1), 0)
    query_pos = jnp.where(
        row < span_rows,
        span_order[2 * own_index] * span_rows + row,
        span_order[2 * own_index + 1] * span_rows + row - span_rows,
    )

    def bias_of(owners):
        column = lax.broadcasted_iota(jnp.int32, (1, len(owners) * rows), 1)
        key_pos = jnp.zeros(column.shape, jnp.int32)
        for index, owner in enumerate(owners):
            for side in range(2):
                start = index * rows + side * span_rows
                first = span_order[2 * owner + side] * span_rows
                key_pos = jnp.where(column >= start, first + column - start, key_pos)
        return jnp.where(key_pos <= query_pos, F32(0.0), F32(MASKED))

    if order is not None:
        for steps, bias_ref in zip(order, biases):
            bias_ref[0] = bias_of(
                [own_index ^ jnp.where(core == 0, step[0], step[1]) for step in steps]
            )
    else:
        bias_ref = biases[0]

        def step(block, carry):
            bias_ref[block] = bias_of([block * BLOCK_CHUNKS + index for index in range(BLOCK_CHUNKS)])
            return carry

        lax.fori_loop(0, bias_ref.shape[0], step, 0)

    fetches[4].wait()
    columns = value_up.shape[1]
    for block in range(DC // depth):
        part = value_up[block * depth : (block + 1) * depth, :]
        weights[:, width + block * columns : width + (block + 1) * columns] = part


def attend_block(queries, keys, bias, old):
    copies = len(queries) * queries[0].shape[0] // bias.shape[0]
    scale = math.log2(math.e) / math.sqrt(DH + DR)
    heads = jnp.concatenate([part[...] for part in queries], axis=0)
    scores = lax.dot_general(
        heads, keys[...], (((1,), (1,)), ((), ())), preferred_element_type=F32
    )
    scores = scores + jnp.concatenate([bias] * copies, axis=0)
    top = jnp.max(scores, axis=-1, keepdims=True)
    if old is not None:
        top = jnp.maximum(old[0], top)
        rescale = jnp.exp2((old[0] - top) * scale)
    expo = jnp.exp2((scores - top) * scale)
    total = jnp.sum(expo, axis=-1, keepdims=True)
    added = jnp.dot(expo.astype(BF16), keys[:, :DC], preferred_element_type=F32)
    if old is not None:
        total = old[1] * rescale + total
        added = old[2] * rescale + added
    return top, total, added


def chunks_kernel(chunk_count, old_count, paired, *rest):
    queries, bias, rest = rest[:2], rest[2], rest[3:]
    chunks, rest = rest[:chunk_count], rest[chunk_count:]
    old, rest = rest[:old_count], rest[old_count:]
    if len(rest) == 6:
        passed, handed = rest[0], rest[4]
        handed[...] = passed[...]
        rest = rest[1:4] + rest[5:]
    running, keys = rest[:3], rest[3]
    rows = bias.shape[1]
    if paired:
        unpack(chunks[0], keys, 0, chunks[1])
        chunks = chunks[1:]
    for index, chunk in enumerate(chunks):
        if index or not paired:
            unpack(chunk, keys, index * rows)
    before = [state[...] for state in old] if old else None
    values = attend_block(queries, keys, bias[0], before)
    for state, value in zip(running, values):
        state[...] = value


def gathered_kernel(queries_own, queries_other, bias, gathered, *rest):
    queries = (queries_own, queries_other)
    running, keys = rest[:3], rest[3]
    blocks, rows, _ = bias.shape

    def fill(block):
        for index in range(BLOCK_CHUNKS):
            unpack(gathered.at[block * BLOCK_CHUNKS + index], keys, index * rows)

    first = lax.axis_index("ctx") // BLOCK_CHUNKS
    fill(first)
    values = attend_block(queries, keys, bias[first], None)
    for state, value in zip(running, values):
        state[...] = value

    def step(index, carry):
        block = index + jnp.where(index >= first, 1, 0)
        fill(block)
        new = attend_block(queries, keys, bias[block], [state[...] for state in running])
        for state, value in zip(running, new):
            state[...] = value
        return carry

    lax.fori_loop(0, blocks - 1, step, 0)


def finish_kernel(heads, chunk_count, *rest):
    queries, (top, total, context), rest = rest[:2], rest[2:5], rest[5:]
    bias, chunks = rest[:chunk_count][:1], rest[1 : 1 + chunk_count]
    rest = rest[len(bias) + len(chunks) :]
    value_own, proj_own, weights, out_ref, out_tiles, keys, out_sems = rest
    rows, width = out_ref.shape
    running = (top[...], total[...], context[...])
    if chunk_count:
        for index, chunk in enumerate(chunks):
            unpack(chunk, keys, index * rows)
        running = attend_block(queries, keys, bias[0][0], running)
    mixed = (running[2] * (1.0 / running[1])).astype(BF16)
    half = heads // 2
    depth = weights.shape[0]
    base = lax.axis_index("heads") * width
    parts = []
    for place in range(heads):
        group, head = divmod(place, half)
        if group == 0:
            value = value_own[:, head * DH : (head + 1) * DH]
        else:
            starts = [width + (block * half + head) * DH for block in range(DC // depth)]
            value = jnp.concatenate([weights[:, start : start + DH] for start in starts], axis=0)
        per_head = jnp.dot(
            mixed[place * rows : (place + 1) * rows], value, preferred_element_type=F32
        )
        parts.append(per_head.astype(BF16))
    heads_out = jnp.concatenate(parts, axis=1)
    tiles = out_sems.shape[0]
    tile = width // tiles
    sends = []
    for index in range(tiles):
        part = pl.ds(index * tile, tile)
        own = proj_own[:, pl.ds(pl.multiple_of(base + index * tile, 128), tile)]
        both = jnp.concatenate([own, weights[:, part]], axis=0)
        out = jnp.dot(heads_out, both, preferred_element_type=F32)
        out_tiles[:, part] = out.astype(BF16)
        sends.append(
            pltpu.make_async_copy(out_tiles.at[:, part], out_ref.at[:, part], out_sems.at[index])
        )
        sends[-1].start()
    for send in sends:
        send.wait()


def per_device(
    count, queries_nope, queries_rope, latent, key_rope, key_up, value_up, out_proj, span_order
):
    rows = latent.shape[0]
    depth, width = out_proj.shape[0], out_proj.shape[1] // 2
    heads = 2 * (key_up.shape[1] // DH)
    query_rows = heads * rows
    direct = count == 8
    small = pltpu.CompilerParams(vmem_limit_bytes=SMALL_VMEM)

    def in_hbm(*arrays):
        return [pltpu.with_memory_space_constraint(array, pltpu.HBM) for array in arrays]

    def other_core(array):
        return lax.ppermute(array, "heads", [(0, 1), (1, 0)])

    def partners(array, steps, cores=(0, 1)):
        pairs = [
            (2 * index + core, 2 * (index ^ steps[core]) + core)
            for index in range(count)
            for core in cores
        ]
        return lax.ppermute(array, ("ctx", "heads"), pairs)

    def attend(name, estimate, queries, bias, chunks, old=(), passed=(), paired=False):
        return pl.pallas_call(
            functools.partial(chunks_kernel, len(chunks), len(old), paired),
            out_shape=[jax.ShapeDtypeStruct((query_rows, size), F32) for size in (1, 1, DC)]
            + [jax.ShapeDtypeStruct(chunk.shape, BF16) for chunk in passed],
            in_specs=[vmem()] * (3 + len(chunks) + len(old) + len(passed)),
            out_specs=[vmem()] * (3 + len(passed)),
            scratch_shapes=[pltpu.VMEM((bias.shape[2], DC + DR), BF16)],
            compiler_params=small,
            cost_estimate=cost(estimate),
            name=name,
        )(*queries, bias, *chunks, *old, *passed)

    packed = pl.pallas_call(
        pack_kernel,
        out_shape=jax.ShapeDtypeStruct((2 * rows + rows // 4, DC // 2), BF16),
        in_specs=[hbm()] * 2,
        out_specs=vmem(),
        scratch_shapes=[
            pltpu.VMEM((DR, rows), BF16),
            pltpu.SemaphoreType.DMA((3,)),
        ],
        compiler_params=small,
        name="pack",
    )(*in_hbm(latent, key_rope.T))
    if direct:
        order = [
            [(0, 0), NEAR],
            [CORNER, NEAR[::-1], FAR, FAR[::-1], RELAYED],
            [RELAYED[::-1]],
        ]
        bias_shapes = [(1, rows, len(steps) * rows) for steps in order]
    else:
        order = None
        bias_shapes = [(count // BLOCK_CHUNKS, rows, BLOCK_CHUNKS * rows)]
    outs = pl.pallas_call(
        functools.partial(prepare_kernel, order),
        out_shape=[jax.ShapeDtypeStruct((query_rows // 2, DC + DR), BF16)]
        + [jax.ShapeDtypeStruct(shape, F32) for shape in bias_shapes]
        + [jax.ShapeDtypeStruct((depth, width + DC // depth * key_up.shape[1]), BF16)],
        in_specs=[hbm()] * 5 + [vmem(), anywhere()],
        out_specs=[vmem()] * (len(bias_shapes) + 2),
        scratch_shapes=[
            pltpu.VMEM(queries_nope.shape, BF16),
            pltpu.VMEM(queries_rope.shape, BF16),
            pltpu.VMEM(key_up.shape, BF16),
            pltpu.SMEM(span_order.shape, jnp.int32),
            pltpu.VMEM(value_up.shape, BF16),
            pltpu.SemaphoreType.DMA((5,)),
        ],
        compiler_params=small,
        cost_estimate=cost(PREPARE_COST),
        name="prepare",
    )(*in_hbm(queries_nope, queries_rope, key_up, span_order, value_up), out_proj, packed)
    queries, biases = outs[0], outs[1:-1]
    weights_other = other_core(outs[-1])
    both = [queries, other_core(queries)]

    if direct:
        far = partners(packed, FAR)
        room = pl.pallas_call(
            gate_kernel,
            out_shape=jax.ShapeDtypeStruct(packed.shape, BF16),
            in_specs=[vmem()],
            out_specs=vmem(),
            compiler_params=small,
            cost_estimate=cost(ROOM_COST),
            name="room",
        )(packed)
        near = partners(room, NEAR)
        corner = partners(room, CORNER, cores=(1,))
        relayed = partners(far, (1, 1))
        gated = pl.pallas_call(
            gate_kernel,
            out_shape=jax.ShapeDtypeStruct(far.shape, BF16),
            in_specs=[vmem()],
            out_specs=vmem(),
            compiler_params=small,
            cost_estimate=cost(GATE_COST),
            name="gate",
        )(far)
        *running, far_after = attend(
            "first", FIRST_COST, both, biases[0], [packed, near], passed=[gated]
        )
        last = [other_core(relayed)]
        running = attend(
            "second",
            SECOND_COST,
            both,
            biases[1],
            [corner, other_core(corner), other_core(near), far, other_core(far_after), relayed],
            running,
            paired=True,
        )
    else:
        last = []
        running = pl.pallas_call(
            gathered_kernel,
            out_shape=[jax.ShapeDtypeStruct((query_rows, size), F32) for size in (1, 1, DC)],
            in_specs=[vmem()] * 4,
            out_specs=[vmem()] * 3,
            scratch_shapes=[pltpu.VMEM((BLOCK_CHUNKS * rows, DC + DR), BF16)],
            compiler_params=pltpu.CompilerParams(vmem_limit_bytes=LARGE_VMEM),
            name="gathered",
        )(*both, biases[0], lax.all_gather(packed, "ctx", axis=0))

    tiles = 7 if width % 896 == 0 else 1
    return pl.pallas_call(
        functools.partial(finish_kernel, heads, len(last)),
        out_shape=jax.ShapeDtypeStruct((rows, width), BF16),
        in_specs=[vmem()] * (5 + len(biases[2:]) + len(last) + 3),
        out_specs=anywhere(),
        scratch_shapes=[
            pltpu.VMEM((rows, width), BF16),
            pltpu.VMEM((rows, DC + DR), BF16),
            pltpu.SemaphoreType.DMA((tiles,)),
        ],
        compiler_params=small,
        name="finish",
    )(*both, *running, *biases[2:], *last, value_up, out_proj, weights_other)


def solution(mesh):
    in_specs = (
        P(("docs", "ctx"), "heads"),
        P(("docs", "ctx"), "heads"),
        P(("docs", "ctx"), None),
        P(("docs", "ctx"), None),
        P(None, "heads"),
        P(None, "heads"),
        P("heads", None),
        P("docs"),
    )
    out_specs = P(("docs", "ctx"), "heads")
    return jax.shard_map(
        functools.partial(per_device, mesh.shape["ctx"]),
        mesh=mesh,
        in_specs=in_specs,
        out_specs=out_specs,
        check_vma=False,
    )
```

```python
import functools
import math

import jax
import jax.numpy as jnp
from jax import lax
from jax.experimental import pallas as pl
from jax.experimental.pallas import tpu as pltpu
from jax.sharding import PartitionSpec as P

DC = 512
DH = 128
DR = 64
BF16 = jnp.bfloat16
F32 = jnp.float32
MASKED = -1e30
BLOCK_CHUNKS = 8
PREPARE_COST, ROOM_COST, GATE_COST, FIRST_COST, SECOND_COST = 0, 4, 8, 20, 1
SMALL_VMEM = 20 * 1024 * 1024
LARGE_VMEM = 56 * 1024 * 1024
FAR = (6, 4)
NEAR = (2, 1)
CORNER = (3, 3)
RELAYED = (7, 5)


def vmem():
    return pl.BlockSpec(memory_space=pltpu.VMEM)


def anywhere():
    return pl.BlockSpec(memory_space=pl.ANY)


def hbm():
    return pl.BlockSpec(memory_space=pltpu.HBM)


def cost(microseconds):
    return pl.CostEstimate(flops=int(microseconds * 1.1e9), bytes_accessed=0, transcendentals=0)


def pack_kernel(latent, key_rope_turned, out_ref, turned, sems):
    rows = latent.shape[0]
    group = rows // 6
    half = DC // 2
    fetches = [pltpu.make_async_copy(key_rope_turned, turned, sems.at[2])]
    for side in range(2):
        fetches.append(
            pltpu.make_async_copy(
                latent.at[:, pl.ds(side * half, half)],
                out_ref.at[pl.ds(side * rows, rows)],
                sems.at[side],
            )
        )
    for fetch in fetches:
        fetch.start()
    fetches[0].wait()
    rope = turned[...].astype(F32).T.astype(BF16)
    first = 0
    base = 2 * rows
    for size in (group, group // 2):
        parts = [rope[first + index * size : first + (index + 1) * size] for index in range(4)]
        out_ref[pl.ds(base, size), :] = jnp.concatenate(parts, axis=1)
        first += 4 * size
        base += size
    for fetch in fetches[1:]:
        fetch.wait()


def gate_kernel(chunk, out_ref):
    out_ref[...] = chunk[...]


def unpack(chunk, keys, base, other=None):
    chunk = chunk[...]
    if other is not None:
        chunk = jnp.where(lax.axis_index("heads") == 0, other[...], chunk)
    rows = 4 * chunk.shape[0] // 9
    group = rows // 6
    keys[pl.ds(base, rows), : DC // 2] = chunk[:rows]
    keys[pl.ds(base, rows), DC // 2 : DC] = chunk[rows : 2 * rows]
    place = 2 * rows
    for size in (group, group // 2):
        for index in range(4):
            part = chunk[place : place + size, index * DR : (index + 1) * DR]
            keys[pl.ds(base, size), DC:] = part
            base += size
        place += size


def prepare_kernel(order, *refs):
    sources, out_proj, rest = refs[:5], refs[5], refs[7:]
    outs, copied, sems = rest[:-6], rest[-6:-1], rest[-1]
    weights = outs[-1]
    depth, width = out_proj.shape[0], out_proj.shape[1] // 2
    fetches = [
        pltpu.make_async_copy(source, target, sems.at[index])
        for index, (source, target) in enumerate(zip(sources, copied))
    ]
    base = pl.multiple_of((1 - lax.axis_index("heads")) * width, 128)
    for fetch in fetches:
        fetch.start()
    nope, rope, up, span_order, value_up = copied
    weights[:, :width] = out_proj[:, pl.ds(base, width)]
    rows = nope.shape[0]
    heads = nope.shape[1] // DH
    span_rows = rows // 2
    for fetch in fetches[:3]:
        fetch.wait()
    own_index = lax.axis_index("ctx")
    core = lax.axis_index("heads")
    for head in range(heads):
        latent = lax.dot_general(
            nope[:, head * DH : (head + 1) * DH],
            up[:, head * DH : (head + 1) * DH],
            (((1,), (1,)), ((), ())),
            preferred_element_type=F32,
        )
        part = pl.ds(head * rows, rows)
        outs[0][part, :DC] = latent.astype(BF16)
        outs[0][part, DC:] = rope[:, head * DR : (head + 1) * DR]
    biases = outs[1:-1]
    fetches[3].wait()
    row = lax.broadcasted_iota(jnp.int32, (rows, 1), 0)
    query_pos = jnp.where(
        row < span_rows,
        span_order[2 * own_index] * span_rows + row,
        span_order[2 * own_index + 1] * span_rows + row - span_rows,
    )

    def bias_of(owners):
        column = lax.broadcasted_iota(jnp.int32, (1, len(owners) * rows), 1)
        key_pos = jnp.zeros(column.shape, jnp.int32)
        for index, owner in enumerate(owners):
            for side in range(2):
                start = index * rows + side * span_rows
                first = span_order[2 * owner + side] * span_rows
                key_pos = jnp.where(column >= start, first + column - start, key_pos)
        return jnp.where(key_pos <= query_pos, F32(0.0), F32(MASKED))

    if order is not None:
        for steps, bias_ref in zip(order, biases):
            bias_ref[0] = bias_of(
                [own_index ^ jnp.where(core == 0, step[0], step[1]) for step in steps]
            )
    else:
        bias_ref = biases[0]

        def step(block, carry):
            bias_ref[block] = bias_of([block * BLOCK_CHUNKS + index for index in range(BLOCK_CHUNKS)])
            return carry

        lax.fori_loop(0, bias_ref.shape[0], step, 0)

    fetches[4].wait()
    columns = value_up.shape[1]
    for block in range(DC // depth):
        part = value_up[block * depth : (block + 1) * depth, :]
        weights[:, width + block * columns : width + (block + 1) * columns] = part


def attend_block(queries, keys, bias, old):
    copies = len(queries) * queries[0].shape[0] // bias.shape[0]
    scale = math.log2(math.e) / math.sqrt(DH + DR)
    heads = jnp.concatenate([part[...] for part in queries], axis=0)
    scores = lax.dot_general(
        heads, keys[...], (((1,), (1,)), ((), ())), preferred_element_type=F32
    )
    scores = scores + jnp.concatenate([bias] * copies, axis=0)
    top = jnp.max(scores, axis=-1, keepdims=True)
    if old is not None:
        top = jnp.maximum(old[0], top)
        rescale = jnp.exp2((old[0] - top) * scale)
    expo = jnp.exp2((scores - top) * scale)
    total = jnp.sum(expo, axis=-1, keepdims=True)
    added = jnp.dot(expo.astype(BF16), keys[:, :DC], preferred_element_type=F32)
    if old is not None:
        total = old[1] * rescale + total
        added = old[2] * rescale + added
    return top, total, added


def chunks_kernel(chunk_count, old_count, paired, *rest):
    queries, bias, rest = rest[:2], rest[2], rest[3:]
    chunks, rest = rest[:chunk_count], rest[chunk_count:]
    old, rest = rest[:old_count], rest[old_count:]
    if len(rest) == 6:
        passed, handed = rest[0], rest[4]
        handed[...] = passed[...]
        rest = rest[1:4] + rest[5:]
    running, keys = rest[:3], rest[3]
    rows = bias.shape[1]
    if paired:
        unpack(chunks[0], keys, 0, chunks[1])
        chunks = chunks[1:]
    for index, chunk in enumerate(chunks):
        if index or not paired:
            unpack(chunk, keys, index * rows)
    before = [state[...] for state in old] if old else None
    values = attend_block(queries, keys, bias[0], before)
    for state, value in zip(running, values):
        state[...] = value


def gathered_kernel(queries_own, queries_other, bias, gathered, *rest):
    queries = (queries_own, queries_other)
    running, keys = rest[:3], rest[3]
    blocks, rows, _ = bias.shape

    def fill(block):
        for index in range(BLOCK_CHUNKS):
            unpack(gathered.at[block * BLOCK_CHUNKS + index], keys, index * rows)

    first = lax.axis_index("ctx") // BLOCK_CHUNKS
    fill(first)
    values = attend_block(queries, keys, bias[first], None)
    for state, value in zip(running, values):
        state[...] = value

    def step(index, carry):
        block = index + jnp.where(index >= first, 1, 0)
        fill(block)
        new = attend_block(queries, keys, bias[block], [state[...] for state in running])
        for state, value in zip(running, new):
            state[...] = value
        return carry

    lax.fori_loop(0, blocks - 1, step, 0)


def finish_kernel(heads, chunk_count, *rest):
    queries, (top, total, context), rest = rest[:2], rest[2:5], rest[5:]
    bias, chunks = rest[:chunk_count][:1], rest[1 : 1 + chunk_count]
    rest = rest[len(bias) + len(chunks) :]
    value_own, proj_own, weights, out_ref, out_tiles, keys, out_sems = rest
    rows, width = out_ref.shape
    running = (top[...], total[...], context[...])
    if chunk_count:
        for index, chunk in enumerate(chunks):
            unpack(chunk, keys, index * rows)
        running = attend_block(queries, keys, bias[0][0], running)
    mixed = (running[2] * (1.0 / running[1])).astype(BF16)
    half = heads // 2
    depth = weights.shape[0]
    base = lax.axis_index("heads") * width
    parts = []
    for place in range(heads):
        group, head = divmod(place, half)
        if group == 0:
            value = value_own[:, head * DH : (head + 1) * DH]
        else:
            starts = [width + (block * half + head) * DH for block in range(DC // depth)]
            value = jnp.concatenate([weights[:, start : start + DH] for start in starts], axis=0)
        per_head = jnp.dot(
            mixed[place * rows : (place + 1) * rows], value, preferred_element_type=F32
        )
        parts.append(per_head.astype(BF16))
    heads_out = jnp.concatenate(parts, axis=1)
    tiles = out_sems.shape[0]
    tile = width // tiles
    sends = []
    for index in range(tiles):
        part = pl.ds(index * tile, tile)
        own = proj_own[:, pl.ds(pl.multiple_of(base + index * tile, 128), tile)]
        both = jnp.concatenate([own, weights[:, part]], axis=0)
        out = jnp.dot(heads_out, both, preferred_element_type=F32)
        out_tiles[:, part] = out.astype(BF16)
        sends.append(
            pltpu.make_async_copy(out_tiles.at[:, part], out_ref.at[:, part], out_sems.at[index])
        )
        sends[-1].start()
    for send in sends:
        send.wait()


def per_device(
    count, queries_nope, queries_rope, latent, key_rope, key_up, value_up, out_proj, span_order
):
    rows = latent.shape[0]
    depth, width = out_proj.shape[0], out_proj.shape[1] // 2
    heads = 2 * (key_up.shape[1] // DH)
    query_rows = heads * rows
    direct = count == 8
    small = pltpu.CompilerParams(vmem_limit_bytes=SMALL_VMEM)

    def in_hbm(*arrays):
        return [pltpu.with_memory_space_constraint(array, pltpu.HBM) for array in arrays]

    def other_core(array):
        return lax.ppermute(array, "heads", [(0, 1), (1, 0)])

    def partners(array, steps, cores=(0, 1)):
        pairs = [
            (2 * index + core, 2 * (index ^ steps[core]) + core)
            for index in range(count)
            for core in cores
        ]
        return lax.ppermute(array, ("ctx", "heads"), pairs)

    def attend(name, estimate, queries, bias, chunks, old=(), passed=(), paired=False):
        return pl.pallas_call(
            functools.partial(chunks_kernel, len(chunks), len(old), paired),
            out_shape=[jax.ShapeDtypeStruct((query_rows, size), F32) for size in (1, 1, DC)]
            + [jax.ShapeDtypeStruct(chunk.shape, BF16) for chunk in passed],
            in_specs=[vmem()] * (3 + len(chunks) + len(old) + len(passed)),
            out_specs=[vmem()] * (3 + len(passed)),
            scratch_shapes=[pltpu.VMEM((bias.shape[2], DC + DR), BF16)],
            compiler_params=small,
            cost_estimate=cost(estimate),
            name=name,
        )(*queries, bias, *chunks, *old, *passed)

    packed = pl.pallas_call(
        pack_kernel,
        out_shape=jax.ShapeDtypeStruct((2 * rows + rows // 4, DC // 2), BF16),
        in_specs=[hbm()] * 2,
        out_specs=vmem(),
        scratch_shapes=[
            pltpu.VMEM((DR, rows), BF16),
            pltpu.SemaphoreType.DMA((3,)),
        ],
        compiler_params=small,
        name="pack",
    )(*in_hbm(latent, key_rope.T))
    if direct:
        order = [
            [(0, 0), NEAR],
            [CORNER, NEAR[::-1], FAR, FAR[::-1], RELAYED],
            [RELAYED[::-1]],
        ]
        bias_shapes = [(1, rows, len(steps) * rows) for steps in order]
    else:
        order = None
        bias_shapes = [(count // BLOCK_CHUNKS, rows, BLOCK_CHUNKS * rows)]
    outs = pl.pallas_call(
        functools.partial(prepare_kernel, order),
        out_shape=[jax.ShapeDtypeStruct((query_rows // 2, DC + DR), BF16)]
        + [jax.ShapeDtypeStruct(shape, F32) for shape in bias_shapes]
        + [jax.ShapeDtypeStruct((depth, width + DC // depth * key_up.shape[1]), BF16)],
        in_specs=[hbm()] * 5 + [vmem(), anywhere()],
        out_specs=[vmem()] * (len(bias_shapes) + 2),
        scratch_shapes=[
            pltpu.VMEM(queries_nope.shape, BF16),
            pltpu.VMEM(queries_rope.shape, BF16),
            pltpu.VMEM(key_up.shape, BF16),
            pltpu.SMEM(span_order.shape, jnp.int32),
            pltpu.VMEM(value_up.shape, BF16),
            pltpu.SemaphoreType.DMA((5,)),
        ],
        compiler_params=small,
        cost_estimate=cost(PREPARE_COST),
        name="prepare",
    )(*in_hbm(queries_nope, queries_rope, key_up, span_order, value_up), out_proj, packed)
    queries, biases = outs[0], outs[1:-1]
    weights_other = other_core(outs[-1])
    both = [queries, other_core(queries)]

    if direct:
        far = partners(packed, FAR)
        room = pl.pallas_call(
            gate_kernel,
            out_shape=jax.ShapeDtypeStruct(packed.shape, BF16),
            in_specs=[vmem()],
            out_specs=vmem(),
            compiler_params=small,
            cost_estimate=cost(ROOM_COST),
            name="room",
        )(packed)
        near = partners(room, NEAR)
        corner = partners(room, CORNER, cores=(1,))
        relayed = partners(far, (1, 1))
        gated = pl.pallas_call(
            gate_kernel,
            out_shape=jax.ShapeDtypeStruct(far.shape, BF16),
            in_specs=[vmem()],
            out_specs=vmem(),
            compiler_params=small,
            cost_estimate=cost(GATE_COST),
            name="gate",
        )(far)
        *running, far_after = attend(
            "first", FIRST_COST, both, biases[0], [packed, near], passed=[gated]
        )
        last = [other_core(relayed)]
        running = attend(
            "second",
            SECOND_COST,
            both,
            biases[1],
            [corner, other_core(corner), other_core(near), far, other_core(far_after), relayed],
            running,
            paired=True,
        )
    else:
        last = []
        running = pl.pallas_call(
            gathered_kernel,
            out_shape=[jax.ShapeDtypeStruct((query_rows, size), F32) for size in (1, 1, DC)],
            in_specs=[vmem()] * 4,
            out_specs=[vmem()] * 3,
            scratch_shapes=[pltpu.VMEM((BLOCK_CHUNKS * rows, DC + DR), BF16)],
            compiler_params=pltpu.CompilerParams(vmem_limit_bytes=LARGE_VMEM),
            name="gathered",
        )(*both, biases[0], lax.all_gather(packed, "ctx", axis=0))

    tiles = 7 if width % 896 == 0 else 1
    return pl.pallas_call(
        functools.partial(finish_kernel, heads, len(last)),
        out_shape=jax.ShapeDtypeStruct((rows, width), BF16),
        in_specs=[vmem()] * (5 + len(biases[2:]) + len(last) + 3),
        out_specs=anywhere(),
        scratch_shapes=[
            pltpu.VMEM((rows, width), BF16),
            pltpu.VMEM((rows, DC + DR), BF16),
            pltpu.SemaphoreType.DMA((tiles,)),
        ],
        compiler_params=small,
        name="finish",
    )(*both, *running, *biases[2:], *last, value_up, out_proj, weights_other)


def solution(mesh):
    in_specs = (
        P(("docs", "ctx"), "heads"),
        P(("docs", "ctx"), "heads"),
        P(("docs", "ctx"), None),
        P(("docs", "ctx"), None),
        P(None, "heads"),
        P(None, "heads"),
        P("heads", None),
        P("docs"),
    )
    out_specs = P(("docs", "ctx"), "heads")
    return jax.shard_map(
        functools.partial(per_device, mesh.shape["ctx"]),
        mesh=mesh,
        in_specs=in_specs,
        out_specs=out_specs,
        check_vma=False,
    )
```

```python
import functools
import math

import jax
import jax.numpy as jnp
from jax import lax
from jax.experimental import pallas as pl
from jax.experimental.pallas import tpu as pltpu
from jax.sharding import PartitionSpec as P

DC = 512
DH = 128
DR = 64
BF16 = jnp.bfloat16
F32 = jnp.float32
MASKED = -1e30
BLOCK_CHUNKS = 8
PREPARE_COST, ROOM_COST, GATE_COST, FIRST_COST, SECOND_COST = 0, 4, 8, 20, 1
SMALL_VMEM = 20 * 1024 * 1024
LARGE_VMEM = 56 * 1024 * 1024
FAR = (4, 6)
NEAR = (2, 1)
CORNER = (3, 3)
RELAYED = (5, 7)


def vmem():
    return pl.BlockSpec(memory_space=pltpu.VMEM)


def anywhere():
    return pl.BlockSpec(memory_space=pl.ANY)


def hbm():
    return pl.BlockSpec(memory_space=pltpu.HBM)


def cost(microseconds):
    return pl.CostEstimate(flops=int(microseconds * 1.1e9), bytes_accessed=0, transcendentals=0)


def pack_kernel(latent, key_rope_turned, out_ref, turned, sems):
    rows = latent.shape[0]
    group = rows // 6
    half = DC // 2
    fetches = [pltpu.make_async_copy(key_rope_turned, turned, sems.at[2])]
    for side in range(2):
        fetches.append(
            pltpu.make_async_copy(
                latent.at[:, pl.ds(side * half, half)],
                out_ref.at[pl.ds(side * rows, rows)],
                sems.at[side],
            )
        )
    for fetch in fetches:
        fetch.start()
    fetches[0].wait()
    rope = turned[...].astype(F32).T.astype(BF16)
    first = 0
    base = 2 * rows
    for size in (group, group // 2):
        parts = [rope[first + index * size : first + (index + 1) * size] for index in range(4)]
        out_ref[pl.ds(base, size), :] = jnp.concatenate(parts, axis=1)
        first += 4 * size
        base += size
    for fetch in fetches[1:]:
        fetch.wait()


def gate_kernel(chunk, out_ref):
    out_ref[...] = chunk[...]


def unpack(chunk, keys, base, other=None):
    chunk = chunk[...]
    if other is not None:
        chunk = jnp.where(lax.axis_index("heads") == 0, other[...], chunk)
    rows = 4 * chunk.shape[0] // 9
    group = rows // 6
    keys[pl.ds(base, rows), : DC // 2] = chunk[:rows]
    keys[pl.ds(base, rows), DC // 2 : DC] = chunk[rows : 2 * rows]
    place = 2 * rows
    for size in (group, group // 2):
        for index in range(4):
            part = chunk[place : place + size, index * DR : (index + 1) * DR]
            keys[pl.ds(base, size), DC:] = part
            base += size
        place += size


def prepare_kernel(order, *refs):
    sources, out_proj, rest = refs[:5], refs[5], refs[7:]
    outs, copied, sems = rest[:-6], rest[-6:-1], rest[-1]
    weights = outs[-1]
    depth, width = out_proj.shape[0], out_proj.shape[1] // 2
    fetches = [
        pltpu.make_async_copy(source, target, sems.at[index])
        for index, (source, target) in enumerate(zip(sources, copied))
    ]
    base = pl.multiple_of((1 - lax.axis_index("heads")) * width, 128)
    for fetch in fetches:
        fetch.start()
    nope, rope, up, span_order, value_up = copied
    weights[:, :width] = out_proj[:, pl.ds(base, width)]
    rows = nope.shape[0]
    heads = nope.shape[1] // DH
    span_rows = rows // 2
    for fetch in fetches[:3]:
        fetch.wait()
    own_index = lax.axis_index("ctx")
    core = lax.axis_index("heads")
    for head in range(heads):
        latent = lax.dot_general(
            nope[:, head * DH : (head + 1) * DH],
            up[:, head * DH : (head + 1) * DH],
            (((1,), (1,)), ((), ())),
            preferred_element_type=F32,
        )
        part = pl.ds(head * rows, rows)
        outs[0][part, :DC] = latent.astype(BF16)
        outs[0][part, DC:] = rope[:, head * DR : (head + 1) * DR]
    biases = outs[1:-1]
    fetches[3].wait()
    row = lax.broadcasted_iota(jnp.int32, (rows, 1), 0)
    query_pos = jnp.where(
        row < span_rows,
        span_order[2 * own_index] * span_rows + row,
        span_order[2 * own_index + 1] * span_rows + row - span_rows,
    )

    def bias_of(owners):
        column = lax.broadcasted_iota(jnp.int32, (1, len(owners) * rows), 1)
        key_pos = jnp.zeros(column.shape, jnp.int32)
        for index, owner in enumerate(owners):
            for side in range(2):
                start = index * rows + side * span_rows
                first = span_order[2 * owner + side] * span_rows
                key_pos = jnp.where(column >= start, first + column - start, key_pos)
        return jnp.where(key_pos <= query_pos, F32(0.0), F32(MASKED))

    if order is not None:
        for steps, bias_ref in zip(order, biases):
            bias_ref[0] = bias_of(
                [own_index ^ jnp.where(core == 0, step[0], step[1]) for step in steps]
            )
    else:
        bias_ref = biases[0]

        def step(block, carry):
            bias_ref[block] = bias_of([block * BLOCK_CHUNKS + index for index in range(BLOCK_CHUNKS)])
            return carry

        lax.fori_loop(0, bias_ref.shape[0], step, 0)

    fetches[4].wait()
    columns = value_up.shape[1]
    for block in range(DC // depth):
        part = value_up[block * depth : (block + 1) * depth, :]
        weights[:, width + block * columns : width + (block + 1) * columns] = part


def attend_block(queries, keys, bias, old):
    copies = len(queries) * queries[0].shape[0] // bias.shape[0]
    scale = math.log2(math.e) / math.sqrt(DH + DR)
    heads = jnp.concatenate([part[...] for part in queries], axis=0)
    scores = lax.dot_general(
        heads, keys[...], (((1,), (1,)), ((), ())), preferred_element_type=F32
    )
    scores = scores + jnp.concatenate([bias] * copies, axis=0)
    top = jnp.max(scores, axis=-1, keepdims=True)
    if old is not None:
        top = jnp.maximum(old[0], top)
        rescale = jnp.exp2((old[0] - top) * scale)
    expo = jnp.exp2((scores - top) * scale)
    total = jnp.sum(expo, axis=-1, keepdims=True)
    added = jnp.dot(expo.astype(BF16), keys[:, :DC], preferred_element_type=F32)
    if old is not None:
        total = old[1] * rescale + total
        added = old[2] * rescale + added
    return top, total, added


def chunks_kernel(chunk_count, old_count, paired, *rest):
    queries, bias, rest = rest[:2], rest[2], rest[3:]
    chunks, rest = rest[:chunk_count], rest[chunk_count:]
    old, rest = rest[:old_count], rest[old_count:]
    if len(rest) == 6:
        passed, handed = rest[0], rest[4]
        handed[...] = passed[...]
        rest = rest[1:4] + rest[5:]
    running, keys = rest[:3], rest[3]
    rows = bias.shape[1]
    if paired:
        unpack(chunks[0], keys, 0, chunks[1])
        chunks = chunks[1:]
    for index, chunk in enumerate(chunks):
        if index or not paired:
            unpack(chunk, keys, index * rows)
    before = [state[...] for state in old] if old else None
    values = attend_block(queries, keys, bias[0], before)
    for state, value in zip(running, values):
        state[...] = value


def gathered_kernel(queries_own, queries_other, bias, gathered, *rest):
    queries = (queries_own, queries_other)
    running, keys = rest[:3], rest[3]
    blocks, rows, _ = bias.shape

    def fill(block):
        for index in range(BLOCK_CHUNKS):
            unpack(gathered.at[block * BLOCK_CHUNKS + index], keys, index * rows)

    first = lax.axis_index("ctx") // BLOCK_CHUNKS
    fill(first)
    values = attend_block(queries, keys, bias[first], None)
    for state, value in zip(running, values):
        state[...] = value

    def step(index, carry):
        block = index + jnp.where(index >= first, 1, 0)
        fill(block)
        new = attend_block(queries, keys, bias[block], [state[...] for state in running])
        for state, value in zip(running, new):
            state[...] = value
        return carry

    lax.fori_loop(0, blocks - 1, step, 0)


def finish_kernel(heads, chunk_count, *rest):
    queries, (top, total, context), rest = rest[:2], rest[2:5], rest[5:]
    bias, chunks = rest[:chunk_count][:1], rest[1 : 1 + chunk_count]
    rest = rest[len(bias) + len(chunks) :]
    value_own, proj_own, weights, out_ref, out_tiles, keys, out_sems = rest
    rows, width = out_ref.shape
    running = (top[...], total[...], context[...])
    if chunk_count:
        for index, chunk in enumerate(chunks):
            unpack(chunk, keys, index * rows)
        running = attend_block(queries, keys, bias[0][0], running)
    mixed = (running[2] * (1.0 / running[1])).astype(BF16)
    half = heads // 2
    depth = weights.shape[0]
    base = lax.axis_index("heads") * width
    parts = []
    for place in range(heads):
        group, head = divmod(place, half)
        if group == 0:
            value = value_own[:, head * DH : (head + 1) * DH]
        else:
            starts = [width + (block * half + head) * DH for block in range(DC // depth)]
            value = jnp.concatenate([weights[:, start : start + DH] for start in starts], axis=0)
        per_head = jnp.dot(
            mixed[place * rows : (place + 1) * rows], value, preferred_element_type=F32
        )
        parts.append(per_head.astype(BF16))
    heads_out = jnp.concatenate(parts, axis=1)
    tiles = out_sems.shape[0]
    tile = width // tiles
    sends = []
    for index in range(tiles):
        part = pl.ds(index * tile, tile)
        own = proj_own[:, pl.ds(pl.multiple_of(base + index * tile, 128), tile)]
        both = jnp.concatenate([own, weights[:, part]], axis=0)
        out = jnp.dot(heads_out, both, preferred_element_type=F32)
        out_tiles[:, part] = out.astype(BF16)
        sends.append(
            pltpu.make_async_copy(out_tiles.at[:, part], out_ref.at[:, part], out_sems.at[index])
        )
        sends[-1].start()
    for send in sends:
        send.wait()


def per_device(
    count, queries_nope, queries_rope, latent, key_rope, key_up, value_up, out_proj, span_order
):
    rows = latent.shape[0]
    depth, width = out_proj.shape[0], out_proj.shape[1] // 2
    heads = 2 * (key_up.shape[1] // DH)
    query_rows = heads * rows
    direct = count == 8
    small = pltpu.CompilerParams(vmem_limit_bytes=SMALL_VMEM)

    def in_hbm(*arrays):
        return [pltpu.with_memory_space_constraint(array, pltpu.HBM) for array in arrays]

    def other_core(array):
        return lax.ppermute(array, "heads", [(0, 1), (1, 0)])

    def partners(array, steps, cores=(0, 1)):
        pairs = [
            (2 * index + core, 2 * (index ^ steps[core]) + core)
            for index in range(count)
            for core in cores
        ]
        return lax.ppermute(array, ("ctx", "heads"), pairs)

    def attend(name, estimate, queries, bias, chunks, old=(), passed=(), paired=False):
        return pl.pallas_call(
            functools.partial(chunks_kernel, len(chunks), len(old), paired),
            out_shape=[jax.ShapeDtypeStruct((query_rows, size), F32) for size in (1, 1, DC)]
            + [jax.ShapeDtypeStruct(chunk.shape, BF16) for chunk in passed],
            in_specs=[vmem()] * (3 + len(chunks) + len(old) + len(passed)),
            out_specs=[vmem()] * (3 + len(passed)),
            scratch_shapes=[pltpu.VMEM((bias.shape[2], DC + DR), BF16)],
            compiler_params=small,
            cost_estimate=cost(estimate),
            name=name,
        )(*queries, bias, *chunks, *old, *passed)

    packed = pl.pallas_call(
        pack_kernel,
        out_shape=jax.ShapeDtypeStruct((2 * rows + rows // 4, DC // 2), BF16),
        in_specs=[hbm()] * 2,
        out_specs=vmem(),
        scratch_shapes=[
            pltpu.VMEM((DR, rows), BF16),
            pltpu.SemaphoreType.DMA((3,)),
        ],
        compiler_params=small,
        name="pack",
    )(*in_hbm(latent, key_rope.T))
    if direct:
        order = [
            [(0, 0), NEAR],
            [CORNER, NEAR[::-1], FAR, FAR[::-1], RELAYED],
            [RELAYED[::-1]],
        ]
        bias_shapes = [(1, rows, len(steps) * rows) for steps in order]
    else:
        order = None
        bias_shapes = [(count // BLOCK_CHUNKS, rows, BLOCK_CHUNKS * rows)]
    outs = pl.pallas_call(
        functools.partial(prepare_kernel, order),
        out_shape=[jax.ShapeDtypeStruct((query_rows // 2, DC + DR), BF16)]
        + [jax.ShapeDtypeStruct(shape, F32) for shape in bias_shapes]
        + [jax.ShapeDtypeStruct((depth, width + DC // depth * key_up.shape[1]), BF16)],
        in_specs=[hbm()] * 5 + [vmem(), anywhere()],
        out_specs=[vmem()] * (len(bias_shapes) + 2),
        scratch_shapes=[
            pltpu.VMEM(queries_nope.shape, BF16),
            pltpu.VMEM(queries_rope.shape, BF16),
            pltpu.VMEM(key_up.shape, BF16),
            pltpu.SMEM(span_order.shape, jnp.int32),
            pltpu.VMEM(value_up.shape, BF16),
            pltpu.SemaphoreType.DMA((5,)),
        ],
        compiler_params=small,
        cost_estimate=cost(PREPARE_COST),
        name="prepare",
    )(*in_hbm(queries_nope, queries_rope, key_up, span_order, value_up), out_proj, packed)
    queries, biases = outs[0], outs[1:-1]
    weights_other = other_core(outs[-1])
    both = [queries, other_core(queries)]

    if direct:
        far = partners(packed, FAR)
        room = pl.pallas_call(
            gate_kernel,
            out_shape=jax.ShapeDtypeStruct(packed.shape, BF16),
            in_specs=[vmem()],
            out_specs=vmem(),
            compiler_params=small,
            cost_estimate=cost(ROOM_COST),
            name="room",
        )(packed)
        near = partners(room, NEAR)
        corner = partners(room, CORNER, cores=(1,))
        relayed = partners(far, (1, 1))
        gated = pl.pallas_call(
            gate_kernel,
            out_shape=jax.ShapeDtypeStruct(far.shape, BF16),
            in_specs=[vmem()],
            out_specs=vmem(),
            compiler_params=small,
            cost_estimate=cost(GATE_COST),
            name="gate",
        )(far)
        *running, far_after = attend(
            "first", FIRST_COST, both, biases[0], [packed, near], passed=[gated]
        )
        last = [other_core(relayed)]
        running = attend(
            "second",
            SECOND_COST,
            both,
            biases[1],
            [corner, other_core(corner), other_core(near), far, other_core(far_after), relayed],
            running,
            paired=True,
        )
    else:
        last = []
        running = pl.pallas_call(
            gathered_kernel,
            out_shape=[jax.ShapeDtypeStruct((query_rows, size), F32) for size in (1, 1, DC)],
            in_specs=[vmem()] * 4,
            out_specs=[vmem()] * 3,
            scratch_shapes=[pltpu.VMEM((BLOCK_CHUNKS * rows, DC + DR), BF16)],
            compiler_params=pltpu.CompilerParams(vmem_limit_bytes=LARGE_VMEM),
            name="gathered",
        )(*both, biases[0], lax.all_gather(packed, "ctx", axis=0))

    tiles = 7 if width % 896 == 0 else 1
    return pl.pallas_call(
        functools.partial(finish_kernel, heads, len(last)),
        out_shape=jax.ShapeDtypeStruct((rows, width), BF16),
        in_specs=[vmem()] * (5 + len(biases[2:]) + len(last) + 3),
        out_specs=anywhere(),
        scratch_shapes=[
            pltpu.VMEM((rows, width), BF16),
            pltpu.VMEM((rows, DC + DR), BF16),
            pltpu.SemaphoreType.DMA((tiles,)),
        ],
        compiler_params=small,
        name="finish",
    )(*both, *running, *biases[2:], *last, value_up, out_proj, weights_other)


def solution(mesh):
    in_specs = (
        P(("docs", "ctx"), "heads"),
        P(("docs", "ctx"), "heads"),
        P(("docs", "ctx"), None),
        P(("docs", "ctx"), None),
        P(None, "heads"),
        P(None, "heads"),
        P("heads", None),
        P("docs"),
    )
    out_specs = P(("docs", "ctx"), "heads")
    return jax.shard_map(
        functools.partial(per_device, mesh.shape["ctx"]),
        mesh=mesh,
        in_specs=in_specs,
        out_specs=out_specs,
        check_vma=False,
    )
```
